32 devices in a mesh: dom: 4 (over z), sub: 8 (over y, x, core).
Axes of the slice: x: 2, y: 2, z: 4, core: 2. Of those that a mesh axis runs over, the one named last changes fastest.
Arguments:
- positions: float32 [3, 16, 64, 128], P(None, 'dom', 'sub'), may hold values from 0 to 1
- velocities: float32 [3, 16, 64, 128], P(None, 'dom', 'sub'), may hold values from -6 to 6
- masses: float32 [16, 64, 128], P('dom', 'sub'), may hold values from 0.0004 to 0.004
- smoothing: float32 [16, 64, 128], P('dom', 'sub'), may hold values from 0.3 to 0.6
- neighbours: int32 [16, 64, 5], P('dom', 'sub'), may hold values from 0 to 8, as said below
- particle_group: int32 [16, 64, 128], P('dom', 'sub'), may hold values from 0 to 1023, as said below
- group_row: int32 [1024], replicated, may hold values from 0 to 1023, as said below
Outputs:
- density: float32 [16, 64, 128], P('dom', 'sub')
- catalog: float32 [17, 1024], P(None, 'sub')
The draws below stay inside these ranges and needn't reach their ends.
Inputs may be any that keep to these rules, and one draw needn't show every extreme that they name: `neighbours`: each block lists 5 different codes of 0 to 8, the first one 4, the block itself. `particle_group`: a group g is owned by index group_row[g] // 128 of sub; at most 2048 of one device's particles belong to groups of any one owner, and on every device some owner gets exactly 2048 of them. `group_row`: a permutation of the catalog rows.
All inputs are finite; a program needn't handle non-finite values.
Results may differ from the reference program's by a relative error of at most 0.0003.
Values sent between devices are 32-bit elements; how exact they have to be, the bound alone decides.
No kernel may reach another device: no remote copies, remote signals or barrier semaphores. Data moves between devices by JAX's collectives and lax.ppermute only.
A program may use at most 64 MiB of HBM per device.

```python
import math
import jax
import jax.numpy as jnp
from jax import lax

BLOCK = 128
NBK = 5
BX = 4
BY = 8
GPD = 128
NXB = 16
NYB = 64
GROUPS = 1024
N_DOM = 4
N_SUB = 8


def catalog_rows(key):
    return jax.random.permutation(key, GROUPS)


def draw_group_row(key, part):
    row_of = catalog_rows(key)
    return row_of.astype(jnp.int32)


def draw_neighbours(key, part):
    key = jax.random.fold_in(key, 2)
    scores = jax.random.randint(key, (NXB, NYB, 8), 0, 1048576) * 8 + jnp.arange(8)
    order = jnp.argsort(scores, axis=-1)[..., :NBK - 1]
    others = jnp.array([0, 1, 2, 3, 5, 6, 7, 8], jnp.int32)
    picked = others[order]
    itself = jnp.full((NXB, NYB, 1), 4, jnp.int32)
    return jnp.concatenate([itself, picked], axis=-1).astype(jnp.int32)


def draw_particle_group(key, part):
    row_of = catalog_rows(key)
    key = jax.random.fold_in(key, 3)
    per_dev = BX * BY * BLOCK
    limit_cap = 4 * per_dev // N_SUB

    def one_device(dev_key):
        keys = jax.random.split(dev_key, 5)
        heavy = jax.random.randint(keys[0], (), 0, N_SUB)
        spread = jax.random.permutation(keys[1], (N_SUB - 1) * limit_cap)[:per_dev - limit_cap] // limit_cap
        owners = jnp.concatenate([jnp.full((limit_cap,), heavy), (heavy + 1 + spread) % N_SUB])
        owners = jax.random.permutation(keys[2], owners)
        upper = jax.random.randint(keys[3], (per_dev,), 1, GPD + 1)
        slot_ids = jax.random.randint(keys[4], (per_dev,), 0, upper)
        return owners * GPD + slot_ids
    rows = jax.vmap(one_device)(jax.random.split(key, N_DOM * N_SUB))
    rows = rows.reshape(N_DOM, N_SUB, BX, BY, BLOCK).transpose(0, 2, 1, 3, 4).reshape(NXB, NYB, BLOCK)
    inverse = jnp.argsort(row_of)
    return inverse[rows].astype(jnp.int32)


def block_scale(key, shape, shards, low, largest):
    def one(dim, blocks):
        draws = jax.random.uniform(jax.random.fold_in(jax.random.fold_in(key, 6), dim), (blocks,), jnp.float32, low / len(shards), largest / len(shards))
        return jnp.repeat(jnp.exp(draws), shape[dim] // blocks).reshape((-1,) + (1,) * (len(shape) - dim - 1))

    factor_of = one(*shards[0])
    for cut in shards[1:]:
        factor_of = factor_of * one(*cut)
    return factor_of


def normal_values(rng, shape, deviation, most, cuts=(), dtype=jnp.bfloat16):
    level = block_scale(rng, shape, cuts, -0.22, 0.18) if cuts else 1.0
    values = jax.random.normal(rng, shape, jnp.float32) * deviation * level
    return jnp.minimum(jnp.maximum(values, -most), most).astype(dtype)


def setup_inputs(seed: int = 0) -> dict:
    splits = jax.random.split(jax.random.key(seed), 8)
    return {
        "positions": jnp.clip(1.0 * jax.random.uniform(splits[0], (3, NXB, NYB, BLOCK), jnp.float32) ** block_scale(splits[0], (3, NXB, NYB, BLOCK), ((1, 4), (2, 8)), -0.2, 0.2), 0.0, 1.0),
        "velocities": normal_values(splits[1], (3, NXB, NYB, BLOCK), 1.0, 6.0, ((1, 4), (2, 8)), jnp.float32),
        "masses": jnp.clip(jnp.exp(math.log(0.004) - 2.3025852 * jax.random.uniform(splits[2], (NXB, NYB, BLOCK), jnp.float32) ** block_scale(splits[2], (NXB, NYB, BLOCK), ((0, 4), (1, 8)), -0.2, 0.2)), 0.0004, 0.004),
        "smoothing": jnp.clip(jnp.exp(math.log(0.6) - 0.6931472 * jax.random.uniform(splits[3], (NXB, NYB, BLOCK), jnp.float32) ** block_scale(splits[3], (NXB, NYB, BLOCK), ((0, 4), (1, 8)), -0.2, 0.2)), 0.3, 0.6),
        "neighbours": draw_neighbours(jax.random.fold_in(splits[7], 71), 0),
        "particle_group": draw_particle_group(jax.random.fold_in(splits[7], 71), 0),
        "group_row": draw_group_row(jax.random.fold_in(splits[7], 71), 0),
    }


def split_lead(array, axis_pos, parts):
    shape = array.shape
    reshaped = array.reshape(shape[:axis_pos] + (parts, shape[axis_pos] // parts) + shape[axis_pos + 1:])
    return jnp.moveaxis(reshaped, axis_pos, 0)

def pair_density(own_pos, radius, nearby, offset):
    separation = own_pos[:, :, None, :, None] - nearby[:3, :, :, None, :] - offset[:, :, :, None, None]
    distance = jnp.sqrt(lax.optimization_barrier(jnp.sum(separation * separation, axis=0)))
    scaled = distance / radius[:, None, :, None]
    falloff = jnp.maximum(1.0 - 0.5 * scaled, 0.0)
    kernel = falloff * falloff * falloff * falloff * (1.0 + 2.0 * scaled)
    summed = lax.optimization_barrier(jnp.sum(kernel * nearby[3][:, :, None, :], axis=(1, 3)))
    return summed * (21.0 / (16.0 * math.pi)) / (radius * radius * radius)

def moments(columns):
    mass_col, pos_x, pos_y, pos_z, vel_x, vel_y, vel_z, dens_col = [columns[i] for i in range(8)]
    return jnp.stack([mass_col, mass_col * pos_x, mass_col * pos_y, mass_col * pos_z, mass_col * vel_x, mass_col * vel_y, mass_col * vel_z, mass_col * (pos_y * vel_z - pos_z * vel_y), mass_col * (pos_z * vel_x - pos_x * vel_z), mass_col * (pos_x * vel_y - pos_y * vel_x), mass_col * pos_x * pos_x, mass_col * pos_y * pos_y, mass_col * pos_z * pos_z, mass_col * pos_x * pos_y, mass_col * pos_x * pos_z, mass_col * pos_y * pos_z, mass_col * dens_col])

def reference(positions, velocities, masses, smoothing, neighbours, particle_group, group_row):
    packed = jnp.concatenate([positions, masses[None]], axis=0)
    step_x = neighbours // 3 - 1
    step_y = neighbours % 3 - 1
    group_len = math.gcd(NYB, 32)
    turns = NYB // group_len

    def one_row(row_index):
        sx = step_x[row_index]
        sy = step_y[row_index]
        x_rows = (row_index + sx) % NXB
        y_rows = (jnp.arange(NYB)[:, None] + sy) % NYB
        nearby = packed[:, x_rows, y_rows]
        offset = jnp.stack([sx, sy, jnp.zeros_like(sx)]).astype(jnp.float32)
        own_pos = positions[:, row_index]
        radius = smoothing[row_index]

        def one_turn(pieces):
            return pair_density(pieces[0], pieces[1], pieces[2], pieces[3])
        result = lax.map(one_turn, (split_lead(own_pos, 1, turns), split_lead(radius, 0, turns), split_lead(nearby, 1, turns), split_lead(offset, 1, turns)))
        return result.reshape(NYB, BLOCK)
    density = lax.map(one_row, jnp.arange(NXB))
    x_index = jnp.arange(NXB).astype(jnp.float32)[:, None, None]
    y_index = jnp.arange(NYB).astype(jnp.float32)[None, :, None]
    glob_x = (x_index + positions[0]) / jnp.float32(NXB)
    glob_y = (y_index + positions[1]) / jnp.float32(NYB)
    columns = jnp.stack([masses, glob_x, glob_y, positions[2], velocities[0], velocities[1], velocities[2], density]).reshape(8, -1)
    features = moments(columns)
    rows_flat = group_row[particle_group.reshape(-1)]
    catalog = jnp.zeros((17, GROUPS), jnp.float32).at[:, rows_flat].add(features)
    return (density, catalog)
```

```python
import functools
import math

import jax
import jax.numpy as jnp
from jax import lax
from jax.experimental import pallas as pl
from jax.experimental.pallas import tpu as pltpu
from jax.sharding import PartitionSpec as P

F32 = jnp.float32
BF16 = jnp.bfloat16
LANES = 128
EARLY = 16
DENSITY_FACTOR = 21.0 / (16.0 * math.pi) / 256.0
VMEM = pl.BlockSpec(memory_space=pltpu.VMEM)
SMEM = pl.BlockSpec(memory_space=pltpu.SMEM)
NT = (((1,), (1,)), ((), ()))


def params():
    return pltpu.CompilerParams(vmem_limit_bytes=40 * 1024 * 1024)


def rounded(value):
    return value.astype(BF16).astype(F32)


def three_parts(value):
    first = rounded(value)
    rest = value - first
    second = rounded(rest)
    return first, second, rest - second


def slot_one_hot(slots, y):
    row = jnp.broadcast_to(slots[y : y + 1, :], (LANES, LANES))
    ids = lax.broadcasted_iota(jnp.int32, (LANES, LANES), 0)
    return jnp.where(ids == row, 1.0, 0.0).astype(BF16)


def moments_kernel(
    nx_total, ny_total, pos_ref, vel_ref, mass_ref, group_ref, row_ref,
    table_ref, rows_ref, feat_ref, lhs_ref, hot_ref,
):
    blocks_x, blocks_y, _ = mass_ref.shape
    owners = table_ref.shape[0]
    table_rows = row_ref.shape[0]
    base_x = (lax.axis_index("dom") * blocks_x).astype(F32)
    base_y = (lax.axis_index("sub") * blocks_y).astype(F32)
    y_iota = lax.broadcasted_iota(jnp.int32, (blocks_y, LANES), 0).astype(F32)
    total = jnp.zeros((owners * 2 * EARLY, LANES), F32)
    for x in range(blocks_x):
        group = group_ref[x]
        low = group & (LANES - 1)
        high = group >> 7
        rows = jnp.zeros_like(group)
        for r in range(table_rows):
            line = jnp.broadcast_to(row_ref[r : r + 1, :], group.shape)
            picked = jnp.take_along_axis(line, low, axis=1)
            rows = jnp.where(high == r, picked, rows)
        rows_ref[x] = rows
        mass = mass_ref[x]
        gx = (base_x + float(x) + pos_ref[0, x]) / float(nx_total)
        gy = (base_y + y_iota + pos_ref[1, x]) / float(ny_total)
        gz = pos_ref[2, x]
        vx, vy, vz = vel_ref[0, x], vel_ref[1, x], vel_ref[2, x]
        mx, my, mz = mass * gx, mass * gy, mass * gz
        features = (
            mass, mx, my, mz, mass * vx, mass * vy, mass * vz,
            mass * (gy * vz - gz * vy), mass * (gz * vx - gx * vz), mass * (gx * vy - gy * vx),
            mx * gx, my * gy, mz * gz, mx * gy, mx * gz, my * gz,
        )
        for f, feature in enumerate(features):
            start = (x * EARLY + f) * blocks_y
            feat_ref[start : start + blocks_y, :] = feature
        slots = rows & (LANES - 1)
        owner = rows >> 7
        for y in range(blocks_y):
            lanes = slice(y * LANES, (y + 1) * LANES)
            feats = feat_ref[pl.ds(x * EARLY * blocks_y + y, EARLY, stride=blocks_y), :]
            high_part = rounded(feats)
            both = jnp.concatenate([high_part, feats - high_part], axis=0)
            owner_row = jnp.broadcast_to(owner[y : y + 1, :], both.shape)
            for o in range(owners):
                lhs_ref[o * 2 * EARLY : (o + 1) * 2 * EARLY, lanes] = jnp.where(
                    owner_row == o, both, 0.0
                ).astype(BF16)
            hot_ref[:, lanes] = slot_one_hot(slots, y)
        total = total + lax.dot_general(
            lhs_ref[...], hot_ref[...], NT, preferred_element_type=F32
        )
    total = total.reshape(owners, 2 * EARLY, LANES)
    table_ref[...] = total[:, :EARLY, :] + total[:, EARLY:, :]


def target_rows(pos, radius):
    weight = 4.0 / (radius * radius)
    cx, cy, cz = pos[0] - 0.5, pos[1] - 0.5, pos[2] - 0.5
    lines = (
        -2.0 * cx * weight, -2.0 * cy * weight, -2.0 * cz * weight,
        weight, weight, weight,
        (cx * cx + cy * cy + cz * cz) * weight, jnp.zeros_like(weight),
    )
    parts = [three_parts(line) for line in lines]
    return [part[k] for k in range(3) for part in parts]


def target_matrix(coef):
    one, two, three = coef[0:8], coef[8:16], coef[16:24]
    stacked = jnp.concatenate([one, one, two, two, one, three], axis=0)
    return stacked.T.astype(BF16)


def source_matrix(line, squares):
    value = jnp.where(squares, line * line, line)
    one, two, three = three_parts(value)
    first = jnp.concatenate([one, two], axis=0).astype(BF16)
    last = jnp.concatenate([three, one], axis=0).astype(BF16)
    return jnp.concatenate([first, first, last], axis=0)


def store_source(nat_ref, start, count, columns):
    cx, cy, cz = [column - 0.5 for column in columns]
    one = jnp.ones_like(cx)
    zero = jnp.zeros_like(cx)
    for kind, line in enumerate((cx, cy, cz, cx, cy, cz, one, zero)):
        nat_ref[start + kind * 8 : start + kind * 8 + count, :] = line


def pair_sum(target, sources, weights):
    total = None
    for first in range(0, len(sources), 2):
        group = sources[first : first + 2]
        right = group[0] if len(group) == 1 else jnp.concatenate(group, axis=1)
        squared = jnp.dot(target, right, preferred_element_type=F32)
        for k in range(len(group)):
            t = squared[:, k * LANES : (k + 1) * LANES]
            t = jnp.minimum(jnp.maximum(t, 1e-12), 16.0)
            u = t * lax.rsqrt(t)
            f = 4.0 - u
            f = f * f
            f = f * f
            w = weights[first + k]
            term = f * (w + w * u)
            total = term if total is None else total + term
    return total


def row_sum(total):
    return jnp.sum(total.T, axis=0, keepdims=True)


def square_mask():
    kind = lax.broadcasted_iota(jnp.int32, (8, LANES), 0)
    return (kind >= 3) & (kind < 6)


def near_kernel(
    code_ref, pos_ref, mass_ref, smooth_ref, prev_ref, next_ref,
    out_ref, nat_ref, src_ref, weight_ref, shift_ref, tgt_ref,
):
    blocks_x, blocks_y, _ = mass_ref.shape
    listed = code_ref.shape[0] // (blocks_x * blocks_y)
    null = (blocks_x + 2) * blocks_y
    for xe in range(blocks_x + 2):
        if xe == 0:
            columns, mass = [prev_ref[c, 0] for c in range(3)], prev_ref[3, 0]
        elif xe == blocks_x + 1:
            columns, mass = [next_ref[c, 0] for c in range(3)], next_ref[3, 0]
        else:
            columns, mass = [pos_ref[c, xe - 1] for c in range(3)], mass_ref[xe - 1]
        store_source(nat_ref, xe * 64, blocks_y, columns)
        weight_ref[xe * blocks_y : (xe + 1) * blocks_y, :] = mass
        for y in range(blocks_y):
            src_ref[xe * blocks_y + y] = nat_ref[pl.ds(xe * 64 + y, 8, stride=8), :]
    src_ref[null] = jnp.zeros((8, LANES), F32)
    weight_ref[null : null + 8, :] = jnp.zeros((8, LANES), F32)
    kind = lax.broadcasted_iota(jnp.int32, (8, LANES), 0)
    for code in range(9):
        along_x = jnp.where((kind == 0) | (kind == 3), float(code // 3 - 1), 0.0)
        along_y = jnp.where((kind == 1) | (kind == 4), float(code % 3 - 1), 0.0)
        shift_ref[code] = along_x + along_y
    squares = square_mask()
    for x in range(blocks_x):
        lines = target_rows([pos_ref[c, x] for c in range(3)], smooth_ref[x])
        for k, line in enumerate(lines):
            tgt_ref[x, k * blocks_y : (k + 1) * blocks_y, :] = line

    def one_x(x, carry):
        sums = []
        for y in range(blocks_y):
            target = target_matrix(tgt_ref[x, pl.ds(y, 24, stride=blocks_y), :])
            sources, weights = [], []
            for k in range(listed):
                code = code_ref[(x * blocks_y + y) * listed + k]
                step_x = (code * 11) >> 5
                near_y = y + code - 3 * step_x - 1
                inside = (near_y >= 0) & (near_y < blocks_y)
                index = jnp.where(inside, (x + step_x) * blocks_y + near_y, null)
                sources.append(source_matrix(src_ref[index] + shift_ref[code], squares))
                weights.append(
                    jnp.broadcast_to(weight_ref[pl.ds(index, 1), :], (LANES, LANES))
                )
            sums.append(row_sum(pair_sum(target, sources, weights)))
        out_ref[x] = jnp.concatenate(sums, axis=0)
        return carry

    lax.fori_loop(0, blocks_x, one_x, 0)


def rim_kernel(
    code_ref, near_ref, pos_ref, mass_ref, smooth_ref, low_ref, high_ref, rows_ref, early_ref,
    density_ref, table_ref, nat_ref, tgt_ref, sum_ref, md_ref, lhs_ref, hot_ref,
):
    blocks_x, blocks_y, _ = mass_ref.shape
    owners = early_ref.shape[0]
    listed = code_ref.shape[0] // (blocks_x * blocks_y)
    for side, ref in enumerate((low_ref, high_ref)):
        store_source(nat_ref, side * 64, blocks_x + 2, [ref[c] for c in range(3)])
    kind = lax.broadcasted_iota(jnp.int32, (8, LANES), 0)
    squares = square_mask()
    total = jnp.zeros((2 * owners, LANES), F32)
    owner_ids = lax.broadcasted_iota(jnp.int32, (owners, LANES), 0)
    for x in range(blocks_x):
        lines = target_rows([pos_ref[c, x] for c in range(3)], smooth_ref[x])
        for k, line in enumerate(lines):
            tgt_ref[x, k * blocks_y : (k + 1) * blocks_y, :] = line
        sum_ref[x] = near_ref[x]
        for side, ref in enumerate((low_ref, high_ref)):
            y = side * (blocks_y - 1)
            target = target_matrix(tgt_ref[x, pl.ds(y, 24, stride=blocks_y), :])
            sources, weights = [], []
            for step_x in range(3):
                wanted = step_x * 3 + side * 2
                found = code_ref[(x * blocks_y + y) * listed] == wanted
                for k in range(1, listed):
                    found = found | (code_ref[(x * blocks_y + y) * listed + k] == wanted)
                flag = jnp.where(found, 1.0, 0.0)
                along_x = jnp.where((kind == 0) | (kind == 3), float(step_x - 1), 0.0)
                along_y = jnp.where((kind == 1) | (kind == 4), float(side * 2 - 1), 0.0)
                line = nat_ref[pl.ds(side * 64 + x + step_x, 8, stride=8), :]
                sources.append(source_matrix(line + along_x + along_y, squares))
                mass = ref[3, x + step_x : x + step_x + 1, :] * flag
                weights.append(jnp.broadcast_to(mass, (LANES, LANES)))
            sum_ref[x, y : y + 1, :] += row_sum(pair_sum(target, sources, weights))
        radius = smooth_ref[x]
        density = sum_ref[x] * DENSITY_FACTOR / (radius * radius * radius)
        density_ref[x] = density
        moment = mass_ref[x] * density
        high_part = rounded(moment)
        low_part = moment - high_part
        rows = rows_ref[x]
        slots = rows & (LANES - 1)
        owner = rows >> 7
        for y in range(blocks_y):
            lanes = slice(y * LANES, (y + 1) * LANES)
            mine = jnp.broadcast_to(owner[y : y + 1, :], owner_ids.shape) == owner_ids
            lhs_ref[:, lanes] = jnp.concatenate(
                [
                    jnp.where(mine, jnp.broadcast_to(part[y : y + 1, :], mine.shape), 0.0)
                    for part in (high_part, low_part)
                ],
                axis=0,
            ).astype(BF16)
            hot_ref[:, lanes] = slot_one_hot(slots, y)
        total = total + lax.dot_general(
            lhs_ref[...], hot_ref[...], NT, preferred_element_type=F32
        )
    md_ref[...] = total[:owners] + total[owners:]
    for o in range(owners):
        table_ref[o, :EARLY, :] = early_ref[o]
        table_ref[o, EARLY : EARLY + 1, :] = md_ref[o : o + 1, :]


def ring(value, axis, step):
    count = lax.axis_size(axis)
    return lax.ppermute(value, axis, [(i, (i + step) % count) for i in range(count)])


def summed(value, axis):
    count = lax.axis_size(axis)
    if count & (count - 1):
        return lax.psum(value, axis)
    parts = [value] + [
        lax.ppermute(value, axis, [(i, i ^ step) for i in range(count)])
        for step in range(1, count)
    ]
    while len(parts) > 1:
        parts = [parts[k] + parts[k + 1] for k in range(0, len(parts), 2)]
    return parts[0]


def shards(positions, velocities, masses, smoothing, neighbours, particle_group, group_row):
    blocks_x, blocks_y, block_len = masses.shape
    dom_count, sub_count = lax.axis_size("dom"), lax.axis_size("sub")
    owners = sub_count
    chunk = blocks_y * block_len
    packed = jnp.concatenate([positions, masses[None]], axis=0)
    prev = ring(packed[:, blocks_x - 1 :], "dom", 1)
    following = ring(packed[:, :1], "dom", -1)
    early, rows = pl.pallas_call(
        functools.partial(moments_kernel, blocks_x * dom_count, blocks_y * sub_count),
        out_shape=(
            jax.ShapeDtypeStruct((owners, EARLY, LANES), F32),
            jax.ShapeDtypeStruct(masses.shape, jnp.int32),
        ),
        in_specs=[VMEM] * 5,
        out_specs=(VMEM, VMEM),
        scratch_shapes=[
            pltpu.VMEM((blocks_x * EARLY * blocks_y, LANES), F32),
            pltpu.VMEM((owners * 2 * EARLY, chunk), BF16),
            pltpu.VMEM((LANES, chunk), BF16),
        ],
        compiler_params=params(),
        cost_estimate=pl.CostEstimate(flops=500_000_000, bytes_accessed=400_000, transcendentals=0),
        name="moments_by_row",
    )(positions, velocities, masses, particle_group, group_row.reshape(-1, LANES))
    whole = jnp.concatenate([prev, packed, following], axis=1)
    low = ring(whole[:, :, blocks_y - 1, :], "sub", 1)
    high = ring(whole[:, :, 0, :], "sub", -1)
    codes = neighbours.reshape(-1)
    near = pl.pallas_call(
        near_kernel,
        out_shape=jax.ShapeDtypeStruct(masses.shape, F32),
        in_specs=[SMEM] + [VMEM] * 5,
        out_specs=VMEM,
        scratch_shapes=[
            pltpu.VMEM(((blocks_x + 2) * 64, LANES), F32),
            pltpu.VMEM(((blocks_x + 2) * blocks_y + 1, 8, LANES), F32),
            pltpu.VMEM(((blocks_x + 2) * blocks_y + 8, LANES), F32),
            pltpu.VMEM((9, 8, LANES), F32),
            pltpu.VMEM((blocks_x, 24 * blocks_y, LANES), F32),
        ],
        compiler_params=params(),
        cost_estimate=pl.CostEstimate(
            flops=1_000_000_000, bytes_accessed=400_000, transcendentals=2_600_000
        ),
        name="near_pairs",
    )(codes, positions, masses, smoothing, prev, following)
    density, table = pl.pallas_call(
        rim_kernel,
        out_shape=(
            jax.ShapeDtypeStruct(masses.shape, F32),
            jax.ShapeDtypeStruct((owners, EARLY + 1, LANES), F32),
        ),
        in_specs=[SMEM] + [VMEM] * 8,
        out_specs=(VMEM, VMEM),
        scratch_shapes=[
            pltpu.VMEM((128, LANES), F32),
            pltpu.VMEM((blocks_x, 24 * blocks_y, LANES), F32),
            pltpu.VMEM(masses.shape, F32),
            pltpu.VMEM((owners, LANES), F32),
            pltpu.VMEM((2 * owners, chunk), BF16),
            pltpu.VMEM((LANES, chunk), BF16),
        ],
        compiler_params=params(),
        cost_estimate=pl.CostEstimate(
            flops=200_000_000, bytes_accessed=400_000, transcendentals=400_000
        ),
        name="rim_pairs",
    )(codes, near, positions, masses, smoothing, low, high, rows, early)
    got = lax.all_to_all(table, "sub", split_axis=0, concat_axis=0, tiled=True)
    mine = jnp.sum(got, axis=0)
    return (density, summed(mine, "dom"))


def solution(mesh):
    in_specs = (
        P(None, "dom", "sub", None),
        P(None, "dom", "sub", None),
        P("dom", "sub", None),
        P("dom", "sub", None),
        P("dom", "sub", None),
        P("dom", "sub", None),
        P(),
    )
    out_specs = (P("dom", "sub", None), P(None, "sub"))
    return jax.shard_map(shards, mesh=mesh, in_specs=in_specs, out_specs=out_specs, check_vma=False)
```

```python
import functools
import math

import jax
import jax.numpy as jnp
from jax import lax
from jax.experimental import pallas as pl
from jax.experimental.pallas import tpu as pltpu
from jax.sharding import PartitionSpec as P

F32 = jnp.float32
BF16 = jnp.bfloat16
LANES = 128
EARLY = 16
DENSITY_FACTOR = 21.0 / (16.0 * math.pi) / 256.0
VMEM = pl.BlockSpec(memory_space=pltpu.VMEM)
SMEM = pl.BlockSpec(memory_space=pltpu.SMEM)
NT = (((1,), (1,)), ((), ()))


def params():
    return pltpu.CompilerParams(vmem_limit_bytes=40 * 1024 * 1024)


def rounded(value):
    return value.astype(BF16).astype(F32)


def three_parts(value):
    first = rounded(value)
    rest = value - first
    second = rounded(rest)
    return first, second, rest - second


def slot_one_hot(slots, y):
    row = jnp.broadcast_to(slots[y : y + 1, :], (LANES, LANES))
    ids = lax.broadcasted_iota(jnp.int32, (LANES, LANES), 0)
    return jnp.where(ids == row, 1.0, 0.0).astype(BF16)


def sum_moments(
    nx_total, ny_total, pos_ref, vel_ref, mass_ref, group_ref, row_ref,
    table_ref, rows_ref, hot_ref, feat_ref, lhs_ref,
):
    blocks_x, blocks_y, _ = mass_ref.shape
    owners = table_ref.shape[0]
    table_rows = row_ref.shape[0]
    base_x = (lax.axis_index("dom") * blocks_x).astype(F32)
    base_y = (lax.axis_index("sub") * blocks_y).astype(F32)
    y_iota = lax.broadcasted_iota(jnp.int32, (blocks_y, LANES), 0).astype(F32)
    total = jnp.zeros((owners * 2 * EARLY, LANES), F32)
    for x in range(blocks_x):
        group = group_ref[x]
        low = group & (LANES - 1)
        high = group >> 7
        rows = jnp.zeros_like(group)
        for r in range(table_rows):
            line = jnp.broadcast_to(row_ref[r : r + 1, :], group.shape)
            picked = jnp.take_along_axis(line, low, axis=1)
            rows = jnp.where(high == r, picked, rows)
        rows_ref[x] = rows
        mass = mass_ref[x]
        gx = (base_x + float(x) + pos_ref[0, x]) / float(nx_total)
        gy = (base_y + y_iota + pos_ref[1, x]) / float(ny_total)
        gz = pos_ref[2, x]
        vx, vy, vz = vel_ref[0, x], vel_ref[1, x], vel_ref[2, x]
        mx, my, mz = mass * gx, mass * gy, mass * gz
        features = (
            mass, mx, my, mz, mass * vx, mass * vy, mass * vz,
            mass * (gy * vz - gz * vy), mass * (gz * vx - gx * vz), mass * (gx * vy - gy * vx),
            mx * gx, my * gy, mz * gz, mx * gy, mx * gz, my * gz,
        )
        for f, feature in enumerate(features):
            start = (x * EARLY + f) * blocks_y
            feat_ref[start : start + blocks_y, :] = feature
        slots = rows & (LANES - 1)
        owner = rows >> 7
        for y in range(blocks_y):
            lanes = slice(y * LANES, (y + 1) * LANES)
            feats = feat_ref[pl.ds(x * EARLY * blocks_y + y, EARLY, stride=blocks_y), :]
            high_part = rounded(feats)
            both = jnp.concatenate([high_part, feats - high_part], axis=0)
            owner_row = jnp.broadcast_to(owner[y : y + 1, :], both.shape)
            for o in range(owners):
                lhs_ref[o * 2 * EARLY : (o + 1) * 2 * EARLY, lanes] = jnp.where(
                    owner_row == o, both, 0.0
                ).astype(BF16)
            hot_ref[x, :, lanes] = slot_one_hot(slots, y)
        total = total + lax.dot_general(
            lhs_ref[...], hot_ref[x], NT, preferred_element_type=F32
        )
    total = total.reshape(owners, 2 * EARLY, LANES)
    table_ref[...] = total[:, :EARLY, :] + total[:, EARLY:, :]


def target_rows(pos, radius):
    weight = 4.0 / (radius * radius)
    cx, cy, cz = pos[0] - 0.5, pos[1] - 0.5, pos[2] - 0.5
    lines = (
        -2.0 * cx * weight, -2.0 * cy * weight, -2.0 * cz * weight,
        weight, weight, weight,
        (cx * cx + cy * cy + cz * cz) * weight, jnp.zeros_like(weight),
    )
    parts = [three_parts(line) for line in lines]
    return [part[k] for k in range(3) for part in parts]


def target_matrix(coef):
    one, two, three = coef[0:8], coef[8:16], coef[16:24]
    stacked = jnp.concatenate([one, one, two, two, one, three], axis=0)
    return stacked.T.astype(BF16)


def source_matrix(line, squares):
    value = jnp.where(squares, line * line, line)
    one, two, three = three_parts(value)
    first = jnp.concatenate([one, two], axis=0).astype(BF16)
    last = jnp.concatenate([three, one], axis=0).astype(BF16)
    return jnp.concatenate([first, first, last], axis=0)


def store_source(nat_ref, start, count, columns):
    cx, cy, cz = [column - 0.5 for column in columns]
    one = jnp.ones_like(cx)
    zero = jnp.zeros_like(cx)
    for kind, line in enumerate((cx, cy, cz, cx, cy, cz, one, zero)):
        nat_ref[start + kind * 8 : start + kind * 8 + count, :] = line


def pair_sum(target, sources, weights):
    total = None
    for first in range(0, len(sources), 2):
        group = sources[first : first + 2]
        right = group[0] if len(group) == 1 else jnp.concatenate(group, axis=1)
        squared = jnp.dot(target, right, preferred_element_type=F32)
        for k in range(len(group)):
            t = squared[:, k * LANES : (k + 1) * LANES]
            t = jnp.minimum(jnp.maximum(t, 1e-12), 16.0)
            u = t * lax.rsqrt(t)
            f = 4.0 - u
            f = f * f
            f = f * f
            w = weights[first + k]
            term = f * (w + w * u)
            total = term if total is None else total + term
    return total


def column_sums(totals):
    lane = lax.broadcasted_iota(jnp.int32, (LANES, LANES), 1)
    columns = jnp.zeros((LANES, LANES), F32)
    for k, total in enumerate(totals):
        columns = jnp.where(lane == k, jnp.sum(total, axis=1, keepdims=True), columns)
    return columns.T[: len(totals), :]


def square_mask():
    kind = lax.broadcasted_iota(jnp.int32, (8, LANES), 0)
    return (kind >= 3) & (kind < 6)


def block_pairs(
    x_first, x_step, x_count, code_ref, pos_ref, mass_ref, smooth_ref, prev_ref, next_ref,
    out_ref, match_ref, nat_ref, src_ref, weight_ref, shift_ref, tgt_ref,
):
    blocks_x, blocks_y, _ = mass_ref.shape
    listed = code_ref.shape[0] // (blocks_x * blocks_y)
    null = (blocks_x + 2) * blocks_y
    for xe in range(blocks_x + 2):
        if xe == 0 or xe == blocks_x + 1:
            ref = prev_ref if xe == 0 else next_ref
            if ref is None:
                continue
            columns, mass = [ref[c] for c in range(3)], ref[3]
        else:
            columns, mass = [pos_ref[c, xe - 1] for c in range(3)], mass_ref[xe - 1]
        store_source(nat_ref, xe * 64, blocks_y, columns)
        weight_ref[xe * blocks_y : (xe + 1) * blocks_y, :] = mass
        for y in range(blocks_y):
            src_ref[xe * blocks_y + y] = nat_ref[pl.ds(xe * 64 + y, 8, stride=8), :]
    src_ref[null] = jnp.zeros((8, LANES), F32)
    weight_ref[null : null + 8, :] = jnp.zeros((8, LANES), F32)
    kind = lax.broadcasted_iota(jnp.int32, (8, LANES), 0)
    for code in range(9):
        along_x = jnp.where((kind == 0) | (kind == 3), float(code // 3 - 1), 0.0)
        along_y = jnp.where((kind == 1) | (kind == 4), float(code % 3 - 1), 0.0)
        shift_ref[code] = along_x + along_y
    squares = square_mask()
    for k in range(x_count):
        x = x_first + k * x_step
        lines = target_rows([pos_ref[c, x] for c in range(3)], smooth_ref[x])
        for row, line in enumerate(lines):
            tgt_ref[k, row * blocks_y : (row + 1) * blocks_y, :] = line

    def one_x(turn, carry):
        x = x_first + turn * x_step
        totals = []
        for y in range(blocks_y):
            target = target_matrix(tgt_ref[turn, pl.ds(y, 24, stride=blocks_y), :])
            if y == 0:
                match_ref[turn, 0] = target
            if y == blocks_y - 1:
                match_ref[turn, 1] = target
            sources, weights = [], []
            for k in range(listed):
                code = code_ref[(x * blocks_y + y) * listed + k]
                step_x = (code * 11) >> 5
                near_y = y + code - 3 * step_x - 1
                inside = (near_y >= 0) & (near_y < blocks_y)
                index = jnp.where(inside, (x + step_x) * blocks_y + near_y, null)
                sources.append(source_matrix(src_ref[index] + shift_ref[code], squares))
                weights.append(
                    jnp.broadcast_to(weight_ref[pl.ds(index, 1), :], (LANES, LANES))
                )
            totals.append(pair_sum(target, sources, weights))
        out_ref[turn] = column_sums(totals)
        return carry

    lax.fori_loop(0, x_count, one_x, 0)


def first_kernel(
    nx_total, ny_total, code_ref, pos_ref, vel_ref, mass_ref, smooth_ref, group_ref, row_ref,
    table_ref, rows_ref, hot_ref, column_ref, out_ref, match_ref,
    feat_ref, lhs_ref, *scratch,
):
    blocks_x, blocks_y, _ = mass_ref.shape
    for side in range(2):
        y = side * (blocks_y - 1)
        for x in range(blocks_x):
            for c in range(3):
                column_ref[side, c, x : x + 1, :] = pos_ref[c, x, y : y + 1, :]
            column_ref[side, 3, x : x + 1, :] = mass_ref[x, y : y + 1, :]
    sum_moments(
        nx_total, ny_total, pos_ref, vel_ref, mass_ref, group_ref, row_ref,
        table_ref, rows_ref, hot_ref, feat_ref, lhs_ref,
    )
    block_pairs(
        1, 1, blocks_x - 2, code_ref, pos_ref, mass_ref, smooth_ref, None, None,
        out_ref, match_ref, *scratch,
    )


def edge_kernel(
    code_ref, pos_ref, mass_ref, smooth_ref, prev_ref, next_ref, out_ref, match_ref, *scratch
):
    blocks_x = mass_ref.shape[0]
    block_pairs(
        0, blocks_x - 1, 2, code_ref, pos_ref, mass_ref, smooth_ref, prev_ref, next_ref,
        out_ref, match_ref, *scratch,
    )


def pair_scratch(blocks_x, blocks_y, x_count):
    return [
        pltpu.VMEM(((blocks_x + 2) * 64, LANES), F32),
        pltpu.VMEM(((blocks_x + 2) * blocks_y + 1, 8, LANES), F32),
        pltpu.VMEM(((blocks_x + 2) * blocks_y + 8, LANES), F32),
        pltpu.VMEM((9, 8, LANES), F32),
        pltpu.VMEM((x_count, 24 * blocks_y, LANES), F32),
    ]


def reversed_bits(value, bits):
    return sum(((value >> k) & 1) << (bits - 1 - k) for k in range(bits))


def rim_kernel(
    code_ref, middle_ref, edge_ref, middle_match_ref, edge_match_ref, mass_ref, smooth_ref,
    low_ref, high_ref, rows_ref, hot_ref, early_ref,
    density_ref, table_ref, nat_ref, sum_ref, md_ref, lhs_ref,
):
    blocks_x, blocks_y, _ = mass_ref.shape
    owners = early_ref.shape[0]
    listed = code_ref.shape[0] // (blocks_x * blocks_y)
    for side, ref in enumerate((low_ref, high_ref)):
        store_source(nat_ref, side * 64, blocks_x + 2, [ref[c] for c in range(3)])
    kind = lax.broadcasted_iota(jnp.int32, (8, LANES), 0)
    squares = square_mask()
    totals = []
    for x in range(blocks_x):
        edge = x == 0 or x == blocks_x - 1
        turn = (1 if x else 0) if edge else x - 1
        sum_ref[x] = (edge_ref if edge else middle_ref)[turn]
        for side, ref in enumerate((low_ref, high_ref)):
            y = side * (blocks_y - 1)
            target = (edge_match_ref if edge else middle_match_ref)[turn, side]
            sources, weights = [], []
            for step_x in range(3):
                wanted = step_x * 3 + side * 2
                found = code_ref[(x * blocks_y + y) * listed] == wanted
                for k in range(1, listed):
                    found = found | (code_ref[(x * blocks_y + y) * listed + k] == wanted)
                flag = jnp.where(found, 1.0, 0.0)
                along_x = jnp.where((kind == 0) | (kind == 3), float(step_x - 1), 0.0)
                along_y = jnp.where((kind == 1) | (kind == 4), float(side * 2 - 1), 0.0)
                line = nat_ref[pl.ds(side * 64 + x + step_x, 8, stride=8), :]
                sources.append(source_matrix(line + along_x + along_y, squares))
                mass = ref[3, x + step_x : x + step_x + 1, :] * flag
                weights.append(jnp.broadcast_to(mass, (LANES, LANES)))
            totals.append(pair_sum(target, sources, weights))
    sums = column_sums(totals)
    total = jnp.zeros((LANES, 2 * owners), F32)
    owner_ids = lax.broadcasted_iota(jnp.int32, (owners, LANES), 0)
    for x in range(blocks_x):
        for side in range(2):
            y = side * (blocks_y - 1)
            sum_ref[x, y : y + 1, :] += sums[2 * x + side : 2 * x + side + 1, :]
        radius = smooth_ref[x]
        density = sum_ref[x] * DENSITY_FACTOR / (radius * radius * radius)
        density_ref[x] = density
        moment = mass_ref[x] * density
        high_part = rounded(moment)
        low_part = moment - high_part
        owner = rows_ref[x] >> 7
        for y in range(blocks_y):
            lanes = slice(y * LANES, (y + 1) * LANES)
            mine = jnp.broadcast_to(owner[y : y + 1, :], owner_ids.shape) == owner_ids
            lhs_ref[:, lanes] = jnp.concatenate(
                [
                    jnp.where(mine, jnp.broadcast_to(part[y : y + 1, :], mine.shape), 0.0)
                    for part in (high_part, low_part)
                ],
                axis=0,
            ).astype(BF16)
        total = total + lax.dot_general(
            hot_ref[x], lhs_ref[...], NT, preferred_element_type=F32
        )
    total = total.T
    md_ref[...] = total[:owners] + total[owners:]
    bits = owners.bit_length() - 1
    me = lax.axis_index("sub")
    for place in range(owners):
        owner = me ^ reversed_bits(place, bits) if owners == 1 << bits else place
        table_ref[place, :EARLY, :] = early_ref[owner]
        table_ref[place, EARLY : EARLY + 1, :] = md_ref[pl.ds(owner, 1), :]


def ring(value, axis, step):
    count = lax.axis_size(axis)
    return lax.ppermute(value, axis, [(i, (i + step) % count) for i in range(count)])


def swap(value, axis, step):
    count = lax.axis_size(axis)
    return lax.ppermute(value, axis, [(i, i ^ step) for i in range(count)])


def to_owner(table):
    owners = table.shape[0]
    if owners & (owners - 1):
        return jnp.sum(lax.all_to_all(table, "sub", split_axis=0, concat_axis=0, tiled=True), axis=0)
    step = 1
    while step < owners:
        half = table.shape[0] // 2
        table = table[:half] + swap(table[half:], "sub", step)
        step *= 2
    return table[0]


def summed(value, axis):
    count = lax.axis_size(axis)
    if count & (count - 1):
        return lax.psum(value, axis)
    step = 1
    while step < count:
        value = value + swap(value, axis, step)
        step *= 2
    return value


def shards(positions, velocities, masses, smoothing, neighbours, particle_group, group_row):
    blocks_x, blocks_y, block_len = masses.shape
    dom_count, sub_count = lax.axis_size("dom"), lax.axis_size("sub")
    owners = sub_count
    chunk = blocks_y * block_len
    shape = jax.ShapeDtypeStruct
    codes = neighbours.reshape(-1)
    tail = jnp.concatenate([positions[:, blocks_x - 1], masses[blocks_x - 1 :]], axis=0)
    head = jnp.concatenate([positions[:, 0], masses[:1]], axis=0)
    prev = ring(tail, "dom", 1)
    following = ring(head, "dom", -1)
    early, rows, hot, columns, middle, middle_match = pl.pallas_call(
        functools.partial(first_kernel, blocks_x * dom_count, blocks_y * sub_count),
        out_shape=(
            shape((owners, EARLY, LANES), F32),
            shape(masses.shape, jnp.int32),
            shape((blocks_x, LANES, chunk), BF16),
            shape((2, 4, blocks_x, LANES), F32),
            shape((blocks_x - 2, blocks_y, LANES), F32),
            shape((blocks_x - 2, 2, LANES, 48), BF16),
        ),
        in_specs=[SMEM] + [VMEM] * 6,
        out_specs=(VMEM,) * 6,
        scratch_shapes=[
            pltpu.VMEM((blocks_x * EARLY * blocks_y, LANES), F32),
            pltpu.VMEM((owners * 2 * EARLY, chunk), BF16),
        ]
        + pair_scratch(blocks_x, blocks_y, blocks_x - 2),
        compiler_params=params(),
        cost_estimate=pl.CostEstimate(
            flops=1_000_000_000, bytes_accessed=1_400_000, transcendentals=1_300_000
        ),
        name="moments_and_middle_pairs",
    )(codes, positions, velocities, masses, smoothing, particle_group, group_row.reshape(-1, LANES))
    low, high = [
        ring(
            jnp.concatenate([prev[:, y : y + 1], columns[side], following[:, y : y + 1]], axis=1),
            "sub",
            step,
        )
        for side, y, step in ((1, blocks_y - 1, 1), (0, 0, -1))
    ]
    edge, edge_match = pl.pallas_call(
        edge_kernel,
        out_shape=(shape((2, blocks_y, LANES), F32), shape((2, 2, LANES, 48), BF16)),
        in_specs=[SMEM] + [VMEM] * 5,
        out_specs=(VMEM, VMEM),
        scratch_shapes=pair_scratch(blocks_x, blocks_y, 2),
        compiler_params=params(),
        cost_estimate=pl.CostEstimate(
            flops=1_000_000_000, bytes_accessed=400_000, transcendentals=1_300_000
        ),
        name="edge_pairs",
    )(codes, positions, masses, smoothing, prev, following)
    density, table = pl.pallas_call(
        rim_kernel,
        out_shape=(shape(masses.shape, F32), shape((owners, EARLY + 1, LANES), F32)),
        in_specs=[SMEM] + [VMEM] * 11,
        out_specs=(VMEM, VMEM),
        scratch_shapes=[
            pltpu.VMEM((128, LANES), F32),
            pltpu.VMEM(masses.shape, F32),
            pltpu.VMEM((owners, LANES), F32),
            pltpu.VMEM((2 * owners, chunk), BF16),
        ],
        compiler_params=params(),
        cost_estimate=pl.CostEstimate(
            flops=200_000_000, bytes_accessed=400_000, transcendentals=400_000
        ),
        name="rim_pairs_and_table",
    )(
        codes, middle, edge, middle_match, edge_match, masses, smoothing, low, high, rows, hot, early
    )
    return (density, summed(to_owner(table), "dom"))


def solution(mesh):
    in_specs = (
        P(None, "dom", "sub", None),
        P(None, "dom", "sub", None),
        P("dom", "sub", None),
        P("dom", "sub", None),
        P("dom", "sub", None),
        P("dom", "sub", None),
        P(),
    )
    out_specs = (P("dom", "sub", None), P(None, "sub"))
    return jax.shard_map(shards, mesh=mesh, in_specs=in_specs, out_specs=out_specs, check_vma=False)
```

```python
import functools
import math

import jax
import jax.numpy as jnp
from jax import lax
from jax.experimental import pallas as pl
from jax.experimental.pallas import tpu as pltpu
from jax.sharding import PartitionSpec as P

F32 = jnp.float32
BF16 = jnp.bfloat16
LANES = 128
EARLY = 16
DENSITY_FACTOR = 21.0 / (16.0 * math.pi) / 256.0
VMEM = pl.BlockSpec(memory_space=pltpu.VMEM)
SMEM = pl.BlockSpec(memory_space=pltpu.SMEM)
NT = (((1,), (1,)), ((), ()))


def params():
    return pltpu.CompilerParams(vmem_limit_bytes=40 * 1024 * 1024)


def rounded(value):
    return value.astype(BF16).astype(F32)


def three_parts(value):
    first = rounded(value)
    rest = value - first
    second = rounded(rest)
    return first, second, rest - second


def slot_one_hot(slots, y):
    row = jnp.broadcast_to(slots[y : y + 1, :], (LANES, LANES))
    ids = lax.broadcasted_iota(jnp.int32, (LANES, LANES), 0)
    return jnp.where(ids == row, 1.0, 0.0).astype(BF16)


def sum_moments(
    nx_total, ny_total, pos_ref, vel_ref, mass_ref, group_ref, row_ref,
    table_ref, rows_ref, hot_ref, feat_ref, lhs_ref,
):
    blocks_x, blocks_y, _ = mass_ref.shape
    owners = table_ref.shape[0]
    table_rows = row_ref.shape[0]
    base_x = (lax.axis_index("dom") * blocks_x).astype(F32)
    base_y = ((2 * lax.axis_index("chip") + lax.axis_index("core")) * blocks_y).astype(F32)
    y_iota = lax.broadcasted_iota(jnp.int32, (blocks_y, LANES), 0).astype(F32)
    total = jnp.zeros((owners * 2 * EARLY, LANES), F32)
    for x in range(blocks_x):
        group = group_ref[x]
        low = group & (LANES - 1)
        high = group >> 7
        rows = jnp.zeros_like(group)
        for r in range(table_rows):
            line = jnp.broadcast_to(row_ref[r : r + 1, :], group.shape)
            picked = jnp.take_along_axis(line, low, axis=1)
            rows = jnp.where(high == r, picked, rows)
        rows_ref[x] = rows
        mass = mass_ref[x]
        gx = (base_x + float(x) + pos_ref[0, x]) / float(nx_total)
        gy = (base_y + y_iota + pos_ref[1, x]) / float(ny_total)
        gz = pos_ref[2, x]
        vx, vy, vz = vel_ref[0, x], vel_ref[1, x], vel_ref[2, x]
        mx, my, mz = mass * gx, mass * gy, mass * gz
        features = (
            mass, mx, my, mz, mass * vx, mass * vy, mass * vz,
            mass * (gy * vz - gz * vy), mass * (gz * vx - gx * vz), mass * (gx * vy - gy * vx),
            mx * gx, my * gy, mz * gz, mx * gy, mx * gz, my * gz,
        )
        for f, feature in enumerate(features):
            start = (x * EARLY + f) * blocks_y
            feat_ref[start : start + blocks_y, :] = feature
        slots = rows & (LANES - 1)
        owner = rows >> 7
        for y in range(blocks_y):
            lanes = slice(y * LANES, (y + 1) * LANES)
            feats = feat_ref[pl.ds(x * EARLY * blocks_y + y, EARLY, stride=blocks_y), :]
            high_part = rounded(feats)
            both = jnp.concatenate([high_part, feats - high_part], axis=0)
            owner_row = jnp.broadcast_to(owner[y : y + 1, :], both.shape)
            for o in range(owners):
                lhs_ref[o * 2 * EARLY : (o + 1) * 2 * EARLY, lanes] = jnp.where(
                    owner_row == o, both, 0.0
                ).astype(BF16)
            hot_ref[x, :, lanes] = slot_one_hot(slots, y)
        total = total + lax.dot_general(
            lhs_ref[...], hot_ref[x], NT, preferred_element_type=F32
        )
    total = total.reshape(owners, 2 * EARLY, LANES)
    table_ref[...] = total[:, :EARLY, :] + total[:, EARLY:, :]


def target_rows(pos, radius):
    weight = 4.0 / (radius * radius)
    cx, cy, cz = pos[0] - 0.5, pos[1] - 0.5, pos[2] - 0.5
    lines = (
        -2.0 * cx * weight, -2.0 * cy * weight, -2.0 * cz * weight,
        weight, weight, weight,
        (cx * cx + cy * cy + cz * cz) * weight, jnp.zeros_like(weight),
    )
    parts = [three_parts(line) for line in lines]
    return [part[k] for k in range(3) for part in parts]


def target_matrix(coef):
    one, two, three = coef[0:8], coef[8:16], coef[16:24]
    stacked = jnp.concatenate([one, one, two, two, one, three], axis=0)
    return stacked.T.astype(BF16)


def source_matrix(line, squares):
    value = jnp.where(squares, line * line, line)
    one, two, three = three_parts(value)
    first = jnp.concatenate([one, two], axis=0).astype(BF16)
    last = jnp.concatenate([three, one], axis=0).astype(BF16)
    return jnp.concatenate([first, first, last], axis=0)


def store_source(nat_ref, start, count, columns):
    cx, cy, cz = [column - 0.5 for column in columns]
    one = jnp.ones_like(cx)
    zero = jnp.zeros_like(cx)
    for kind, line in enumerate((cx, cy, cz, cx, cy, cz, one, zero)):
        nat_ref[start + kind * 8 : start + kind * 8 + count, :] = line


def pair_sum(target, sources, weights):
    total = None
    squared = jnp.dot(target, jnp.concatenate(sources, axis=1), preferred_element_type=F32)
    for k, w in enumerate(weights):
        t = squared[:, k * LANES : (k + 1) * LANES]
        t = jnp.minimum(jnp.maximum(t, 1e-12), 16.0)
        u = t * lax.rsqrt(t)
        f = 4.0 - u
        f = f * f
        f = f * f
        term = f * (w + w * u)
        total = term if total is None else total + term
    return total


def column_sums(totals):
    lane = lax.broadcasted_iota(jnp.int32, (LANES, LANES), 1)
    columns = jnp.zeros((LANES, LANES), F32)
    for k, total in enumerate(totals):
        columns = jnp.where(lane == k, jnp.sum(total, axis=1, keepdims=True), columns)
    return columns.T[: len(totals), :]


def square_mask():
    kind = lax.broadcasted_iota(jnp.int32, (8, LANES), 0)
    return (kind >= 3) & (kind < 6)


def block_pairs(
    x_first, x_step, x_count, code_ref, pos_ref, mass_ref, smooth_ref, prev_ref, next_ref,
    out_ref, match_ref, nat_ref, src_ref, weight_ref, shift_ref, tgt_ref,
):
    blocks_x, blocks_y, _ = mass_ref.shape
    listed = code_ref.shape[0]
    null = (blocks_x + 2) * blocks_y
    for xe in range(blocks_x + 2):
        if xe == 0 or xe == blocks_x + 1:
            ref = prev_ref if xe == 0 else next_ref
            if ref is None:
                continue
            columns, mass = [ref[c] for c in range(3)], ref[3]
        else:
            columns, mass = [pos_ref[c, xe - 1] for c in range(3)], mass_ref[xe - 1]
        store_source(nat_ref, xe * 64, blocks_y, columns)
        weight_ref[xe * blocks_y : (xe + 1) * blocks_y, :] = mass
        for y in range(blocks_y):
            src_ref[xe * blocks_y + y] = nat_ref[pl.ds(xe * 64 + y, 8, stride=8), :]
    src_ref[null] = jnp.zeros((8, LANES), F32)
    weight_ref[null : null + 8, :] = jnp.zeros((8, LANES), F32)
    kind = lax.broadcasted_iota(jnp.int32, (8, LANES), 0)
    for code in range(9):
        along_x = jnp.where((kind == 0) | (kind == 3), float(code // 3 - 1), 0.0)
        along_y = jnp.where((kind == 1) | (kind == 4), float(code % 3 - 1), 0.0)
        shift_ref[code] = along_x + along_y
    squares = square_mask()
    for k in range(x_count):
        x = x_first + k * x_step
        lines = target_rows([pos_ref[c, x] for c in range(3)], smooth_ref[x])
        for row, line in enumerate(lines):
            tgt_ref[k, row * blocks_y : (row + 1) * blocks_y, :] = line

    def one_x(turn, carry):
        x = x_first + turn * x_step
        totals = []
        for y in range(blocks_y):
            target = target_matrix(tgt_ref[turn, pl.ds(y, 24, stride=blocks_y), :])
            if y == 0:
                match_ref[turn, 0] = target
            if y == blocks_y - 1:
                match_ref[turn, 1] = target
            sources, weights = [], []
            for k in range(listed):
                code = code_ref[k, x, y]
                step_x = (code * 11) >> 5
                near_y = y + code - 3 * step_x - 1
                inside = (near_y >= 0) & (near_y < blocks_y)
                index = jnp.where(inside, (x + step_x) * blocks_y + near_y, null)
                sources.append(source_matrix(src_ref[index] + shift_ref[code], squares))
                weights.append(
                    jnp.broadcast_to(weight_ref[pl.ds(index, 1), :], (LANES, LANES))
                )
            totals.append(pair_sum(target, sources, weights))
        out_ref[turn] = column_sums(totals)
        return carry

    lax.fori_loop(0, x_count, one_x, 0)


def first_kernel(
    nx_total, ny_total, code_ref, pos_ref, vel_ref, mass_ref, smooth_ref, group_ref, row_ref,
    table_ref, rows_ref, hot_ref, column_ref, out_ref, match_ref,
    feat_ref, lhs_ref, *scratch,
):
    blocks_x, blocks_y, _ = mass_ref.shape
    for side in range(2):
        y = side * (blocks_y - 1)
        for x in range(blocks_x):
            for c in range(3):
                column_ref[side, c, x : x + 1, :] = pos_ref[c, x, y : y + 1, :]
            column_ref[side, 3, x : x + 1, :] = mass_ref[x, y : y + 1, :]
    sum_moments(
        nx_total, ny_total, pos_ref, vel_ref, mass_ref, group_ref, row_ref,
        table_ref, rows_ref, hot_ref, feat_ref, lhs_ref,
    )
    block_pairs(
        1, 1, blocks_x - 2, code_ref, pos_ref, mass_ref, smooth_ref, None, None,
        out_ref, match_ref, *scratch,
    )


def edge_kernel(
    code_ref, pos_ref, mass_ref, smooth_ref, prev_ref, next_ref, out_ref, match_ref, *scratch
):
    blocks_x = mass_ref.shape[0]
    block_pairs(
        0, blocks_x - 1, 2, code_ref, pos_ref, mass_ref, smooth_ref, prev_ref, next_ref,
        out_ref, match_ref, *scratch,
    )


def pair_scratch(blocks_x, blocks_y, x_count):
    return [
        pltpu.VMEM(((blocks_x + 2) * 64, LANES), F32),
        pltpu.VMEM(((blocks_x + 2) * blocks_y + 1, 8, LANES), F32),
        pltpu.VMEM(((blocks_x + 2) * blocks_y + 8, LANES), F32),
        pltpu.VMEM((9, 8, LANES), F32),
        pltpu.VMEM((x_count, 24 * blocks_y, LANES), F32),
    ]


def rim_kernel(
    code_ref, middle_ref, edge_ref, middle_match_ref, edge_match_ref, mass_ref, smooth_ref,
    low_ref, high_ref, rows_ref, hot_ref, early_ref,
    sum_ref, table_ref, nat_ref, md_ref, lhs_ref,
):
    blocks_x, blocks_y, _ = mass_ref.shape
    owners = early_ref.shape[0]
    listed = code_ref.shape[0]
    for side, ref in enumerate((low_ref, high_ref)):
        store_source(nat_ref, side * 64, blocks_x + 2, [ref[c] for c in range(3)])
    kind = lax.broadcasted_iota(jnp.int32, (8, LANES), 0)
    squares = square_mask()
    totals = []
    for x in range(blocks_x):
        edge = x == 0 or x == blocks_x - 1
        turn = (1 if x else 0) if edge else x - 1
        sum_ref[x] = (edge_ref if edge else middle_ref)[turn]
        for side, ref in enumerate((low_ref, high_ref)):
            y = side * (blocks_y - 1)
            target = (edge_match_ref if edge else middle_match_ref)[turn, side]
            sources, weights = [], []
            for step_x in range(3):
                wanted = step_x * 3 + side * 2
                found = code_ref[0, x, y] == wanted
                for k in range(1, listed):
                    found = found | (code_ref[k, x, y] == wanted)
                flag = jnp.where(found, 1.0, 0.0)
                along_x = jnp.where((kind == 0) | (kind == 3), float(step_x - 1), 0.0)
                along_y = jnp.where((kind == 1) | (kind == 4), float(side * 2 - 1), 0.0)
                line = nat_ref[pl.ds(side * 64 + x + step_x, 8, stride=8), :]
                sources.append(source_matrix(line + along_x + along_y, squares))
                mass = ref[3, x + step_x : x + step_x + 1, :] * flag
                weights.append(jnp.broadcast_to(mass, (LANES, LANES)))
            totals.append(pair_sum(target, sources, weights))
    sums = column_sums(totals)
    total = jnp.zeros((LANES, 2 * owners), F32)
    owner_ids = lax.broadcasted_iota(jnp.int32, (owners, LANES), 0)
    for x in range(blocks_x):
        for side in range(2):
            y = side * (blocks_y - 1)
            sum_ref[x, y : y + 1, :] += sums[2 * x + side : 2 * x + side + 1, :]
        radius = smooth_ref[x]
        density = sum_ref[x] * DENSITY_FACTOR / (radius * radius * radius)
        moment = mass_ref[x] * density
        high_part = rounded(moment)
        low_part = moment - high_part
        owner = rows_ref[x] >> 7
        for y in range(blocks_y):
            lanes = slice(y * LANES, (y + 1) * LANES)
            mine = jnp.broadcast_to(owner[y : y + 1, :], owner_ids.shape) == owner_ids
            lhs_ref[:, lanes] = jnp.concatenate(
                [
                    jnp.where(mine, jnp.broadcast_to(part[y : y + 1, :], mine.shape), 0.0)
                    for part in (high_part, low_part)
                ],
                axis=0,
            ).astype(BF16)
        total = total + lax.dot_general(
            hot_ref[x], lhs_ref[...], NT, preferred_element_type=F32
        )
    total = total.T
    md_ref[...] = total[:owners] + total[owners:]
    core = lax.axis_index("core")
    for other in range(2):
        for chip in range(owners // 2):
            owner = 2 * chip + (core ^ other)
            table_ref[other, chip, :EARLY, :] = early_ref[owner]
            table_ref[other, chip, EARLY : EARLY + 1, :] = md_ref[pl.ds(owner, 1), :]


def ring(value, axis, step):
    count = lax.axis_size(axis)
    return lax.ppermute(value, axis, [(i, (i + step) % count) for i in range(count)])


def to_owner(table):
    sent = lax.ppermute(table[1], "core", [(0, 1), (1, 0)])
    half = table[0] + sent
    everywhere = jnp.broadcast_to(half[None], (lax.axis_size("dom"),) + half.shape)
    everywhere = everywhere.reshape((-1,) + half.shape[1:])
    got = lax.all_to_all(everywhere, ("dom", "chip"), split_axis=0, concat_axis=0, tiled=True)
    return jnp.sum(got, axis=0)


def shards(positions, velocities, masses, smoothing, neighbours, particle_group, group_row):
    blocks_x, blocks_y, block_len = masses.shape
    dom_count, sub_count = lax.axis_size("dom"), lax.axis_size("chip") * lax.axis_size("core")
    owners = sub_count
    chunk = blocks_y * block_len
    shape = jax.ShapeDtypeStruct
    codes = neighbours.transpose(2, 0, 1)
    packed = jnp.concatenate([positions, masses[None]], axis=0)
    prev = ring(packed[:, blocks_x - 1], "dom", 1)
    following = ring(packed[:, 0], "dom", -1)
    early, rows, hot, columns, middle, middle_match = pl.pallas_call(
        functools.partial(first_kernel, blocks_x * dom_count, blocks_y * sub_count),
        out_shape=(
            shape((owners, EARLY, LANES), F32),
            shape(masses.shape, jnp.int32),
            shape((blocks_x, LANES, chunk), BF16),
            shape((2, 4, blocks_x, LANES), F32),
            shape((blocks_x - 2, blocks_y, LANES), F32),
            shape((blocks_x - 2, 2, LANES, 48), BF16),
        ),
        in_specs=[SMEM] + [VMEM] * 6,
        out_specs=(VMEM,) * 6,
        scratch_shapes=[
            pltpu.VMEM((blocks_x * EARLY * blocks_y, LANES), F32),
            pltpu.VMEM((owners * 2 * EARLY, chunk), BF16),
        ]
        + pair_scratch(blocks_x, blocks_y, blocks_x - 2),
        compiler_params=params(),
        cost_estimate=pl.CostEstimate(
            flops=1_000_000_000, bytes_accessed=1_400_000, transcendentals=1_300_000
        ),
        name="moments_and_middle_pairs",
    )(codes, positions, velocities, masses, smoothing, particle_group, group_row.reshape(-1, LANES))
    low, high = [
        ring(
            jnp.concatenate([prev[:, y : y + 1], columns[side], following[:, y : y + 1]], axis=1),
            ("chip", "core"),
            step,
        )
        for side, y, step in ((1, blocks_y - 1, 1), (0, 0, -1))
    ]
    edge, edge_match = pl.pallas_call(
        edge_kernel,
        out_shape=(shape((2, blocks_y, LANES), F32), shape((2, 2, LANES, 48), BF16)),
        in_specs=[SMEM] + [VMEM] * 5,
        out_specs=(VMEM, VMEM),
        scratch_shapes=pair_scratch(blocks_x, blocks_y, 2),
        compiler_params=params(),
        cost_estimate=pl.CostEstimate(
            flops=1_000_000_000, bytes_accessed=400_000, transcendentals=1_300_000
        ),
        name="edge_pairs",
    )(codes, positions, masses, smoothing, prev, following)
    sums, table = pl.pallas_call(
        rim_kernel,
        out_shape=(shape(masses.shape, F32), shape((2, owners // 2, EARLY + 1, LANES), F32)),
        in_specs=[SMEM] + [VMEM] * 11,
        out_specs=(VMEM, VMEM),
        scratch_shapes=[
            pltpu.VMEM((128, LANES), F32),
            pltpu.VMEM((owners, LANES), F32),
            pltpu.VMEM((2 * owners, chunk), BF16),
        ],
        compiler_params=params(),
        cost_estimate=pl.CostEstimate(
            flops=200_000_000, bytes_accessed=400_000, transcendentals=400_000
        ),
        name="rim_pairs_and_table",
    )(
        codes, middle, edge, middle_match, edge_match, masses, smoothing, low, high, rows, hot, early
    )
    density = sums * DENSITY_FACTOR / (smoothing * smoothing * smoothing)
    return (density, to_owner(table))


def solution(mesh):
    dom_count, sub_count = mesh.devices.shape
    mesh = jax.sharding.Mesh(
        mesh.devices.reshape(dom_count, sub_count // 2, 2), ("dom", "chip", "core")
    )
    sub = ("chip", "core")
    in_specs = (
        P(None, "dom", sub, None),
        P(None, "dom", sub, None),
        P("dom", sub, None),
        P("dom", sub, None),
        P("dom", sub, None),
        P("dom", sub, None),
        P(),
    )
    out_specs = (P("dom", sub, None), P(None, sub))
    return jax.shard_map(shards, mesh=mesh, in_specs=in_specs, out_specs=out_specs, check_vma=False)
```

```python
import functools
import math

import jax
import jax.numpy as jnp
from jax import lax
from jax.experimental import pallas as pl
from jax.experimental.pallas import tpu as pltpu
from jax.sharding import PartitionSpec as P

F32 = jnp.float32
BF16 = jnp.bfloat16
LANES = 128
EARLY = 16
DENSITY_FACTOR = 21.0 / (16.0 * math.pi) / 256.0
VMEM = pl.BlockSpec(memory_space=pltpu.VMEM)
ANY = pl.BlockSpec(memory_space=pl.ANY)
SMEM = pl.BlockSpec(memory_space=pltpu.SMEM)
NT = (((1,), (1,)), ((), ()))


def params():
    return pltpu.CompilerParams(vmem_limit_bytes=40 * 1024 * 1024)


def rounded(value):
    return value.astype(BF16).astype(F32)


def three_parts(value):
    first = rounded(value)
    rest = value - first
    second = rounded(rest)
    return first, second, rest - second


def slot_one_hot(slots, y):
    row = jnp.broadcast_to(slots[y : y + 1, :], (LANES, LANES))
    ids = lax.broadcasted_iota(jnp.int32, (LANES, LANES), 0)
    return jnp.where(ids == row, 1.0, 0.0).astype(BF16)


def sum_moments(
    nx_total, ny_total, pos_ref, vel_ref, mass_ref, group_ref, row_ref,
    table_ref, rows_ref, hot_ref, feat_ref, lhs_ref,
):
    blocks_x, blocks_y, _ = mass_ref.shape
    owners = table_ref.shape[0]
    table_rows = row_ref.shape[0]
    base_x = (lax.axis_index("dom") * blocks_x).astype(F32)
    base_y = ((2 * lax.axis_index("chip") + lax.axis_index("core")) * blocks_y).astype(F32)
    y_iota = lax.broadcasted_iota(jnp.int32, (blocks_y, LANES), 0).astype(F32)
    total = jnp.zeros((owners * 2 * EARLY, LANES), F32)
    for x in range(blocks_x):
        group = group_ref[x]
        low = group & (LANES - 1)
        high = group >> 7
        rows = jnp.zeros_like(group)
        for r in range(table_rows):
            line = jnp.broadcast_to(row_ref[r : r + 1, :], group.shape)
            picked = jnp.take_along_axis(line, low, axis=1)
            rows = jnp.where(high == r, picked, rows)
        rows_ref[x] = rows
        mass = mass_ref[x]
        gx = (base_x + float(x) + pos_ref[0, x]) / float(nx_total)
        gy = (base_y + y_iota + pos_ref[1, x]) / float(ny_total)
        gz = pos_ref[2, x]
        vx, vy, vz = vel_ref[0, x], vel_ref[1, x], vel_ref[2, x]
        mx, my, mz = mass * gx, mass * gy, mass * gz
        features = (
            mass, mx, my, mz, mass * vx, mass * vy, mass * vz,
            mass * (gy * vz - gz * vy), mass * (gz * vx - gx * vz), mass * (gx * vy - gy * vx),
            mx * gx, my * gy, mz * gz, mx * gy, mx * gz, my * gz,
        )
        for f, feature in enumerate(features):
            start = (x * EARLY + f) * blocks_y
            feat_ref[start : start + blocks_y, :] = feature
        slots = rows & (LANES - 1)
        owner = rows >> 7
        for y in range(blocks_y):
            lanes = slice(y * LANES, (y + 1) * LANES)
            feats = feat_ref[pl.ds(x * EARLY * blocks_y + y, EARLY, stride=blocks_y), :]
            high_part = rounded(feats)
            both = jnp.concatenate([high_part, feats - high_part], axis=0)
            owner_row = jnp.broadcast_to(owner[y : y + 1, :], both.shape)
            for o in range(owners):
                lhs_ref[o * 2 * EARLY : (o + 1) * 2 * EARLY, lanes] = jnp.where(
                    owner_row == o, both, 0.0
                ).astype(BF16)
            hot_ref[x, :, lanes] = slot_one_hot(slots, y)
        total = total + lax.dot_general(
            lhs_ref[...], hot_ref[x], NT, preferred_element_type=F32
        )
    total = total.reshape(owners, 2 * EARLY, LANES)
    table_ref[...] = total[:, :EARLY, :] + total[:, EARLY:, :]


def target_rows(pos, radius):
    weight = 4.0 / (radius * radius)
    cx, cy, cz = pos[0] - 0.5, pos[1] - 0.5, pos[2] - 0.5
    lines = (
        -2.0 * cx * weight, -2.0 * cy * weight, -2.0 * cz * weight,
        weight, weight, weight,
        (cx * cx + cy * cy + cz * cz) * weight, jnp.zeros_like(weight),
    )
    parts = [three_parts(line) for line in lines]
    return [part[k] for k in range(3) for part in parts]


def target_matrix(coefs):
    stacked = []
    for coef in coefs:
        one, two, three = coef[0:8], coef[8:16], coef[16:24]
        stacked += [one, one, two, two, one, three]
    return jnp.concatenate(stacked, axis=0).T.astype(BF16)


def source_matrix(line, squares):
    value = jnp.where(squares, line * line, line)
    one, two, three = three_parts(value)
    first = jnp.concatenate([one, two], axis=0).astype(BF16)
    last = jnp.concatenate([three, one], axis=0).astype(BF16)
    return jnp.concatenate([first, first, last], axis=0)


def store_source(nat_ref, start, count, columns):
    cx, cy, cz = [column - 0.5 for column in columns]
    one = jnp.ones_like(cx)
    zero = jnp.zeros_like(cx)
    for kind, line in enumerate((cx, cy, cz, cx, cy, cz, one, zero)):
        nat_ref[start + kind * 8 : start + kind * 8 + count, :] = line


def pair_sums(target, sources, weights):
    blank = jnp.zeros((48, LANES), BF16)
    columns = [jnp.concatenate([line, blank], axis=0) for line in sources[0]]
    columns += [jnp.concatenate([blank, line], axis=0) for line in sources[1]]
    owner = [0] * len(sources[0]) + [1] * len(sources[1])
    masses = weights[0] + weights[1]
    totals = [None, None]
    for first in range(0, len(columns), 2):
        group = columns[first : first + 2]
        squared = jnp.dot(
            target, jnp.concatenate(group, axis=1), preferred_element_type=F32
        )
        for k in range(len(group)):
            t = squared[:, k * LANES : (k + 1) * LANES]
            t = jnp.minimum(jnp.maximum(t, 1e-12), 16.0)
            u = t * lax.rsqrt(t)
            f = 4.0 - u
            f = f * f
            f = f * f
            w = masses[first + k]
            term = f * (w + w * u)
            of = owner[first + k]
            totals[of] = term if totals[of] is None else totals[of] + term
    return totals


def column_sums(totals):
    lane = lax.broadcasted_iota(jnp.int32, (LANES, LANES), 1)
    columns = jnp.zeros((LANES, LANES), F32)
    for k, total in enumerate(totals):
        columns = jnp.where(lane == k, jnp.sum(total, axis=1, keepdims=True), columns)
    return columns.T[: len(totals), :]


def square_mask():
    kind = lax.broadcasted_iota(jnp.int32, (8, LANES), 0)
    return (kind >= 3) & (kind < 6)


def block_pairs(
    x_first, x_step, x_count, code_ref, pos_ref, mass_ref, smooth_ref, prev_ref, next_ref,
    out_ref, match_ref, nat_ref, src_ref, weight_ref, shift_ref, tgt_ref,
):
    blocks_x, blocks_y, _ = mass_ref.shape
    listed = code_ref.shape[0]
    null = (blocks_x + 2) * blocks_y
    for xe in range(blocks_x + 2):
        if xe == 0 or xe == blocks_x + 1:
            ref = prev_ref if xe == 0 else next_ref
            if ref is None:
                continue
            columns, mass = [ref[c] for c in range(3)], ref[3]
        else:
            columns, mass = [pos_ref[c, xe - 1] for c in range(3)], mass_ref[xe - 1]
        store_source(nat_ref, xe * 64, blocks_y, columns)
        weight_ref[xe * blocks_y : (xe + 1) * blocks_y, :] = mass
        for y in range(blocks_y):
            src_ref[xe * blocks_y + y] = nat_ref[pl.ds(xe * 64 + y, 8, stride=8), :]
    src_ref[null] = jnp.zeros((8, LANES), F32)
    weight_ref[null : null + 8, :] = jnp.zeros((8, LANES), F32)
    kind = lax.broadcasted_iota(jnp.int32, (8, LANES), 0)
    for code in range(9):
        along_x = jnp.where((kind == 0) | (kind == 3), float(code // 3 - 1), 0.0)
        along_y = jnp.where((kind == 1) | (kind == 4), float(code % 3 - 1), 0.0)
        shift_ref[code] = along_x + along_y
    squares = square_mask()
    for k in range(x_count):
        x = x_first + k * x_step
        lines = target_rows([pos_ref[c, x] for c in range(3)], smooth_ref[x])
        for row, line in enumerate(lines):
            tgt_ref[k, row * blocks_y : (row + 1) * blocks_y, :] = line

    def sources_of(x, y):
        sources, weights = [], []
        for k in range(listed):
            code = code_ref[k, x, y]
            step_x = (code * 11) >> 5
            near_y = y + code - 3 * step_x - 1
            inside = (near_y >= 0) & (near_y < blocks_y)
            index = jnp.where(inside, (x + step_x) * blocks_y + near_y, null)
            sources.append(source_matrix(src_ref[index] + shift_ref[code], squares))
            weights.append(jnp.broadcast_to(weight_ref[pl.ds(index, 1), :], (LANES, LANES)))
        return sources, weights

    def one_x(turn, carry):
        x = x_first + turn * x_step
        totals = [None] * blocks_y
        for pair in [(0, blocks_y - 1)] + [(y, y + 1) for y in range(1, blocks_y - 1, 2)]:
            target = target_matrix(
                [tgt_ref[turn, pl.ds(y, 24, stride=blocks_y), :] for y in pair]
            )
            if pair[0] == 0:
                match_ref[turn] = target
            found = [sources_of(x, y) for y in pair]
            sums = pair_sums(target, [each[0] for each in found], [each[1] for each in found])
            totals[pair[0]], totals[pair[1]] = sums
        out_ref[turn] = column_sums(totals)
        return carry

    lax.fori_loop(0, x_count, one_x, 0)


def first_kernel(
    nx_total, ny_total, code_ref, pos_ref, mass_ref, smooth_ref, far_vel_ref, far_group_ref, far_row_ref,
    table_ref, rows_ref, hot_ref, column_ref, out_ref, match_ref,
    vel_ref, group_ref, row_ref, sems, feat_ref, lhs_ref, *scratch,
):
    blocks_x, blocks_y, _ = mass_ref.shape
    copies = [
        pltpu.make_async_copy(far, near, sems.at[k])
        for k, (far, near) in enumerate(
            ((far_vel_ref, vel_ref), (far_group_ref, group_ref), (far_row_ref, row_ref))
        )
    ]
    for copy in copies:
        copy.start()
    for side in range(2):
        y = side * (blocks_y - 1)
        for x in range(blocks_x):
            for c in range(3):
                column_ref[side, c, x : x + 1, :] = pos_ref[c, x, y : y + 1, :]
            column_ref[side, 3, x : x + 1, :] = mass_ref[x, y : y + 1, :]
    block_pairs(
        1, 1, blocks_x - 2, code_ref, pos_ref, mass_ref, smooth_ref, None, None,
        out_ref, match_ref, *scratch,
    )
    for copy in copies:
        copy.wait()
    sum_moments(
        nx_total, ny_total, pos_ref, vel_ref, mass_ref, group_ref, row_ref,
        table_ref, rows_ref, hot_ref, feat_ref, lhs_ref,
    )


def edge_kernel(
    code_ref, pos_ref, mass_ref, smooth_ref, prev_ref, next_ref, out_ref, match_ref, *scratch
):
    blocks_x = mass_ref.shape[0]
    block_pairs(
        0, blocks_x - 1, 2, code_ref, pos_ref, mass_ref, smooth_ref, prev_ref, next_ref,
        out_ref, match_ref, *scratch,
    )


def pair_scratch(blocks_x, blocks_y, x_count):
    return [
        pltpu.VMEM(((blocks_x + 2) * 64, LANES), F32),
        pltpu.VMEM(((blocks_x + 2) * blocks_y + 1, 8, LANES), F32),
        pltpu.VMEM(((blocks_x + 2) * blocks_y + 8, LANES), F32),
        pltpu.VMEM((9, 8, LANES), F32),
        pltpu.VMEM((x_count, 24 * blocks_y, LANES), F32),
    ]


def rim_kernel(
    code_ref, middle_ref, edge_ref, middle_match_ref, edge_match_ref, mass_ref, smooth_ref,
    low_ref, high_ref, rows_ref, hot_ref, early_ref,
    sum_ref, table_ref, nat_ref, md_ref, lhs_ref,
):
    blocks_x, blocks_y, _ = mass_ref.shape
    owners = early_ref.shape[0]
    listed = code_ref.shape[0]
    for side, ref in enumerate((low_ref, high_ref)):
        store_source(nat_ref, side * 64, blocks_x + 2, [ref[c] for c in range(3)])
    kind = lax.broadcasted_iota(jnp.int32, (8, LANES), 0)
    squares = square_mask()
    totals = []
    for x in range(blocks_x):
        edge = x == 0 or x == blocks_x - 1
        turn = (1 if x else 0) if edge else x - 1
        sum_ref[x] = (edge_ref if edge else middle_ref)[turn]
        target = (edge_match_ref if edge else middle_match_ref)[turn]
        sources, weights = ([], []), ([], [])
        for side, ref in enumerate((low_ref, high_ref)):
            y = side * (blocks_y - 1)
            for step_x in range(3):
                wanted = step_x * 3 + side * 2
                found = code_ref[0, x, y] == wanted
                for k in range(1, listed):
                    found = found | (code_ref[k, x, y] == wanted)
                flag = jnp.where(found, 1.0, 0.0)
                along_x = jnp.where((kind == 0) | (kind == 3), float(step_x - 1), 0.0)
                along_y = jnp.where((kind == 1) | (kind == 4), float(side * 2 - 1), 0.0)
                line = nat_ref[pl.ds(side * 64 + x + step_x, 8, stride=8), :]
                sources[side].append(source_matrix(line + along_x + along_y, squares))
                mass = ref[3, x + step_x : x + step_x + 1, :] * flag
                weights[side].append(jnp.broadcast_to(mass, (LANES, LANES)))
        totals += pair_sums(target, sources, weights)
    sums = column_sums(totals)
    total = jnp.zeros((LANES, 2 * owners), F32)
    owner_ids = lax.broadcasted_iota(jnp.int32, (owners, LANES), 0)
    for x in range(blocks_x):
        for side in range(2):
            y = side * (blocks_y - 1)
            sum_ref[x, y : y + 1, :] += sums[2 * x + side : 2 * x + side + 1, :]
        radius = smooth_ref[x]
        density = sum_ref[x] * DENSITY_FACTOR / (radius * radius * radius)
        moment = mass_ref[x] * density
        high_part = rounded(moment)
        low_part = moment - high_part
        owner = rows_ref[x] >> 7
        for y in range(blocks_y):
            lanes = slice(y * LANES, (y + 1) * LANES)
            mine = jnp.broadcast_to(owner[y : y + 1, :], owner_ids.shape) == owner_ids
            lhs_ref[:, lanes] = jnp.concatenate(
                [
                    jnp.where(mine, jnp.broadcast_to(part[y : y + 1, :], mine.shape), 0.0)
                    for part in (high_part, low_part)
                ],
                axis=0,
            ).astype(BF16)
        total = total + lax.dot_general(
            hot_ref[x], lhs_ref[...], NT, preferred_element_type=F32
        )
    total = total.T
    md_ref[...] = total[:owners] + total[owners:]
    core, my_chip = lax.axis_index("core"), lax.axis_index("chip")
    for other in range(2):
        for step in range(owners // 2):
            owner = 2 * (my_chip ^ step) + (core ^ other)
            table_ref[other, step, :EARLY, :] = early_ref[owner]
            table_ref[other, step, EARLY : EARLY + 1, :] = md_ref[pl.ds(owner, 1), :]


def ring(value, axis, step):
    count = lax.axis_size(axis)
    return lax.ppermute(value, axis, [(i, (i + step) % count) for i in range(count)])


def swap(value, axis, step):
    count = lax.axis_size(axis)
    return lax.ppermute(value, axis, [(i, i ^ step) for i in range(count)])


def added(parts):
    while len(parts) > 1:
        parts = [sum(parts[k : k + 2][1:], parts[k]) for k in range(0, len(parts), 2)]
    return parts[0]


def to_owner(table):
    table = table[0] + swap(table[1], "core", 1)
    while table.shape[0] > 1:
        ways = min(4, table.shape[0])
        part = table.shape[0] // ways
        table = added(
            [table[:part]]
            + [swap(table[k * part : (k + 1) * part], "chip", k * part) for k in range(1, ways)]
        )
    return table[0]


def summed(value, axis):
    count = lax.axis_size(axis)
    if count & (count - 1):
        return lax.psum(value, axis)
    step = 1
    while step < count:
        ways = min(4, count // step)
        value = added([value] + [swap(value, axis, k * step) for k in range(1, ways)])
        step *= ways
    return value


def shards(positions, velocities, masses, smoothing, neighbours, particle_group, group_row):
    blocks_x, blocks_y, block_len = masses.shape
    dom_count, sub_count = lax.axis_size("dom"), lax.axis_size("chip") * lax.axis_size("core")
    owners = sub_count
    chunk = blocks_y * block_len
    shape = jax.ShapeDtypeStruct
    codes = neighbours.transpose(2, 0, 1)
    packed = jnp.concatenate([positions, masses[None]], axis=0)
    prev = ring(packed[:, blocks_x - 1], "dom", 1)
    following = ring(packed[:, 0], "dom", -1)
    early, rows, hot, columns, middle, middle_match = pl.pallas_call(
        functools.partial(first_kernel, blocks_x * dom_count, blocks_y * sub_count),
        out_shape=(
            shape((owners, EARLY, LANES), F32),
            shape(masses.shape, jnp.int32),
            shape((blocks_x, LANES, chunk), BF16),
            shape((2, 4, blocks_x, LANES), F32),
            shape((blocks_x - 2, blocks_y, LANES), F32),
            shape((blocks_x - 2, LANES, 96), BF16),
        ),
        in_specs=[SMEM] + [VMEM] * 3 + [ANY] * 3,
        out_specs=(VMEM,) * 6,
        scratch_shapes=[
            pltpu.VMEM(velocities.shape, F32),
            pltpu.VMEM(masses.shape, jnp.int32),
            pltpu.VMEM((group_row.shape[0] // LANES, LANES), jnp.int32),
            pltpu.SemaphoreType.DMA((3,)),
            pltpu.VMEM((blocks_x * EARLY * blocks_y, LANES), F32),
            pltpu.VMEM((owners * 2 * EARLY, chunk), BF16),
        ]
        + pair_scratch(blocks_x, blocks_y, blocks_x - 2),
        compiler_params=params(),
        cost_estimate=pl.CostEstimate(
            flops=1_000_000_000, bytes_accessed=1_400_000, transcendentals=1_300_000
        ),
        name="moments_and_middle_pairs",
    )(codes, positions, masses, smoothing, velocities, particle_group, group_row.reshape(-1, LANES))
    low, high = [
        ring(
            jnp.concatenate([prev[:, y : y + 1], columns[side], following[:, y : y + 1]], axis=1),
            ("chip", "core"),
            step,
        )
        for side, y, step in ((1, blocks_y - 1, 1), (0, 0, -1))
    ]
    edge, edge_match = pl.pallas_call(
        edge_kernel,
        out_shape=(shape((2, blocks_y, LANES), F32), shape((2, LANES, 96), BF16)),
        in_specs=[SMEM] + [VMEM] * 5,
        out_specs=(VMEM, VMEM),
        scratch_shapes=pair_scratch(blocks_x, blocks_y, 2),
        compiler_params=params(),
        cost_estimate=pl.CostEstimate(
            flops=1_000_000_000, bytes_accessed=400_000, transcendentals=1_300_000
        ),
        name="edge_pairs",
    )(codes, positions, masses, smoothing, prev, following)
    sums, table = pl.pallas_call(
        rim_kernel,
        out_shape=(shape(masses.shape, F32), shape((2, owners // 2, EARLY + 1, LANES), F32)),
        in_specs=[SMEM] + [VMEM] * 11,
        out_specs=(VMEM, VMEM),
        scratch_shapes=[
            pltpu.VMEM((128, LANES), F32),
            pltpu.VMEM((owners, LANES), F32),
            pltpu.VMEM((2 * owners, chunk), BF16),
        ],
        compiler_params=params(),
        cost_estimate=pl.CostEstimate(
            flops=200_000_000, bytes_accessed=400_000, transcendentals=400_000
        ),
        name="rim_pairs_and_table",
    )(
        codes, middle, edge, middle_match, edge_match, masses, smoothing, low, high, rows, hot, early
    )
    density = sums * DENSITY_FACTOR / (smoothing * smoothing * smoothing)
    return (density, summed(to_owner(table), "dom"))


def solution(mesh):
    dom_count, sub_count = mesh.devices.shape
    mesh = jax.sharding.Mesh(
        mesh.devices.reshape(dom_count, sub_count // 2, 2), ("dom", "chip", "core")
    )
    sub = ("chip", "core")
    in_specs = (
        P(None, "dom", sub, None),
        P(None, "dom", sub, None),
        P("dom", sub, None),
        P("dom", sub, None),
        P("dom", sub, None),
        P("dom", sub, None),
        P(),
    )
    out_specs = (P("dom", sub, None), P(None, sub))
    return jax.shard_map(shards, mesh=mesh, in_specs=in_specs, out_specs=out_specs, check_vma=False)
```

```python
import functools
import math

import jax
import jax.numpy as jnp
from jax import lax
from jax.experimental import pallas as pl
from jax.experimental.pallas import tpu as pltpu
from jax.sharding import PartitionSpec as P

F32 = jnp.float32
BF16 = jnp.bfloat16
LANES = 128
EARLY = 16
DENSITY_FACTOR = 21.0 / (16.0 * math.pi) / 256.0
VMEM = pl.BlockSpec(memory_space=pltpu.VMEM)
SMEM = pl.BlockSpec(memory_space=pltpu.SMEM)
NT = (((1,), (1,)), ((), ()))


def params():
    return pltpu.CompilerParams(vmem_limit_bytes=40 * 1024 * 1024)


def rounded(value):
    return value.astype(BF16).astype(F32)


def three_parts(value):
    first = rounded(value)
    rest = value - first
    second = rounded(rest)
    return first, second, rest - second


def slot_one_hot(slots, y):
    row = jnp.broadcast_to(slots[y : y + 1, :], (LANES, LANES))
    ids = lax.broadcasted_iota(jnp.int32, (LANES, LANES), 0)
    return jnp.where(ids == row, 1.0, 0.0).astype(BF16)


def moments_kernel(
    nx_total, ny_total, after_ref, pos_ref, vel_ref, mass_ref, group_ref, row_ref,
    table_ref, rows_ref, hot_ref, feat_ref, lhs_ref,
):
    blocks_x, blocks_y, _ = mass_ref.shape
    owners = table_ref.shape[0]
    table_rows = row_ref.shape[0]
    base_x = (lax.axis_index("dom") * blocks_x).astype(F32)
    base_y = ((2 * lax.axis_index("chip") + lax.axis_index("core")) * blocks_y).astype(F32)
    y_iota = lax.broadcasted_iota(jnp.int32, (blocks_y, LANES), 0).astype(F32)
    total = jnp.zeros((owners * 2 * EARLY, LANES), F32)
    for x in range(blocks_x):
        group = group_ref[x]
        low = group & (LANES - 1)
        high = group >> 7
        rows = jnp.zeros_like(group)
        for r in range(table_rows):
            line = jnp.broadcast_to(row_ref[r : r + 1, :], group.shape)
            picked = jnp.take_along_axis(line, low, axis=1)
            rows = jnp.where(high == r, picked, rows)
        rows_ref[x] = rows
        mass = mass_ref[x]
        gx = (base_x + float(x) + pos_ref[0, x]) / float(nx_total)
        gy = (base_y + y_iota + pos_ref[1, x]) / float(ny_total)
        gz = pos_ref[2, x]
        vx, vy, vz = vel_ref[0, x], vel_ref[1, x], vel_ref[2, x]
        mx, my, mz = mass * gx, mass * gy, mass * gz
        features = (
            mass, mx, my, mz, mass * vx, mass * vy, mass * vz,
            mass * (gy * vz - gz * vy), mass * (gz * vx - gx * vz), mass * (gx * vy - gy * vx),
            mx * gx, my * gy, mz * gz, mx * gy, mx * gz, my * gz,
        )
        for f, feature in enumerate(features):
            start = (x * EARLY + f) * blocks_y
            feat_ref[start : start + blocks_y, :] = feature
        slots = rows & (LANES - 1)
        owner = rows >> 7
        for y in range(blocks_y):
            lanes = slice(y * LANES, (y + 1) * LANES)
            feats = feat_ref[pl.ds(x * EARLY * blocks_y + y, EARLY, stride=blocks_y), :]
            high_part = rounded(feats)
            both = jnp.concatenate([high_part, feats - high_part], axis=0)
            owner_row = jnp.broadcast_to(owner[y : y + 1, :], both.shape)
            for o in range(owners):
                lhs_ref[o * 2 * EARLY : (o + 1) * 2 * EARLY, lanes] = jnp.where(
                    owner_row == o, both, 0.0
                ).astype(BF16)
            hot_ref[x, :, lanes] = slot_one_hot(slots, y)
        total = total + lax.dot_general(
            lhs_ref[...], hot_ref[x], NT, preferred_element_type=F32
        )
    total = total.reshape(owners, 2 * EARLY, LANES)
    table_ref[...] = total[:, :EARLY, :] + total[:, EARLY:, :]


def target_rows(pos, radius):
    weight = 4.0 / (radius * radius)
    cx, cy, cz = pos[0] - 0.5, pos[1] - 0.5, pos[2] - 0.5
    lines = (
        -2.0 * cx * weight, -2.0 * cy * weight, -2.0 * cz * weight,
        weight, weight, weight,
        (cx * cx + cy * cy + cz * cz) * weight, jnp.zeros_like(weight),
    )
    parts = [three_parts(line) for line in lines]
    return [part[k] for k in range(3) for part in parts]


def target_matrix(coef):
    one, two, three = coef[0:8], coef[8:16], coef[16:24]
    stacked = jnp.concatenate([one, one, two, two, one, three], axis=0)
    return stacked.T.astype(BF16)


def source_matrix(line, root, squares):
    value = jnp.where(squares, line * line, line) * (root * root)
    one, two, three = three_parts(value)
    first = jnp.concatenate([one, two], axis=0).astype(BF16)
    last = jnp.concatenate([three, one], axis=0).astype(BF16)
    return jnp.concatenate([first, first, last], axis=0)


def fifth_root(mass):
    root = jnp.exp(0.2 * jnp.log(mass))
    square = root * root
    return 0.8 * root + 0.2 * mass / (square * square)


def store_source(nat_ref, start, count, columns, mass):
    cx, cy, cz = [column - 0.5 for column in columns]
    one = jnp.ones_like(cx)
    for kind, line in enumerate((cx, cy, cz, cx, cy, cz, one, fifth_root(mass))):
        nat_ref[start + kind * 8 : start + kind * 8 + count, :] = line


def pair_sum(target, sources, roots):
    rows = 32
    chunks = [None] * (LANES // rows)
    for first in range(0, len(sources), 2):
        group = sources[first : first + 2]
        right = group[0] if len(group) == 1 else jnp.concatenate(group, axis=1)
        squared = jnp.dot(target, right, preferred_element_type=F32)
        limits = []
        for root in roots[first : first + 2]:
            reach = 4.0 * root
            limits.append(
                [jnp.broadcast_to(line, (rows, LANES)) for line in (root, reach, reach * reach)]
            )
        for r in range(len(chunks)):
            for k, (root, reach, most) in enumerate(limits):
                t = squared[r * rows : (r + 1) * rows, k * LANES : (k + 1) * LANES]
                t = jnp.maximum(jnp.minimum(t, most), 1e-12)
                u = t * lax.rsqrt(t)
                f = reach - u
                f = f * f
                f = f * f
                term = f * (root + u)
                chunks[r] = term if chunks[r] is None else chunks[r] + term
    return jnp.concatenate(chunks, axis=0)


def column_sums(totals):
    lane = lax.broadcasted_iota(jnp.int32, (LANES, LANES), 1)
    columns = jnp.zeros((LANES, LANES), F32)
    for k, total in enumerate(totals):
        columns = jnp.where(lane == k, jnp.sum(total, axis=1, keepdims=True), columns)
    return columns.T[: len(totals), :]


def square_mask():
    kind = lax.broadcasted_iota(jnp.int32, (8, LANES), 0)
    return (kind >= 3) & (kind < 6)


def block_pairs(
    x_first, x_step, x_count, code_ref, pos_ref, mass_ref, smooth_ref, prev_ref, next_ref,
    out_ref, match_ref, nat_ref, src_ref, shift_ref, tgt_ref,
):
    blocks_x, blocks_y, _ = mass_ref.shape
    listed = code_ref.shape[0]
    null = (blocks_x + 2) * blocks_y
    for xe in range(blocks_x + 2):
        if xe == 0 or xe == blocks_x + 1:
            ref = prev_ref if xe == 0 else next_ref
            if ref is None:
                continue
            store_source(nat_ref, xe * 64, blocks_y, [ref[c] for c in range(3)], ref[3])
        else:
            columns = [pos_ref[c, xe - 1] for c in range(3)]
            store_source(nat_ref, xe * 64, blocks_y, columns, mass_ref[xe - 1])
        for y in range(blocks_y):
            src_ref[xe * blocks_y + y] = nat_ref[pl.ds(xe * 64 + y, 8, stride=8), :]
    src_ref[null] = jnp.zeros((8, LANES), F32)
    kind = lax.broadcasted_iota(jnp.int32, (8, LANES), 0)
    for code in range(9):
        along_x = jnp.where((kind == 0) | (kind == 3), float(code // 3 - 1), 0.0)
        along_y = jnp.where((kind == 1) | (kind == 4), float(code % 3 - 1), 0.0)
        shift_ref[code] = along_x + along_y
    squares = square_mask()
    for k in range(x_count):
        x = x_first + k * x_step
        lines = target_rows([pos_ref[c, x] for c in range(3)], smooth_ref[x])
        for row, line in enumerate(lines):
            tgt_ref[k, row * blocks_y : (row + 1) * blocks_y, :] = line

    def one_x(turn, carry):
        x = x_first + turn * x_step
        totals = []
        for y in range(blocks_y):
            target = target_matrix(tgt_ref[turn, pl.ds(y, 24, stride=blocks_y), :])
            if y == 0:
                match_ref[turn, 0] = target
            if y == blocks_y - 1:
                match_ref[turn, 1] = target
            sources, roots = [], []
            for k in range(listed):
                code = code_ref[k, x, y]
                step_x = (code * 11) >> 5
                near_y = y + code - 3 * step_x - 1
                inside = (near_y >= 0) & (near_y < blocks_y)
                line = src_ref[jnp.where(inside, (x + step_x) * blocks_y + near_y, null)]
                root = jnp.broadcast_to(line[7:8], line.shape)
                sources.append(source_matrix(line + shift_ref[code], root, squares))
                roots.append(root[0:1])
            totals.append(pair_sum(target, sources, roots))
        out_ref[turn] = column_sums(totals)
        return carry

    lax.fori_loop(0, x_count, one_x, 0)


def middle_kernel(
    code_ref, pos_ref, mass_ref, smooth_ref, column_ref, out_ref, match_ref, *scratch
):
    blocks_x, blocks_y, _ = mass_ref.shape
    for side in range(2):
        y = side * (blocks_y - 1)
        for x in range(blocks_x):
            for c in range(3):
                column_ref[side, c, x : x + 1, :] = pos_ref[c, x, y : y + 1, :]
            column_ref[side, 3, x : x + 1, :] = mass_ref[x, y : y + 1, :]
    block_pairs(
        1, 1, blocks_x - 2, code_ref, pos_ref, mass_ref, smooth_ref, None, None,
        out_ref, match_ref, *scratch,
    )


def edge_kernel(
    code_ref, pos_ref, mass_ref, smooth_ref, prev_ref, next_ref, out_ref, match_ref, *scratch
):
    blocks_x = mass_ref.shape[0]
    block_pairs(
        0, blocks_x - 1, 2, code_ref, pos_ref, mass_ref, smooth_ref, prev_ref, next_ref,
        out_ref, match_ref, *scratch,
    )


def pair_scratch(blocks_x, blocks_y, x_count):
    return [
        pltpu.VMEM(((blocks_x + 2) * 64, LANES), F32),
        pltpu.VMEM(((blocks_x + 2) * blocks_y + 1, 8, LANES), F32),
        pltpu.VMEM((9, 8, LANES), F32),
        pltpu.VMEM((x_count, 24 * blocks_y, LANES), F32),
    ]


def rim_kernel(
    code_ref, middle_ref, edge_ref, middle_match_ref, edge_match_ref, mass_ref, smooth_ref,
    low_ref, high_ref, rows_ref, hot_ref, early_ref,
    sum_ref, table_ref, nat_ref, md_ref, lhs_ref,
):
    blocks_x, blocks_y, _ = mass_ref.shape
    owners = early_ref.shape[0]
    listed = code_ref.shape[0]
    for side, ref in enumerate((low_ref, high_ref)):
        store_source(nat_ref, side * 64, blocks_x + 2, [ref[c] for c in range(3)], ref[3])
    kind = lax.broadcasted_iota(jnp.int32, (8, LANES), 0)
    squares = square_mask()
    totals = []
    for x in range(blocks_x):
        edge = x == 0 or x == blocks_x - 1
        turn = (1 if x else 0) if edge else x - 1
        sum_ref[x] = (edge_ref if edge else middle_ref)[turn]
        for side in range(2):
            y = side * (blocks_y - 1)
            target = (edge_match_ref if edge else middle_match_ref)[turn, side]
            sources, roots = [], []
            for step_x in range(3):
                wanted = step_x * 3 + side * 2
                found = code_ref[0, x, y] == wanted
                for k in range(1, listed):
                    found = found | (code_ref[k, x, y] == wanted)
                along_x = jnp.where((kind == 0) | (kind == 3), float(step_x - 1), 0.0)
                along_y = jnp.where((kind == 1) | (kind == 4), float(side * 2 - 1), 0.0)
                line = nat_ref[pl.ds(side * 64 + x + step_x, 8, stride=8), :]
                root = jnp.broadcast_to(line[7:8], line.shape) * jnp.where(found, 1.0, 0.0)
                sources.append(source_matrix(line + along_x + along_y, root, squares))
                roots.append(root[0:1])
            totals.append(pair_sum(target, sources, roots))
    sums = column_sums(totals)
    total = jnp.zeros((LANES, 2 * owners), F32)
    owner_ids = lax.broadcasted_iota(jnp.int32, (owners, LANES), 0)
    for x in range(blocks_x):
        for side in range(2):
            y = side * (blocks_y - 1)
            sum_ref[x, y : y + 1, :] += sums[2 * x + side : 2 * x + side + 1, :]
        radius = smooth_ref[x]
        density = sum_ref[x] * DENSITY_FACTOR / (radius * radius * radius)
        moment = mass_ref[x] * density
        high_part = rounded(moment)
        low_part = moment - high_part
        owner = rows_ref[x] >> 7
        for y in range(blocks_y):
            lanes = slice(y * LANES, (y + 1) * LANES)
            mine = jnp.broadcast_to(owner[y : y + 1, :], owner_ids.shape) == owner_ids
            lhs_ref[:, lanes] = jnp.concatenate(
                [
                    jnp.where(mine, jnp.broadcast_to(part[y : y + 1, :], mine.shape), 0.0)
                    for part in (high_part, low_part)
                ],
                axis=0,
            ).astype(BF16)
        total = total + lax.dot_general(
            hot_ref[x], lhs_ref[...], NT, preferred_element_type=F32
        )
    total = total.T
    md_ref[...] = total[:owners] + total[owners:]
    core, my_chip = lax.axis_index("core"), lax.axis_index("chip")
    for other in range(2):
        for step in range(owners // 2):
            owner = 2 * (my_chip ^ step) + (core ^ other)
            table_ref[other, step, :EARLY, :] = early_ref[owner]
            table_ref[other, step, EARLY : EARLY + 1, :] = md_ref[pl.ds(owner, 1), :]


def ring(value, axis, step):
    count = lax.axis_size(axis)
    return lax.ppermute(value, axis, [(i, (i + step) % count) for i in range(count)])


def swap(value, axis, step):
    count = lax.axis_size(axis)
    return lax.ppermute(value, axis, [(i, i ^ step) for i in range(count)])


def added(parts):
    while len(parts) > 1:
        parts = [sum(parts[k : k + 2][1:], parts[k]) for k in range(0, len(parts), 2)]
    return parts[0]


def to_owner(table):
    table = table[0] + swap(table[1], "core", 1)
    while table.shape[0] > 1:
        ways = min(4, table.shape[0])
        part = table.shape[0] // ways
        table = added(
            [table[:part]]
            + [swap(table[k * part : (k + 1) * part], "chip", k * part) for k in range(1, ways)]
        )
    return table[0]


def summed(value, axis):
    count = lax.axis_size(axis)
    if count & (count - 1):
        return lax.psum(value, axis)
    step = 1
    while step < count:
        ways = min(4, count // step)
        value = added([value] + [swap(value, axis, k * step) for k in range(1, ways)])
        step *= ways
    return value


def shards(positions, velocities, masses, smoothing, neighbours, particle_group, group_row):
    blocks_x, blocks_y, block_len = masses.shape
    dom_count, sub_count = lax.axis_size("dom"), lax.axis_size("chip") * lax.axis_size("core")
    owners = sub_count
    chunk = blocks_y * block_len
    shape = jax.ShapeDtypeStruct
    codes = neighbours.transpose(2, 0, 1)
    packed = jnp.concatenate([positions, masses[None]], axis=0)
    prev = ring(packed[:, blocks_x - 1], "dom", 1)
    following = ring(packed[:, 0], "dom", -1)
    columns, middle, middle_match = pl.pallas_call(
        middle_kernel,
        out_shape=(
            shape((2, 4, blocks_x, LANES), F32),
            shape((blocks_x - 2, blocks_y, LANES), F32),
            shape((blocks_x - 2, 2, LANES, 48), BF16),
        ),
        in_specs=[SMEM] + [VMEM] * 3,
        out_specs=(VMEM,) * 3,
        scratch_shapes=pair_scratch(blocks_x, blocks_y, blocks_x - 2),
        compiler_params=params(),
        cost_estimate=pl.CostEstimate(
            flops=1_000_000_000, bytes_accessed=400_000, transcendentals=1_300_000
        ),
        name="middle_pairs",
    )(codes, positions, masses, smoothing)
    early, rows, hot = pl.pallas_call(
        functools.partial(moments_kernel, blocks_x * dom_count, blocks_y * sub_count),
        out_shape=(
            shape((owners, EARLY, LANES), F32),
            shape(masses.shape, jnp.int32),
            shape((blocks_x, LANES, chunk), BF16),
        ),
        in_specs=[VMEM] * 6,
        out_specs=(VMEM,) * 3,
        scratch_shapes=[
            pltpu.VMEM((blocks_x * EARLY * blocks_y, LANES), F32),
            pltpu.VMEM((owners * 2 * EARLY, chunk), BF16),
        ],
        compiler_params=params(),
        cost_estimate=pl.CostEstimate(
            flops=500_000_000, bytes_accessed=1_400_000, transcendentals=0
        ),
        name="moments_by_row",
    )(middle, positions, velocities, masses, particle_group, group_row.reshape(-1, LANES))
    low, high = [
        ring(
            jnp.concatenate([prev[:, y : y + 1], columns[side], following[:, y : y + 1]], axis=1),
            ("chip", "core"),
            step,
        )
        for side, y, step in ((1, blocks_y - 1, 1), (0, 0, -1))
    ]
    edge, edge_match = pl.pallas_call(
        edge_kernel,
        out_shape=(shape((2, blocks_y, LANES), F32), shape((2, 2, LANES, 48), BF16)),
        in_specs=[SMEM] + [VMEM] * 5,
        out_specs=(VMEM, VMEM),
        scratch_shapes=pair_scratch(blocks_x, blocks_y, 2),
        compiler_params=params(),
        cost_estimate=pl.CostEstimate(
            flops=1_000_000_000, bytes_accessed=400_000, transcendentals=1_300_000
        ),
        name="edge_pairs",
    )(codes, positions, masses, smoothing, prev, following)
    sums, table = pl.pallas_call(
        rim_kernel,
        out_shape=(shape(masses.shape, F32), shape((2, owners // 2, EARLY + 1, LANES), F32)),
        in_specs=[SMEM] + [VMEM] * 11,
        out_specs=(VMEM, VMEM),
        scratch_shapes=[
            pltpu.VMEM((128, LANES), F32),
            pltpu.VMEM((owners, LANES), F32),
            pltpu.VMEM((2 * owners, chunk), BF16),
        ],
        compiler_params=params(),
        cost_estimate=pl.CostEstimate(
            flops=200_000_000, bytes_accessed=400_000, transcendentals=400_000
        ),
        name="rim_pairs_and_table",
    )(
        codes, middle, edge, middle_match, edge_match, masses, smoothing, low, high, rows, hot, early
    )
    density = sums * DENSITY_FACTOR / (smoothing * smoothing * smoothing)
    return (density, summed(to_owner(table), "dom"))


def solution(mesh):
    dom_count, sub_count = mesh.devices.shape
    mesh = jax.sharding.Mesh(
        mesh.devices.reshape(dom_count, sub_count // 2, 2), ("dom", "chip", "core")
    )
    sub = ("chip", "core")
    in_specs = (
        P(None, "dom", sub, None),
        P(None, "dom", sub, None),
        P("dom", sub, None),
        P("dom", sub, None),
        P("dom", sub, None),
        P("dom", sub, None),
        P(),
    )
    out_specs = (P("dom", sub, None), P(None, sub))
    return jax.shard_map(shards, mesh=mesh, in_specs=in_specs, out_specs=out_specs, check_vma=False)
```

```python
import functools
import math

import jax
import jax.numpy as jnp
from jax import lax
from jax.experimental import pallas as pl
from jax.experimental.pallas import tpu as pltpu
from jax.sharding import PartitionSpec as P

F32 = jnp.float32
BF16 = jnp.bfloat16
LANES = 128
EARLY = 16
DENSITY_FACTOR = 21.0 / (16.0 * math.pi) / 256.0
VMEM = pl.BlockSpec(memory_space=pltpu.VMEM)
SMEM = pl.BlockSpec(memory_space=pltpu.SMEM)
NT = (((1,), (1,)), ((), ()))


def params():
    return pltpu.CompilerParams(vmem_limit_bytes=40 * 1024 * 1024)


def rounded(value):
    return value.astype(BF16).astype(F32)


def three_parts(value):
    first = rounded(value)
    rest = value - first
    second = rounded(rest)
    return first, second, rest - second


def slot_one_hot(slots, y):
    row = jnp.broadcast_to(slots[y : y + 1, :], (LANES, LANES))
    ids = lax.broadcasted_iota(jnp.int32, (LANES, LANES), 0)
    return jnp.where(ids == row, 1.0, 0.0).astype(BF16)


def moments_kernel(
    nx_total, ny_total, after_ref, pos_ref, vel_ref, mass_ref, group_ref, row_ref,
    table_ref, rows_ref, hot_ref, feat_ref, lhs_ref,
):
    blocks_x, blocks_y, _ = mass_ref.shape
    owners = table_ref.shape[0]
    table_rows = row_ref.shape[0]
    base_x = (lax.axis_index("dom") * blocks_x).astype(F32)
    base_y = ((2 * lax.axis_index("chip") + lax.axis_index("core")) * blocks_y).astype(F32)
    y_iota = lax.broadcasted_iota(jnp.int32, (blocks_y, LANES), 0).astype(F32)
    total = jnp.zeros((owners * 2 * EARLY, LANES), F32)
    for x in range(blocks_x):
        group = group_ref[x]
        low = group & (LANES - 1)
        high = group >> 7
        rows = jnp.zeros_like(group)
        for r in range(table_rows):
            line = jnp.broadcast_to(row_ref[r : r + 1, :], group.shape)
            picked = jnp.take_along_axis(line, low, axis=1)
            rows = jnp.where(high == r, picked, rows)
        rows_ref[x] = rows
        mass = mass_ref[x]
        gx = (base_x + float(x) + pos_ref[0, x]) / float(nx_total)
        gy = (base_y + y_iota + pos_ref[1, x]) / float(ny_total)
        gz = pos_ref[2, x]
        vx, vy, vz = vel_ref[0, x], vel_ref[1, x], vel_ref[2, x]
        mx, my, mz = mass * gx, mass * gy, mass * gz
        features = (
            mass, mx, my, mz, mass * vx, mass * vy, mass * vz,
            mass * (gy * vz - gz * vy), mass * (gz * vx - gx * vz), mass * (gx * vy - gy * vx),
            mx * gx, my * gy, mz * gz, mx * gy, mx * gz, my * gz,
        )
        for f, feature in enumerate(features):
            start = (x * EARLY + f) * blocks_y
            feat_ref[start : start + blocks_y, :] = feature
        slots = rows & (LANES - 1)
        owner = rows >> 7
        for y in range(blocks_y):
            lanes = slice(y * LANES, (y + 1) * LANES)
            feats = feat_ref[pl.ds(x * EARLY * blocks_y + y, EARLY, stride=blocks_y), :]
            high_part = rounded(feats)
            both = jnp.concatenate([high_part, feats - high_part], axis=0)
            owner_row = jnp.broadcast_to(owner[y : y + 1, :], both.shape)
            for o in range(owners):
                lhs_ref[o * 2 * EARLY : (o + 1) * 2 * EARLY, lanes] = jnp.where(
                    owner_row == o, both, 0.0
                ).astype(BF16)
            hot_ref[x, :, lanes] = slot_one_hot(slots, y)
        total = total + lax.dot_general(
            lhs_ref[...], hot_ref[x], NT, preferred_element_type=F32
        )
    total = total.reshape(owners, 2 * EARLY, LANES)
    table_ref[...] = total[:, :EARLY, :] + total[:, EARLY:, :]


def target_rows(pos, radius):
    weight = 4.0 / (radius * radius)
    cx, cy, cz = pos[0] - 0.5, pos[1] - 0.5, pos[2] - 0.5
    lines = (
        -2.0 * cx * weight, -2.0 * cy * weight, -2.0 * cz * weight,
        weight, weight, weight,
        (cx * cx + cy * cy + cz * cz) * weight, jnp.zeros_like(weight),
    )
    parts = [three_parts(line) for line in lines]
    return [part[k] for k in range(3) for part in parts]


def target_matrix(coef):
    one, two, three = coef[0:8], coef[8:16], coef[16:24]
    stacked = jnp.concatenate([one, one, two, two, one, three], axis=0)
    return stacked.T.astype(BF16)


def source_matrix(line, root, squares):
    value = jnp.where(squares, line * line, line) * (root * root)
    one, two, three = three_parts(value)
    first = jnp.concatenate([one, two], axis=0).astype(BF16)
    last = jnp.concatenate([three, one], axis=0).astype(BF16)
    return jnp.concatenate([first, first, last], axis=0)


def fifth_root(mass):
    root = jnp.exp(0.2 * jnp.log(mass))
    square = root * root
    return 0.8 * root + 0.2 * mass / (square * square)


def store_source(nat_ref, start, count, columns, mass):
    cx, cy, cz = [column - 0.5 for column in columns]
    one = jnp.ones_like(cx)
    for kind, line in enumerate((cx, cy, cz, cx, cy, cz, one, fifth_root(mass))):
        nat_ref[start + kind * 8 : start + kind * 8 + count, :] = line


def pair_sums(sides):
    rows = 32
    steps = []
    for target, sources, roots, total in sides:
        count = roots.shape[0]
        for first in range(0, count, 2):
            steps.append((target, sources, roots, total, first, min(2, count - first), count))

    def product(step):
        target, sources, _, _, first, width, _ = step
        right = sources[:, first * LANES : (first + width) * LANES]
        return jnp.dot(target[...], right, preferred_element_type=F32)

    ready = product(steps[0])
    chunks = None
    for number, (_, _, roots, total, first, width, count) in enumerate(steps):
        squared = ready
        if number + 1 < len(steps):
            ready = product(steps[number + 1])
        if first == 0:
            chunks = [None] * (LANES // rows)
        limits = []
        for k in range(width):
            root = roots[first + k : first + k + 1, :]
            reach = 4.0 * root
            limits.append(
                [jnp.broadcast_to(line, (rows, LANES)) for line in (root, reach, reach * reach)]
            )
        for r in range(len(chunks)):
            for k, (root, reach, most) in enumerate(limits):
                t = squared[r * rows : (r + 1) * rows, k * LANES : (k + 1) * LANES]
                t = jnp.maximum(jnp.minimum(t, most), 1e-12)
                u = t * lax.rsqrt(t)
                f = reach - u
                f = f * f
                f = f * f
                term = f * (root + u)
                chunks[r] = term if chunks[r] is None else chunks[r] + term
        if first + width == count:
            for r, chunk in enumerate(chunks):
                total[r * rows : (r + 1) * rows, :] = chunk


def column_sums(totals):
    lane = lax.broadcasted_iota(jnp.int32, (LANES, LANES), 1)
    columns = jnp.zeros((LANES, LANES), F32)
    for k, total in enumerate(totals):
        columns = jnp.where(lane == k, jnp.sum(total, axis=1, keepdims=True), columns)
    return columns.T[: len(totals), :]


def square_mask():
    kind = lax.broadcasted_iota(jnp.int32, (8, LANES), 0)
    return (kind >= 3) & (kind < 6)


def block_pairs(
    x_first, x_step, x_count, code_ref, pos_ref, mass_ref, smooth_ref, prev_ref, next_ref,
    out_ref, match_ref, nat_ref, src_ref, shift_ref, tgt_ref, mat_ref, near_ref, root_ref, total_ref,
):
    blocks_x, blocks_y, _ = mass_ref.shape
    listed = code_ref.shape[0]
    null = (blocks_x + 2) * blocks_y
    for xe in range(blocks_x + 2):
        if xe == 0 or xe == blocks_x + 1:
            ref = prev_ref if xe == 0 else next_ref
            if ref is None:
                continue
            store_source(nat_ref, xe * 64, blocks_y, [ref[c] for c in range(3)], ref[3])
        else:
            columns = [pos_ref[c, xe - 1] for c in range(3)]
            store_source(nat_ref, xe * 64, blocks_y, columns, mass_ref[xe - 1])
        for y in range(blocks_y):
            src_ref[xe * blocks_y + y] = nat_ref[pl.ds(xe * 64 + y, 8, stride=8), :]
    src_ref[null] = jnp.zeros((8, LANES), F32)
    kind = lax.broadcasted_iota(jnp.int32, (8, LANES), 0)
    for code in range(9):
        along_x = jnp.where((kind == 0) | (kind == 3), float(code // 3 - 1), 0.0)
        along_y = jnp.where((kind == 1) | (kind == 4), float(code % 3 - 1), 0.0)
        shift_ref[code] = along_x + along_y
    squares = square_mask()
    for k in range(x_count):
        x = x_first + k * x_step
        lines = target_rows([pos_ref[c, x] for c in range(3)], smooth_ref[x])
        for row, line in enumerate(lines):
            tgt_ref[k, row * blocks_y : (row + 1) * blocks_y, :] = line

    blocks = [(turn, y) for turn in range(x_count) for y in range(blocks_y)]
    for number, (turn, y) in enumerate(blocks):
        target = target_matrix(tgt_ref[turn, pl.ds(y, 24, stride=blocks_y), :])
        mat_ref[number] = target
        if y == 0:
            match_ref[turn, 0] = target
        if y == blocks_y - 1:
            match_ref[turn, 1] = target
    for number, (turn, y) in enumerate(blocks):
        x = x_first + turn * x_step
        for k in range(listed):
            code = code_ref[k, x, y]
            step_x = (code * 11) >> 5
            near_y = y + code - 3 * step_x - 1
            inside = (near_y >= 0) & (near_y < blocks_y)
            line = src_ref[jnp.where(inside, (x + step_x) * blocks_y + near_y, null)]
            root = jnp.broadcast_to(line[7:8], line.shape)
            near_ref[number, :, k * LANES : (k + 1) * LANES] = source_matrix(
                line + shift_ref[code], root, squares
            )
            root_ref[number, k : k + 1, :] = root[0:1]
    pair_sums(
        [
            (mat_ref.at[n], near_ref.at[n], root_ref.at[n, pl.ds(0, listed)], total_ref.at[n])
            for n in range(len(blocks))
        ]
    )
    for turn in range(x_count):
        out_ref[turn] = column_sums([total_ref[turn * blocks_y + y] for y in range(blocks_y)])


def middle_kernel(
    code_ref, pos_ref, mass_ref, smooth_ref, column_ref, out_ref, match_ref, *scratch
):
    blocks_x, blocks_y, _ = mass_ref.shape
    for side in range(2):
        y = side * (blocks_y - 1)
        for x in range(blocks_x):
            for c in range(3):
                column_ref[side, c, x : x + 1, :] = pos_ref[c, x, y : y + 1, :]
            column_ref[side, 3, x : x + 1, :] = mass_ref[x, y : y + 1, :]
    block_pairs(
        1, 1, blocks_x - 2, code_ref, pos_ref, mass_ref, smooth_ref, None, None,
        out_ref, match_ref, *scratch,
    )


def edge_kernel(
    code_ref, pos_ref, mass_ref, smooth_ref, prev_ref, next_ref, out_ref, match_ref, *scratch
):
    blocks_x = mass_ref.shape[0]
    block_pairs(
        0, blocks_x - 1, 2, code_ref, pos_ref, mass_ref, smooth_ref, prev_ref, next_ref,
        out_ref, match_ref, *scratch,
    )


def pair_scratch(blocks_x, blocks_y, x_count, listed):
    return [
        pltpu.VMEM(((blocks_x + 2) * 64, LANES), F32),
        pltpu.VMEM(((blocks_x + 2) * blocks_y + 1, 8, LANES), F32),
        pltpu.VMEM((9, 8, LANES), F32),
        pltpu.VMEM((x_count, 24 * blocks_y, LANES), F32),
    ] + product_scratch(x_count * blocks_y, listed)


def product_scratch(blocks, listed):
    return [
        pltpu.VMEM((blocks, LANES, 48), BF16),
        pltpu.VMEM((blocks, 48, listed * LANES), BF16),
        pltpu.VMEM((blocks, 8, LANES), F32),
        pltpu.VMEM((blocks, LANES, LANES), F32),
    ]


def rim_kernel(
    code_ref, middle_ref, edge_ref, middle_match_ref, edge_match_ref, mass_ref, smooth_ref,
    low_ref, high_ref, rows_ref, hot_ref, early_ref,
    sum_ref, table_ref, nat_ref, md_ref, lhs_ref, near_ref, root_ref, total_ref,
):
    blocks_x, blocks_y, _ = mass_ref.shape
    owners = early_ref.shape[0]
    listed = code_ref.shape[0]
    for side, ref in enumerate((low_ref, high_ref)):
        store_source(nat_ref, side * 64, blocks_x + 2, [ref[c] for c in range(3)], ref[3])
    kind = lax.broadcasted_iota(jnp.int32, (8, LANES), 0)
    squares = square_mask()
    sides = []
    for x in range(blocks_x):
        edge = x == 0 or x == blocks_x - 1
        turn = (1 if x else 0) if edge else x - 1
        sum_ref[x] = (edge_ref if edge else middle_ref)[turn]
        for side in range(2):
            y = side * (blocks_y - 1)
            number = 2 * x + side
            for step_x in range(3):
                wanted = step_x * 3 + side * 2
                found = code_ref[0, x, y] == wanted
                for k in range(1, listed):
                    found = found | (code_ref[k, x, y] == wanted)
                along_x = jnp.where((kind == 0) | (kind == 3), float(step_x - 1), 0.0)
                along_y = jnp.where((kind == 1) | (kind == 4), float(side * 2 - 1), 0.0)
                line = nat_ref[pl.ds(side * 64 + x + step_x, 8, stride=8), :]
                root = jnp.broadcast_to(line[7:8], line.shape) * jnp.where(found, 1.0, 0.0)
                near_ref[number, :, step_x * LANES : (step_x + 1) * LANES] = source_matrix(
                    line + along_x + along_y, root, squares
                )
                root_ref[number, step_x : step_x + 1, :] = root[0:1]
            match_ref = (edge_match_ref if edge else middle_match_ref).at[turn, side]
            sides.append(
                (match_ref, near_ref.at[number], root_ref.at[number, pl.ds(0, 3)], total_ref.at[number])
            )
    pair_sums(sides)
    totals = [total_ref[number] for number in range(len(sides))]
    sums = column_sums(totals)
    total = jnp.zeros((LANES, 2 * owners), F32)
    owner_ids = lax.broadcasted_iota(jnp.int32, (owners, LANES), 0)
    for x in range(blocks_x):
        for side in range(2):
            y = side * (blocks_y - 1)
            sum_ref[x, y : y + 1, :] += sums[2 * x + side : 2 * x + side + 1, :]
        radius = smooth_ref[x]
        density = sum_ref[x] * DENSITY_FACTOR / (radius * radius * radius)
        moment = mass_ref[x] * density
        high_part = rounded(moment)
        low_part = moment - high_part
        owner = rows_ref[x] >> 7
        for y in range(blocks_y):
            lanes = slice(y * LANES, (y + 1) * LANES)
            mine = jnp.broadcast_to(owner[y : y + 1, :], owner_ids.shape) == owner_ids
            lhs_ref[:, lanes] = jnp.concatenate(
                [
                    jnp.where(mine, jnp.broadcast_to(part[y : y + 1, :], mine.shape), 0.0)
                    for part in (high_part, low_part)
                ],
                axis=0,
            ).astype(BF16)
        total = total + lax.dot_general(
            hot_ref[x], lhs_ref[...], NT, preferred_element_type=F32
        )
    total = total.T
    md_ref[...] = total[:owners] + total[owners:]
    core, my_chip = lax.axis_index("core"), lax.axis_index("chip")
    for other in range(2):
        for step in range(owners // 2):
            owner = 2 * (my_chip ^ step) + (core ^ other)
            table_ref[other, step, :EARLY, :] = early_ref[owner]
            table_ref[other, step, EARLY : EARLY + 1, :] = md_ref[pl.ds(owner, 1), :]


def ring(value, axis, step):
    count = lax.axis_size(axis)
    return lax.ppermute(value, axis, [(i, (i + step) % count) for i in range(count)])


def swap(value, axis, step):
    count = lax.axis_size(axis)
    return lax.ppermute(value, axis, [(i, i ^ step) for i in range(count)])


def added(parts):
    while len(parts) > 1:
        parts = [sum(parts[k : k + 2][1:], parts[k]) for k in range(0, len(parts), 2)]
    return parts[0]


def to_owner(table):
    table = table[0] + swap(table[1], "core", 1)
    while table.shape[0] > 1:
        ways = min(4, table.shape[0])
        part = table.shape[0] // ways
        table = added(
            [table[:part]]
            + [swap(table[k * part : (k + 1) * part], "chip", k * part) for k in range(1, ways)]
        )
    return table[0]


def summed(value, axis):
    count = lax.axis_size(axis)
    if count & (count - 1):
        return lax.psum(value, axis)
    step = 1
    while step < count:
        ways = min(4, count // step)
        value = added([value] + [swap(value, axis, k * step) for k in range(1, ways)])
        step *= ways
    return value


def shards(positions, velocities, masses, smoothing, neighbours, particle_group, group_row):
    blocks_x, blocks_y, block_len = masses.shape
    dom_count, sub_count = lax.axis_size("dom"), lax.axis_size("chip") * lax.axis_size("core")
    owners = sub_count
    chunk = blocks_y * block_len
    shape = jax.ShapeDtypeStruct
    codes = neighbours.transpose(2, 0, 1)
    packed = jnp.concatenate([positions, masses[None]], axis=0)
    prev = ring(packed[:, blocks_x - 1], "dom", 1)
    following = ring(packed[:, 0], "dom", -1)
    columns, middle, middle_match = pl.pallas_call(
        middle_kernel,
        out_shape=(
            shape((2, 4, blocks_x, LANES), F32),
            shape((blocks_x - 2, blocks_y, LANES), F32),
            shape((blocks_x - 2, 2, LANES, 48), BF16),
        ),
        in_specs=[SMEM] + [VMEM] * 3,
        out_specs=(VMEM,) * 3,
        scratch_shapes=pair_scratch(blocks_x, blocks_y, blocks_x - 2, codes.shape[0]),
        compiler_params=params(),
        cost_estimate=pl.CostEstimate(
            flops=4_000_000_000, bytes_accessed=400_000, transcendentals=1_300_000
        ),
        name="middle_pairs",
    )(codes, positions, masses, smoothing)
    early, rows, hot = pl.pallas_call(
        functools.partial(moments_kernel, blocks_x * dom_count, blocks_y * sub_count),
        out_shape=(
            shape((owners, EARLY, LANES), F32),
            shape(masses.shape, jnp.int32),
            shape((blocks_x, LANES, chunk), BF16),
        ),
        in_specs=[VMEM] * 6,
        out_specs=(VMEM,) * 3,
        scratch_shapes=[
            pltpu.VMEM((blocks_x * EARLY * blocks_y, LANES), F32),
            pltpu.VMEM((owners * 2 * EARLY, chunk), BF16),
        ],
        compiler_params=params(),
        cost_estimate=pl.CostEstimate(
            flops=500_000_000, bytes_accessed=1_400_000, transcendentals=0
        ),
        name="moments_by_row",
    )(middle, positions, velocities, masses, particle_group, group_row.reshape(-1, LANES))
    low, high = [
        ring(
            jnp.concatenate([prev[:, y : y + 1], columns[side], following[:, y : y + 1]], axis=1),
            ("chip", "core"),
            step,
        )
        for side, y, step in ((1, blocks_y - 1, 1), (0, 0, -1))
    ]
    edge, edge_match = pl.pallas_call(
        edge_kernel,
        out_shape=(shape((2, blocks_y, LANES), F32), shape((2, 2, LANES, 48), BF16)),
        in_specs=[SMEM] + [VMEM] * 5,
        out_specs=(VMEM, VMEM),
        scratch_shapes=pair_scratch(blocks_x, blocks_y, 2, codes.shape[0]),
        compiler_params=params(),
        cost_estimate=pl.CostEstimate(
            flops=4_000_000_000, bytes_accessed=400_000, transcendentals=1_300_000
        ),
        name="edge_pairs",
    )(codes, positions, masses, smoothing, prev, following)
    sums, table = pl.pallas_call(
        rim_kernel,
        out_shape=(shape(masses.shape, F32), shape((2, owners // 2, EARLY + 1, LANES), F32)),
        in_specs=[SMEM] + [VMEM] * 11,
        out_specs=(VMEM, VMEM),
        scratch_shapes=[
            pltpu.VMEM((128, LANES), F32),
            pltpu.VMEM((owners, LANES), F32),
            pltpu.VMEM((2 * owners, chunk), BF16),
        ]
        + product_scratch(2 * blocks_x, 3)[1:],
        compiler_params=params(),
        cost_estimate=pl.CostEstimate(
            flops=200_000_000, bytes_accessed=400_000, transcendentals=400_000
        ),
        name="rim_pairs_and_table",
    )(
        codes, middle, edge, middle_match, edge_match, masses, smoothing, low, high, rows, hot, early
    )
    density = sums * DENSITY_FACTOR / (smoothing * smoothing * smoothing)
    return (density, summed(to_owner(table), "dom"))


def solution(mesh):
    dom_count, sub_count = mesh.devices.shape
    mesh = jax.sharding.Mesh(
        mesh.devices.reshape(dom_count, sub_count // 2, 2), ("dom", "chip", "core")
    )
    sub = ("chip", "core")
    in_specs = (
        P(None, "dom", sub, None),
        P(None, "dom", sub, None),
        P("dom", sub, None),
        P("dom", sub, None),
        P("dom", sub, None),
        P("dom", sub, None),
        P(),
    )
    out_specs = (P("dom", sub, None), P(None, sub))
    return jax.shard_map(shards, mesh=mesh, in_specs=in_specs, out_specs=out_specs, check_vma=False)
```

```python
import functools
import math

import jax
import jax.numpy as jnp
from jax import lax
from jax.experimental import pallas as pl
from jax.experimental.pallas import tpu as pltpu
from jax.sharding import PartitionSpec as P

F32 = jnp.float32
BF16 = jnp.bfloat16
LANES = 128
EARLY = 16
DENSITY_FACTOR = 21.0 / (16.0 * math.pi) / 256.0
VMEM = pl.BlockSpec(memory_space=pltpu.VMEM)
SMEM = pl.BlockSpec(memory_space=pltpu.SMEM)
NT = (((1,), (1,)), ((), ()))


def params():
    return pltpu.CompilerParams(vmem_limit_bytes=40 * 1024 * 1024)


def rounded(value):
    return value.astype(BF16).astype(F32)


def three_parts(value):
    first = rounded(value)
    rest = value - first
    second = rounded(rest)
    return first, second, rest - second


def slot_one_hot(slots, y):
    row = jnp.broadcast_to(slots[y : y + 1, :], (LANES, LANES))
    ids = lax.broadcasted_iota(jnp.int32, (LANES, LANES), 0)
    return jnp.where(ids == row, 1.0, 0.0).astype(BF16)


def moment_pieces(
    nx_total, ny_total, pos_ref, vel_ref, mass_ref, group_ref, row_ref,
    table_ref, rows_ref, hot_ref, feat_ref, lhs_ref, total_ref,
):
    blocks_x, blocks_y, _ = mass_ref.shape
    owners = table_ref.shape[0]
    table_rows = row_ref.shape[0]
    base_x = (lax.axis_index("dom") * blocks_x).astype(F32)
    base_y = ((2 * lax.axis_index("chip") + lax.axis_index("core")) * blocks_y).astype(F32)
    y_iota = lax.broadcasted_iota(jnp.int32, (blocks_y, LANES), 0).astype(F32)

    def features_of(x):
        group = group_ref[x]
        low = group & (LANES - 1)
        high = group >> 7
        rows = jnp.zeros_like(group)
        for r in range(table_rows):
            line = jnp.broadcast_to(row_ref[r : r + 1, :], group.shape)
            picked = jnp.take_along_axis(line, low, axis=1)
            rows = jnp.where(high == r, picked, rows)
        rows_ref[x] = rows
        mass = mass_ref[x]
        gx = (base_x + float(x) + pos_ref[0, x]) / float(nx_total)
        gy = (base_y + y_iota + pos_ref[1, x]) / float(ny_total)
        gz = pos_ref[2, x]
        vx, vy, vz = vel_ref[0, x], vel_ref[1, x], vel_ref[2, x]
        mx, my, mz = mass * gx, mass * gy, mass * gz
        features = (
            mass, mx, my, mz, mass * vx, mass * vy, mass * vz,
            mass * (gy * vz - gz * vy), mass * (gz * vx - gx * vz), mass * (gx * vy - gy * vx),
            mx * gx, my * gy, mz * gz, mx * gy, mx * gz, my * gz,
        )
        for f, feature in enumerate(features):
            start = (x * EARLY + f) * blocks_y
            feat_ref[start : start + blocks_y, :] = feature

    def operands_of(x, y):
        lanes = slice(y * LANES, (y + 1) * LANES)
        feats = feat_ref[pl.ds(x * EARLY * blocks_y + y, EARLY, stride=blocks_y), :]
        high_part = rounded(feats)
        both = jnp.concatenate([high_part, feats - high_part], axis=0)
        rows = rows_ref[x]
        owner_row = jnp.broadcast_to((rows >> 7)[y : y + 1, :], both.shape)
        for o in range(owners):
            lhs_ref[x, o * 2 * EARLY : (o + 1) * 2 * EARLY, lanes] = jnp.where(
                owner_row == o, both, 0.0
            ).astype(BF16)
        hot_ref[x, :, lanes] = slot_one_hot(rows & (LANES - 1), y)

    def add_product(x):
        product = lax.dot_general(lhs_ref[x], hot_ref[x], NT, preferred_element_type=F32)
        total_ref[...] = product if x == 0 else total_ref[...] + product

    def finish():
        total = total_ref[...].reshape(owners, 2 * EARLY, LANES)
        table_ref[...] = total[:, :EARLY, :] + total[:, EARLY:, :]

    pieces = []
    for x in range(blocks_x):
        pieces.append(functools.partial(features_of, x))
        pieces += [functools.partial(operands_of, x, y) for y in range(blocks_y)]
        pieces.append(functools.partial(add_product, x))
    return pieces + [finish]


def target_rows(pos, radius):
    weight = 1.0 / (radius * radius)
    cx, cy, cz = pos[0] - 0.5, pos[1] - 0.5, pos[2] - 0.5
    lines = (
        -2.0 * cx * weight, -2.0 * cy * weight, -2.0 * cz * weight,
        weight, weight, weight,
        (cx * cx + cy * cy + cz * cz) * weight, jnp.zeros_like(weight),
    )
    parts = [three_parts(line) for line in lines]
    return [part[k] for k in range(3) for part in parts]


def target_matrix(coef):
    one, two, three = coef[0:8], coef[8:16], coef[16:24]
    stacked = jnp.concatenate([one, one, two, two, one, three], axis=0)
    return stacked.T.astype(BF16)


def source_matrix(line, root, squares):
    value = jnp.where(squares, line * line, line) * (root * root)
    one, two, three = three_parts(value)
    first = jnp.concatenate([one, two], axis=0).astype(BF16)
    last = jnp.concatenate([three, one], axis=0).astype(BF16)
    return jnp.concatenate([first, first, last], axis=0)


def fifth_root(mass):
    root = jnp.exp(0.2 * jnp.log(mass))
    square = root * root
    return 0.8 * root + 0.2 * mass / (square * square)


def store_source(nat_ref, start, count, columns, mass):
    cx, cy, cz = [column - 0.5 for column in columns]
    one = jnp.ones_like(cx)
    for kind, line in enumerate((cx, cy, cz, cx, cy, cz, one, fifth_root(mass))):
        nat_ref[start + kind * 8 : start + kind * 8 + count, :] = line


def pair_sums(sides, pieces=()):
    rows = 32
    steps = []
    for target, sources, roots, total in sides:
        count = roots.shape[0]
        for first in range(0, count, 2):
            steps.append((target, sources, roots, total, first, min(2, count - first), count))

    def product(step):
        target, sources, _, _, first, width, _ = step
        right = sources[:, first * LANES : (first + width) * LANES]
        return jnp.dot(target[...], right, preferred_element_type=F32)

    ready = product(steps[0])
    chunks = None
    for number, (_, _, roots, total, first, width, count) in enumerate(steps):
        squared = ready
        if number + 1 < len(steps):
            ready = product(steps[number + 1])
        if first == 0:
            chunks = [None] * (LANES // rows)
        limits = []
        for k in range(width):
            root = roots[first + k : first + k + 1, :]
            reach = 4.0 * root
            limits.append(
                [jnp.broadcast_to(line, (rows, LANES)) for line in (root, reach, reach * root)]
            )
        for r in range(len(chunks)):
            for k, (root, reach, most) in enumerate(limits):
                t = squared[r * rows : (r + 1) * rows, k * LANES : (k + 1) * LANES]
                t = jnp.maximum(jnp.minimum(t, most), 1e-12)
                guess = lax.rsqrt(t.astype(BF16)).astype(F32)
                u = t * guess
                u = u * (3.0 - u * guess)
                f = reach - u
                f = f * f
                f = f * f
                term = f * (root + u)
                chunks[r] = term if chunks[r] is None else chunks[r] + term
        if first + width == count:
            for r, chunk in enumerate(chunks):
                total[r * rows : (r + 1) * rows, :] = chunk
        if number < len(pieces):
            pieces[number]()
    for piece in pieces[len(steps) :]:
        piece()


def column_sums(totals):
    lane = lax.broadcasted_iota(jnp.int32, (LANES, LANES), 1)
    columns = jnp.zeros((LANES, LANES), F32)
    for k, total in enumerate(totals):
        columns = jnp.where(lane == k, jnp.sum(total, axis=1, keepdims=True), columns)
    return columns.T[: len(totals), :]


def square_mask():
    kind = lax.broadcasted_iota(jnp.int32, (8, LANES), 0)
    return (kind >= 3) & (kind < 6)


def block_pairs(
    x_first, x_step, x_count, code_ref, pos_ref, mass_ref, smooth_ref, prev_ref, next_ref,
    out_ref, match_ref, nat_ref, src_ref, shift_ref, tgt_ref, mat_ref, near_ref, root_ref, total_ref,
    pieces=(),
):
    blocks_x, blocks_y, _ = mass_ref.shape
    listed = code_ref.shape[0]
    null = (blocks_x + 2) * blocks_y
    for xe in range(blocks_x + 2):
        if xe == 0 or xe == blocks_x + 1:
            ref = prev_ref if xe == 0 else next_ref
            if ref is None:
                continue
            store_source(nat_ref, xe * 64, blocks_y, [ref[c] for c in range(3)], ref[3])
        else:
            columns = [pos_ref[c, xe - 1] for c in range(3)]
            store_source(nat_ref, xe * 64, blocks_y, columns, mass_ref[xe - 1])
        for y in range(blocks_y):
            src_ref[xe * blocks_y + y] = nat_ref[pl.ds(xe * 64 + y, 8, stride=8), :]
    src_ref[null] = jnp.zeros((8, LANES), F32)
    kind = lax.broadcasted_iota(jnp.int32, (8, LANES), 0)
    for code in range(9):
        along_x = jnp.where((kind == 0) | (kind == 3), float(code // 3 - 1), 0.0)
        along_y = jnp.where((kind == 1) | (kind == 4), float(code % 3 - 1), 0.0)
        shift_ref[code] = along_x + along_y
    squares = square_mask()
    for k in range(x_count):
        x = x_first + k * x_step
        lines = target_rows([pos_ref[c, x] for c in range(3)], smooth_ref[x])
        for row, line in enumerate(lines):
            tgt_ref[k, row * blocks_y : (row + 1) * blocks_y, :] = line

    blocks = [(turn, y) for turn in range(x_count) for y in range(blocks_y)]
    for number, (turn, y) in enumerate(blocks):
        target = target_matrix(tgt_ref[turn, pl.ds(y, 24, stride=blocks_y), :])
        mat_ref[number] = target
        if y == 0:
            match_ref[turn, 0] = target
        if y == blocks_y - 1:
            match_ref[turn, 1] = target
    for number, (turn, y) in enumerate(blocks):
        x = x_first + turn * x_step
        for k in range(listed):
            code = code_ref[k, x, y]
            step_x = (code * 11) >> 5
            near_y = y + code - 3 * step_x - 1
            inside = (near_y >= 0) & (near_y < blocks_y)
            line = src_ref[jnp.where(inside, (x + step_x) * blocks_y + near_y, null)]
            root = jnp.broadcast_to(line[7:8], line.shape)
            near_ref[number, :, k * LANES : (k + 1) * LANES] = source_matrix(
                line + shift_ref[code], root, squares
            )
            root_ref[number, k : k + 1, :] = root[0:1]
    pair_sums(
        [
            (mat_ref.at[n], near_ref.at[n], root_ref.at[n, pl.ds(0, listed)], total_ref.at[n])
            for n in range(len(blocks))
        ],
        pieces,
    )
    for turn in range(x_count):
        out_ref[turn] = column_sums([total_ref[turn * blocks_y + y] for y in range(blocks_y)])


def middle_kernel(
    code_ref, pos_ref, mass_ref, smooth_ref, column_ref, out_ref, match_ref, *scratch
):
    blocks_x, blocks_y, _ = mass_ref.shape
    for side in range(2):
        y = side * (blocks_y - 1)
        for x in range(blocks_x):
            for c in range(3):
                column_ref[side, c, x : x + 1, :] = pos_ref[c, x, y : y + 1, :]
            column_ref[side, 3, x : x + 1, :] = mass_ref[x, y : y + 1, :]
    block_pairs(
        1, 1, blocks_x - 2, code_ref, pos_ref, mass_ref, smooth_ref, None, None,
        out_ref, match_ref, *scratch,
    )


def edge_kernel(
    nx_total, ny_total, code_ref, pos_ref, mass_ref, smooth_ref, prev_ref, next_ref,
    vel_ref, group_ref, row_ref, out_ref, match_ref, table_ref, rows_ref, hot_ref,
    feat_ref, lhs_ref, sum_ref, *scratch
):
    blocks_x = mass_ref.shape[0]
    pieces = moment_pieces(
        nx_total, ny_total, pos_ref, vel_ref, mass_ref, group_ref, row_ref,
        table_ref, rows_ref, hot_ref, feat_ref, lhs_ref, sum_ref,
    )
    block_pairs(
        0, blocks_x - 1, 2, code_ref, pos_ref, mass_ref, smooth_ref, prev_ref, next_ref,
        out_ref, match_ref, *scratch, pieces=pieces,
    )


def pair_scratch(blocks_x, blocks_y, x_count, listed):
    return [
        pltpu.VMEM(((blocks_x + 2) * 64, LANES), F32),
        pltpu.VMEM(((blocks_x + 2) * blocks_y + 1, 8, LANES), F32),
        pltpu.VMEM((9, 8, LANES), F32),
        pltpu.VMEM((x_count, 24 * blocks_y, LANES), F32),
    ] + product_scratch(x_count * blocks_y, listed)


def product_scratch(blocks, listed):
    return [
        pltpu.VMEM((blocks, LANES, 48), BF16),
        pltpu.VMEM((blocks, 48, listed * LANES), BF16),
        pltpu.VMEM((blocks, 8, LANES), F32),
        pltpu.VMEM((blocks, LANES, LANES), F32),
    ]


def rim_kernel(
    code_ref, middle_ref, edge_ref, middle_match_ref, edge_match_ref, mass_ref, smooth_ref,
    low_ref, high_ref, rows_ref, hot_ref, early_ref,
    sum_ref, table_ref, nat_ref, md_ref, lhs_ref, near_ref, root_ref, total_ref,
):
    blocks_x, blocks_y, _ = mass_ref.shape
    owners = early_ref.shape[0]
    listed = code_ref.shape[0]
    for side, ref in enumerate((low_ref, high_ref)):
        store_source(nat_ref, side * 64, blocks_x + 2, [ref[c] for c in range(3)], ref[3])
    kind = lax.broadcasted_iota(jnp.int32, (8, LANES), 0)
    squares = square_mask()
    sides = []
    for x in range(blocks_x):
        edge = x == 0 or x == blocks_x - 1
        turn = (1 if x else 0) if edge else x - 1
        sum_ref[x] = (edge_ref if edge else middle_ref)[turn]
        for side in range(2):
            y = side * (blocks_y - 1)
            number = 2 * x + side
            for step_x in range(3):
                wanted = step_x * 3 + side * 2
                found = code_ref[0, x, y] == wanted
                for k in range(1, listed):
                    found = found | (code_ref[k, x, y] == wanted)
                along_x = jnp.where((kind == 0) | (kind == 3), float(step_x - 1), 0.0)
                along_y = jnp.where((kind == 1) | (kind == 4), float(side * 2 - 1), 0.0)
                line = nat_ref[pl.ds(side * 64 + x + step_x, 8, stride=8), :]
                root = jnp.broadcast_to(line[7:8], line.shape) * jnp.where(found, 1.0, 0.0)
                near_ref[number, :, step_x * LANES : (step_x + 1) * LANES] = source_matrix(
                    line + along_x + along_y, root, squares
                )
                root_ref[number, step_x : step_x + 1, :] = root[0:1]
            match_ref = (edge_match_ref if edge else middle_match_ref).at[turn, side]
            sides.append(
                (match_ref, near_ref.at[number], root_ref.at[number, pl.ds(0, 3)], total_ref.at[number])
            )
    pair_sums(sides)
    totals = [total_ref[number] for number in range(len(sides))]
    sums = column_sums(totals)
    total = jnp.zeros((LANES, 2 * owners), F32)
    owner_ids = lax.broadcasted_iota(jnp.int32, (owners, LANES), 0)
    for x in range(blocks_x):
        for side in range(2):
            y = side * (blocks_y - 1)
            sum_ref[x, y : y + 1, :] += sums[2 * x + side : 2 * x + side + 1, :]
        radius = smooth_ref[x]
        density = sum_ref[x] * DENSITY_FACTOR / (radius * radius * radius)
        moment = mass_ref[x] * density
        high_part = rounded(moment)
        low_part = moment - high_part
        owner = rows_ref[x] >> 7
        for y in range(blocks_y):
            lanes = slice(y * LANES, (y + 1) * LANES)
            mine = jnp.broadcast_to(owner[y : y + 1, :], owner_ids.shape) == owner_ids
            lhs_ref[:, lanes] = jnp.concatenate(
                [
                    jnp.where(mine, jnp.broadcast_to(part[y : y + 1, :], mine.shape), 0.0)
                    for part in (high_part, low_part)
                ],
                axis=0,
            ).astype(BF16)
        total = total + lax.dot_general(
            hot_ref[x], lhs_ref[...], NT, preferred_element_type=F32
        )
    total = total.T
    md_ref[...] = total[:owners] + total[owners:]
    core, my_chip = lax.axis_index("core"), lax.axis_index("chip")
    for other in range(2):
        for step in range(owners // 2):
            owner = 2 * (my_chip ^ step) + (core ^ other)
            table_ref[other, step, :EARLY, :] = early_ref[owner]
            table_ref[other, step, EARLY : EARLY + 1, :] = md_ref[pl.ds(owner, 1), :]


def swap(value, axis, step):
    count = lax.axis_size(axis)
    return lax.ppermute(value, axis, [(i, i ^ step) for i in range(count)])


def neighbours_of(low_edge, high_edge, axis, parity):
    count = lax.axis_size(axis)
    even = parity == 0
    inner = lax.ppermute(
        jnp.where(even, high_edge, low_edge), axis, [(i, i ^ 1) for i in range(count)]
    )
    outer = lax.ppermute(
        jnp.where(even, low_edge, high_edge),
        axis,
        [(i, (i + 1 if i & 1 else i - 1) % count) for i in range(count)],
    )
    return jnp.where(even, outer, inner), jnp.where(even, inner, outer)


def added(parts):
    while len(parts) > 1:
        parts = [sum(parts[k : k + 2][1:], parts[k]) for k in range(0, len(parts), 2)]
    return parts[0]


def to_owner(table):
    table = table[0] + swap(table[1], "core", 1)
    while table.shape[0] > 1:
        ways = min(4, table.shape[0])
        part = table.shape[0] // ways
        table = added(
            [table[:part]]
            + [swap(table[k * part : (k + 1) * part], "chip", k * part) for k in range(1, ways)]
        )
    return table[0]


def summed(value, axis):
    count = lax.axis_size(axis)
    if count & (count - 1):
        return lax.psum(value, axis)
    return added(list(lax.all_gather(value, axis)))


def shards(positions, velocities, masses, smoothing, neighbours, particle_group, group_row):
    blocks_x, blocks_y, block_len = masses.shape
    dom_count, sub_count = lax.axis_size("dom"), lax.axis_size("chip") * lax.axis_size("core")
    owners = sub_count
    chunk = blocks_y * block_len
    shape = jax.ShapeDtypeStruct
    codes = neighbours.transpose(2, 0, 1)
    packed = jnp.concatenate([positions, masses[None]], axis=0)
    prev, following = neighbours_of(
        packed[:, 0], packed[:, blocks_x - 1], "dom", lax.axis_index("dom") & 1
    )
    columns, middle, middle_match = pl.pallas_call(
        middle_kernel,
        out_shape=(
            shape((2, 4, blocks_x, LANES), F32),
            shape((blocks_x - 2, blocks_y, LANES), F32),
            shape((blocks_x - 2, 2, LANES, 48), BF16),
        ),
        in_specs=[SMEM] + [VMEM] * 3,
        out_specs=(VMEM,) * 3,
        scratch_shapes=pair_scratch(blocks_x, blocks_y, blocks_x - 2, codes.shape[0]),
        compiler_params=params(),
        cost_estimate=pl.CostEstimate(
            flops=4_000_000_000, bytes_accessed=400_000, transcendentals=1_300_000
        ),
        name="middle_pairs",
    )(codes, positions, masses, smoothing)
    edges = [
        jnp.concatenate([prev[:, y : y + 1], columns[side], following[:, y : y + 1]], axis=1)
        for side, y in ((0, 0), (1, blocks_y - 1))
    ]
    low, high = neighbours_of(*edges, ("chip", "core"), lax.axis_index("core"))
    edge, edge_match, early, rows, hot = pl.pallas_call(
        functools.partial(edge_kernel, blocks_x * dom_count, blocks_y * sub_count),
        out_shape=(
            shape((2, blocks_y, LANES), F32),
            shape((2, 2, LANES, 48), BF16),
            shape((owners, EARLY, LANES), F32),
            shape(masses.shape, jnp.int32),
            shape((blocks_x, LANES, chunk), BF16),
        ),
        in_specs=[SMEM] + [VMEM] * 8,
        out_specs=(VMEM,) * 5,
        scratch_shapes=[
            pltpu.VMEM((blocks_x * EARLY * blocks_y, LANES), F32),
            pltpu.VMEM((blocks_x, owners * 2 * EARLY, chunk), BF16),
            pltpu.VMEM((owners * 2 * EARLY, LANES), F32),
        ]
        + pair_scratch(blocks_x, blocks_y, 2, codes.shape[0]),
        compiler_params=params(),
        cost_estimate=pl.CostEstimate(
            flops=5_000_000_000, bytes_accessed=1_400_000, transcendentals=1_300_000
        ),
        name="edge_pairs_and_moments",
    )(
        codes, positions, masses, smoothing, prev, following,
        velocities, particle_group, group_row.reshape(-1, LANES),
    )
    sums, table = pl.pallas_call(
        rim_kernel,
        out_shape=(shape(masses.shape, F32), shape((2, owners // 2, EARLY + 1, LANES), F32)),
        in_specs=[SMEM] + [VMEM] * 11,
        out_specs=(VMEM, VMEM),
        scratch_shapes=[
            pltpu.VMEM((128, LANES), F32),
            pltpu.VMEM((owners, LANES), F32),
            pltpu.VMEM((2 * owners, chunk), BF16),
        ]
        + product_scratch(2 * blocks_x, 3)[1:],
        compiler_params=params(),
        cost_estimate=pl.CostEstimate(
            flops=200_000_000, bytes_accessed=400_000, transcendentals=400_000
        ),
        name="rim_pairs_and_table",
    )(
        codes, middle, edge, middle_match, edge_match, masses, smoothing, low, high, rows, hot, early
    )
    density = sums * DENSITY_FACTOR / (smoothing * smoothing * smoothing)
    return (density, summed(to_owner(table), "dom"))


def solution(mesh):
    dom_count, sub_count = mesh.devices.shape
    mesh = jax.sharding.Mesh(
        mesh.devices.reshape(dom_count, sub_count // 2, 2), ("dom", "chip", "core")
    )
    sub = ("chip", "core")
    in_specs = (
        P(None, "dom", sub, None),
        P(None, "dom", sub, None),
        P("dom", sub, None),
        P("dom", sub, None),
        P("dom", sub, None),
        P("dom", sub, None),
        P(),
    )
    out_specs = (P("dom", sub, None), P(None, sub))
    return jax.shard_map(shards, mesh=mesh, in_specs=in_specs, out_specs=out_specs, check_vma=False)
```

```python
import functools
import math

import jax
import jax.numpy as jnp
from jax import lax
from jax.experimental import pallas as pl
from jax.experimental.pallas import tpu as pltpu
from jax.sharding import PartitionSpec as P

F32 = jnp.float32
BF16 = jnp.bfloat16
LANES = 128
EARLY = 16
DENSITY_FACTOR = 21.0 / (16.0 * math.pi) / 256.0
VMEM = pl.BlockSpec(memory_space=pltpu.VMEM)
SMEM = pl.BlockSpec(memory_space=pltpu.SMEM)
NT = (((1,), (1,)), ((), ()))


def params():
    return pltpu.CompilerParams(vmem_limit_bytes=40 * 1024 * 1024)


def rounded(value):
    return value.astype(BF16).astype(F32)


def three_parts(value):
    first = rounded(value)
    rest = value - first
    second = rounded(rest)
    return first, second, rest - second


def spread(numbers, y, count):
    row = jnp.broadcast_to(numbers[y : y + 1, :].astype(F32), (16, LANES)).astype(BF16)
    return jnp.concatenate([row] * (count // 16), axis=0)


def row_numbers(count):
    return lax.broadcasted_iota(jnp.int32, (count, LANES), 0).astype(F32).astype(BF16)


def slot_one_hot(slots, y):
    return jnp.where(
        row_numbers(LANES) == spread(slots, y, LANES), jnp.ones((), BF16), jnp.zeros((), BF16)
    )


def moment_pieces(
    nx_total, ny_total, pos_ref, vel_ref, mass_ref, group_ref, row_ref,
    table_ref, rows_ref, hot_ref, feat_ref, lhs_ref, total_ref,
):
    blocks_x, blocks_y, _ = mass_ref.shape
    owners = table_ref.shape[0]
    table_rows = row_ref.shape[0]
    base_x = (lax.axis_index("dom") * blocks_x).astype(F32)
    base_y = ((2 * lax.axis_index("chip") + lax.axis_index("core")) * blocks_y).astype(F32)
    y_iota = lax.broadcasted_iota(jnp.int32, (blocks_y, LANES), 0).astype(F32)

    def features_of(x):
        group = group_ref[x]
        low = group & (LANES - 1)
        high = group >> 7
        rows = jnp.zeros_like(group)
        for r in range(table_rows):
            line = jnp.broadcast_to(row_ref[r : r + 1, :], group.shape)
            picked = jnp.take_along_axis(line, low, axis=1)
            rows = jnp.where(high == r, picked, rows)
        rows_ref[x] = rows
        mass = mass_ref[x]
        gx = (base_x + float(x) + pos_ref[0, x]) / float(nx_total)
        gy = (base_y + y_iota + pos_ref[1, x]) / float(ny_total)
        gz = pos_ref[2, x]
        vx, vy, vz = vel_ref[0, x], vel_ref[1, x], vel_ref[2, x]
        mx, my, mz = mass * gx, mass * gy, mass * gz
        features = (
            mass, mx, my, mz, mass * vx, mass * vy, mass * vz,
            mass * (gy * vz - gz * vy), mass * (gz * vx - gx * vz), mass * (gx * vy - gy * vx),
            mx * gx, my * gy, mz * gz, mx * gy, mx * gz, my * gz,
        )
        for f, feature in enumerate(features):
            start = (x * EARLY + f) * blocks_y
            feat_ref[start : start + blocks_y, :] = feature

    def operands_of(x, y):
        lanes = slice(y * LANES, (y + 1) * LANES)
        feats = feat_ref[pl.ds(x * EARLY * blocks_y + y, EARLY, stride=blocks_y), :]
        high_part = rounded(feats)
        both = jnp.concatenate([high_part, feats - high_part], axis=0).astype(BF16)
        rows = rows_ref[x]
        owner_row = spread(rows >> 7, y, 2 * EARLY)
        for o in range(owners):
            lhs_ref[x, o * 2 * EARLY : (o + 1) * 2 * EARLY, lanes] = jnp.where(
                owner_row == jnp.asarray(o, BF16), both, jnp.zeros((), BF16)
            )
        hot_ref[x, :, lanes] = slot_one_hot(rows & (LANES - 1), y)

    def add_product(x):
        product = lax.dot_general(lhs_ref[x], hot_ref[x], NT, preferred_element_type=F32)
        total_ref[...] = product if x == 0 else total_ref[...] + product

    def finish():
        total = total_ref[...].reshape(owners, 2 * EARLY, LANES)
        table_ref[...] = total[:, :EARLY, :] + total[:, EARLY:, :]

    pieces = []
    for x in range(blocks_x):
        pieces.append(functools.partial(features_of, x))
        pieces += [functools.partial(operands_of, x, y) for y in range(blocks_y)]
        pieces.append(functools.partial(add_product, x))
    return pieces + [finish]


def target_rows(pos, radius):
    weight = 4.0 / (radius * radius)
    cx, cy, cz = pos[0] - 0.5, pos[1] - 0.5, pos[2] - 0.5
    lines = (
        -2.0 * cx * weight, -2.0 * cy * weight, -2.0 * cz * weight,
        weight, weight, weight,
        (cx * cx + cy * cy + cz * cz) * weight, jnp.zeros_like(weight),
    )
    parts = [three_parts(line) for line in lines]
    return [part[k] for k in range(3) for part in parts]


def target_matrix(coef):
    one, two, three = coef[0:8], coef[8:16], coef[16:24]
    stacked = jnp.concatenate([one, one, two, two, one, three], axis=0)
    return stacked.T.astype(BF16)


def source_matrix(line, root, squares):
    value = jnp.where(squares, line * line, line) * (root * root)
    one, two, three = three_parts(value)
    first = jnp.concatenate([one, two], axis=0).astype(BF16)
    last = jnp.concatenate([three, one], axis=0).astype(BF16)
    return jnp.concatenate([first, first, last], axis=0)


def fifth_root(mass):
    root = jnp.exp(0.2 * jnp.log(mass))
    square = root * root
    return 0.8 * root + 0.2 * mass / (square * square)


def store_source(nat_ref, start, count, columns, mass):
    cx, cy, cz = [column - 0.5 for column in columns]
    one = jnp.ones_like(cx)
    for kind, line in enumerate((cx, cy, cz, cx, cy, cz, one, fifth_root(mass))):
        nat_ref[start + kind * 8 : start + kind * 8 + count, :] = line


def pair_sums(sides, pieces=()):
    rows = 32
    steps = []
    for target, sources, roots, total in sides:
        count = roots.shape[0]
        for first in range(0, count, 2):
            steps.append((target, sources, roots, total, first, min(2, count - first), count))

    def product(step):
        target, sources, _, _, first, width, _ = step
        right = sources[:, first * LANES : (first + width) * LANES]
        return jnp.dot(target[...], right, preferred_element_type=F32)

    ready = product(steps[0])
    chunks = None
    for number, (_, _, roots, total, first, width, count) in enumerate(steps):
        squared = ready
        if number + 1 < len(steps):
            ready = product(steps[number + 1])
        if first == 0:
            chunks = [None] * (LANES // rows)
        limits = []
        for k in range(width):
            root = roots[first + k : first + k + 1, :]
            reach = 4.0 * root
            limits.append(
                [jnp.broadcast_to(line, (rows, LANES)) for line in (root, reach, reach * reach)]
            )
        for r in range(len(chunks)):
            for k, (root, reach, most) in enumerate(limits):
                t = squared[r * rows : (r + 1) * rows, k * LANES : (k + 1) * LANES]
                t = jnp.maximum(jnp.minimum(t, most), 0.0)
                u = pl.reciprocal(lax.rsqrt(t), approx=True)
                f = reach - u
                f = f * f
                f = f * f
                term = f * (root + u)
                chunks[r] = term if chunks[r] is None else chunks[r] + term
        if first + width == count:
            for r, chunk in enumerate(chunks):
                total[r * rows : (r + 1) * rows, :] = chunk
        if number < len(pieces):
            pieces[number]()
    for piece in pieces[len(steps) :]:
        piece()


def column_sums(totals):
    lane = lax.broadcasted_iota(jnp.int32, (LANES, LANES), 1)
    columns = jnp.zeros((LANES, LANES), F32)
    for k, total in enumerate(totals):
        columns = jnp.where(lane == k, jnp.sum(total, axis=1, keepdims=True), columns)
    return columns.T[: len(totals), :]


def square_mask():
    kind = lax.broadcasted_iota(jnp.int32, (8, LANES), 0)
    return (kind >= 3) & (kind < 6)


def block_pairs(
    x_first, x_step, x_count, code_ref, pos_ref, mass_ref, smooth_ref, prev_ref, next_ref,
    out_ref, match_ref, nat_ref, src_ref, shift_ref, tgt_ref, mat_ref, near_ref, root_ref, total_ref,
    pieces=(),
):
    blocks_x, blocks_y, _ = mass_ref.shape
    listed = code_ref.shape[0]
    null = (blocks_x + 2) * blocks_y
    for xe in range(blocks_x + 2):
        if xe == 0 or xe == blocks_x + 1:
            ref = prev_ref if xe == 0 else next_ref
            if ref is None:
                continue
            store_source(nat_ref, xe * 64, blocks_y, [ref[c] for c in range(3)], ref[3])
        else:
            columns = [pos_ref[c, xe - 1] for c in range(3)]
            store_source(nat_ref, xe * 64, blocks_y, columns, mass_ref[xe - 1])
        for y in range(blocks_y):
            src_ref[xe * blocks_y + y] = nat_ref[pl.ds(xe * 64 + y, 8, stride=8), :]
    src_ref[null] = jnp.zeros((8, LANES), F32)
    kind = lax.broadcasted_iota(jnp.int32, (8, LANES), 0)
    for code in range(9):
        along_x = jnp.where((kind == 0) | (kind == 3), float(code // 3 - 1), 0.0)
        along_y = jnp.where((kind == 1) | (kind == 4), float(code % 3 - 1), 0.0)
        shift_ref[code] = along_x + along_y
    squares = square_mask()
    for k in range(x_count):
        x = x_first + k * x_step
        lines = target_rows([pos_ref[c, x] for c in range(3)], smooth_ref[x])
        for row, line in enumerate(lines):
            tgt_ref[k, row * blocks_y : (row + 1) * blocks_y, :] = line

    blocks = [(turn, y) for turn in range(x_count) for y in range(blocks_y)]
    for number, (turn, y) in enumerate(blocks):
        target = target_matrix(tgt_ref[turn, pl.ds(y, 24, stride=blocks_y), :])
        mat_ref[number] = target
        if y == 0:
            match_ref[turn, 0] = target
        if y == blocks_y - 1:
            match_ref[turn, 1] = target
    for number, (turn, y) in enumerate(blocks):
        x = x_first + turn * x_step
        for k in range(listed):
            code = code_ref[k, x, y]
            step_x = (code * 11) >> 5
            near_y = y + code - 3 * step_x - 1
            inside = (near_y >= 0) & (near_y < blocks_y)
            line = src_ref[jnp.where(inside, (x + step_x) * blocks_y + near_y, null)]
            root = jnp.broadcast_to(line[7:8], line.shape)
            near_ref[number, :, k * LANES : (k + 1) * LANES] = source_matrix(
                line + shift_ref[code], root, squares
            )
            root_ref[number, k : k + 1, :] = root[0:1]
    pair_sums(
        [
            (mat_ref.at[n], near_ref.at[n], root_ref.at[n, pl.ds(0, listed)], total_ref.at[n])
            for n in range(len(blocks))
        ],
        pieces,
    )
    for turn in range(x_count):
        out_ref[turn] = column_sums([total_ref[turn * blocks_y + y] for y in range(blocks_y)])


def middle_kernel(
    code_ref, pos_ref, mass_ref, smooth_ref, column_ref, out_ref, match_ref, *scratch
):
    blocks_x, blocks_y, _ = mass_ref.shape
    for side in range(2):
        y = side * (blocks_y - 1)
        for x in range(blocks_x):
            for c in range(3):
                column_ref[side, c, x : x + 1, :] = pos_ref[c, x, y : y + 1, :]
            column_ref[side, 3, x : x + 1, :] = mass_ref[x, y : y + 1, :]
    block_pairs(
        1, 1, blocks_x - 2, code_ref, pos_ref, mass_ref, smooth_ref, None, None,
        out_ref, match_ref, *scratch,
    )


def edge_kernel(
    nx_total, ny_total, code_ref, pos_ref, mass_ref, smooth_ref, prev_ref, next_ref,
    vel_ref, group_ref, row_ref, out_ref, match_ref, table_ref, rows_ref, hot_ref,
    feat_ref, lhs_ref, sum_ref, *scratch
):
    blocks_x = mass_ref.shape[0]
    pieces = moment_pieces(
        nx_total, ny_total, pos_ref, vel_ref, mass_ref, group_ref, row_ref,
        table_ref, rows_ref, hot_ref, feat_ref, lhs_ref, sum_ref,
    )
    block_pairs(
        0, blocks_x - 1, 2, code_ref, pos_ref, mass_ref, smooth_ref, prev_ref, next_ref,
        out_ref, match_ref, *scratch, pieces=pieces,
    )


def pair_scratch(blocks_x, blocks_y, x_count, listed):
    return [
        pltpu.VMEM(((blocks_x + 2) * 64, LANES), F32),
        pltpu.VMEM(((blocks_x + 2) * blocks_y + 1, 8, LANES), F32),
        pltpu.VMEM((9, 8, LANES), F32),
        pltpu.VMEM((x_count, 24 * blocks_y, LANES), F32),
    ] + product_scratch(x_count * blocks_y, listed)


def product_scratch(blocks, listed):
    return [
        pltpu.VMEM((blocks, LANES, 48), BF16),
        pltpu.VMEM((blocks, 48, listed * LANES), BF16),
        pltpu.VMEM((blocks, 8, LANES), F32),
        pltpu.VMEM((blocks, LANES, LANES), F32),
    ]


def rim_kernel(
    code_ref, middle_ref, edge_ref, middle_match_ref, edge_match_ref, mass_ref, smooth_ref,
    low_ref, high_ref, rows_ref, hot_ref, early_ref,
    sum_ref, table_ref, nat_ref, md_ref, lhs_ref, row_sum_ref, near_ref, root_ref, total_ref,
):
    blocks_x, blocks_y, _ = mass_ref.shape
    owners = early_ref.shape[0]
    listed = code_ref.shape[0]
    for side, ref in enumerate((low_ref, high_ref)):
        store_source(nat_ref, side * 64, blocks_x + 2, [ref[c] for c in range(3)], ref[3])
    kind = lax.broadcasted_iota(jnp.int32, (8, LANES), 0)
    squares = square_mask()
    sides = []
    for x in range(blocks_x):
        edge = x == 0 or x == blocks_x - 1
        turn = (1 if x else 0) if edge else x - 1
        sum_ref[x] = (edge_ref if edge else middle_ref)[turn]
        for side in range(2):
            y = side * (blocks_y - 1)
            number = 2 * x + side
            for step_x in range(3):
                wanted = step_x * 3 + side * 2
                found = code_ref[0, x, y] == wanted
                for k in range(1, listed):
                    found = found | (code_ref[k, x, y] == wanted)
                along_x = jnp.where((kind == 0) | (kind == 3), float(step_x - 1), 0.0)
                along_y = jnp.where((kind == 1) | (kind == 4), float(side * 2 - 1), 0.0)
                line = nat_ref[pl.ds(side * 64 + x + step_x, 8, stride=8), :]
                root = jnp.broadcast_to(line[7:8], line.shape) * jnp.where(found, 1.0, 0.0)
                near_ref[number, :, step_x * LANES : (step_x + 1) * LANES] = source_matrix(
                    line + along_x + along_y, root, squares
                )
                root_ref[number, step_x : step_x + 1, :] = root[0:1]
            match_ref = (edge_match_ref if edge else middle_match_ref).at[turn, side]
            sides.append(
                (match_ref, near_ref.at[number], root_ref.at[number, pl.ds(0, 3)], total_ref.at[number])
            )
    owner_ids = lax.broadcasted_iota(jnp.int32, (owners, LANES), 0)
    last = blocks_y - 1

    def put_moments(x, ys):
        radius = smooth_ref[x]
        moment = mass_ref[x] * (sum_ref[x] * DENSITY_FACTOR / (radius * radius * radius))
        high_part = rounded(moment)
        low_part = moment - high_part
        owner = rows_ref[x] >> 7
        for y in ys:
            mine = jnp.broadcast_to(owner[y : y + 1, :], owner_ids.shape) == owner_ids
            lhs_ref[x, :, y * LANES : (y + 1) * LANES] = jnp.concatenate(
                [
                    jnp.where(mine, jnp.broadcast_to(part[y : y + 1, :], mine.shape), 0.0)
                    for part in (high_part, low_part)
                ],
                axis=0,
            ).astype(BF16)

    def inner_moments(x):
        put_moments(x, range(1, last))
        lanes = slice(LANES, last * LANES)
        product = lax.dot_general(
            hot_ref[x, :, lanes], lhs_ref[x, :, lanes], NT, preferred_element_type=F32
        )
        row_sum_ref[...] = product if x == 0 else row_sum_ref[...] + product

    pair_sums(sides, [functools.partial(inner_moments, x) for x in range(blocks_x)])
    sums = column_sums([total_ref[number] for number in range(len(sides))])
    for x in range(blocks_x):
        for side in range(2):
            y = side * last
            sum_ref[x, y : y + 1, :] += sums[2 * x + side : 2 * x + side + 1, :]
        put_moments(x, (0, last))
    ends = [(x, slice(y * LANES, (y + 1) * LANES)) for x in range(blocks_x) for y in (0, last)]
    total = row_sum_ref[...] + lax.dot_general(
        jnp.concatenate([hot_ref[x, :, lanes] for x, lanes in ends], axis=1),
        jnp.concatenate([lhs_ref[x, :, lanes] for x, lanes in ends], axis=1),
        NT,
        preferred_element_type=F32,
    )
    total = total.T
    md_ref[...] = total[:owners] + total[owners:]
    core, my_chip = lax.axis_index("core"), lax.axis_index("chip")
    for other in range(2):
        for step in range(owners // 2):
            owner = 2 * (my_chip ^ step) + (core ^ other)
            table_ref[other, step, :EARLY, :] = early_ref[owner]
            table_ref[other, step, EARLY : EARLY + 1, :] = md_ref[pl.ds(owner, 1), :]


def swap(value, axis, step):
    count = lax.axis_size(axis)
    return lax.ppermute(value, axis, [(i, i ^ step) for i in range(count)])


def neighbours_of(low_edge, high_edge, axis, parity):
    count = lax.axis_size(axis)
    even = parity == 0
    inner = lax.ppermute(
        jnp.where(even, high_edge, low_edge), axis, [(i, i ^ 1) for i in range(count)]
    )
    outer = lax.ppermute(
        jnp.where(even, low_edge, high_edge),
        axis,
        [(i, (i + 1 if i & 1 else i - 1) % count) for i in range(count)],
    )
    return jnp.where(even, outer, inner), jnp.where(even, inner, outer)


def added(parts):
    while len(parts) > 1:
        parts = [sum(parts[k : k + 2][1:], parts[k]) for k in range(0, len(parts), 2)]
    return parts[0]


def to_owner(table):
    table = table[0] + swap(table[1], "core", 1)
    while table.shape[0] > 1:
        ways = min(4, table.shape[0])
        part = table.shape[0] // ways
        table = added(
            [table[:part]]
            + [swap(table[k * part : (k + 1) * part], "chip", k * part) for k in range(1, ways)]
        )
    return table[0]


def summed(value, axis):
    count = lax.axis_size(axis)
    if count & (count - 1):
        return lax.psum(value, axis)
    copies = jnp.broadcast_to(value[None], (count,) + value.shape)
    return added(list(lax.all_to_all(copies, axis, split_axis=0, concat_axis=0, tiled=True)))


def shards(positions, velocities, masses, smoothing, neighbours, particle_group, group_row):
    blocks_x, blocks_y, block_len = masses.shape
    dom_count, sub_count = lax.axis_size("dom"), lax.axis_size("chip") * lax.axis_size("core")
    owners = sub_count
    chunk = blocks_y * block_len
    shape = jax.ShapeDtypeStruct
    codes = neighbours.transpose(2, 0, 1)
    packed = jnp.concatenate([positions, masses[None]], axis=0)
    prev, following = neighbours_of(
        packed[:, 0], packed[:, blocks_x - 1], "dom", lax.axis_index("dom") & 1
    )
    columns, middle, middle_match = pl.pallas_call(
        middle_kernel,
        out_shape=(
            shape((2, 4, blocks_x, LANES), F32),
            shape((blocks_x - 2, blocks_y, LANES), F32),
            shape((blocks_x - 2, 2, LANES, 48), BF16),
        ),
        in_specs=[SMEM] + [VMEM] * 3,
        out_specs=(VMEM,) * 3,
        scratch_shapes=pair_scratch(blocks_x, blocks_y, blocks_x - 2, codes.shape[0]),
        compiler_params=params(),
        cost_estimate=pl.CostEstimate(
            flops=4_000_000_000, bytes_accessed=400_000, transcendentals=1_300_000
        ),
        name="middle_pairs",
    )(codes, positions, masses, smoothing)
    edges = [
        jnp.concatenate([prev[:, y : y + 1], columns[side], following[:, y : y + 1]], axis=1)
        for side, y in ((0, 0), (1, blocks_y - 1))
    ]
    low, high = neighbours_of(*edges, ("chip", "core"), lax.axis_index("core"))
    edge, edge_match, early, rows, hot = pl.pallas_call(
        functools.partial(edge_kernel, blocks_x * dom_count, blocks_y * sub_count),
        out_shape=(
            shape((2, blocks_y, LANES), F32),
            shape((2, 2, LANES, 48), BF16),
            shape((owners, EARLY, LANES), F32),
            shape(masses.shape, jnp.int32),
            shape((blocks_x, LANES, chunk), BF16),
        ),
        in_specs=[SMEM] + [VMEM] * 8,
        out_specs=(VMEM,) * 5,
        scratch_shapes=[
            pltpu.VMEM((blocks_x * EARLY * blocks_y, LANES), F32),
            pltpu.VMEM((blocks_x, owners * 2 * EARLY, chunk), BF16),
            pltpu.VMEM((owners * 2 * EARLY, LANES), F32),
        ]
        + pair_scratch(blocks_x, blocks_y, 2, codes.shape[0]),
        compiler_params=params(),
        cost_estimate=pl.CostEstimate(
            flops=5_000_000_000, bytes_accessed=1_400_000, transcendentals=1_300_000
        ),
        name="edge_pairs_and_moments",
    )(
        codes, positions, masses, smoothing, prev, following,
        velocities, particle_group, group_row.reshape(-1, LANES),
    )
    sums, table = pl.pallas_call(
        rim_kernel,
        out_shape=(shape(masses.shape, F32), shape((2, owners // 2, EARLY + 1, LANES), F32)),
        in_specs=[SMEM] + [VMEM] * 11,
        out_specs=(VMEM, VMEM),
        scratch_shapes=[
            pltpu.VMEM((128, LANES), F32),
            pltpu.VMEM((owners, LANES), F32),
            pltpu.VMEM((blocks_x, 2 * owners, chunk), BF16),
            pltpu.VMEM((LANES, 2 * owners), F32),
        ]
        + product_scratch(2 * blocks_x, 3)[1:],
        compiler_params=params(),
        cost_estimate=pl.CostEstimate(
            flops=200_000_000, bytes_accessed=400_000, transcendentals=400_000
        ),
        name="rim_pairs_and_table",
    )(
        codes, middle, edge, middle_match, edge_match, masses, smoothing, low, high, rows, hot, early
    )
    density = sums * DENSITY_FACTOR / (smoothing * smoothing * smoothing)
    return (density, summed(to_owner(table), "dom"))


def solution(mesh):
    dom_count, sub_count = mesh.devices.shape
    mesh = jax.sharding.Mesh(
        mesh.devices.reshape(dom_count, sub_count // 2, 2), ("dom", "chip", "core")
    )
    sub = ("chip", "core")
    in_specs = (
        P(None, "dom", sub, None),
        P(None, "dom", sub, None),
        P("dom", sub, None),
        P("dom", sub, None),
        P("dom", sub, None),
        P("dom", sub, None),
        P(),
    )
    out_specs = (P("dom", sub, None), P(None, sub))
    return jax.shard_map(shards, mesh=mesh, in_specs=in_specs, out_specs=out_specs, check_vma=False)
```

```python
import functools
import math

import jax
import jax.numpy as jnp
from jax import lax
from jax.experimental import pallas as pl
from jax.experimental.pallas import tpu as pltpu
from jax.sharding import PartitionSpec as P

F32 = jnp.float32
BF16 = jnp.bfloat16
LANES = 128
EARLY = 16
DENSITY_FACTOR = 21.0 / (16.0 * math.pi) / 256.0
VMEM = pl.BlockSpec(memory_space=pltpu.VMEM)
SMEM = pl.BlockSpec(memory_space=pltpu.SMEM)
NT = (((1,), (1,)), ((), ()))


def params():
    return pltpu.CompilerParams(vmem_limit_bytes=40 * 1024 * 1024)


def rounded(value):
    return value.astype(BF16).astype(F32)


def three_parts(value):
    first = rounded(value)
    rest = value - first
    second = rounded(rest)
    return first, second, rest - second


def spread(numbers, y, count):
    row = jnp.broadcast_to(numbers[y : y + 1, :].astype(F32), (16, LANES)).astype(BF16)
    return jnp.concatenate([row] * (count // 16), axis=0)


def row_numbers(count):
    return lax.broadcasted_iota(jnp.int32, (count, LANES), 0).astype(F32).astype(BF16)


def slot_one_hot(slots, y):
    return jnp.where(
        row_numbers(LANES) == spread(slots, y, LANES), jnp.ones((), BF16), jnp.zeros((), BF16)
    )


def sum_moments(
    nx_total, ny_total, pos_ref, vel_ref, mass_ref, group_ref, row_ref,
    table_ref, rows_ref, hot_ref, feat_ref, lhs_ref, total_ref,
):
    blocks_x, blocks_y, _ = mass_ref.shape
    owners = table_ref.shape[0]
    table_rows = row_ref.shape[0]
    base_x = (lax.axis_index("dom") * blocks_x).astype(F32)
    base_y = ((2 * lax.axis_index("chip") + lax.axis_index("core")) * blocks_y).astype(F32)
    y_iota = lax.broadcasted_iota(jnp.int32, (blocks_y, LANES), 0).astype(F32)

    total_ref[...] = jnp.zeros_like(total_ref)

    def one_row(x, carry):
        group = group_ref[x]
        low = group & (LANES - 1)
        high = group >> 7
        rows = jnp.zeros_like(group)
        for r in range(table_rows):
            line = jnp.broadcast_to(row_ref[r : r + 1, :], group.shape)
            picked = jnp.take_along_axis(line, low, axis=1)
            rows = jnp.where(high == r, picked, rows)
        rows_ref[x] = rows
        mass = mass_ref[x]
        gx = (base_x + lax.convert_element_type(x, F32) + pos_ref[0, x]) / float(nx_total)
        gy = (base_y + y_iota + pos_ref[1, x]) / float(ny_total)
        gz = pos_ref[2, x]
        vx, vy, vz = vel_ref[0, x], vel_ref[1, x], vel_ref[2, x]
        mx, my, mz = mass * gx, mass * gy, mass * gz
        features = (
            mass, mx, my, mz, mass * vx, mass * vy, mass * vz,
            mass * (gy * vz - gz * vy), mass * (gz * vx - gx * vz), mass * (gx * vy - gy * vx),
            mx * gx, my * gy, mz * gz, mx * gy, mx * gz, my * gz,
        )
        for f, feature in enumerate(features):
            feat_ref[f * blocks_y : (f + 1) * blocks_y, :] = feature
        for y in range(blocks_y):
            lanes = slice(y * LANES, (y + 1) * LANES)
            feats = feat_ref[pl.ds(y, EARLY, stride=blocks_y), :]
            high_part = rounded(feats)
            both = jnp.concatenate([high_part, feats - high_part], axis=0).astype(BF16)
            owner_row = spread(rows >> 7, y, 2 * EARLY)
            for o in range(owners):
                lhs_ref[o * 2 * EARLY : (o + 1) * 2 * EARLY, lanes] = jnp.where(
                    owner_row == jnp.asarray(o, BF16), both, jnp.zeros((), BF16)
                )
            hot_ref[x, :, lanes] = slot_one_hot(rows & (LANES - 1), y)
        total_ref[...] += lax.dot_general(
            lhs_ref[...], hot_ref[x], NT, preferred_element_type=F32
        )
        return carry

    lax.fori_loop(0, blocks_x, one_row, 0)
    total = total_ref[...].reshape(owners, 2 * EARLY, LANES)
    table_ref[...] = total[:, :EARLY, :] + total[:, EARLY:, :]


def target_rows(pos, radius):
    weight = 4.0 / (radius * radius)
    cx, cy, cz = pos[0] - 0.5, pos[1] - 0.5, pos[2] - 0.5
    lines = (
        -2.0 * cx * weight, -2.0 * cy * weight, -2.0 * cz * weight,
        weight, weight, weight,
        (cx * cx + cy * cy + cz * cz) * weight, jnp.zeros_like(weight),
    )
    parts = [three_parts(line) for line in lines]
    return [part[k] for k in range(3) for part in parts]


def target_matrix(coef):
    one, two, three = coef[0:8], coef[8:16], coef[16:24]
    stacked = jnp.concatenate([one, one, two, two, one, three], axis=0)
    return stacked.T.astype(BF16)


def source_matrix(line, root, squares):
    value = jnp.where(squares, line * line, line) * (root * root)
    one, two, three = three_parts(value)
    first = jnp.concatenate([one, two], axis=0).astype(BF16)
    last = jnp.concatenate([three, one], axis=0).astype(BF16)
    return jnp.concatenate([first, first, last], axis=0)


def fifth_root(mass):
    root = jnp.exp(0.2 * jnp.log(mass))
    square = root * root
    return 0.8 * root + 0.2 * mass / (square * square)


def store_source(nat_ref, start, count, columns, mass):
    cx, cy, cz = [column - 0.5 for column in columns]
    one = jnp.ones_like(cx)
    for kind, line in enumerate((cx, cy, cz, cx, cy, cz, one, fifth_root(mass))):
        nat_ref[start + kind * 8 : start + kind * 8 + count, :] = line


def pair_sums(count, listed, mat_ref, near_ref, root_ref, total_ref, even_ref, odd_ref):
    rows = 16

    def products(n, out_ref):
        for first in range(0, listed, 2):
            lanes = slice(first * LANES, min(first + 2, listed) * LANES)
            out_ref[:, lanes] = jnp.dot(
                mat_ref[n], near_ref[n, :, lanes], preferred_element_type=F32
            )

    def chain(n, squared_ref):
        limits = []
        for k in range(listed):
            root = root_ref[n, k : k + 1, :]
            reach = 4.0 * root
            limits.append(
                [jnp.broadcast_to(line, (rows, LANES)) for line in (root, reach, reach * reach)]
            )
        for first in range(0, LANES, rows):
            total = None
            for k, (root, reach, most) in enumerate(limits):
                t = squared_ref[first : first + rows, k * LANES : (k + 1) * LANES]
                t = jnp.maximum(jnp.minimum(t, most), 0.0)
                u = pl.reciprocal(lax.rsqrt(t), approx=True)
                f = reach - u
                f = f * f
                f = f * f
                term = f * (root + u)
                total = term if total is None else total + term
            total_ref[n, first : first + rows, :] = total

    products(0, even_ref)

    def two_blocks(turn, carry):
        n = 2 * turn
        products(n + 1, odd_ref)
        chain(n, even_ref)
        products(jnp.minimum(n + 2, count - 1), even_ref)
        chain(n + 1, odd_ref)
        return carry

    lax.fori_loop(0, count // 2, two_blocks, 0)


def column_sums(totals):
    lane = lax.broadcasted_iota(jnp.int32, (LANES, LANES), 1)
    columns = jnp.zeros((LANES, LANES), F32)
    for k, total in enumerate(totals):
        columns = jnp.where(lane == k, jnp.sum(total, axis=1, keepdims=True), columns)
    return columns.T[: len(totals), :]


def square_mask():
    kind = lax.broadcasted_iota(jnp.int32, (8, LANES), 0)
    return (kind >= 3) & (kind < 6)


def block_pairs(
    x_first, x_step, x_count, code_ref, pos_ref, mass_ref, smooth_ref, prev_ref, next_ref,
    out_ref, match_ref, nat_ref, src_ref, shift_ref, tgt_ref, *product_refs,
):
    blocks_x, blocks_y, _ = mass_ref.shape
    listed = code_ref.shape[0]
    null = (blocks_x + 2) * blocks_y
    mat_ref, near_ref, root_ref, total_ref = product_refs[:4]

    def one_source_row(xe, columns, mass):
        store_source(nat_ref, 0, blocks_y, columns, mass)
        for y in range(blocks_y):
            src_ref[xe * blocks_y + y] = nat_ref[pl.ds(y, 8, stride=8), :]

    for xe, ref in ((0, prev_ref), (blocks_x + 1, next_ref)):
        if ref is not None:
            one_source_row(xe, [ref[c] for c in range(3)], ref[3])

    def own_row(x, carry):
        one_source_row(x + 1, [pos_ref[c, x] for c in range(3)], mass_ref[x])
        return carry

    lax.fori_loop(0, blocks_x, own_row, 0)
    src_ref[null] = jnp.zeros((8, LANES), F32)
    kind = lax.broadcasted_iota(jnp.int32, (8, LANES), 0)
    for code in range(9):
        along_x = jnp.where((kind == 0) | (kind == 3), float(code // 3 - 1), 0.0)
        along_y = jnp.where((kind == 1) | (kind == 4), float(code % 3 - 1), 0.0)
        shift_ref[code] = along_x + along_y
    squares = square_mask()

    def one_target_row(turn, carry):
        x = x_first + turn * x_step
        lines = target_rows([pos_ref[c, x] for c in range(3)], smooth_ref[x])
        for row, line in enumerate(lines):
            tgt_ref[row * blocks_y : (row + 1) * blocks_y, :] = line
        for y in range(blocks_y):
            target = target_matrix(tgt_ref[pl.ds(y, 24, stride=blocks_y), :])
            mat_ref[turn * blocks_y + y] = target
            if y == 0:
                match_ref[turn, 0] = target
            if y == blocks_y - 1:
                match_ref[turn, 1] = target
        return carry

    lax.fori_loop(0, x_count, one_target_row, 0)

    def one_block(number, carry):
        turn = number // blocks_y
        y = number - turn * blocks_y
        x = x_first + turn * x_step
        for k in range(listed):
            code = code_ref[k, x, y]
            step_x = (code * 11) >> 5
            near_y = y + code - 3 * step_x - 1
            inside = (near_y >= 0) & (near_y < blocks_y)
            line = src_ref[jnp.where(inside, (x + step_x) * blocks_y + near_y, null)]
            root = jnp.broadcast_to(line[7:8], line.shape)
            near_ref[number, :, k * LANES : (k + 1) * LANES] = source_matrix(
                line + shift_ref[code], root, squares
            )
            root_ref[number, k : k + 1, :] = root[0:1]
        return carry

    lax.fori_loop(0, x_count * blocks_y, one_block, 0, unroll=2)
    pair_sums(x_count * blocks_y, listed, *product_refs)

    def one_sum_row(turn, carry):
        out_ref[turn] = column_sums([total_ref[turn * blocks_y + y] for y in range(blocks_y)])
        return carry

    lax.fori_loop(0, x_count, one_sum_row, 0)


def middle_kernel(
    code_ref, pos_ref, mass_ref, smooth_ref, column_ref, out_ref, match_ref, *scratch
):
    blocks_x, blocks_y, _ = mass_ref.shape
    for side in range(2):
        y = side * (blocks_y - 1)
        for x in range(blocks_x):
            for c in range(3):
                column_ref[side, c, x : x + 1, :] = pos_ref[c, x, y : y + 1, :]
            column_ref[side, 3, x : x + 1, :] = mass_ref[x, y : y + 1, :]
    block_pairs(
        1, 1, blocks_x - 2, code_ref, pos_ref, mass_ref, smooth_ref, None, None,
        out_ref, match_ref, *scratch,
    )


def edge_kernel(
    nx_total, ny_total, code_ref, pos_ref, mass_ref, smooth_ref, prev_ref, next_ref,
    vel_ref, group_ref, row_ref, out_ref, match_ref, table_ref, rows_ref, hot_ref,
    feat_ref, lhs_ref, sum_ref, *scratch
):
    blocks_x = mass_ref.shape[0]
    sum_moments(
        nx_total, ny_total, pos_ref, vel_ref, mass_ref, group_ref, row_ref,
        table_ref, rows_ref, hot_ref, feat_ref, lhs_ref, sum_ref,
    )
    block_pairs(
        0, blocks_x - 1, 2, code_ref, pos_ref, mass_ref, smooth_ref, prev_ref, next_ref,
        out_ref, match_ref, *scratch,
    )


def pair_scratch(blocks_x, blocks_y, x_count, listed):
    return [
        pltpu.VMEM((64, LANES), F32),
        pltpu.VMEM(((blocks_x + 2) * blocks_y + 1, 8, LANES), F32),
        pltpu.VMEM((9, 8, LANES), F32),
        pltpu.VMEM((24 * blocks_y, LANES), F32),
    ] + product_scratch(x_count * blocks_y, listed)


def product_scratch(blocks, listed):
    return [
        pltpu.VMEM((blocks, LANES, 48), BF16),
        pltpu.VMEM((blocks, 48, listed * LANES), BF16),
        pltpu.VMEM((blocks, 8, LANES), F32),
        pltpu.VMEM((blocks, LANES, LANES), F32),
        pltpu.VMEM((LANES, listed * LANES), F32),
        pltpu.VMEM((LANES, listed * LANES), F32),
    ]


def rim_kernel(
    code_ref, middle_ref, edge_ref, middle_match_ref, edge_match_ref, mass_ref, smooth_ref,
    low_ref, high_ref, rows_ref, hot_ref, early_ref,
    sum_ref, table_ref, nat_ref, md_ref, lhs_ref, row_sum_ref, *product_refs,
):
    blocks_x, blocks_y, _ = mass_ref.shape
    owners = early_ref.shape[0]
    listed = code_ref.shape[0]
    for side, ref in enumerate((low_ref, high_ref)):
        store_source(nat_ref, side * 64, blocks_x + 2, [ref[c] for c in range(3)], ref[3])
    kind = lax.broadcasted_iota(jnp.int32, (8, LANES), 0)
    squares = square_mask()
    mat_ref, near_ref, root_ref, total_ref = product_refs[:4]
    for x in range(blocks_x):
        edge = x == 0 or x == blocks_x - 1
        turn = (1 if x else 0) if edge else x - 1
        sum_ref[x] = (edge_ref if edge else middle_ref)[turn]
        for side in range(2):
            y = side * (blocks_y - 1)
            number = 2 * x + side
            for step_x in range(3):
                wanted = step_x * 3 + side * 2
                found = code_ref[0, x, y] == wanted
                for k in range(1, listed):
                    found = found | (code_ref[k, x, y] == wanted)
                along_x = jnp.where((kind == 0) | (kind == 3), float(step_x - 1), 0.0)
                along_y = jnp.where((kind == 1) | (kind == 4), float(side * 2 - 1), 0.0)
                line = nat_ref[pl.ds(side * 64 + x + step_x, 8, stride=8), :]
                root = jnp.broadcast_to(line[7:8], line.shape) * jnp.where(found, 1.0, 0.0)
                near_ref[number, :, step_x * LANES : (step_x + 1) * LANES] = source_matrix(
                    line + along_x + along_y, root, squares
                )
                root_ref[number, step_x : step_x + 1, :] = root[0:1]
            mat_ref[number] = (edge_match_ref if edge else middle_match_ref)[turn, side]
    owner_ids = lax.broadcasted_iota(jnp.int32, (owners, LANES), 0)
    last = blocks_y - 1

    def put_moments(x, ys):
        radius = smooth_ref[x]
        moment = mass_ref[x] * (sum_ref[x] * DENSITY_FACTOR / (radius * radius * radius))
        high_part = rounded(moment)
        low_part = moment - high_part
        owner = rows_ref[x] >> 7
        for y in ys:
            mine = jnp.broadcast_to(owner[y : y + 1, :], owner_ids.shape) == owner_ids
            lhs_ref[x, :, y * LANES : (y + 1) * LANES] = jnp.concatenate(
                [
                    jnp.where(mine, jnp.broadcast_to(part[y : y + 1, :], mine.shape), 0.0)
                    for part in (high_part, low_part)
                ],
                axis=0,
            ).astype(BF16)

    def inner_moments(x):
        put_moments(x, range(1, last))
        lanes = slice(LANES, last * LANES)
        product = lax.dot_general(
            hot_ref[x, :, lanes], lhs_ref[x, :, lanes], NT, preferred_element_type=F32
        )
        row_sum_ref[...] = product if x == 0 else row_sum_ref[...] + product

    for x in range(blocks_x):
        inner_moments(x)
    pair_sums(2 * blocks_x, 3, *product_refs)
    sums = column_sums([total_ref[number] for number in range(2 * blocks_x)])
    for x in range(blocks_x):
        for side in range(2):
            y = side * last
            sum_ref[x, y : y + 1, :] += sums[2 * x + side : 2 * x + side + 1, :]
        put_moments(x, (0, last))
    ends = [(x, slice(y * LANES, (y + 1) * LANES)) for x in range(blocks_x) for y in (0, last)]
    total = row_sum_ref[...] + lax.dot_general(
        jnp.concatenate([hot_ref[x, :, lanes] for x, lanes in ends], axis=1),
        jnp.concatenate([lhs_ref[x, :, lanes] for x, lanes in ends], axis=1),
        NT,
        preferred_element_type=F32,
    )
    total = total.T
    md_ref[...] = total[:owners] + total[owners:]
    core, my_chip = lax.axis_index("core"), lax.axis_index("chip")
    for other in range(2):
        for step in range(owners // 2):
            owner = 2 * (my_chip ^ step) + (core ^ other)
            table_ref[other, step, :EARLY, :] = early_ref[owner]
            table_ref[other, step, EARLY : EARLY + 1, :] = md_ref[pl.ds(owner, 1), :]


def swap(value, axis, step):
    count = lax.axis_size(axis)
    return lax.ppermute(value, axis, [(i, i ^ step) for i in range(count)])


def neighbours_of(low_edge, high_edge, axis, parity):
    count = lax.axis_size(axis)
    even = parity == 0
    inner = lax.ppermute(
        jnp.where(even, high_edge, low_edge), axis, [(i, i ^ 1) for i in range(count)]
    )
    outer = lax.ppermute(
        jnp.where(even, low_edge, high_edge),
        axis,
        [(i, (i + 1 if i & 1 else i - 1) % count) for i in range(count)],
    )
    return jnp.where(even, outer, inner), jnp.where(even, inner, outer)


def added(parts):
    while len(parts) > 1:
        parts = [sum(parts[k : k + 2][1:], parts[k]) for k in range(0, len(parts), 2)]
    return parts[0]


def to_owner(table):
    table = table[0] + swap(table[1], "core", 1)
    while table.shape[0] > 1:
        ways = min(4, table.shape[0])
        part = table.shape[0] // ways
        table = added(
            [table[:part]]
            + [swap(table[k * part : (k + 1) * part], "chip", k * part) for k in range(1, ways)]
        )
    return table[0]


def summed(value, axis):
    count = lax.axis_size(axis)
    if count & (count - 1):
        return lax.psum(value, axis)
    step = 1
    while step < count:
        ways = min(4, count // step)
        value = added([value] + [swap(value, axis, k * step) for k in range(1, ways)])
        step *= ways
    return value


def shards(positions, velocities, masses, smoothing, neighbours, particle_group, group_row):
    blocks_x, blocks_y, block_len = masses.shape
    dom_count, sub_count = lax.axis_size("dom"), lax.axis_size("chip") * lax.axis_size("core")
    owners = sub_count
    chunk = blocks_y * block_len
    shape = jax.ShapeDtypeStruct
    codes = neighbours.transpose(2, 0, 1)
    packed = jnp.concatenate([positions, masses[None]], axis=0)
    prev, following = neighbours_of(
        packed[:, 0], packed[:, blocks_x - 1], "dom", lax.axis_index("dom") & 1
    )
    columns, middle, middle_match = pl.pallas_call(
        middle_kernel,
        out_shape=(
            shape((2, 4, blocks_x, LANES), F32),
            shape((blocks_x - 2, blocks_y, LANES), F32),
            shape((blocks_x - 2, 2, LANES, 48), BF16),
        ),
        in_specs=[SMEM] + [VMEM] * 3,
        out_specs=(VMEM,) * 3,
        scratch_shapes=pair_scratch(blocks_x, blocks_y, blocks_x - 2, codes.shape[0]),
        compiler_params=params(),
        cost_estimate=pl.CostEstimate(
            flops=4_000_000_000, bytes_accessed=400_000, transcendentals=1_300_000
        ),
        name="middle_pairs",
    )(codes, positions, masses, smoothing)
    edges = [
        jnp.concatenate([prev[:, y : y + 1], columns[side], following[:, y : y + 1]], axis=1)
        for side, y in ((0, 0), (1, blocks_y - 1))
    ]
    low, high = neighbours_of(*edges, ("chip", "core"), lax.axis_index("core"))
    edge, edge_match, early, rows, hot = pl.pallas_call(
        functools.partial(edge_kernel, blocks_x * dom_count, blocks_y * sub_count),
        out_shape=(
            shape((2, blocks_y, LANES), F32),
            shape((2, 2, LANES, 48), BF16),
            shape((owners, EARLY, LANES), F32),
            shape(masses.shape, jnp.int32),
            shape((blocks_x, LANES, chunk), BF16),
        ),
        in_specs=[SMEM] + [VMEM] * 8,
        out_specs=(VMEM,) * 5,
        scratch_shapes=[
            pltpu.VMEM((EARLY * blocks_y, LANES), F32),
            pltpu.VMEM((owners * 2 * EARLY, chunk), BF16),
            pltpu.VMEM((owners * 2 * EARLY, LANES), F32),
        ]
        + pair_scratch(blocks_x, blocks_y, 2, codes.shape[0]),
        compiler_params=params(),
        cost_estimate=pl.CostEstimate(
            flops=5_000_000_000, bytes_accessed=1_400_000, transcendentals=1_300_000
        ),
        name="edge_pairs_and_moments",
    )(
        codes, positions, masses, smoothing, prev, following,
        velocities, particle_group, group_row.reshape(-1, LANES),
    )
    sums, table = pl.pallas_call(
        rim_kernel,
        out_shape=(shape(masses.shape, F32), shape((2, owners // 2, EARLY + 1, LANES), F32)),
        in_specs=[SMEM] + [VMEM] * 11,
        out_specs=(VMEM, VMEM),
        scratch_shapes=[
            pltpu.VMEM((128, LANES), F32),
            pltpu.VMEM((owners, LANES), F32),
            pltpu.VMEM((blocks_x, 2 * owners, chunk), BF16),
            pltpu.VMEM((LANES, 2 * owners), F32),
        ]
        + product_scratch(2 * blocks_x, 3),
        compiler_params=params(),
        cost_estimate=pl.CostEstimate(
            flops=200_000_000, bytes_accessed=400_000, transcendentals=400_000
        ),
        name="rim_pairs_and_table",
    )(
        codes, middle, edge, middle_match, edge_match, masses, smoothing, low, high, rows, hot, early
    )
    density = sums * DENSITY_FACTOR / (smoothing * smoothing * smoothing)
    return (density, summed(to_owner(table), "dom"))


def solution(mesh):
    dom_count, sub_count = mesh.devices.shape
    mesh = jax.sharding.Mesh(
        mesh.devices.reshape(dom_count, sub_count // 2, 2), ("dom", "chip", "core")
    )
    sub = ("chip", "core")
    in_specs = (
        P(None, "dom", sub, None),
        P(None, "dom", sub, None),
        P("dom", sub, None),
        P("dom", sub, None),
        P("dom", sub, None),
        P("dom", sub, None),
        P(),
    )
    out_specs = (P("dom", sub, None), P(None, sub))
    return jax.shard_map(shards, mesh=mesh, in_specs=in_specs, out_specs=out_specs, check_vma=False)
```

```python
import functools
import math

import jax
import jax.numpy as jnp
from jax import lax
from jax.experimental import pallas as pl
from jax.experimental.pallas import tpu as pltpu
from jax.sharding import PartitionSpec as P

F32 = jnp.float32
BF16 = jnp.bfloat16
LANES = 128
EARLY = 16
DENSITY_FACTOR = 21.0 / (16.0 * math.pi) / 256.0
VMEM = pl.BlockSpec(memory_space=pltpu.VMEM)
SMEM = pl.BlockSpec(memory_space=pltpu.SMEM)
NT = (((1,), (1,)), ((), ()))


def params():
    return pltpu.CompilerParams(vmem_limit_bytes=40 * 1024 * 1024)


def rounded(value):
    return value.astype(BF16).astype(F32)


def three_parts(value):
    first = rounded(value)
    rest = value - first
    second = rounded(rest)
    return first, second, rest - second


def spread(numbers, y, count):
    row = jnp.broadcast_to(numbers[y : y + 1, :].astype(F32), (16, LANES)).astype(BF16)
    return jnp.concatenate([row] * (count // 16), axis=0)


def row_numbers(count):
    return lax.broadcasted_iota(jnp.int32, (count, LANES), 0).astype(F32).astype(BF16)


def slot_one_hot(slots, y):
    return jnp.where(
        row_numbers(LANES) == spread(slots, y, LANES), jnp.ones((), BF16), jnp.zeros((), BF16)
    )


def moments_kernel(
    nx_total, ny_total, after_ref, pos_ref, vel_ref, mass_ref, group_ref, row_ref,
    table_ref, rows_ref, hot_ref, feat_ref, lhs_ref, total_ref,
):
    blocks_x, blocks_y, _ = mass_ref.shape
    owners = table_ref.shape[0]
    table_rows = row_ref.shape[0]
    base_x = (lax.axis_index("dom") * blocks_x).astype(F32)
    base_y = ((2 * lax.axis_index("chip") + lax.axis_index("core")) * blocks_y).astype(F32)
    y_iota = lax.broadcasted_iota(jnp.int32, (blocks_y, LANES), 0).astype(F32)

    def features_of(x):
        group = group_ref[x]
        low = group & (LANES - 1)
        high = group >> 7
        rows = jnp.zeros_like(group)
        for r in range(table_rows):
            line = jnp.broadcast_to(row_ref[r : r + 1, :], group.shape)
            picked = jnp.take_along_axis(line, low, axis=1)
            rows = jnp.where(high == r, picked, rows)
        rows_ref[x] = rows
        mass = mass_ref[x]
        gx = (base_x + float(x) + pos_ref[0, x]) / float(nx_total)
        gy = (base_y + y_iota + pos_ref[1, x]) / float(ny_total)
        gz = pos_ref[2, x]
        vx, vy, vz = vel_ref[0, x], vel_ref[1, x], vel_ref[2, x]
        mx, my, mz = mass * gx, mass * gy, mass * gz
        features = (
            mass, mx, my, mz, mass * vx, mass * vy, mass * vz,
            mass * (gy * vz - gz * vy), mass * (gz * vx - gx * vz), mass * (gx * vy - gy * vx),
            mx * gx, my * gy, mz * gz, mx * gy, mx * gz, my * gz,
        )
        for f, feature in enumerate(features):
            start = (x * EARLY + f) * blocks_y
            feat_ref[start : start + blocks_y, :] = feature

    def operands_of(x, y):
        lanes = slice(y * LANES, (y + 1) * LANES)
        feats = feat_ref[pl.ds(x * EARLY * blocks_y + y, EARLY, stride=blocks_y), :]
        high_part = rounded(feats)
        both = jnp.concatenate([high_part, feats - high_part], axis=0).astype(BF16)
        rows = rows_ref[x]
        owner_row = spread(rows >> 7, y, 2 * EARLY)
        for o in range(owners):
            lhs_ref[x, o * 2 * EARLY : (o + 1) * 2 * EARLY, lanes] = jnp.where(
                owner_row == jnp.asarray(o, BF16), both, jnp.zeros((), BF16)
            )
        hot_ref[x, :, lanes] = slot_one_hot(rows & (LANES - 1), y)

    def add_product(x):
        product = lax.dot_general(lhs_ref[x], hot_ref[x], NT, preferred_element_type=F32)
        total_ref[...] = product if x == 0 else total_ref[...] + product

    def finish():
        total = total_ref[...].reshape(owners, 2 * EARLY, LANES)
        table_ref[...] = total[:, :EARLY, :] + total[:, EARLY:, :]

    for x in range(blocks_x):
        features_of(x)
        for y in range(blocks_y):
            operands_of(x, y)
        add_product(x)
    finish()


def target_rows(pos, radius):
    weight = 4.0 / (radius * radius)
    cx, cy, cz = pos[0] - 0.5, pos[1] - 0.5, pos[2] - 0.5
    lines = (
        -2.0 * cx * weight, -2.0 * cy * weight, -2.0 * cz * weight,
        weight, weight, weight,
        (cx * cx + cy * cy + cz * cz) * weight, jnp.zeros_like(weight),
    )
    parts = [three_parts(line) for line in lines]
    return [part[k] for k in range(3) for part in parts]


def target_matrix(coef):
    one, two, three = coef[0:8], coef[8:16], coef[16:24]
    stacked = jnp.concatenate([one, one, two, two, one, three], axis=0)
    return stacked.T.astype(BF16)


def source_matrix(line, root, squares):
    value = jnp.where(squares, line * line, line) * (root * root)
    one, two, three = three_parts(value)
    first = jnp.concatenate([one, two], axis=0).astype(BF16)
    last = jnp.concatenate([three, one], axis=0).astype(BF16)
    return jnp.concatenate([first, first, last], axis=0)


def fifth_root(mass):
    root = jnp.exp(0.2 * jnp.log(mass))
    square = root * root
    return 0.8 * root + 0.2 * mass / (square * square)


def store_source(nat_ref, start, count, columns, mass):
    cx, cy, cz = [column - 0.5 for column in columns]
    one = jnp.ones_like(cx)
    for kind, line in enumerate((cx, cy, cz, cx, cy, cz, one, fifth_root(mass))):
        nat_ref[start + kind * 8 : start + kind * 8 + count, :] = line


def pair_sums(sides, pieces=()):
    rows = 32
    steps = []
    for target, sources, roots, total in sides:
        count = roots.shape[0]
        for first in range(0, count, 2):
            steps.append((target, sources, roots, total, first, min(2, count - first), count))

    def product(step):
        target, sources, _, _, first, width, _ = step
        right = sources[:, first * LANES : (first + width) * LANES]
        return jnp.dot(target[...], right, preferred_element_type=F32)

    ready = product(steps[0])
    chunks = None
    for number, (_, _, roots, total, first, width, count) in enumerate(steps):
        squared = ready
        if number + 1 < len(steps):
            ready = product(steps[number + 1])
        if first == 0:
            chunks = [None] * (LANES // rows)
        limits = []
        for k in range(width):
            root = roots[first + k : first + k + 1, :]
            reach = 4.0 * root
            limits.append(
                [jnp.broadcast_to(line, (rows, LANES)) for line in (root, reach, reach * reach)]
            )
        for r in range(len(chunks)):
            for k, (root, reach, most) in enumerate(limits):
                t = squared[r * rows : (r + 1) * rows, k * LANES : (k + 1) * LANES]
                t = jnp.maximum(jnp.minimum(t, most), 1e-12)
                u = t * lax.rsqrt(t)
                f = reach - u
                f = f * f
                f = f * f
                term = f * (root + u)
                chunks[r] = term if chunks[r] is None else chunks[r] + term
        if first + width == count:
            for r, chunk in enumerate(chunks):
                total[r * rows : (r + 1) * rows, :] = chunk
        if number < len(pieces):
            pieces[number]()
    for piece in pieces[len(steps) :]:
        piece()


def column_sums(totals):
    lane = lax.broadcasted_iota(jnp.int32, (LANES, LANES), 1)
    columns = jnp.zeros((LANES, LANES), F32)
    for k, total in enumerate(totals):
        columns = jnp.where(lane == k, jnp.sum(total, axis=1, keepdims=True), columns)
    return columns.T[: len(totals), :]


def square_mask():
    kind = lax.broadcasted_iota(jnp.int32, (8, LANES), 0)
    return (kind >= 3) & (kind < 6)


def shift_rows(step_x, step_y):
    kind = lax.broadcasted_iota(jnp.int32, (8, LANES), 0)
    along_x = jnp.where((kind == 0) | (kind == 3), float(step_x), 0.0)
    return along_x + jnp.where((kind == 1) | (kind == 4), float(step_y), 0.0)


def put_shifts(shift_ref):
    for code in range(9):
        shift_ref[code] = shift_rows(code // 3 - 1, code % 3 - 1)


def put_source(near_ref, root_ref, number, k, line, shift, squares):
    root = jnp.broadcast_to(line[7:8], line.shape)
    near_ref[number, :, k * LANES : (k + 1) * LANES] = source_matrix(line + shift, root, squares)
    root_ref[number, k : k + 1, :] = root[0:1]


def block_pairs(
    x_first, x_step, x_count, code_ref, pos_ref, mass_ref, smooth_ref, prev_ref, next_ref,
    out_ref, src_ref, nat_ref, shift_ref, tgt_ref, mat_ref, near_ref, root_ref, total_ref,
):
    blocks_x, blocks_y, _ = mass_ref.shape
    listed = code_ref.shape[0]
    for xe in range(blocks_x + 2):
        if xe == 0 or xe == blocks_x + 1:
            ref = prev_ref if xe == 0 else next_ref
            if ref is None:
                continue
            store_source(nat_ref, xe * 64, blocks_y, [ref[c] for c in range(3)], ref[3])
        else:
            columns = [pos_ref[c, xe - 1] for c in range(3)]
            store_source(nat_ref, xe * 64, blocks_y, columns, mass_ref[xe - 1])
        for y in range(blocks_y):
            src_ref[xe * blocks_y + y] = nat_ref[pl.ds(xe * 64 + y, 8, stride=8), :]
    put_shifts(shift_ref)
    squares = square_mask()
    blocks = [(turn, y) for turn in range(x_count) for y in range(1, blocks_y - 1)]
    for turn in range(x_count):
        x = x_first + turn * x_step
        lines = target_rows([pos_ref[c, x] for c in range(3)], smooth_ref[x])
        for row, line in enumerate(lines):
            tgt_ref[turn, row * blocks_y : (row + 1) * blocks_y, :] = line
    for number, (turn, y) in enumerate(blocks):
        mat_ref[number] = target_matrix(tgt_ref[turn, pl.ds(y, 24, stride=blocks_y), :])
    for number, (turn, y) in enumerate(blocks):
        x = x_first + turn * x_step
        for k in range(listed):
            code = code_ref[k, x, y]
            step_x = (code * 11) >> 5
            line = src_ref[(x + step_x) * blocks_y + y + code - 3 * step_x - 1]
            put_source(near_ref, root_ref, number, k, line, shift_ref[code], squares)
    pair_sums(
        [
            (mat_ref.at[n], near_ref.at[n], root_ref.at[n, pl.ds(0, listed)], total_ref.at[n])
            for n in range(len(blocks))
        ]
    )
    inner = blocks_y - 2
    for turn in range(x_count):
        sums = column_sums([total_ref[turn * inner + k] for k in range(inner)])
        out_ref[turn, 1 : blocks_y - 1, :] = sums


def middle_kernel(
    code_ref, pos_ref, mass_ref, smooth_ref, group_ref, row_ref, column_ref, out_ref, *scratch
):
    blocks_x, blocks_y, _ = mass_ref.shape
    for side in range(2):
        y = side * (blocks_y - 1)
        for x in range(blocks_x):
            for c in range(3):
                column_ref[side, c, x : x + 1, :] = pos_ref[c, x, y : y + 1, :]
            column_ref[side, 3, x : x + 1, :] = mass_ref[x, y : y + 1, :]
    block_pairs(
        1, 1, blocks_x - 2, code_ref, pos_ref, mass_ref, smooth_ref, None, None, out_ref, *scratch
    )


def edge_kernel(
    code_ref, pos_ref, mass_ref, smooth_ref, prev_ref, next_ref, out_ref, src_ref, *scratch
):
    blocks_x = mass_ref.shape[0]
    block_pairs(
        0, blocks_x - 1, 2, code_ref, pos_ref, mass_ref, smooth_ref, prev_ref, next_ref,
        out_ref, src_ref, *scratch,
    )


def pair_scratch(blocks_x, blocks_y, x_count, listed):
    return [
        pltpu.VMEM(((blocks_x + 2) * 64, LANES), F32),
        pltpu.VMEM((9, 8, LANES), F32),
        pltpu.VMEM((x_count, 24 * blocks_y, LANES), F32),
    ] + product_scratch(x_count * (blocks_y - 2), listed)


def product_scratch(blocks, listed):
    return [
        pltpu.VMEM((blocks, LANES, 48), BF16),
        pltpu.VMEM((blocks, 48, listed * LANES), BF16),
        pltpu.VMEM((blocks, 8, LANES), F32),
        pltpu.VMEM((blocks, LANES, LANES), F32),
    ]


def rim_kernel(
    code_ref, middle_ref, edge_ref, known_ref, pos_ref, mass_ref, smooth_ref,
    low_ref, high_ref, rows_ref, hot_ref, early_ref,
    sum_ref, table_ref, nat_ref, src_ref, md_ref, lhs_ref, row_sum_ref,
    shift_ref, tgt_ref, mat_ref, near_ref, root_ref, total_ref,
):
    blocks_x, blocks_y, _ = mass_ref.shape
    owners = early_ref.shape[0]
    listed = code_ref.shape[0]
    wide = blocks_x + 2
    for side, ref in enumerate((low_ref, high_ref)):
        store_source(nat_ref, side * 64, wide, [ref[c] for c in range(3)], ref[3])
        for xe in range(wide):
            ghost = 5 * side * wide + xe
            src_ref[ghost] = nat_ref[pl.ds(side * 64 + xe, 8, stride=8), :]
            for k in range(2):
                y = k + side * (blocks_y - 2)
                place = (1 + k + 2 * side) * wide + xe
                src_ref[place] = known_ref[xe * blocks_y + y]
    put_shifts(shift_ref)
    squares = square_mask()
    for x in range(blocks_x):
        edge = x == 0 or x == blocks_x - 1
        turn = (1 if x else 0) if edge else x - 1
        sum_ref[x] = (edge_ref if edge else middle_ref)[turn]
        lines = target_rows([pos_ref[c, x] for c in range(3)], smooth_ref[x])
        for row, line in enumerate(lines):
            tgt_ref[x, row * blocks_y : (row + 1) * blocks_y, :] = line
    for x in range(blocks_x):
        for side in range(2):
            y = side * (blocks_y - 1)
            mat_ref[2 * x + side] = target_matrix(tgt_ref[x, pl.ds(y, 24, stride=blocks_y), :])
    for x in range(blocks_x):
        for side in range(2):
            y = side * (blocks_y - 1)
            for k in range(listed):
                code = code_ref[k, x, y]
                step_x = (code * 11) >> 5
                line = src_ref[(3 * side + code - 3 * step_x) * wide + x + step_x]
                put_source(near_ref, root_ref, 2 * x + side, k, line, shift_ref[code], squares)
    sides = [
        (mat_ref.at[n], near_ref.at[n], root_ref.at[n, pl.ds(0, listed)], total_ref.at[n])
        for n in range(2 * blocks_x)
    ]
    owner_ids = lax.broadcasted_iota(jnp.int32, (owners, LANES), 0)
    last = blocks_y - 1

    def put_moments(x, ys):
        radius = smooth_ref[x]
        moment = mass_ref[x] * (sum_ref[x] * DENSITY_FACTOR / (radius * radius * radius))
        high_part = rounded(moment)
        low_part = moment - high_part
        owner = rows_ref[x] >> 7
        for y in ys:
            mine = jnp.broadcast_to(owner[y : y + 1, :], owner_ids.shape) == owner_ids
            lhs_ref[x, :, y * LANES : (y + 1) * LANES] = jnp.concatenate(
                [
                    jnp.where(mine, jnp.broadcast_to(part[y : y + 1, :], mine.shape), 0.0)
                    for part in (high_part, low_part)
                ],
                axis=0,
            ).astype(BF16)

    def inner_moments(x):
        put_moments(x, range(1, last))
        lanes = slice(LANES, last * LANES)
        product = lax.dot_general(
            hot_ref[x, :, lanes], lhs_ref[x, :, lanes], NT, preferred_element_type=F32
        )
        row_sum_ref[...] = product if x == 0 else row_sum_ref[...] + product

    pair_sums(sides, [functools.partial(inner_moments, x) for x in range(blocks_x)])
    sums = column_sums([total_ref[number] for number in range(len(sides))])
    for x in range(blocks_x):
        for side in range(2):
            y = side * last
            sum_ref[x, y : y + 1, :] = sums[2 * x + side : 2 * x + side + 1, :]
        put_moments(x, (0, last))
    ends = [(x, slice(y * LANES, (y + 1) * LANES)) for x in range(blocks_x) for y in (0, last)]
    total = row_sum_ref[...] + lax.dot_general(
        jnp.concatenate([hot_ref[x, :, lanes] for x, lanes in ends], axis=1),
        jnp.concatenate([lhs_ref[x, :, lanes] for x, lanes in ends], axis=1),
        NT,
        preferred_element_type=F32,
    )
    total = total.T
    md_ref[...] = total[:owners] + total[owners:]
    core, my_chip = lax.axis_index("core"), lax.axis_index("chip")
    for other in range(2):
        for step in range(owners // 2):
            owner = 2 * (my_chip ^ step) + (core ^ other)
            table_ref[other, step, :EARLY, :] = early_ref[owner]
            table_ref[other, step, EARLY : EARLY + 1, :] = md_ref[pl.ds(owner, 1), :]


def swap(value, axis, step):
    count = lax.axis_size(axis)
    return lax.ppermute(value, axis, [(i, i ^ step) for i in range(count)])


def neighbours_of(low_edge, high_edge, axis, parity):
    count = lax.axis_size(axis)
    even = parity == 0
    inner = lax.ppermute(
        jnp.where(even, high_edge, low_edge), axis, [(i, i ^ 1) for i in range(count)]
    )
    outer = lax.ppermute(
        jnp.where(even, low_edge, high_edge),
        axis,
        [(i, (i + 1 if i & 1 else i - 1) % count) for i in range(count)],
    )
    return jnp.where(even, outer, inner), jnp.where(even, inner, outer)


def added(parts):
    while len(parts) > 1:
        parts = [sum(parts[k : k + 2][1:], parts[k]) for k in range(0, len(parts), 2)]
    return parts[0]


def to_owner(table):
    table = table[0] + swap(table[1], "core", 1)
    while table.shape[0] > 1:
        ways = min(4, table.shape[0])
        part = table.shape[0] // ways
        table = added(
            [table[:part]]
            + [swap(table[k * part : (k + 1) * part], "chip", k * part) for k in range(1, ways)]
        )
    return table[0]


def summed(value, axis):
    count = lax.axis_size(axis)
    if count & (count - 1):
        return lax.psum(value, axis)
    step = 1
    while step < count:
        ways = min(4, count // step)
        value = added([value] + [swap(value, axis, k * step) for k in range(1, ways)])
        step *= ways
    return value


def shards(positions, velocities, masses, smoothing, neighbours, particle_group, group_row):
    blocks_x, blocks_y, block_len = masses.shape
    dom_count, sub_count = lax.axis_size("dom"), lax.axis_size("chip") * lax.axis_size("core")
    owners = sub_count
    chunk = blocks_y * block_len
    shape = jax.ShapeDtypeStruct
    codes = neighbours.transpose(2, 0, 1)
    table_rows = group_row.reshape(-1, LANES)
    packed = jnp.concatenate([positions, masses[None]], axis=0)
    prev, following = neighbours_of(
        packed[:, 0], packed[:, blocks_x - 1], "dom", lax.axis_index("dom") & 1
    )
    sources = ((blocks_x + 2) * blocks_y, 8, LANES)
    columns, middle = pl.pallas_call(
        middle_kernel,
        out_shape=(
            shape((2, 4, blocks_x, LANES), F32),
            shape((blocks_x - 2, blocks_y, LANES), F32),
        ),
        in_specs=[SMEM] + [VMEM] * 5,
        out_specs=(VMEM,) * 2,
        scratch_shapes=[pltpu.VMEM(sources, F32)]
        + pair_scratch(blocks_x, blocks_y, blocks_x - 2, codes.shape[0]),
        compiler_params=params(),
        cost_estimate=pl.CostEstimate(
            flops=4_000_000_000, bytes_accessed=400_000, transcendentals=1_300_000
        ),
        name="middle_pairs",
    )(codes, positions, masses, smoothing, particle_group, table_rows)
    early, rows, hot = pl.pallas_call(
        functools.partial(moments_kernel, blocks_x * dom_count, blocks_y * sub_count),
        out_shape=(
            shape((owners, EARLY, LANES), F32),
            shape(masses.shape, jnp.int32),
            shape((blocks_x, LANES, chunk), BF16),
        ),
        in_specs=[VMEM] * 6,
        out_specs=(VMEM,) * 3,
        scratch_shapes=[
            pltpu.VMEM((blocks_x * EARLY * blocks_y, LANES), F32),
            pltpu.VMEM((blocks_x, owners * 2 * EARLY, chunk), BF16),
            pltpu.VMEM((owners * 2 * EARLY, LANES), F32),
        ],
        compiler_params=params(),
        cost_estimate=pl.CostEstimate(
            flops=2_000_000_000, bytes_accessed=1_400_000, transcendentals=0
        ),
        name="moments_by_row",
    )(middle, positions, velocities, masses, particle_group, table_rows)
    edges = [
        jnp.concatenate([prev[:, y : y + 1], columns[side], following[:, y : y + 1]], axis=1)
        for side, y in ((0, 0), (1, blocks_y - 1))
    ]
    low, high = neighbours_of(*edges, ("chip", "core"), lax.axis_index("core"))
    edge, known = pl.pallas_call(
        edge_kernel,
        out_shape=(shape((2, blocks_y, LANES), F32), shape(sources, F32)),
        in_specs=[SMEM] + [VMEM] * 5,
        out_specs=(VMEM,) * 2,
        scratch_shapes=pair_scratch(blocks_x, blocks_y, 2, codes.shape[0]),
        compiler_params=params(),
        cost_estimate=pl.CostEstimate(
            flops=4_000_000_000, bytes_accessed=400_000, transcendentals=1_300_000
        ),
        name="edge_pairs",
    )(codes, positions, masses, smoothing, prev, following)
    sums, table = pl.pallas_call(
        rim_kernel,
        out_shape=(shape(masses.shape, F32), shape((2, owners // 2, EARLY + 1, LANES), F32)),
        in_specs=[SMEM] + [VMEM] * 11,
        out_specs=(VMEM, VMEM),
        scratch_shapes=[
            pltpu.VMEM((128, LANES), F32),
            pltpu.VMEM((6 * (blocks_x + 2), 8, LANES), F32),
            pltpu.VMEM((owners, LANES), F32),
            pltpu.VMEM((blocks_x, 2 * owners, chunk), BF16),
            pltpu.VMEM((LANES, 2 * owners), F32),
            pltpu.VMEM((9, 8, LANES), F32),
            pltpu.VMEM((blocks_x, 24 * blocks_y, LANES), F32),
        ]
        + product_scratch(2 * blocks_x, codes.shape[0]),
        compiler_params=params(),
        cost_estimate=pl.CostEstimate(
            flops=200_000_000, bytes_accessed=400_000, transcendentals=400_000
        ),
        name="rim_pairs_and_table",
    )(
        codes, middle, edge, known, positions, masses, smoothing, low, high, rows, hot, early
    )
    density = sums * DENSITY_FACTOR / (smoothing * smoothing * smoothing)
    return (density, summed(to_owner(table), "dom"))


def solution(mesh):
    dom_count, sub_count = mesh.devices.shape
    mesh = jax.sharding.Mesh(
        mesh.devices.reshape(dom_count, sub_count // 2, 2), ("dom", "chip", "core")
    )
    sub = ("chip", "core")
    in_specs = (
        P(None, "dom", sub, None),
        P(None, "dom", sub, None),
        P("dom", sub, None),
        P("dom", sub, None),
        P("dom", sub, None),
        P("dom", sub, None),
        P(),
    )
    out_specs = (P("dom", sub, None), P(None, sub))
    return jax.shard_map(shards, mesh=mesh, in_specs=in_specs, out_specs=out_specs, check_vma=False)
```

```python
import functools
import math

import jax
import jax.numpy as jnp
from jax import lax
from jax.experimental import pallas as pl
from jax.experimental.pallas import tpu as pltpu
from jax.sharding import PartitionSpec as P

F32 = jnp.float32
BF16 = jnp.bfloat16
LANES = 128
EARLY = 16
DENSITY_FACTOR = 21.0 / (16.0 * math.pi) / 256.0
VMEM = pl.BlockSpec(memory_space=pltpu.VMEM)
ANY = pl.BlockSpec(memory_space=pl.ANY)
NT = (((1,), (1,)), ((), ()))


def params():
    return pltpu.CompilerParams(vmem_limit_bytes=40 * 1024 * 1024)


def rounded(value):
    return value.astype(BF16).astype(F32)


def three_parts(value):
    first = rounded(value)
    rest = value - first
    second = rounded(rest)
    return first, second, rest - second


def spread(numbers, y, count):
    row = jnp.broadcast_to(numbers[y : y + 1, :].astype(F32), (16, LANES)).astype(BF16)
    return jnp.concatenate([row] * (count // 16), axis=0)


def row_numbers(count):
    return lax.broadcasted_iota(jnp.int32, (count, LANES), 0).astype(F32).astype(BF16)


def slot_one_hot(slots, y):
    return jnp.where(
        row_numbers(LANES) == spread(slots, y, LANES), jnp.ones((), BF16), jnp.zeros((), BF16)
    )


def moments_kernel(
    nx_total, ny_total, after_ref, pos_ref, vel_ref, mass_ref, group_ref, row_ref,
    table_ref, rows_ref, hot_ref, feat_ref, lhs_ref, total_ref,
):
    blocks_x, blocks_y, _ = mass_ref.shape
    owners = table_ref.shape[0]
    table_rows = row_ref.shape[0]
    base_x = (lax.axis_index("dom") * blocks_x).astype(F32)
    base_y = ((2 * lax.axis_index("chip") + lax.axis_index("core")) * blocks_y).astype(F32)
    y_iota = lax.broadcasted_iota(jnp.int32, (blocks_y, LANES), 0).astype(F32)

    def features_of(x):
        group = group_ref[x]
        low = group & (LANES - 1)
        high = group >> 7
        rows = jnp.zeros_like(group)
        for r in range(table_rows):
            line = jnp.broadcast_to(row_ref[r : r + 1, :], group.shape)
            picked = jnp.take_along_axis(line, low, axis=1)
            rows = jnp.where(high == r, picked, rows)
        rows_ref[x] = rows
        mass = mass_ref[x]
        gx = (base_x + float(x) + pos_ref[0, x]) / float(nx_total)
        gy = (base_y + y_iota + pos_ref[1, x]) / float(ny_total)
        gz = pos_ref[2, x]
        vx, vy, vz = vel_ref[0, x], vel_ref[1, x], vel_ref[2, x]
        mx, my, mz = mass * gx, mass * gy, mass * gz
        features = (
            mass, mx, my, mz, mass * vx, mass * vy, mass * vz,
            mass * (gy * vz - gz * vy), mass * (gz * vx - gx * vz), mass * (gx * vy - gy * vx),
            mx * gx, my * gy, mz * gz, mx * gy, mx * gz, my * gz,
        )
        for f, feature in enumerate(features):
            start = (x * EARLY + f) * blocks_y
            feat_ref[start : start + blocks_y, :] = feature

    def operands_of(x, y):
        lanes = slice(y * LANES, (y + 1) * LANES)
        feats = feat_ref[pl.ds(x * EARLY * blocks_y + y, EARLY, stride=blocks_y), :]
        high_part = rounded(feats)
        both = jnp.concatenate([high_part, feats - high_part], axis=0).astype(BF16)
        rows = rows_ref[x]
        owner_row = spread(rows >> 7, y, 2 * EARLY)
        for o in range(owners):
            lhs_ref[x, o * 2 * EARLY : (o + 1) * 2 * EARLY, lanes] = jnp.where(
                owner_row == jnp.asarray(o, BF16), both, jnp.zeros((), BF16)
            )
        hot_ref[x, :, lanes] = slot_one_hot(rows & (LANES - 1), y)

    def add_product(x):
        product = lax.dot_general(lhs_ref[x], hot_ref[x], NT, preferred_element_type=F32)
        total_ref[...] = product if x == 0 else total_ref[...] + product

    def finish():
        total = total_ref[...].reshape(owners, 2 * EARLY, LANES)
        table_ref[...] = total[:, :EARLY, :] + total[:, EARLY:, :]

    for x in range(blocks_x):
        features_of(x)
        for y in range(blocks_y):
            operands_of(x, y)
        add_product(x)
    finish()


def target_rows(pos, radius):
    weight = 4.0 / (radius * radius)
    cx, cy, cz = pos[0] - 0.5, pos[1] - 0.5, pos[2] - 0.5
    lines = (
        -2.0 * cx * weight, -2.0 * cy * weight, -2.0 * cz * weight,
        weight, weight, weight,
        (cx * cx + cy * cy + cz * cz) * weight, jnp.zeros_like(weight),
    )
    parts = [three_parts(line) for line in lines]
    return [part[k] for k in range(3) for part in parts]


def target_matrix(coef):
    one, two, three = coef[0:8], coef[8:16], coef[16:24]
    stacked = jnp.concatenate([one, one, two, two, one, three], axis=0)
    return stacked.T.astype(BF16)


def source_matrix(line, root, squares):
    value = jnp.where(squares, line * line, line) * (root * root)
    one, two, three = three_parts(value)
    first = jnp.concatenate([one, two], axis=0).astype(BF16)
    last = jnp.concatenate([three, one], axis=0).astype(BF16)
    return jnp.concatenate([first, first, last], axis=0)


def fifth_root(mass):
    root = jnp.exp(0.2 * jnp.log(mass))
    square = root * root
    return 0.8 * root + 0.2 * mass / (square * square)


def store_source(nat_ref, start, count, columns, mass):
    cx, cy, cz = [column - 0.5 for column in columns]
    one = jnp.ones_like(cx)
    for kind, line in enumerate((cx, cy, cz, cx, cy, cz, one, fifth_root(mass))):
        nat_ref[start + kind * 8 : start + kind * 8 + count, :] = line


def pair_sums(sides, pieces=()):
    rows = 32
    steps = []
    for target, sources, roots, total in sides:
        count = roots.shape[0]
        for first in range(0, count, 2):
            steps.append((target, sources, roots, total, first, min(2, count - first), count))

    def product(step):
        target, sources, _, _, first, width, _ = step
        right = sources[:, first * LANES : (first + width) * LANES]
        return jnp.dot(target[...], right, preferred_element_type=F32)

    ready = product(steps[0])
    chunks = None
    for number, (_, _, roots, total, first, width, count) in enumerate(steps):
        squared = ready
        if number + 1 < len(steps):
            ready = product(steps[number + 1])
        if first == 0:
            chunks = [None] * (LANES // rows)
        limits = []
        for k in range(width):
            root = roots[first + k : first + k + 1, :]
            reach = 4.0 * root
            limits.append(
                [jnp.broadcast_to(line, (rows, LANES)) for line in (root, reach, reach * reach)]
            )
        for r in range(len(chunks)):
            for k, (root, reach, most) in enumerate(limits):
                t = squared[r * rows : (r + 1) * rows, k * LANES : (k + 1) * LANES]
                t = jnp.maximum(jnp.minimum(t, most), 1e-12)
                u = t * lax.rsqrt(t)
                f = reach - u
                f = f * f
                f = f * f
                term = f * (root + u)
                chunks[r] = term if chunks[r] is None else chunks[r] + term
        if first + width == count:
            for r, chunk in enumerate(chunks):
                total[r * rows : (r + 1) * rows, :] = chunk
        if number < len(pieces) and pieces[number] is not None:
            pieces[number]()
    for piece in pieces[len(steps) :]:
        piece()


def column_sums(totals):
    lane = lax.broadcasted_iota(jnp.int32, (LANES, LANES), 1)
    columns = jnp.zeros((LANES, LANES), F32)
    for k, total in enumerate(totals):
        columns = jnp.where(lane == k, jnp.sum(total, axis=1, keepdims=True), columns)
    return columns.T[: len(totals), :]


def square_mask():
    kind = lax.broadcasted_iota(jnp.int32, (8, LANES), 0)
    return (kind >= 3) & (kind < 6)


def shift_rows(step_x, step_y):
    kind = lax.broadcasted_iota(jnp.int32, (8, LANES), 0)
    along_x = jnp.where((kind == 0) | (kind == 3), float(step_x), 0.0)
    return along_x + jnp.where((kind == 1) | (kind == 4), float(step_y), 0.0)


def put_shifts(shift_ref):
    for code in range(9):
        shift_ref[code] = shift_rows(code // 3 - 1, code % 3 - 1)


def put_source(near_ref, root_ref, number, k, line, shift, squares):
    root = jnp.broadcast_to(line[7:8], line.shape)
    near_ref[number, :, k * LANES : (k + 1) * LANES] = source_matrix(line + shift, root, squares)
    root_ref[number, k : k + 1, :] = root[0:1]


def load_codes(far_ref, code_ref, sem):
    copy = pltpu.make_async_copy(far_ref, code_ref, sem)
    copy.start()
    return copy


def block_pairs(
    x_first, x_step, x_count, known_ref, far_code_ref, pos_ref, mass_ref, smooth_ref, prev_ref, next_ref,
    out_ref, src_ref, code_ref, sem, nat_ref, shift_ref, tgt_ref, mat_ref, near_ref, root_ref, total_ref,
):
    blocks_x, blocks_y, _ = mass_ref.shape
    listed = code_ref.shape[0]
    codes = load_codes(far_code_ref, code_ref, sem)
    for xe in range(blocks_x + 2):
        if xe == 0 or xe == blocks_x + 1:
            ref = prev_ref if xe == 0 else next_ref
            if ref is None:
                continue
            store_source(nat_ref, xe * 64, blocks_y, [ref[c] for c in range(3)], ref[3])
        elif known_ref is None:
            columns = [pos_ref[c, xe - 1] for c in range(3)]
            store_source(nat_ref, xe * 64, blocks_y, columns, mass_ref[xe - 1])
        else:
            part = pl.ds(xe * blocks_y, blocks_y)
            src_ref[part] = known_ref[part]
            continue
        for y in range(blocks_y):
            src_ref[xe * blocks_y + y] = nat_ref[pl.ds(xe * 64 + y, 8, stride=8), :]
    put_shifts(shift_ref)
    squares = square_mask()
    blocks = [(turn, y) for turn in range(x_count) for y in range(1, blocks_y - 1)]
    for turn in range(x_count):
        x = x_first + turn * x_step
        lines = target_rows([pos_ref[c, x] for c in range(3)], smooth_ref[x])
        for row, line in enumerate(lines):
            tgt_ref[turn, row * blocks_y : (row + 1) * blocks_y, :] = line
    for number, (turn, y) in enumerate(blocks):
        mat_ref[number] = target_matrix(tgt_ref[turn, pl.ds(y, 24, stride=blocks_y), :])
    codes.wait()
    for number, (turn, y) in enumerate(blocks):
        x = x_first + turn * x_step
        for k in range(listed):
            code = code_ref[k, x, y]
            step_x = (code * 11) >> 5
            line = src_ref[(x + step_x) * blocks_y + y + code - 3 * step_x - 1]
            put_source(near_ref, root_ref, number, k, line, shift_ref[code], squares)
    inner = blocks_y - 2
    per_row = inner * ((listed + 1) // 2)

    def row_sums(turn):
        sums = column_sums([total_ref[turn * inner + k] for k in range(inner)])
        out_ref[turn, 1 : blocks_y - 1, :] = sums

    pieces = [None] * (x_count * per_row + 1)
    for turn in range(x_count):
        pieces[(turn + 1) * per_row] = functools.partial(row_sums, turn)
    pair_sums(
        [
            (mat_ref.at[n], near_ref.at[n], root_ref.at[n, pl.ds(0, listed)], total_ref.at[n])
            for n in range(len(blocks))
        ],
        pieces,
    )


def middle_kernel(
    code_ref, pos_ref, mass_ref, smooth_ref, group_ref, row_ref, column_ref, out_ref, src_ref, *scratch
):
    blocks_x, blocks_y, _ = mass_ref.shape
    for side in range(2):
        y = side * (blocks_y - 1)
        for x in range(blocks_x):
            for c in range(3):
                column_ref[side, c, x : x + 1, :] = pos_ref[c, x, y : y + 1, :]
            column_ref[side, 3, x : x + 1, :] = mass_ref[x, y : y + 1, :]
    block_pairs(
        1, 1, blocks_x - 2, None, code_ref, pos_ref, mass_ref, smooth_ref, None, None,
        out_ref, src_ref, *scratch,
    )


def edge_kernel(
    code_ref, pos_ref, mass_ref, smooth_ref, prev_ref, next_ref, known_ref, out_ref, src_ref, *scratch
):
    blocks_x = mass_ref.shape[0]
    block_pairs(
        0, blocks_x - 1, 2, known_ref, code_ref, pos_ref, mass_ref, smooth_ref, prev_ref, next_ref,
        out_ref, src_ref, *scratch,
    )


def pair_scratch(blocks_x, blocks_y, x_count, listed):
    return [
        pltpu.SMEM((listed, blocks_x, blocks_y), jnp.int32),
        pltpu.SemaphoreType.DMA(()),
        pltpu.VMEM(((blocks_x + 2) * 64, LANES), F32),
        pltpu.VMEM((9, 8, LANES), F32),
        pltpu.VMEM((x_count, 24 * blocks_y, LANES), F32),
    ] + product_scratch(x_count * (blocks_y - 2), listed)


def product_scratch(blocks, listed):
    return [
        pltpu.VMEM((blocks, LANES, 48), BF16),
        pltpu.VMEM((blocks, 48, listed * LANES), BF16),
        pltpu.VMEM((blocks, 8, LANES), F32),
        pltpu.VMEM((blocks, LANES, LANES), F32),
    ]


def rim_kernel(
    far_code_ref, middle_ref, edge_ref, known_ref, pos_ref, mass_ref, smooth_ref,
    low_ref, high_ref, rows_ref, hot_ref, early_ref,
    sum_ref, table_ref, code_ref, sem, nat_ref, src_ref, md_ref, lhs_ref, row_sum_ref,
    shift_ref, tgt_ref, mat_ref, near_ref, root_ref, total_ref,
):
    blocks_x, blocks_y, _ = mass_ref.shape
    owners = early_ref.shape[0]
    listed = code_ref.shape[0]
    wide = blocks_x + 2
    codes = load_codes(far_code_ref, code_ref, sem)
    for side, ref in enumerate((low_ref, high_ref)):
        store_source(nat_ref, side * 64, wide, [ref[c] for c in range(3)], ref[3])
        for xe in range(wide):
            ghost = 5 * side * wide + xe
            src_ref[ghost] = nat_ref[pl.ds(side * 64 + xe, 8, stride=8), :]
            for k in range(2):
                y = k + side * (blocks_y - 2)
                place = (1 + k + 2 * side) * wide + xe
                src_ref[place] = known_ref[xe * blocks_y + y]
    put_shifts(shift_ref)
    squares = square_mask()
    for x in range(blocks_x):
        edge = x == 0 or x == blocks_x - 1
        turn = (1 if x else 0) if edge else x - 1
        sum_ref[x] = (edge_ref if edge else middle_ref)[turn]
        lines = target_rows([pos_ref[c, x] for c in range(3)], smooth_ref[x])
        for row, line in enumerate(lines):
            tgt_ref[x, row * blocks_y : (row + 1) * blocks_y, :] = line
    for x in range(blocks_x):
        for side in range(2):
            y = side * (blocks_y - 1)
            mat_ref[2 * x + side] = target_matrix(tgt_ref[x, pl.ds(y, 24, stride=blocks_y), :])
    codes.wait()
    for x in range(blocks_x):
        for side in range(2):
            y = side * (blocks_y - 1)
            for k in range(listed):
                code = code_ref[k, x, y]
                step_x = (code * 11) >> 5
                line = src_ref[(3 * side + code - 3 * step_x) * wide + x + step_x]
                put_source(near_ref, root_ref, 2 * x + side, k, line, shift_ref[code], squares)
    sides = [
        (mat_ref.at[n], near_ref.at[n], root_ref.at[n, pl.ds(0, listed)], total_ref.at[n])
        for n in range(2 * blocks_x)
    ]
    owner_ids = lax.broadcasted_iota(jnp.int32, (owners, LANES), 0)
    last = blocks_y - 1

    def put_moments(x, ys):
        radius = smooth_ref[x]
        moment = mass_ref[x] * (sum_ref[x] * DENSITY_FACTOR / (radius * radius * radius))
        high_part = rounded(moment)
        low_part = moment - high_part
        owner = rows_ref[x] >> 7
        for y in ys:
            mine = jnp.broadcast_to(owner[y : y + 1, :], owner_ids.shape) == owner_ids
            lhs_ref[x, :, y * LANES : (y + 1) * LANES] = jnp.concatenate(
                [
                    jnp.where(mine, jnp.broadcast_to(part[y : y + 1, :], mine.shape), 0.0)
                    for part in (high_part, low_part)
                ],
                axis=0,
            ).astype(BF16)

    def inner_moments(x):
        put_moments(x, range(1, last))
        lanes = slice(LANES, last * LANES)
        product = lax.dot_general(
            hot_ref[x, :, lanes], lhs_ref[x, :, lanes], NT, preferred_element_type=F32
        )
        row_sum_ref[...] = product if x == 0 else row_sum_ref[...] + product

    pair_sums(sides, [functools.partial(inner_moments, x) for x in range(blocks_x)])
    sums = column_sums([total_ref[number] for number in range(len(sides))])
    for x in range(blocks_x):
        for side in range(2):
            y = side * last
            sum_ref[x, y : y + 1, :] = sums[2 * x + side : 2 * x + side + 1, :]
        put_moments(x, (0, last))
    ends = [(x, slice(y * LANES, (y + 1) * LANES)) for x in range(blocks_x) for y in (0, last)]
    total = row_sum_ref[...] + lax.dot_general(
        jnp.concatenate([hot_ref[x, :, lanes] for x, lanes in ends], axis=1),
        jnp.concatenate([lhs_ref[x, :, lanes] for x, lanes in ends], axis=1),
        NT,
        preferred_element_type=F32,
    )
    total = total.T
    md_ref[...] = total[:owners] + total[owners:]
    core, my_chip = lax.axis_index("core"), lax.axis_index("chip")
    for other in range(2):
        for step in range(owners // 2):
            owner = 2 * (my_chip ^ step) + (core ^ other)
            table_ref[other, step, :EARLY, :] = early_ref[owner]
            table_ref[other, step, EARLY : EARLY + 1, :] = md_ref[pl.ds(owner, 1), :]


def swap(value, axis, step):
    count = lax.axis_size(axis)
    return lax.ppermute(value, axis, [(i, i ^ step) for i in range(count)])


def neighbours_of(low_edge, high_edge, axis, parity):
    count = lax.axis_size(axis)
    even = parity == 0
    inner = lax.ppermute(
        jnp.where(even, high_edge, low_edge), axis, [(i, i ^ 1) for i in range(count)]
    )
    outer = lax.ppermute(
        jnp.where(even, low_edge, high_edge),
        axis,
        [(i, (i + 1 if i & 1 else i - 1) % count) for i in range(count)],
    )
    return jnp.where(even, outer, inner), jnp.where(even, inner, outer)


def added(parts):
    while len(parts) > 1:
        parts = [sum(parts[k : k + 2][1:], parts[k]) for k in range(0, len(parts), 2)]
    return parts[0]


def to_owner(table):
    table = table[0] + swap(table[1], "core", 1)
    while table.shape[0] > 1:
        ways = min(4, table.shape[0])
        part = table.shape[0] // ways
        table = added(
            [table[:part]]
            + [swap(table[k * part : (k + 1) * part], "chip", k * part) for k in range(1, ways)]
        )
    return table[0]


def summed(value, axis):
    count = lax.axis_size(axis)
    if count & (count - 1):
        return lax.psum(value, axis)
    step = 1
    while step < count:
        ways = min(4, count // step)
        value = added([value] + [swap(value, axis, k * step) for k in range(1, ways)])
        step *= ways
    return value


def shards(positions, velocities, masses, smoothing, neighbours, particle_group, group_row):
    blocks_x, blocks_y, block_len = masses.shape
    dom_count, sub_count = lax.axis_size("dom"), lax.axis_size("chip") * lax.axis_size("core")
    owners = sub_count
    chunk = blocks_y * block_len
    shape = jax.ShapeDtypeStruct
    codes = neighbours.transpose(2, 0, 1)
    table_rows = group_row.reshape(-1, LANES)
    packed = jnp.concatenate([positions, masses[None]], axis=0)
    prev, following = neighbours_of(
        packed[:, 0], packed[:, blocks_x - 1], "dom", lax.axis_index("dom") & 1
    )
    sources = ((blocks_x + 2) * blocks_y, 8, LANES)
    columns, middle, own = pl.pallas_call(
        middle_kernel,
        out_shape=(
            shape((2, 4, blocks_x, LANES), F32),
            shape((blocks_x - 2, blocks_y, LANES), F32),
            shape(sources, F32),
        ),
        in_specs=[ANY] + [VMEM] * 5,
        out_specs=(VMEM,) * 3,
        scratch_shapes=pair_scratch(blocks_x, blocks_y, blocks_x - 2, codes.shape[0]),
        compiler_params=params(),
        cost_estimate=pl.CostEstimate(
            flops=4_000_000_000, bytes_accessed=400_000, transcendentals=1_300_000
        ),
        name="middle_pairs",
    )(codes, positions, masses, smoothing, particle_group, table_rows)
    early, rows, hot = pl.pallas_call(
        functools.partial(moments_kernel, blocks_x * dom_count, blocks_y * sub_count),
        out_shape=(
            shape((owners, EARLY, LANES), F32),
            shape(masses.shape, jnp.int32),
            shape((blocks_x, LANES, chunk), BF16),
        ),
        in_specs=[VMEM] * 6,
        out_specs=(VMEM,) * 3,
        scratch_shapes=[
            pltpu.VMEM((blocks_x * EARLY * blocks_y, LANES), F32),
            pltpu.VMEM((blocks_x, owners * 2 * EARLY, chunk), BF16),
            pltpu.VMEM((owners * 2 * EARLY, LANES), F32),
        ],
        compiler_params=params(),
        cost_estimate=pl.CostEstimate(
            flops=2_000_000_000, bytes_accessed=1_400_000, transcendentals=0
        ),
        name="moments_by_row",
    )(middle, positions, velocities, masses, particle_group, table_rows)
    edges = [
        jnp.concatenate([prev[:, y : y + 1], columns[side], following[:, y : y + 1]], axis=1)
        for side, y in ((0, 0), (1, blocks_y - 1))
    ]
    low, high = neighbours_of(*edges, ("chip", "core"), lax.axis_index("core"))
    edge, known = pl.pallas_call(
        edge_kernel,
        out_shape=(shape((2, blocks_y, LANES), F32), shape(sources, F32)),
        in_specs=[ANY] + [VMEM] * 6,
        out_specs=(VMEM,) * 2,
        scratch_shapes=pair_scratch(blocks_x, blocks_y, 2, codes.shape[0]),
        compiler_params=params(),
        cost_estimate=pl.CostEstimate(
            flops=4_000_000_000, bytes_accessed=400_000, transcendentals=1_300_000
        ),
        name="edge_pairs",
    )(codes, positions, masses, smoothing, prev, following, own)
    sums, table = pl.pallas_call(
        rim_kernel,
        out_shape=(shape(masses.shape, F32), shape((2, owners // 2, EARLY + 1, LANES), F32)),
        in_specs=[ANY] + [VMEM] * 11,
        out_specs=(VMEM, VMEM),
        scratch_shapes=[
            pltpu.SMEM(codes.shape, jnp.int32),
            pltpu.SemaphoreType.DMA(()),
            pltpu.VMEM((128, LANES), F32),
            pltpu.VMEM((6 * (blocks_x + 2), 8, LANES), F32),
            pltpu.VMEM((owners, LANES), F32),
            pltpu.VMEM((blocks_x, 2 * owners, chunk), BF16),
            pltpu.VMEM((LANES, 2 * owners), F32),
            pltpu.VMEM((9, 8, LANES), F32),
            pltpu.VMEM((blocks_x, 24 * blocks_y, LANES), F32),
        ]
        + product_scratch(2 * blocks_x, codes.shape[0]),
        compiler_params=params(),
        cost_estimate=pl.CostEstimate(
            flops=200_000_000, bytes_accessed=400_000, transcendentals=400_000
        ),
        name="rim_pairs_and_table",
    )(
        codes, middle, edge, known, positions, masses, smoothing, low, high, rows, hot, early
    )
    density = sums * DENSITY_FACTOR / (smoothing * smoothing * smoothing)
    return (density, summed(to_owner(table), "dom"))


def solution(mesh):
    dom_count, sub_count = mesh.devices.shape
    mesh = jax.sharding.Mesh(
        mesh.devices.reshape(dom_count, sub_count // 2, 2), ("dom", "chip", "core")
    )
    sub = ("chip", "core")
    in_specs = (
        P(None, "dom", sub, None),
        P(None, "dom", sub, None),
        P("dom", sub, None),
        P("dom", sub, None),
        P("dom", sub, None),
        P("dom", sub, None),
        P(),
    )
    out_specs = (P("dom", sub, None), P(None, sub))
    return jax.shard_map(shards, mesh=mesh, in_specs=in_specs, out_specs=out_specs, check_vma=False)
```

```python
import functools
import math

import jax
import jax.numpy as jnp
from jax import lax
from jax.experimental import pallas as pl
from jax.experimental.pallas import tpu as pltpu
from jax.sharding import PartitionSpec as P

F32 = jnp.float32
BF16 = jnp.bfloat16
LANES = 128
EARLY = 16
DENSITY_FACTOR = 21.0 / (16.0 * math.pi) / 256.0
VMEM = pl.BlockSpec(memory_space=pltpu.VMEM)
ANY = pl.BlockSpec(memory_space=pl.ANY)
NT = (((1,), (1,)), ((), ()))


def params():
    return pltpu.CompilerParams(vmem_limit_bytes=40 * 1024 * 1024)


def rounded(value):
    return value.astype(BF16).astype(F32)


def three_parts(value):
    first = rounded(value)
    rest = value - first
    second = rounded(rest)
    return first, second, rest - second


def spread(numbers, y, count):
    row = jnp.broadcast_to(numbers[y : y + 1, :].astype(F32), (16, LANES)).astype(BF16)
    return jnp.concatenate([row] * (count // 16), axis=0)


def row_numbers(count):
    return lax.broadcasted_iota(jnp.int32, (count, LANES), 0).astype(F32).astype(BF16)


def slot_one_hot(slots, y):
    return jnp.where(
        row_numbers(LANES) == spread(slots, y, LANES), jnp.ones((), BF16), jnp.zeros((), BF16)
    )


def moments_kernel(
    nx_total, ny_total, after_ref, pos_ref, vel_ref, mass_ref, group_ref, row_ref,
    table_ref, rows_ref, hot_ref, feat_ref, lhs_ref, total_ref,
):
    blocks_x, blocks_y, _ = mass_ref.shape
    owners = table_ref.shape[0]
    table_rows = row_ref.shape[0]
    base_x = (lax.axis_index("dom") * blocks_x).astype(F32)
    base_y = ((2 * lax.axis_index("chip") + lax.axis_index("core")) * blocks_y).astype(F32)
    y_iota = lax.broadcasted_iota(jnp.int32, (blocks_y, LANES), 0).astype(F32)

    def features_of(x):
        group = group_ref[x]
        low = group & (LANES - 1)
        high = group >> 7
        rows = jnp.zeros_like(group)
        for r in range(table_rows):
            line = jnp.broadcast_to(row_ref[r : r + 1, :], group.shape)
            picked = jnp.take_along_axis(line, low, axis=1)
            rows = jnp.where(high == r, picked, rows)
        rows_ref[x] = rows
        mass = mass_ref[x]
        gx = (base_x + float(x) + pos_ref[0, x]) / float(nx_total)
        gy = (base_y + y_iota + pos_ref[1, x]) / float(ny_total)
        gz = pos_ref[2, x]
        vx, vy, vz = vel_ref[0, x], vel_ref[1, x], vel_ref[2, x]
        mx, my, mz = mass * gx, mass * gy, mass * gz
        features = (
            mass, mx, my, mz, mass * vx, mass * vy, mass * vz,
            mass * (gy * vz - gz * vy), mass * (gz * vx - gx * vz), mass * (gx * vy - gy * vx),
            mx * gx, my * gy, mz * gz, mx * gy, mx * gz, my * gz,
        )
        for f, feature in enumerate(features):
            start = (x * EARLY + f) * blocks_y
            feat_ref[start : start + blocks_y, :] = feature

    def operands_of(x, y):
        lanes = slice(y * LANES, (y + 1) * LANES)
        feats = feat_ref[pl.ds(x * EARLY * blocks_y + y, EARLY, stride=blocks_y), :]
        high_part = rounded(feats)
        both = jnp.concatenate([high_part, feats - high_part], axis=0).astype(BF16)
        rows = rows_ref[x]
        owner_row = spread(rows >> 7, y, 2 * EARLY)
        for o in range(owners):
            lhs_ref[x, o * 2 * EARLY : (o + 1) * 2 * EARLY, lanes] = jnp.where(
                owner_row == jnp.asarray(o, BF16), both, jnp.zeros((), BF16)
            )
        hot_ref[x, :, lanes] = slot_one_hot(rows & (LANES - 1), y)

    def add_product(x):
        product = lax.dot_general(lhs_ref[x], hot_ref[x], NT, preferred_element_type=F32)
        total_ref[...] = product if x == 0 else total_ref[...] + product

    def finish():
        total = total_ref[...].reshape(owners, 2 * EARLY, LANES)
        table_ref[...] = total[:, :EARLY, :] + total[:, EARLY:, :]

    for x in range(blocks_x):
        features_of(x)
        for y in range(blocks_y):
            operands_of(x, y)
        add_product(x)
    finish()


def target_rows(pos, radius):
    weight = 4.0 / (radius * radius)
    cx, cy, cz = pos[0] - 0.5, pos[1] - 0.5, pos[2] - 0.5
    lines = (
        -2.0 * cx * weight, -2.0 * cy * weight, -2.0 * cz * weight,
        weight, weight, weight,
        (cx * cx + cy * cy + cz * cz) * weight, jnp.zeros_like(weight),
    )
    parts = [three_parts(line) for line in lines]
    return [part[k] for k in range(3) for part in parts]


def target_matrix(coef):
    one, two, three = coef[0:8], coef[8:16], coef[16:24]
    stacked = jnp.concatenate([one, one, two, two, one, three], axis=0)
    return stacked.T.astype(BF16)


def source_matrix(line, root, squares):
    value = jnp.where(squares, line * line, line) * (root * root)
    one, two, three = three_parts(value)
    first = jnp.concatenate([one, two], axis=0).astype(BF16)
    last = jnp.concatenate([three, one], axis=0).astype(BF16)
    return jnp.concatenate([first, first, last], axis=0)


def fifth_root(mass):
    root = jnp.exp(0.2 * jnp.log(mass))
    square = root * root
    return 0.8 * root + 0.2 * mass / (square * square)


def store_source(nat_ref, start, count, columns, mass):
    cx, cy, cz = [column - 0.5 for column in columns]
    one = jnp.ones_like(cx)
    for kind, line in enumerate((cx, cy, cz, cx, cy, cz, one, fifth_root(mass))):
        nat_ref[start + kind * 8 : start + kind * 8 + count, :] = line


def pair_sums(sides, buffers, pieces=()):
    rows = 32

    def products(number):
        target, sources, roots, _ = sides[number]
        for first in range(0, roots.shape[0], 2):
            lanes = slice(first * LANES, min(first + 2, roots.shape[0]) * LANES)
            buffers[number % 2][:, lanes] = jnp.dot(
                target[...], sources[:, lanes], preferred_element_type=F32
            )

    products(0)
    for number, (_, _, roots, total) in enumerate(sides):
        if number + 1 < len(sides):
            products(number + 1)
        limits = []
        for k in range(roots.shape[0]):
            root = roots[k : k + 1, :]
            reach = 4.0 * root
            limits.append(
                [jnp.broadcast_to(line, (rows, LANES)) for line in (root, reach, reach * reach)]
            )
        for first in range(0, LANES, rows):
            chunk = None
            for k, (root, reach, most) in enumerate(limits):
                t = buffers[number % 2][first : first + rows, k * LANES : (k + 1) * LANES]
                t = jnp.maximum(jnp.minimum(t, most), 1e-12)
                u = t * lax.rsqrt(t)
                f = reach - u
                f = f * f
                f = f * f
                term = f * (root + u)
                chunk = term if chunk is None else chunk + term
            total[first : first + rows, :] = chunk
        if number < len(pieces) and pieces[number] is not None:
            pieces[number]()
    for piece in pieces[len(sides) :]:
        piece()


def column_sums(totals):
    lane = lax.broadcasted_iota(jnp.int32, (LANES, LANES), 1)
    columns = jnp.zeros((LANES, LANES), F32)
    for k, total in enumerate(totals):
        columns = jnp.where(lane == k, jnp.sum(total, axis=1, keepdims=True), columns)
    return columns.T[: len(totals), :]


def square_mask():
    kind = lax.broadcasted_iota(jnp.int32, (8, LANES), 0)
    return (kind >= 3) & (kind < 6)


def shift_rows(step_x, step_y):
    kind = lax.broadcasted_iota(jnp.int32, (8, LANES), 0)
    along_x = jnp.where((kind == 0) | (kind == 3), float(step_x), 0.0)
    return along_x + jnp.where((kind == 1) | (kind == 4), float(step_y), 0.0)


def put_shifts(shift_ref):
    for code in range(9):
        shift_ref[code] = shift_rows(code // 3 - 1, code % 3 - 1)


def put_source(near_ref, root_ref, number, k, line, shift, squares):
    root = jnp.broadcast_to(line[7:8], line.shape)
    near_ref[number, :, k * LANES : (k + 1) * LANES] = source_matrix(line + shift, root, squares)
    root_ref[number, k : k + 1, :] = root[0:1]


def load_codes(far_ref, code_ref, sem):
    copy = pltpu.make_async_copy(far_ref, code_ref, sem)
    copy.start()
    return copy


def block_pairs(
    x_first, x_step, x_count, known_ref, far_code_ref, pos_ref, mass_ref, smooth_ref, prev_ref, next_ref,
    out_ref, src_ref, code_ref, sem, nat_ref, shift_ref, tgt_ref, mat_ref, near_ref, root_ref, total_ref, *buffers,
):
    blocks_x, blocks_y, _ = mass_ref.shape
    listed = code_ref.shape[0]
    codes = load_codes(far_code_ref, code_ref, sem)
    for xe in range(blocks_x + 2):
        if xe == 0 or xe == blocks_x + 1:
            ref = prev_ref if xe == 0 else next_ref
            if ref is None:
                continue
            store_source(nat_ref, xe * 64, blocks_y, [ref[c] for c in range(3)], ref[3])
        elif known_ref is None:
            columns = [pos_ref[c, xe - 1] for c in range(3)]
            store_source(nat_ref, xe * 64, blocks_y, columns, mass_ref[xe - 1])
        else:
            part = pl.ds(xe * blocks_y, blocks_y)
            src_ref[part] = known_ref[part]
            continue
        for y in range(blocks_y):
            src_ref[xe * blocks_y + y] = nat_ref[pl.ds(xe * 64 + y, 8, stride=8), :]
    put_shifts(shift_ref)
    squares = square_mask()
    blocks = [(turn, y) for turn in range(x_count) for y in range(1, blocks_y - 1)]
    for turn in range(x_count):
        x = x_first + turn * x_step
        lines = target_rows([pos_ref[c, x] for c in range(3)], smooth_ref[x])
        for row, line in enumerate(lines):
            tgt_ref[turn, row * blocks_y : (row + 1) * blocks_y, :] = line
    for number, (turn, y) in enumerate(blocks):
        mat_ref[number] = target_matrix(tgt_ref[turn, pl.ds(y, 24, stride=blocks_y), :])
    codes.wait()
    for number, (turn, y) in enumerate(blocks):
        x = x_first + turn * x_step
        for k in range(listed):
            code = code_ref[k, x, y]
            step_x = (code * 11) >> 5
            line = src_ref[(x + step_x) * blocks_y + y + code - 3 * step_x - 1]
            put_source(near_ref, root_ref, number, k, line, shift_ref[code], squares)
    inner = blocks_y - 2

    def row_sums(turn):
        sums = column_sums([total_ref[turn * inner + k] for k in range(inner)])
        out_ref[turn, 1 : blocks_y - 1, :] = sums

    pieces = [None] * (x_count * inner + 1)
    for turn in range(x_count):
        pieces[(turn + 1) * inner] = functools.partial(row_sums, turn)
    pair_sums(
        [
            (mat_ref.at[n], near_ref.at[n], root_ref.at[n, pl.ds(0, listed)], total_ref.at[n])
            for n in range(len(blocks))
        ],
        buffers,
        pieces,
    )


def middle_kernel(
    code_ref, pos_ref, mass_ref, smooth_ref, group_ref, row_ref, column_ref, out_ref, src_ref, *scratch
):
    blocks_x, blocks_y, _ = mass_ref.shape
    for side in range(2):
        y = side * (blocks_y - 1)
        for x in range(blocks_x):
            for c in range(3):
                column_ref[side, c, x : x + 1, :] = pos_ref[c, x, y : y + 1, :]
            column_ref[side, 3, x : x + 1, :] = mass_ref[x, y : y + 1, :]
    block_pairs(
        1, 1, blocks_x - 2, None, code_ref, pos_ref, mass_ref, smooth_ref, None, None,
        out_ref, src_ref, *scratch,
    )


def edge_kernel(
    code_ref, pos_ref, mass_ref, smooth_ref, prev_ref, next_ref, known_ref, out_ref, src_ref, *scratch
):
    blocks_x = mass_ref.shape[0]
    block_pairs(
        0, blocks_x - 1, 2, known_ref, code_ref, pos_ref, mass_ref, smooth_ref, prev_ref, next_ref,
        out_ref, src_ref, *scratch,
    )


def pair_scratch(blocks_x, blocks_y, x_count, listed):
    return [
        pltpu.SMEM((listed, blocks_x, blocks_y), jnp.int32),
        pltpu.SemaphoreType.DMA(()),
        pltpu.VMEM(((blocks_x + 2) * 64, LANES), F32),
        pltpu.VMEM((9, 8, LANES), F32),
        pltpu.VMEM((x_count, 24 * blocks_y, LANES), F32),
    ] + product_scratch(x_count * (blocks_y - 2), listed)


def product_scratch(blocks, listed):
    return [
        pltpu.VMEM((blocks, LANES, 48), BF16),
        pltpu.VMEM((blocks, 48, listed * LANES), BF16),
        pltpu.VMEM((blocks, 8, LANES), F32),
        pltpu.VMEM((blocks, LANES, LANES), F32),
        pltpu.VMEM((LANES, listed * LANES), F32),
        pltpu.VMEM((LANES, listed * LANES), F32),
    ]


def rim_kernel(
    far_code_ref, middle_ref, edge_ref, known_ref, pos_ref, mass_ref, smooth_ref,
    low_ref, high_ref, rows_ref, hot_ref, early_ref,
    sum_ref, table_ref, code_ref, sem, nat_ref, src_ref, md_ref, lhs_ref, row_sum_ref,
    shift_ref, tgt_ref, mat_ref, near_ref, root_ref, total_ref, *buffers,
):
    blocks_x, blocks_y, _ = mass_ref.shape
    owners = early_ref.shape[0]
    listed = code_ref.shape[0]
    wide = blocks_x + 2
    codes = load_codes(far_code_ref, code_ref, sem)
    for side, ref in enumerate((low_ref, high_ref)):
        store_source(nat_ref, side * 64, wide, [ref[c] for c in range(3)], ref[3])
        for xe in range(wide):
            ghost = 5 * side * wide + xe
            src_ref[ghost] = nat_ref[pl.ds(side * 64 + xe, 8, stride=8), :]
            for k in range(2):
                y = k + side * (blocks_y - 2)
                place = (1 + k + 2 * side) * wide + xe
                src_ref[place] = known_ref[xe * blocks_y + y]
    put_shifts(shift_ref)
    squares = square_mask()
    for x in range(blocks_x):
        edge = x == 0 or x == blocks_x - 1
        turn = (1 if x else 0) if edge else x - 1
        sum_ref[x] = (edge_ref if edge else middle_ref)[turn]
        lines = target_rows([pos_ref[c, x] for c in range(3)], smooth_ref[x])
        for row, line in enumerate(lines):
            tgt_ref[x, row * blocks_y : (row + 1) * blocks_y, :] = line
    for x in range(blocks_x):
        for side in range(2):
            y = side * (blocks_y - 1)
            mat_ref[2 * x + side] = target_matrix(tgt_ref[x, pl.ds(y, 24, stride=blocks_y), :])
    codes.wait()
    for x in range(blocks_x):
        for side in range(2):
            y = side * (blocks_y - 1)
            for k in range(listed):
                code = code_ref[k, x, y]
                step_x = (code * 11) >> 5
                line = src_ref[(3 * side + code - 3 * step_x) * wide + x + step_x]
                put_source(near_ref, root_ref, 2 * x + side, k, line, shift_ref[code], squares)
    sides = [
        (mat_ref.at[n], near_ref.at[n], root_ref.at[n, pl.ds(0, listed)], total_ref.at[n])
        for n in range(2 * blocks_x)
    ]
    owner_ids = lax.broadcasted_iota(jnp.int32, (owners, LANES), 0)
    last = blocks_y - 1

    def put_moments(x, ys):
        radius = smooth_ref[x]
        moment = mass_ref[x] * (sum_ref[x] * DENSITY_FACTOR / (radius * radius * radius))
        high_part = rounded(moment)
        low_part = moment - high_part
        owner = rows_ref[x] >> 7
        for y in ys:
            mine = jnp.broadcast_to(owner[y : y + 1, :], owner_ids.shape) == owner_ids
            lhs_ref[x, :, y * LANES : (y + 1) * LANES] = jnp.concatenate(
                [
                    jnp.where(mine, jnp.broadcast_to(part[y : y + 1, :], mine.shape), 0.0)
                    for part in (high_part, low_part)
                ],
                axis=0,
            ).astype(BF16)

    def inner_moments(x):
        put_moments(x, range(1, last))
        lanes = slice(LANES, last * LANES)
        product = lax.dot_general(
            hot_ref[x, :, lanes], lhs_ref[x, :, lanes], NT, preferred_element_type=F32
        )
        row_sum_ref[...] = product if x == 0 else row_sum_ref[...] + product

    pair_sums(sides, buffers, [functools.partial(inner_moments, x) for x in range(blocks_x)])
    sums = column_sums([total_ref[number] for number in range(len(sides))])
    for x in range(blocks_x):
        for side in range(2):
            y = side * last
            sum_ref[x, y : y + 1, :] = sums[2 * x + side : 2 * x + side + 1, :]
        put_moments(x, (0, last))
    ends = [(x, slice(y * LANES, (y + 1) * LANES)) for x in range(blocks_x) for y in (0, last)]
    total = row_sum_ref[...] + lax.dot_general(
        jnp.concatenate([hot_ref[x, :, lanes] for x, lanes in ends], axis=1),
        jnp.concatenate([lhs_ref[x, :, lanes] for x, lanes in ends], axis=1),
        NT,
        preferred_element_type=F32,
    )
    total = total.T
    md_ref[...] = total[:owners] + total[owners:]
    core, my_chip = lax.axis_index("core"), lax.axis_index("chip")
    for other in range(2):
        for step in range(owners // 2):
            owner = 2 * (my_chip ^ step) + (core ^ other)
            table_ref[other, step, :EARLY, :] = early_ref[owner]
            table_ref[other, step, EARLY : EARLY + 1, :] = md_ref[pl.ds(owner, 1), :]


def swap(value, axis, step):
    count = lax.axis_size(axis)
    return lax.ppermute(value, axis, [(i, i ^ step) for i in range(count)])


def neighbours_of(low_edge, high_edge, axis, parity):
    count = lax.axis_size(axis)
    even = parity == 0
    inner = lax.ppermute(
        jnp.where(even, high_edge, low_edge), axis, [(i, i ^ 1) for i in range(count)]
    )
    outer = lax.ppermute(
        jnp.where(even, low_edge, high_edge),
        axis,
        [(i, (i + 1 if i & 1 else i - 1) % count) for i in range(count)],
    )
    return jnp.where(even, outer, inner), jnp.where(even, inner, outer)


def added(parts):
    while len(parts) > 1:
        parts = [sum(parts[k : k + 2][1:], parts[k]) for k in range(0, len(parts), 2)]
    return parts[0]


def to_owner(table):
    table = table[0] + swap(table[1], "core", 1)
    while table.shape[0] > 1:
        ways = min(4, table.shape[0])
        part = table.shape[0] // ways
        table = added(
            [table[:part]]
            + [swap(table[k * part : (k + 1) * part], "chip", k * part) for k in range(1, ways)]
        )
    return table[0]


def summed(value, axis):
    count = lax.axis_size(axis)
    if count & (count - 1):
        return lax.psum(value, axis)
    step = 1
    while step < count:
        ways = min(4, count // step)
        value = added([value] + [swap(value, axis, k * step) for k in range(1, ways)])
        step *= ways
    return value


def shards(positions, velocities, masses, smoothing, neighbours, particle_group, group_row):
    blocks_x, blocks_y, block_len = masses.shape
    dom_count, sub_count = lax.axis_size("dom"), lax.axis_size("chip") * lax.axis_size("core")
    owners = sub_count
    chunk = blocks_y * block_len
    shape = jax.ShapeDtypeStruct
    codes = neighbours.transpose(2, 0, 1)
    table_rows = group_row.reshape(-1, LANES)
    packed = jnp.concatenate([positions, masses[None]], axis=0)
    prev, following = neighbours_of(
        packed[:, 0], packed[:, blocks_x - 1], "dom", lax.axis_index("dom") & 1
    )
    sources = ((blocks_x + 2) * blocks_y, 8, LANES)
    columns, middle, own = pl.pallas_call(
        middle_kernel,
        out_shape=(
            shape((2, 4, blocks_x, LANES), F32),
            shape((blocks_x - 2, blocks_y, LANES), F32),
            shape(sources, F32),
        ),
        in_specs=[ANY] + [VMEM] * 5,
        out_specs=(VMEM,) * 3,
        scratch_shapes=pair_scratch(blocks_x, blocks_y, blocks_x - 2, codes.shape[0]),
        compiler_params=params(),
        cost_estimate=pl.CostEstimate(
            flops=4_000_000_000, bytes_accessed=400_000, transcendentals=1_300_000
        ),
        name="middle_pairs",
    )(codes, positions, masses, smoothing, particle_group, table_rows)
    early, rows, hot = pl.pallas_call(
        functools.partial(moments_kernel, blocks_x * dom_count, blocks_y * sub_count),
        out_shape=(
            shape((owners, EARLY, LANES), F32),
            shape(masses.shape, jnp.int32),
            shape((blocks_x, LANES, chunk), BF16),
        ),
        in_specs=[VMEM] * 6,
        out_specs=(VMEM,) * 3,
        scratch_shapes=[
            pltpu.VMEM((blocks_x * EARLY * blocks_y, LANES), F32),
            pltpu.VMEM((blocks_x, owners * 2 * EARLY, chunk), BF16),
            pltpu.VMEM((owners * 2 * EARLY, LANES), F32),
        ],
        compiler_params=params(),
        cost_estimate=pl.CostEstimate(
            flops=2_000_000_000, bytes_accessed=1_400_000, transcendentals=0
        ),
        name="moments_by_row",
    )(middle, positions, velocities, masses, particle_group, table_rows)
    edges = [
        jnp.concatenate([prev[:, y : y + 1], columns[side], following[:, y : y + 1]], axis=1)
        for side, y in ((0, 0), (1, blocks_y - 1))
    ]
    low, high = neighbours_of(*edges, ("chip", "core"), lax.axis_index("core"))
    edge, known = pl.pallas_call(
        edge_kernel,
        out_shape=(shape((2, blocks_y, LANES), F32), shape(sources, F32)),
        in_specs=[ANY] + [VMEM] * 6,
        out_specs=(VMEM,) * 2,
        scratch_shapes=pair_scratch(blocks_x, blocks_y, 2, codes.shape[0]),
        compiler_params=params(),
        cost_estimate=pl.CostEstimate(
            flops=4_000_000_000, bytes_accessed=400_000, transcendentals=1_300_000
        ),
        name="edge_pairs",
    )(codes, positions, masses, smoothing, prev, following, own)
    sums, table = pl.pallas_call(
        rim_kernel,
        out_shape=(shape(masses.shape, F32), shape((2, owners // 2, EARLY + 1, LANES), F32)),
        in_specs=[ANY] + [VMEM] * 11,
        out_specs=(VMEM, VMEM),
        scratch_shapes=[
            pltpu.SMEM(codes.shape, jnp.int32),
            pltpu.SemaphoreType.DMA(()),
            pltpu.VMEM((128, LANES), F32),
            pltpu.VMEM((6 * (blocks_x + 2), 8, LANES), F32),
            pltpu.VMEM((owners, LANES), F32),
            pltpu.VMEM((blocks_x, 2 * owners, chunk), BF16),
            pltpu.VMEM((LANES, 2 * owners), F32),
            pltpu.VMEM((9, 8, LANES), F32),
            pltpu.VMEM((blocks_x, 24 * blocks_y, LANES), F32),
        ]
        + product_scratch(2 * blocks_x, codes.shape[0]),
        compiler_params=params(),
        cost_estimate=pl.CostEstimate(
            flops=200_000_000, bytes_accessed=400_000, transcendentals=400_000
        ),
        name="rim_pairs_and_table",
    )(
        codes, middle, edge, known, positions, masses, smoothing, low, high, rows, hot, early
    )
    density = sums * DENSITY_FACTOR / (smoothing * smoothing * smoothing)
    return (density, summed(to_owner(table), "dom"))


def solution(mesh):
    dom_count, sub_count = mesh.devices.shape
    mesh = jax.sharding.Mesh(
        mesh.devices.reshape(dom_count, sub_count // 2, 2), ("dom", "chip", "core")
    )
    sub = ("chip", "core")
    in_specs = (
        P(None, "dom", sub, None),
        P(None, "dom", sub, None),
        P("dom", sub, None),
        P("dom", sub, None),
        P("dom", sub, None),
        P("dom", sub, None),
        P(),
    )
    out_specs = (P("dom", sub, None), P(None, sub))
    return jax.shard_map(shards, mesh=mesh, in_specs=in_specs, out_specs=out_specs, check_vma=False)
```

```python
import functools
import math

import jax
import jax.numpy as jnp
from jax import lax
from jax.experimental import pallas as pl
from jax.experimental.pallas import tpu as pltpu
from jax.sharding import PartitionSpec as P

F32 = jnp.float32
BF16 = jnp.bfloat16
LANES = 128
EARLY = 16
DENSITY_FACTOR = 21.0 / (16.0 * math.pi) / 256.0
VMEM = pl.BlockSpec(memory_space=pltpu.VMEM)
ANY = pl.BlockSpec(memory_space=pl.ANY)
NT = (((1,), (1,)), ((), ()))


def params():
    return pltpu.CompilerParams(vmem_limit_bytes=40 * 1024 * 1024)


def rounded(value):
    return value.astype(BF16).astype(F32)


def three_parts(value):
    first = rounded(value)
    rest = value - first
    second = rounded(rest)
    return first, second, rest - second


def spread(numbers, y, count):
    row = jnp.broadcast_to(numbers[y : y + 1, :].astype(F32), (16, LANES)).astype(BF16)
    return jnp.concatenate([row] * (count // 16), axis=0)


def row_numbers(count):
    return lax.broadcasted_iota(jnp.int32, (count, LANES), 0).astype(F32).astype(BF16)


def slot_one_hot(slots, y):
    return jnp.where(
        row_numbers(LANES) == spread(slots, y, LANES), jnp.ones((), BF16), jnp.zeros((), BF16)
    )


def moments_kernel(
    nx_total, ny_total, after_ref, pos_ref, vel_ref, mass_ref, group_ref, row_ref,
    table_ref, rows_ref, hot_ref, feat_ref, lhs_ref, total_ref,
):
    blocks_x, blocks_y, _ = mass_ref.shape
    owners = table_ref.shape[0]
    table_rows = row_ref.shape[0]
    base_x = (lax.axis_index("dom") * blocks_x).astype(F32)
    base_y = ((2 * lax.axis_index("chip") + lax.axis_index("core")) * blocks_y).astype(F32)
    y_iota = lax.broadcasted_iota(jnp.int32, (blocks_y, LANES), 0).astype(F32)

    def features_of(x):
        group = group_ref[x]
        low = group & (LANES - 1)
        high = group >> 7
        rows = jnp.zeros_like(group)
        for r in range(table_rows):
            line = jnp.broadcast_to(row_ref[r : r + 1, :], group.shape)
            picked = jnp.take_along_axis(line, low, axis=1)
            rows = jnp.where(high == r, picked, rows)
        rows_ref[x] = rows
        mass = mass_ref[x]
        gx = (base_x + float(x) + pos_ref[0, x]) / float(nx_total)
        gy = (base_y + y_iota + pos_ref[1, x]) / float(ny_total)
        gz = pos_ref[2, x]
        vx, vy, vz = vel_ref[0, x], vel_ref[1, x], vel_ref[2, x]
        mx, my, mz = mass * gx, mass * gy, mass * gz
        features = (
            mass, mx, my, mz, mass * vx, mass * vy, mass * vz,
            mass * (gy * vz - gz * vy), mass * (gz * vx - gx * vz), mass * (gx * vy - gy * vx),
            mx * gx, my * gy, mz * gz, mx * gy, mx * gz, my * gz,
        )
        for f, feature in enumerate(features):
            start = (x * EARLY + f) * blocks_y
            feat_ref[start : start + blocks_y, :] = feature

    def operands_of(x, y):
        lanes = slice(y * LANES, (y + 1) * LANES)
        feats = feat_ref[pl.ds(x * EARLY * blocks_y + y, EARLY, stride=blocks_y), :]
        high_part = rounded(feats)
        both = jnp.concatenate([high_part, feats - high_part], axis=0).astype(BF16)
        rows = rows_ref[x]
        owner_row = spread(rows >> 7, y, 2 * EARLY)
        for o in range(owners):
            lhs_ref[x, o * 2 * EARLY : (o + 1) * 2 * EARLY, lanes] = jnp.where(
                owner_row == jnp.asarray(o, BF16), both, jnp.zeros((), BF16)
            )
        hot_ref[x, :, lanes] = slot_one_hot(rows & (LANES - 1), y)

    def add_product(x):
        product = lax.dot_general(lhs_ref[x], hot_ref[x], NT, preferred_element_type=F32)
        total_ref[...] = product if x == 0 else total_ref[...] + product

    def finish():
        total = total_ref[...].reshape(owners, 2 * EARLY, LANES)
        table_ref[...] = total[:, :EARLY, :] + total[:, EARLY:, :]

    for x in range(blocks_x):
        features_of(x)
        for y in range(blocks_y):
            operands_of(x, y)
        add_product(x)
    finish()


def target_rows(pos, radius):
    weight = 4.0 / (radius * radius)
    cx, cy, cz = pos[0] - 0.5, pos[1] - 0.5, pos[2] - 0.5
    lines = (
        -2.0 * cx * weight, -2.0 * cy * weight, -2.0 * cz * weight,
        weight, weight, weight,
        (cx * cx + cy * cy + cz * cz) * weight, jnp.zeros_like(weight),
    )
    parts = [three_parts(line) for line in lines]
    return [part[k] for k in range(3) for part in parts]


def target_matrix(coef):
    one, two, three = coef[0:8], coef[8:16], coef[16:24]
    stacked = jnp.concatenate([one, one, two, two, one, three], axis=0)
    return stacked.T.astype(BF16)


def source_matrix(line, root, squares):
    value = jnp.where(squares, line * line, line) * (root * root)
    one, two, three = three_parts(value)
    first = jnp.concatenate([one, two], axis=0).astype(BF16)
    last = jnp.concatenate([three, one], axis=0).astype(BF16)
    return jnp.concatenate([first, first, last], axis=0)


def fifth_root(mass):
    root = jnp.exp(0.2 * jnp.log(mass))
    square = root * root
    return 0.8 * root + 0.2 * mass / (square * square)


def store_source(nat_ref, start, count, columns, mass):
    cx, cy, cz = [column - 0.5 for column in columns]
    one = jnp.ones_like(cx)
    for kind, line in enumerate((cx, cy, cz, cx, cy, cz, one, fifth_root(mass))):
        nat_ref[start + kind * 8 : start + kind * 8 + count, :] = line


def pair_sums(sides, pieces=(), add=False):
    rows = 32
    steps = []
    for target, sources, roots, total in sides:
        count = roots.shape[0]
        for first in range(0, count, 2):
            steps.append((target, sources, roots, total, first, min(2, count - first), count))

    def product(step):
        target, sources, _, _, first, width, _ = step
        right = sources[:, first * LANES : (first + width) * LANES]
        return jnp.dot(target[...], right, preferred_element_type=F32)

    ready = product(steps[0])
    chunks = None
    for number, (_, _, roots, total, first, width, count) in enumerate(steps):
        squared = ready
        if number + 1 < len(steps):
            ready = product(steps[number + 1])
        if first == 0:
            chunks = [None] * (LANES // rows)
            if add:
                chunks = [total[r * rows : (r + 1) * rows, :] for r in range(len(chunks))]
        limits = []
        for k in range(width):
            root = roots[first + k : first + k + 1, :]
            reach = 4.0 * root
            limits.append(
                [jnp.broadcast_to(line, (rows, LANES)) for line in (root, reach, reach * reach)]
            )
        for r in range(len(chunks)):
            for k, (root, reach, most) in enumerate(limits):
                t = squared[r * rows : (r + 1) * rows, k * LANES : (k + 1) * LANES]
                t = jnp.maximum(jnp.minimum(t, most), 1e-12)
                u = t * lax.rsqrt(t)
                f = reach - u
                f = f * f
                f = f * f
                term = f * (root + u)
                chunks[r] = term if chunks[r] is None else chunks[r] + term
        if first + width == count:
            for r, chunk in enumerate(chunks):
                total[r * rows : (r + 1) * rows, :] = chunk
        if number < len(pieces) and pieces[number] is not None:
            pieces[number]()
    for piece in pieces[len(steps) :]:
        piece()


def column_sums(totals):
    lane = lax.broadcasted_iota(jnp.int32, (LANES, LANES), 1)
    columns = jnp.zeros((LANES, LANES), F32)
    for k, total in enumerate(totals):
        columns = jnp.where(lane == k, jnp.sum(total, axis=1, keepdims=True), columns)
    return columns.T[: len(totals), :]


def square_mask():
    kind = lax.broadcasted_iota(jnp.int32, (8, LANES), 0)
    return (kind >= 3) & (kind < 6)


def shift_rows(step_x, step_y):
    kind = lax.broadcasted_iota(jnp.int32, (8, LANES), 0)
    along_x = jnp.where((kind == 0) | (kind == 3), float(step_x), 0.0)
    return along_x + jnp.where((kind == 1) | (kind == 4), float(step_y), 0.0)


def put_shifts(shift_ref):
    for code in range(9):
        shift_ref[code] = shift_rows(code // 3 - 1, code % 3 - 1)


def put_source(near_ref, root_ref, number, k, line, shift, squares):
    root = jnp.broadcast_to(line[7:8], line.shape)
    near_ref[number, :, k * LANES : (k + 1) * LANES] = source_matrix(line + shift, root, squares)
    root_ref[number, k : k + 1, :] = root[0:1]


def sides_of(count, first, end, mat_ref, near_ref, root_ref, total_ref):
    lanes, rows = pl.ds(first * LANES, (end - first) * LANES), pl.ds(first, end - first)
    return [
        (mat_ref.at[n], near_ref.at[n, :, lanes], root_ref.at[n, rows], total_ref.at[n])
        for n in range(count)
    ]


def load_codes(far_ref, code_ref, sem):
    copy = pltpu.make_async_copy(far_ref, code_ref, sem)
    copy.start()
    return copy


def block_pairs(
    x_first, x_step, x_count, known_ref, far_code_ref, pos_ref, mass_ref, smooth_ref, prev_ref, next_ref,
    out_ref, src_ref, code_ref, sem, nat_ref, shift_ref, tgt_ref, mat_ref, near_ref, root_ref, total_ref,
):
    blocks_x, blocks_y, _ = mass_ref.shape
    listed = code_ref.shape[0]
    codes = load_codes(far_code_ref, code_ref, sem)
    for xe in range(blocks_x + 2):
        if xe == 0 or xe == blocks_x + 1:
            ref = prev_ref if xe == 0 else next_ref
            if ref is None:
                continue
            store_source(nat_ref, xe * 64, blocks_y, [ref[c] for c in range(3)], ref[3])
        elif known_ref is None:
            columns = [pos_ref[c, xe - 1] for c in range(3)]
            store_source(nat_ref, xe * 64, blocks_y, columns, mass_ref[xe - 1])
        else:
            part = pl.ds(xe * blocks_y, blocks_y)
            src_ref[part] = known_ref[part]
            continue
        for y in range(blocks_y):
            src_ref[xe * blocks_y + y] = nat_ref[pl.ds(xe * 64 + y, 8, stride=8), :]
    put_shifts(shift_ref)
    squares = square_mask()
    blocks = [(turn, y) for turn in range(x_count) for y in range(1, blocks_y - 1)]
    for turn in range(x_count):
        x = x_first + turn * x_step
        lines = target_rows([pos_ref[c, x] for c in range(3)], smooth_ref[x])
        for row, line in enumerate(lines):
            tgt_ref[turn, row * blocks_y : (row + 1) * blocks_y, :] = line
    for number, (turn, y) in enumerate(blocks):
        mat_ref[number] = target_matrix(tgt_ref[turn, pl.ds(y, 24, stride=blocks_y), :])
    for number, (turn, y) in enumerate(blocks):
        line = src_ref[(x_first + turn * x_step + 1) * blocks_y + y]
        put_source(near_ref, root_ref, number, 0, line, 0.0, squares)
    pair_sums(sides_of(len(blocks), 0, 1, mat_ref, near_ref, root_ref, total_ref))
    codes.wait()
    for number, (turn, y) in enumerate(blocks):
        x = x_first + turn * x_step
        for k in range(1, listed):
            code = code_ref[k, x, y]
            step_x = (code * 11) >> 5
            line = src_ref[(x + step_x) * blocks_y + y + code - 3 * step_x - 1]
            put_source(near_ref, root_ref, number, k, line, shift_ref[code], squares)
    inner = blocks_y - 2
    per_row = inner * (listed // 2)

    def row_sums(turn):
        sums = column_sums([total_ref[turn * inner + k] for k in range(inner)])
        out_ref[turn, 1 : blocks_y - 1, :] = sums

    pieces = [None] * (x_count * per_row + 1)
    for turn in range(x_count):
        pieces[(turn + 1) * per_row] = functools.partial(row_sums, turn)
    sides = sides_of(len(blocks), 1, listed, mat_ref, near_ref, root_ref, total_ref)
    pair_sums(sides, pieces, add=True)


def middle_kernel(
    code_ref, pos_ref, mass_ref, smooth_ref, group_ref, row_ref, column_ref, out_ref, src_ref, *scratch
):
    blocks_x, blocks_y, _ = mass_ref.shape
    for side in range(2):
        y = side * (blocks_y - 1)
        for x in range(blocks_x):
            for c in range(3):
                column_ref[side, c, x : x + 1, :] = pos_ref[c, x, y : y + 1, :]
            column_ref[side, 3, x : x + 1, :] = mass_ref[x, y : y + 1, :]
    block_pairs(
        1, 1, blocks_x - 2, None, code_ref, pos_ref, mass_ref, smooth_ref, None, None,
        out_ref, src_ref, *scratch,
    )


def edge_kernel(
    code_ref, pos_ref, mass_ref, smooth_ref, prev_ref, next_ref, known_ref, out_ref, src_ref, *scratch
):
    blocks_x = mass_ref.shape[0]
    block_pairs(
        0, blocks_x - 1, 2, known_ref, code_ref, pos_ref, mass_ref, smooth_ref, prev_ref, next_ref,
        out_ref, src_ref, *scratch,
    )


def pair_scratch(blocks_x, blocks_y, x_count, listed):
    return [
        pltpu.SMEM((listed, blocks_x, blocks_y), jnp.int32),
        pltpu.SemaphoreType.DMA(()),
        pltpu.VMEM(((blocks_x + 2) * 64, LANES), F32),
        pltpu.VMEM((9, 8, LANES), F32),
        pltpu.VMEM((x_count, 24 * blocks_y, LANES), F32),
    ] + product_scratch(x_count * (blocks_y - 2), listed)


def product_scratch(blocks, listed):
    return [
        pltpu.VMEM((blocks, LANES, 48), BF16),
        pltpu.VMEM((blocks, 48, listed * LANES), BF16),
        pltpu.VMEM((blocks, 8, LANES), F32),
        pltpu.VMEM((blocks, LANES, LANES), F32),
    ]


def rim_kernel(
    far_code_ref, middle_ref, edge_ref, known_ref, pos_ref, mass_ref, smooth_ref,
    low_ref, high_ref, rows_ref, hot_ref, early_ref,
    sum_ref, table_ref, code_ref, sem, nat_ref, src_ref, md_ref, lhs_ref, row_sum_ref,
    shift_ref, tgt_ref, mat_ref, near_ref, root_ref, total_ref,
):
    blocks_x, blocks_y, _ = mass_ref.shape
    owners = early_ref.shape[0]
    listed = code_ref.shape[0]
    wide = blocks_x + 2
    codes = load_codes(far_code_ref, code_ref, sem)
    for side, ref in enumerate((low_ref, high_ref)):
        store_source(nat_ref, side * 64, wide, [ref[c] for c in range(3)], ref[3])
        for xe in range(wide):
            ghost = 5 * side * wide + xe
            src_ref[ghost] = nat_ref[pl.ds(side * 64 + xe, 8, stride=8), :]
            for k in range(2):
                y = k + side * (blocks_y - 2)
                place = (1 + k + 2 * side) * wide + xe
                src_ref[place] = known_ref[xe * blocks_y + y]
    put_shifts(shift_ref)
    squares = square_mask()
    for x in range(blocks_x):
        edge = x == 0 or x == blocks_x - 1
        turn = (1 if x else 0) if edge else x - 1
        sum_ref[x] = (edge_ref if edge else middle_ref)[turn]
        lines = target_rows([pos_ref[c, x] for c in range(3)], smooth_ref[x])
        for row, line in enumerate(lines):
            tgt_ref[x, row * blocks_y : (row + 1) * blocks_y, :] = line
    for x in range(blocks_x):
        for side in range(2):
            y = side * (blocks_y - 1)
            mat_ref[2 * x + side] = target_matrix(tgt_ref[x, pl.ds(y, 24, stride=blocks_y), :])
    for x in range(blocks_x):
        for side in range(2):
            line = src_ref[(3 * side + 1) * wide + x + 1]
            put_source(near_ref, root_ref, 2 * x + side, 0, line, 0.0, squares)

    owner_ids = lax.broadcasted_iota(jnp.int32, (owners, LANES), 0)
    last = blocks_y - 1

    def put_moments(x, ys):
        radius = smooth_ref[x]
        moment = mass_ref[x] * (sum_ref[x] * DENSITY_FACTOR / (radius * radius * radius))
        high_part = rounded(moment)
        low_part = moment - high_part
        owner = rows_ref[x] >> 7
        for y in ys:
            mine = jnp.broadcast_to(owner[y : y + 1, :], owner_ids.shape) == owner_ids
            lhs_ref[x, :, y * LANES : (y + 1) * LANES] = jnp.concatenate(
                [
                    jnp.where(mine, jnp.broadcast_to(part[y : y + 1, :], mine.shape), 0.0)
                    for part in (high_part, low_part)
                ],
                axis=0,
            ).astype(BF16)

    def inner_moments(x):
        put_moments(x, range(1, last))
        lanes = slice(LANES, last * LANES)
        product = lax.dot_general(
            hot_ref[x, :, lanes], lhs_ref[x, :, lanes], NT, preferred_element_type=F32
        )
        row_sum_ref[...] = product if x == 0 else row_sum_ref[...] + product

    products = (mat_ref, near_ref, root_ref, total_ref)
    pair_sums(
        sides_of(2 * blocks_x, 0, 1, *products),
        [functools.partial(inner_moments, x) for x in range(blocks_x)],
    )
    codes.wait()
    for x in range(blocks_x):
        for side in range(2):
            for k in range(1, listed):
                code = code_ref[k, x, side * last]
                step_x = (code * 11) >> 5
                line = src_ref[(3 * side + code - 3 * step_x) * wide + x + step_x]
                put_source(near_ref, root_ref, 2 * x + side, k, line, shift_ref[code], squares)
    pair_sums(sides_of(2 * blocks_x, 1, listed, *products), add=True)
    sums = column_sums([total_ref[number] for number in range(2 * blocks_x)])
    for x in range(blocks_x):
        for side in range(2):
            y = side * last
            sum_ref[x, y : y + 1, :] = sums[2 * x + side : 2 * x + side + 1, :]
        put_moments(x, (0, last))
    ends = [(x, slice(y * LANES, (y + 1) * LANES)) for x in range(blocks_x) for y in (0, last)]
    total = row_sum_ref[...] + lax.dot_general(
        jnp.concatenate([hot_ref[x, :, lanes] for x, lanes in ends], axis=1),
        jnp.concatenate([lhs_ref[x, :, lanes] for x, lanes in ends], axis=1),
        NT,
        preferred_element_type=F32,
    )
    total = total.T
    md_ref[...] = total[:owners] + total[owners:]
    core, my_chip = lax.axis_index("core"), lax.axis_index("chip")
    for other in range(2):
        for step in range(owners // 2):
            owner = 2 * (my_chip ^ step) + (core ^ other)
            table_ref[other, step, :EARLY, :] = early_ref[owner]
            table_ref[other, step, EARLY : EARLY + 1, :] = md_ref[pl.ds(owner, 1), :]


def swap(value, axis, step):
    count = lax.axis_size(axis)
    return lax.ppermute(value, axis, [(i, i ^ step) for i in range(count)])


def neighbours_of(low_edge, high_edge, axis, parity):
    count = lax.axis_size(axis)
    even = parity == 0
    inner = lax.ppermute(
        jnp.where(even, high_edge, low_edge), axis, [(i, i ^ 1) for i in range(count)]
    )
    outer = lax.ppermute(
        jnp.where(even, low_edge, high_edge),
        axis,
        [(i, (i + 1 if i & 1 else i - 1) % count) for i in range(count)],
    )
    return jnp.where(even, outer, inner), jnp.where(even, inner, outer)


def added(parts):
    while len(parts) > 1:
        parts = [sum(parts[k : k + 2][1:], parts[k]) for k in range(0, len(parts), 2)]
    return parts[0]


def to_owner(table):
    table = table[0] + swap(table[1], "core", 1)
    while table.shape[0] > 1:
        ways = min(4, table.shape[0])
        part = table.shape[0] // ways
        table = added(
            [table[:part]]
            + [swap(table[k * part : (k + 1) * part], "chip", k * part) for k in range(1, ways)]
        )
    return table[0]


def summed(value, axis):
    count = lax.axis_size(axis)
    if count & (count - 1):
        return lax.psum(value, axis)
    step = 1
    while step < count:
        ways = min(4, count // step)
        value = added([value] + [swap(value, axis, k * step) for k in range(1, ways)])
        step *= ways
    return value


def shards(positions, velocities, masses, smoothing, neighbours, particle_group, group_row):
    blocks_x, blocks_y, block_len = masses.shape
    dom_count, sub_count = lax.axis_size("dom"), lax.axis_size("chip") * lax.axis_size("core")
    owners = sub_count
    chunk = blocks_y * block_len
    shape = jax.ShapeDtypeStruct
    codes = neighbours.transpose(2, 0, 1)
    table_rows = group_row.reshape(-1, LANES)
    packed = jnp.concatenate([positions, masses[None]], axis=0)
    prev, following = neighbours_of(
        packed[:, 0], packed[:, blocks_x - 1], "dom", lax.axis_index("dom") & 1
    )
    sources = ((blocks_x + 2) * blocks_y, 8, LANES)
    columns, middle, own = pl.pallas_call(
        middle_kernel,
        out_shape=(
            shape((2, 4, blocks_x, LANES), F32),
            shape((blocks_x - 2, blocks_y, LANES), F32),
            shape(sources, F32),
        ),
        in_specs=[ANY] + [VMEM] * 5,
        out_specs=(VMEM,) * 3,
        scratch_shapes=pair_scratch(blocks_x, blocks_y, blocks_x - 2, codes.shape[0]),
        compiler_params=params(),
        cost_estimate=pl.CostEstimate(
            flops=4_000_000_000, bytes_accessed=400_000, transcendentals=1_300_000
        ),
        name="middle_pairs",
    )(codes, positions, masses, smoothing, particle_group, table_rows)
    early, rows, hot = pl.pallas_call(
        functools.partial(moments_kernel, blocks_x * dom_count, blocks_y * sub_count),
        out_shape=(
            shape((owners, EARLY, LANES), F32),
            shape(masses.shape, jnp.int32),
            shape((blocks_x, LANES, chunk), BF16),
        ),
        in_specs=[VMEM] * 6,
        out_specs=(VMEM,) * 3,
        scratch_shapes=[
            pltpu.VMEM((blocks_x * EARLY * blocks_y, LANES), F32),
            pltpu.VMEM((blocks_x, owners * 2 * EARLY, chunk), BF16),
            pltpu.VMEM((owners * 2 * EARLY, LANES), F32),
        ],
        compiler_params=params(),
        cost_estimate=pl.CostEstimate(
            flops=2_000_000_000, bytes_accessed=1_400_000, transcendentals=0
        ),
        name="moments_by_row",
    )(middle, positions, velocities, masses, particle_group, table_rows)
    edges = [
        jnp.concatenate([prev[:, y : y + 1], columns[side], following[:, y : y + 1]], axis=1)
        for side, y in ((0, 0), (1, blocks_y - 1))
    ]
    low, high = neighbours_of(*edges, ("chip", "core"), lax.axis_index("core"))
    edge, known = pl.pallas_call(
        edge_kernel,
        out_shape=(shape((2, blocks_y, LANES), F32), shape(sources, F32)),
        in_specs=[ANY] + [VMEM] * 6,
        out_specs=(VMEM,) * 2,
        scratch_shapes=pair_scratch(blocks_x, blocks_y, 2, codes.shape[0]),
        compiler_params=params(),
        cost_estimate=pl.CostEstimate(
            flops=4_000_000_000, bytes_accessed=400_000, transcendentals=1_300_000
        ),
        name="edge_pairs",
    )(codes, positions, masses, smoothing, prev, following, own)
    sums, table = pl.pallas_call(
        rim_kernel,
        out_shape=(shape(masses.shape, F32), shape((2, owners // 2, EARLY + 1, LANES), F32)),
        in_specs=[ANY] + [VMEM] * 11,
        out_specs=(VMEM, VMEM),
        scratch_shapes=[
            pltpu.SMEM(codes.shape, jnp.int32),
            pltpu.SemaphoreType.DMA(()),
            pltpu.VMEM((128, LANES), F32),
            pltpu.VMEM((6 * (blocks_x + 2), 8, LANES), F32),
            pltpu.VMEM((owners, LANES), F32),
            pltpu.VMEM((blocks_x, 2 * owners, chunk), BF16),
            pltpu.VMEM((LANES, 2 * owners), F32),
            pltpu.VMEM((9, 8, LANES), F32),
            pltpu.VMEM((blocks_x, 24 * blocks_y, LANES), F32),
        ]
        + product_scratch(2 * blocks_x, codes.shape[0]),
        compiler_params=params(),
        cost_estimate=pl.CostEstimate(
            flops=200_000_000, bytes_accessed=400_000, transcendentals=400_000
        ),
        name="rim_pairs_and_table",
    )(
        codes, middle, edge, known, positions, masses, smoothing, low, high, rows, hot, early
    )
    density = sums * DENSITY_FACTOR / (smoothing * smoothing * smoothing)
    return (density, summed(to_owner(table), "dom"))


def solution(mesh):
    dom_count, sub_count = mesh.devices.shape
    mesh = jax.sharding.Mesh(
        mesh.devices.reshape(dom_count, sub_count // 2, 2), ("dom", "chip", "core")
    )
    sub = ("chip", "core")
    in_specs = (
        P(None, "dom", sub, None),
        P(None, "dom", sub, None),
        P("dom", sub, None),
        P("dom", sub, None),
        P("dom", sub, None),
        P("dom", sub, None),
        P(),
    )
    out_specs = (P("dom", sub, None), P(None, sub))
    return jax.shard_map(shards, mesh=mesh, in_specs=in_specs, out_specs=out_specs, check_vma=False)
```

```python
import functools
import math

import jax
import jax.numpy as jnp
from jax import lax
from jax.experimental import pallas as pl
from jax.experimental.pallas import tpu as pltpu
from jax.sharding import PartitionSpec as P

F32 = jnp.float32
BF16 = jnp.bfloat16
LANES = 128
EARLY = 16
DENSITY_FACTOR = 21.0 / (16.0 * math.pi) / 256.0
VMEM = pl.BlockSpec(memory_space=pltpu.VMEM)
ANY = pl.BlockSpec(memory_space=pl.ANY)
NT = (((1,), (1,)), ((), ()))


def params():
    return pltpu.CompilerParams(vmem_limit_bytes=40 * 1024 * 1024)


def rounded(value):
    return value.astype(BF16).astype(F32)


def three_parts(value):
    first = rounded(value)
    rest = value - first
    second = rounded(rest)
    return first, second, rest - second


def spread(numbers, y, count):
    row = jnp.broadcast_to(numbers[y : y + 1, :].astype(F32), (16, LANES)).astype(BF16)
    return jnp.concatenate([row] * (count // 16), axis=0)


def row_numbers(count):
    return lax.broadcasted_iota(jnp.int32, (count, LANES), 0).astype(F32).astype(BF16)


def slot_one_hot(slots, y):
    return jnp.where(
        row_numbers(LANES) == spread(slots, y, LANES), jnp.ones((), BF16), jnp.zeros((), BF16)
    )


def moments_kernel(
    nx_total, ny_total, after_ref, pos_ref, vel_ref, mass_ref, group_ref, row_ref,
    table_ref, rows_ref, hot_ref, feat_ref, lhs_ref, total_ref,
):
    blocks_x, blocks_y, _ = mass_ref.shape
    owners = table_ref.shape[0]
    table_rows = row_ref.shape[0]
    base_x = (lax.axis_index("dom") * blocks_x).astype(F32)
    base_y = ((2 * lax.axis_index("chip") + lax.axis_index("core")) * blocks_y).astype(F32)
    y_iota = lax.broadcasted_iota(jnp.int32, (blocks_y, LANES), 0).astype(F32)

    def features_of(x):
        group = group_ref[x]
        low = group & (LANES - 1)
        high = group >> 7
        rows = jnp.zeros_like(group)
        for r in range(table_rows):
            line = jnp.broadcast_to(row_ref[r : r + 1, :], group.shape)
            picked = jnp.take_along_axis(line, low, axis=1)
            rows = jnp.where(high == r, picked, rows)
        rows_ref[x] = rows
        mass = mass_ref[x]
        gx = (base_x + float(x) + pos_ref[0, x]) / float(nx_total)
        gy = (base_y + y_iota + pos_ref[1, x]) / float(ny_total)
        gz = pos_ref[2, x]
        vx, vy, vz = vel_ref[0, x], vel_ref[1, x], vel_ref[2, x]
        mx, my, mz = mass * gx, mass * gy, mass * gz
        features = (
            mass, mx, my, mz, mass * vx, mass * vy, mass * vz,
            mass * (gy * vz - gz * vy), mass * (gz * vx - gx * vz), mass * (gx * vy - gy * vx),
            mx * gx, my * gy, mz * gz, mx * gy, mx * gz, my * gz,
        )
        for f, feature in enumerate(features):
            start = (x * EARLY + f) * blocks_y
            feat_ref[start : start + blocks_y, :] = feature

    def operands_of(x, y):
        lanes = slice(y * LANES, (y + 1) * LANES)
        feats = feat_ref[pl.ds(x * EARLY * blocks_y + y, EARLY, stride=blocks_y), :]
        high_part = rounded(feats)
        both = jnp.concatenate([high_part, feats - high_part], axis=0).astype(BF16)
        rows = rows_ref[x]
        owner_row = spread(rows >> 7, y, 2 * EARLY)
        for o in range(owners):
            lhs_ref[x, o * 2 * EARLY : (o + 1) * 2 * EARLY, lanes] = jnp.where(
                owner_row == jnp.asarray(o, BF16), both, jnp.zeros((), BF16)
            )
        hot_ref[x, :, lanes] = slot_one_hot(rows & (LANES - 1), y)

    def add_product(x):
        product = lax.dot_general(lhs_ref[x], hot_ref[x], NT, preferred_element_type=F32)
        total_ref[...] = product if x == 0 else total_ref[...] + product

    def finish():
        total = total_ref[...].reshape(owners, 2 * EARLY, LANES)
        table_ref[...] = total[:, :EARLY, :] + total[:, EARLY:, :]

    for x in range(blocks_x):
        features_of(x)
        for y in range(blocks_y):
            operands_of(x, y)
        add_product(x)
    finish()


def target_rows(pos, radius):
    weight = 4.0 / (radius * radius)
    cx, cy, cz = pos[0] - 0.5, pos[1] - 0.5, pos[2] - 0.5
    lines = (
        -2.0 * cx * weight, -2.0 * cy * weight, -2.0 * cz * weight,
        weight, weight, weight,
        (cx * cx + cy * cy + cz * cz) * weight, jnp.zeros_like(weight),
    )
    parts = [three_parts(line) for line in lines]
    return [part[k] for k in range(3) for part in parts]


def target_matrix(coef):
    one, two, three = coef[0:8], coef[8:16], coef[16:24]
    stacked = jnp.concatenate([one, one, two, two, one, three], axis=0)
    return stacked.T.astype(BF16)


def source_matrix(line, root, squares):
    value = jnp.where(squares, line * line, line) * (root * root)
    one, two, three = three_parts(value)
    first = jnp.concatenate([one, two], axis=0).astype(BF16)
    last = jnp.concatenate([three, one], axis=0).astype(BF16)
    return jnp.concatenate([first, first, last], axis=0)


def fifth_root(mass):
    root = jnp.exp(0.2 * jnp.log(mass))
    square = root * root
    return 0.8 * root + 0.2 * mass / (square * square)


def store_source(nat_ref, start, count, columns, mass):
    cx, cy, cz = [column - 0.5 for column in columns]
    one = jnp.ones_like(cx)
    for kind, line in enumerate((cx, cy, cz, cx, cy, cz, one, fifth_root(mass))):
        nat_ref[start + kind * 8 : start + kind * 8 + count, :] = line


def pair_sums(sides, pieces=(), add=False):
    rows = 32
    steps = []
    for target, sources, roots, total in sides:
        count = roots.shape[0]
        for first in range(0, count, 2):
            steps.append((target, sources, roots, total, first, min(2, count - first), count))

    def product(step):
        target, sources, _, _, first, width, _ = step
        right = sources[:, first * LANES : (first + width) * LANES]
        return jnp.dot(target[...], right, preferred_element_type=F32)

    ready = product(steps[0])
    chunks = None
    for number, (_, _, roots, total, first, width, count) in enumerate(steps):
        squared = ready
        if number + 1 < len(steps):
            ready = product(steps[number + 1])
        if first == 0:
            chunks = [None] * (LANES // rows)
            if add:
                chunks = [total[r * rows : (r + 1) * rows, :] for r in range(len(chunks))]
        limits = []
        for k in range(width):
            root = roots[first + k : first + k + 1, :]
            reach = 4.0 * root
            limits.append(
                [jnp.broadcast_to(line, (rows, LANES)) for line in (root, reach, reach * reach)]
            )
        for r in range(len(chunks)):
            for k, (root, reach, most) in enumerate(limits):
                t = squared[r * rows : (r + 1) * rows, k * LANES : (k + 1) * LANES]
                t = jnp.maximum(jnp.minimum(t, most), 1e-12)
                u = t * lax.rsqrt(t)
                f = reach - u
                f = f * f
                f = f * f
                term = f * (root + u)
                chunks[r] = term if chunks[r] is None else chunks[r] + term
        if first + width == count:
            for r, chunk in enumerate(chunks):
                total[r * rows : (r + 1) * rows, :] = chunk
        if number < len(pieces) and pieces[number] is not None:
            pieces[number]()
    for piece in pieces[len(steps) :]:
        piece()


def column_sums(totals):
    lane = lax.broadcasted_iota(jnp.int32, (LANES, LANES), 1)
    columns = jnp.zeros((LANES, LANES), F32)
    for k, total in enumerate(totals):
        columns = jnp.where(lane == k, jnp.sum(total, axis=1, keepdims=True), columns)
    return columns.T[: len(totals), :]


def square_mask():
    kind = lax.broadcasted_iota(jnp.int32, (8, LANES), 0)
    return (kind >= 3) & (kind < 6)


def shift_rows(step_x, step_y):
    kind = lax.broadcasted_iota(jnp.int32, (8, LANES), 0)
    along_x = jnp.where((kind == 0) | (kind == 3), float(step_x), 0.0)
    return along_x + jnp.where((kind == 1) | (kind == 4), float(step_y), 0.0)


def put_shifts(shift_ref):
    for code in range(9):
        shift_ref[code] = shift_rows(code // 3 - 1, code % 3 - 1)


def put_source(near_ref, root_ref, number, k, line, shift, squares):
    root = jnp.broadcast_to(line[7:8], line.shape)
    near_ref[number, :, k * LANES : (k + 1) * LANES] = source_matrix(line + shift, root, squares)
    root_ref[number, k : k + 1, :] = root[0:1]


def sides_of(count, first, end, mat_ref, near_ref, root_ref, total_ref):
    lanes, rows = pl.ds(first * LANES, (end - first) * LANES), pl.ds(first, end - first)
    return [
        (mat_ref.at[n], near_ref.at[n, :, lanes], root_ref.at[n, rows], total_ref.at[n])
        for n in range(count)
    ]


def load_codes(far_ref, code_ref, sem):
    copy = pltpu.make_async_copy(far_ref, code_ref, sem)
    copy.start()
    return copy


def block_pairs(
    listed, x_first, x_step, x_count, known_ref, far_code_ref, pos_ref, mass_ref, smooth_ref, prev_ref, next_ref,
    out_ref, src_ref, code_ref, sem, nat_ref, shift_ref, tgt_ref, mat_ref, near_ref, root_ref, total_ref,
):
    blocks_x, blocks_y, _ = mass_ref.shape
    codes = load_codes(far_code_ref, code_ref, sem)
    for xe in range(blocks_x + 2):
        if xe == 0 or xe == blocks_x + 1:
            ref = prev_ref if xe == 0 else next_ref
            if ref is None:
                continue
            store_source(nat_ref, xe * 64, blocks_y, [ref[c] for c in range(3)], ref[3])
        elif known_ref is None:
            columns = [pos_ref[c, xe - 1] for c in range(3)]
            store_source(nat_ref, xe * 64, blocks_y, columns, mass_ref[xe - 1])
        else:
            part = pl.ds(xe * blocks_y, blocks_y)
            src_ref[part] = known_ref[part]
            continue
        for y in range(blocks_y):
            src_ref[xe * blocks_y + y] = nat_ref[pl.ds(xe * 64 + y, 8, stride=8), :]
    put_shifts(shift_ref)
    squares = square_mask()
    blocks = [(turn, y) for turn in range(x_count) for y in range(1, blocks_y - 1)]
    for turn in range(x_count):
        x = x_first + turn * x_step
        lines = target_rows([pos_ref[c, x] for c in range(3)], smooth_ref[x])
        for row, line in enumerate(lines):
            tgt_ref[turn, row * blocks_y : (row + 1) * blocks_y, :] = line
    for number, (turn, y) in enumerate(blocks):
        mat_ref[number] = target_matrix(tgt_ref[turn, pl.ds(y, 24, stride=blocks_y), :])
    for number, (turn, y) in enumerate(blocks):
        line = src_ref[(x_first + turn * x_step + 1) * blocks_y + y]
        put_source(near_ref, root_ref, number, 0, line, 0.0, squares)
    pair_sums(sides_of(len(blocks), 0, 1, mat_ref, near_ref, root_ref, total_ref))
    codes.wait()
    for number, (turn, y) in enumerate(blocks):
        x = x_first + turn * x_step
        word = code_ref[x * blocks_y + y]
        for k in range(1, listed):
            code = (word >> (4 * k)) & 15
            step_x = (code * 11) >> 5
            line = src_ref[(x + step_x) * blocks_y + y + code - 3 * step_x - 1]
            put_source(near_ref, root_ref, number, k, line, shift_ref[code], squares)
    inner = blocks_y - 2
    per_row = inner * (listed // 2)

    def row_sums(turn):
        sums = column_sums([total_ref[turn * inner + k] for k in range(inner)])
        out_ref[turn, 1 : blocks_y - 1, :] = sums

    pieces = [None] * (x_count * per_row + 1)
    for turn in range(x_count):
        pieces[(turn + 1) * per_row] = functools.partial(row_sums, turn)
    sides = sides_of(len(blocks), 1, listed, mat_ref, near_ref, root_ref, total_ref)
    pair_sums(sides, pieces, add=True)


def middle_kernel(
    listed, code_ref, pos_ref, mass_ref, smooth_ref, group_ref, row_ref, column_ref, out_ref, src_ref, *scratch
):
    blocks_x, blocks_y, _ = mass_ref.shape
    for side in range(2):
        y = side * (blocks_y - 1)
        for x in range(blocks_x):
            for c in range(3):
                column_ref[side, c, x : x + 1, :] = pos_ref[c, x, y : y + 1, :]
            column_ref[side, 3, x : x + 1, :] = mass_ref[x, y : y + 1, :]
    block_pairs(
        listed, 1, 1, blocks_x - 2, None, code_ref, pos_ref, mass_ref, smooth_ref, None, None,
        out_ref, src_ref, *scratch,
    )


def edge_kernel(
    listed, code_ref, pos_ref, mass_ref, smooth_ref, prev_ref, next_ref, known_ref, out_ref, src_ref, *scratch
):
    blocks_x = mass_ref.shape[0]
    block_pairs(
        listed, 0, blocks_x - 1, 2, known_ref, code_ref, pos_ref, mass_ref, smooth_ref, prev_ref, next_ref,
        out_ref, src_ref, *scratch,
    )


def pair_scratch(blocks_x, blocks_y, x_count, listed):
    return [
        pltpu.SMEM((blocks_x * blocks_y,), jnp.int32),
        pltpu.SemaphoreType.DMA(()),
        pltpu.VMEM(((blocks_x + 2) * 64, LANES), F32),
        pltpu.VMEM((9, 8, LANES), F32),
        pltpu.VMEM((x_count, 24 * blocks_y, LANES), F32),
    ] + product_scratch(x_count * (blocks_y - 2), listed)


def product_scratch(blocks, listed):
    return [
        pltpu.VMEM((blocks, LANES, 48), BF16),
        pltpu.VMEM((blocks, 48, listed * LANES), BF16),
        pltpu.VMEM((blocks, 8, LANES), F32),
        pltpu.VMEM((blocks, LANES, LANES), F32),
    ]


def rim_kernel(
    listed, far_code_ref, middle_ref, edge_ref, known_ref, pos_ref, mass_ref, smooth_ref,
    low_ref, high_ref, rows_ref, hot_ref, early_ref,
    sum_ref, table_ref, code_ref, sem, nat_ref, src_ref, md_ref, lhs_ref, row_sum_ref,
    shift_ref, tgt_ref, mat_ref, near_ref, root_ref, total_ref,
):
    blocks_x, blocks_y, _ = mass_ref.shape
    owners = early_ref.shape[0]
    wide = blocks_x + 2
    codes = load_codes(far_code_ref, code_ref, sem)
    for side, ref in enumerate((low_ref, high_ref)):
        store_source(nat_ref, side * 64, wide, [ref[c] for c in range(3)], ref[3])
        for xe in range(wide):
            ghost = 5 * side * wide + xe
            src_ref[ghost] = nat_ref[pl.ds(side * 64 + xe, 8, stride=8), :]
            for k in range(2):
                y = k + side * (blocks_y - 2)
                place = (1 + k + 2 * side) * wide + xe
                src_ref[place] = known_ref[xe * blocks_y + y]
    put_shifts(shift_ref)
    squares = square_mask()
    for x in range(blocks_x):
        edge = x == 0 or x == blocks_x - 1
        turn = (1 if x else 0) if edge else x - 1
        sum_ref[x] = (edge_ref if edge else middle_ref)[turn]
        lines = target_rows([pos_ref[c, x] for c in range(3)], smooth_ref[x])
        for row, line in enumerate(lines):
            tgt_ref[x, row * blocks_y : (row + 1) * blocks_y, :] = line
    for x in range(blocks_x):
        for side in range(2):
            y = side * (blocks_y - 1)
            mat_ref[2 * x + side] = target_matrix(tgt_ref[x, pl.ds(y, 24, stride=blocks_y), :])
    for x in range(blocks_x):
        for side in range(2):
            line = src_ref[(3 * side + 1) * wide + x + 1]
            put_source(near_ref, root_ref, 2 * x + side, 0, line, 0.0, squares)

    owner_ids = lax.broadcasted_iota(jnp.int32, (owners, LANES), 0)
    last = blocks_y - 1

    def put_moments(x, ys):
        radius = smooth_ref[x]
        moment = mass_ref[x] * (sum_ref[x] * DENSITY_FACTOR / (radius * radius * radius))
        high_part = rounded(moment)
        low_part = moment - high_part
        owner = rows_ref[x] >> 7
        for y in ys:
            mine = jnp.broadcast_to(owner[y : y + 1, :], owner_ids.shape) == owner_ids
            lhs_ref[x, :, y * LANES : (y + 1) * LANES] = jnp.concatenate(
                [
                    jnp.where(mine, jnp.broadcast_to(part[y : y + 1, :], mine.shape), 0.0)
                    for part in (high_part, low_part)
                ],
                axis=0,
            ).astype(BF16)

    def inner_moments(x):
        put_moments(x, range(1, last))
        lanes = slice(LANES, last * LANES)
        product = lax.dot_general(
            hot_ref[x, :, lanes], lhs_ref[x, :, lanes], NT, preferred_element_type=F32
        )
        row_sum_ref[...] = product if x == 0 else row_sum_ref[...] + product

    products = (mat_ref, near_ref, root_ref, total_ref)
    pair_sums(
        sides_of(2 * blocks_x, 0, 1, *products),
        [functools.partial(inner_moments, x) for x in range(blocks_x)],
    )
    codes.wait()
    for x in range(blocks_x):
        for side in range(2):
            word = code_ref[x * blocks_y + side * last]
            for k in range(1, listed):
                code = (word >> (4 * k)) & 15
                step_x = (code * 11) >> 5
                line = src_ref[(3 * side + code - 3 * step_x) * wide + x + step_x]
                put_source(near_ref, root_ref, 2 * x + side, k, line, shift_ref[code], squares)
    pair_sums(sides_of(2 * blocks_x, 1, listed, *products), add=True)
    sums = column_sums([total_ref[number] for number in range(2 * blocks_x)])
    for x in range(blocks_x):
        for side in range(2):
            y = side * last
            sum_ref[x, y : y + 1, :] = sums[2 * x + side : 2 * x + side + 1, :]
        put_moments(x, (0, last))
    ends = [(x, slice(y * LANES, (y + 1) * LANES)) for x in range(blocks_x) for y in (0, last)]
    total = row_sum_ref[...] + lax.dot_general(
        jnp.concatenate([hot_ref[x, :, lanes] for x, lanes in ends], axis=1),
        jnp.concatenate([lhs_ref[x, :, lanes] for x, lanes in ends], axis=1),
        NT,
        preferred_element_type=F32,
    )
    total = total.T
    md_ref[...] = total[:owners] + total[owners:]
    core, my_chip = lax.axis_index("core"), lax.axis_index("chip")
    for other in range(2):
        for step in range(owners // 2):
            owner = 2 * (my_chip ^ step) + (core ^ other)
            table_ref[other, step, :EARLY, :] = early_ref[owner]
            table_ref[other, step, EARLY : EARLY + 1, :] = md_ref[pl.ds(owner, 1), :]


def swap(value, axis, step):
    count = lax.axis_size(axis)
    return lax.ppermute(value, axis, [(i, i ^ step) for i in range(count)])


def neighbours_of(low_edge, high_edge, axis, parity):
    count = lax.axis_size(axis)
    even = parity == 0
    inner = lax.ppermute(
        jnp.where(even, high_edge, low_edge), axis, [(i, i ^ 1) for i in range(count)]
    )
    outer = lax.ppermute(
        jnp.where(even, low_edge, high_edge),
        axis,
        [(i, (i + 1 if i & 1 else i - 1) % count) for i in range(count)],
    )
    return jnp.where(even, outer, inner), jnp.where(even, inner, outer)


def added(parts):
    while len(parts) > 1:
        parts = [sum(parts[k : k + 2][1:], parts[k]) for k in range(0, len(parts), 2)]
    return parts[0]


def to_owner(table):
    table = table[0] + swap(table[1], "core", 1)
    while table.shape[0] > 1:
        ways = min(4, table.shape[0])
        part = table.shape[0] // ways
        table = added(
            [table[:part]]
            + [swap(table[k * part : (k + 1) * part], "chip", k * part) for k in range(1, ways)]
        )
    return table[0]


def summed(value, axis):
    count = lax.axis_size(axis)
    if count & (count - 1):
        return lax.psum(value, axis)
    step = 1
    while step < count:
        ways = min(4, count // step)
        value = added([value] + [swap(value, axis, k * step) for k in range(1, ways)])
        step *= ways
    return value


def shards(positions, velocities, masses, smoothing, neighbours, particle_group, group_row):
    blocks_x, blocks_y, block_len = masses.shape
    dom_count, sub_count = lax.axis_size("dom"), lax.axis_size("chip") * lax.axis_size("core")
    owners = sub_count
    chunk = blocks_y * block_len
    shape = jax.ShapeDtypeStruct
    listed = neighbours.shape[2]
    codes = sum(neighbours[:, :, k] << (4 * k) for k in range(listed)).reshape(-1)
    table_rows = group_row.reshape(-1, LANES)
    packed = jnp.concatenate([positions, masses[None]], axis=0)
    prev, following = neighbours_of(
        packed[:, 0], packed[:, blocks_x - 1], "dom", lax.axis_index("dom") & 1
    )
    sources = ((blocks_x + 2) * blocks_y, 8, LANES)
    columns, middle, own = pl.pallas_call(
        functools.partial(middle_kernel, listed),
        out_shape=(
            shape((2, 4, blocks_x, LANES), F32),
            shape((blocks_x - 2, blocks_y, LANES), F32),
            shape(sources, F32),
        ),
        in_specs=[ANY] + [VMEM] * 5,
        out_specs=(VMEM,) * 3,
        scratch_shapes=pair_scratch(blocks_x, blocks_y, blocks_x - 2, listed),
        compiler_params=params(),
        cost_estimate=pl.CostEstimate(
            flops=4_000_000_000, bytes_accessed=400_000, transcendentals=1_300_000
        ),
        name="middle_pairs",
    )(codes, positions, masses, smoothing, particle_group, table_rows)
    early, rows, hot = pl.pallas_call(
        functools.partial(moments_kernel, blocks_x * dom_count, blocks_y * sub_count),
        out_shape=(
            shape((owners, EARLY, LANES), F32),
            shape(masses.shape, jnp.int32),
            shape((blocks_x, LANES, chunk), BF16),
        ),
        in_specs=[VMEM] * 6,
        out_specs=(VMEM,) * 3,
        scratch_shapes=[
            pltpu.VMEM((blocks_x * EARLY * blocks_y, LANES), F32),
            pltpu.VMEM((blocks_x, owners * 2 * EARLY, chunk), BF16),
            pltpu.VMEM((owners * 2 * EARLY, LANES), F32),
        ],
        compiler_params=params(),
        cost_estimate=pl.CostEstimate(
            flops=2_000_000_000, bytes_accessed=1_400_000, transcendentals=0
        ),
        name="moments_by_row",
    )(middle, positions, velocities, masses, particle_group, table_rows)
    edges = [
        jnp.concatenate([prev[:, y : y + 1], columns[side], following[:, y : y + 1]], axis=1)
        for side, y in ((0, 0), (1, blocks_y - 1))
    ]
    low, high = neighbours_of(*edges, ("chip", "core"), lax.axis_index("core"))
    edge, known = pl.pallas_call(
        functools.partial(edge_kernel, listed),
        out_shape=(shape((2, blocks_y, LANES), F32), shape(sources, F32)),
        in_specs=[ANY] + [VMEM] * 6,
        out_specs=(VMEM,) * 2,
        scratch_shapes=pair_scratch(blocks_x, blocks_y, 2, listed),
        compiler_params=params(),
        cost_estimate=pl.CostEstimate(
            flops=4_000_000_000, bytes_accessed=400_000, transcendentals=1_300_000
        ),
        name="edge_pairs",
    )(codes, positions, masses, smoothing, prev, following, own)
    sums, table = pl.pallas_call(
        functools.partial(rim_kernel, listed),
        out_shape=(shape(masses.shape, F32), shape((2, owners // 2, EARLY + 1, LANES), F32)),
        in_specs=[ANY] + [VMEM] * 11,
        out_specs=(VMEM, VMEM),
        scratch_shapes=[
            pltpu.SMEM((blocks_x * blocks_y,), jnp.int32),
            pltpu.SemaphoreType.DMA(()),
            pltpu.VMEM((128, LANES), F32),
            pltpu.VMEM((6 * (blocks_x + 2), 8, LANES), F32),
            pltpu.VMEM((owners, LANES), F32),
            pltpu.VMEM((blocks_x, 2 * owners, chunk), BF16),
            pltpu.VMEM((LANES, 2 * owners), F32),
            pltpu.VMEM((9, 8, LANES), F32),
            pltpu.VMEM((blocks_x, 24 * blocks_y, LANES), F32),
        ]
        + product_scratch(2 * blocks_x, listed),
        compiler_params=params(),
        cost_estimate=pl.CostEstimate(
            flops=200_000_000, bytes_accessed=400_000, transcendentals=400_000
        ),
        name="rim_pairs_and_table",
    )(
        codes, middle, edge, known, positions, masses, smoothing, low, high, rows, hot, early
    )
    density = sums * DENSITY_FACTOR / (smoothing * smoothing * smoothing)
    return (density, summed(to_owner(table), "dom"))


def solution(mesh):
    dom_count, sub_count = mesh.devices.shape
    mesh = jax.sharding.Mesh(
        mesh.devices.reshape(dom_count, sub_count // 2, 2), ("dom", "chip", "core")
    )
    sub = ("chip", "core")
    in_specs = (
        P(None, "dom", sub, None),
        P(None, "dom", sub, None),
        P("dom", sub, None),
        P("dom", sub, None),
        P("dom", sub, None),
        P("dom", sub, None),
        P(),
    )
    out_specs = (P("dom", sub, None), P(None, sub))
    return jax.shard_map(shards, mesh=mesh, in_specs=in_specs, out_specs=out_specs, check_vma=False)
```

```python
import functools
import math

import jax
import jax.numpy as jnp
from jax import lax
from jax.experimental import pallas as pl
from jax.experimental.pallas import tpu as pltpu
from jax.sharding import PartitionSpec as P

F32 = jnp.float32
BF16 = jnp.bfloat16
LANES = 128
EARLY = 16
DENSITY_FACTOR = 21.0 / (16.0 * math.pi) / 256.0
VMEM = pl.BlockSpec(memory_space=pltpu.VMEM)
ANY = pl.BlockSpec(memory_space=pl.ANY)
NT = (((1,), (1,)), ((), ()))


def params():
    return pltpu.CompilerParams(vmem_limit_bytes=40 * 1024 * 1024)


def rounded(value):
    return value.astype(BF16).astype(F32)


def three_parts(value):
    first = rounded(value)
    rest = value - first
    second = rounded(rest)
    return first, second, rest - second


def spread(numbers, y, count):
    row = jnp.broadcast_to(numbers[y : y + 1, :].astype(F32), (16, LANES)).astype(BF16)
    return jnp.concatenate([row] * (count // 16), axis=0)


def row_numbers(count):
    return lax.broadcasted_iota(jnp.int32, (count, LANES), 0).astype(F32).astype(BF16)


def slot_one_hot(slots, y):
    return jnp.where(
        row_numbers(LANES) == spread(slots, y, LANES), jnp.ones((), BF16), jnp.zeros((), BF16)
    )


def moments_kernel(
    nx_total, ny_total, after_ref, pos_ref, vel_ref, mass_ref, group_ref, row_ref,
    table_ref, rows_ref, hot_ref, feat_ref, lhs_ref, total_ref,
):
    blocks_x, blocks_y, _ = mass_ref.shape
    owners = table_ref.shape[0]
    table_rows = row_ref.shape[0]
    base_x = (lax.axis_index("dom") * blocks_x).astype(F32)
    base_y = ((2 * lax.axis_index("chip") + lax.axis_index("core")) * blocks_y).astype(F32)
    y_iota = lax.broadcasted_iota(jnp.int32, (blocks_y, LANES), 0).astype(F32)

    def features_of(x):
        group = group_ref[x]
        low = group & (LANES - 1)
        high = group >> 7
        rows = jnp.zeros_like(group)
        for r in range(table_rows):
            line = jnp.broadcast_to(row_ref[r : r + 1, :], group.shape)
            picked = jnp.take_along_axis(line, low, axis=1)
            rows = jnp.where(high == r, picked, rows)
        rows_ref[x] = rows
        mass = mass_ref[x]
        gx = (base_x + float(x) + pos_ref[0, x]) / float(nx_total)
        gy = (base_y + y_iota + pos_ref[1, x]) / float(ny_total)
        gz = pos_ref[2, x]
        vx, vy, vz = vel_ref[0, x], vel_ref[1, x], vel_ref[2, x]
        mx, my, mz = mass * gx, mass * gy, mass * gz
        features = (
            mass, mx, my, mz, mass * vx, mass * vy, mass * vz,
            mass * (gy * vz - gz * vy), mass * (gz * vx - gx * vz), mass * (gx * vy - gy * vx),
            mx * gx, my * gy, mz * gz, mx * gy, mx * gz, my * gz,
        )
        for f, feature in enumerate(features):
            start = (x * EARLY + f) * blocks_y
            feat_ref[start : start + blocks_y, :] = feature

    def operands_of(x, y):
        lanes = slice(y * LANES, (y + 1) * LANES)
        feats = feat_ref[pl.ds(x * EARLY * blocks_y + y, EARLY, stride=blocks_y), :]
        high_part = rounded(feats)
        both = jnp.concatenate([high_part, feats - high_part], axis=0).astype(BF16)
        rows = rows_ref[x]
        owner_row = spread(rows >> 7, y, 2 * EARLY)
        for o in range(owners):
            lhs_ref[x, o * 2 * EARLY : (o + 1) * 2 * EARLY, lanes] = jnp.where(
                owner_row == jnp.asarray(o, BF16), both, jnp.zeros((), BF16)
            )
        hot_ref[x, :, lanes] = slot_one_hot(rows & (LANES - 1), y)

    def add_product(x):
        product = lax.dot_general(lhs_ref[x], hot_ref[x], NT, preferred_element_type=F32)
        total_ref[...] = product if x == 0 else total_ref[...] + product

    def finish():
        total = total_ref[...].reshape(owners, 2 * EARLY, LANES)
        table_ref[...] = total[:, :EARLY, :] + total[:, EARLY:, :]

    for x in range(blocks_x):
        features_of(x)
        for y in range(blocks_y):
            operands_of(x, y)
        add_product(x)
    finish()


def target_rows(pos, radius):
    weight = 4.0 / (radius * radius)
    cx, cy, cz = pos[0] - 0.5, pos[1] - 0.5, pos[2] - 0.5
    lines = (
        -2.0 * cx * weight, -2.0 * cy * weight, -2.0 * cz * weight,
        weight, weight, weight,
        (cx * cx + cy * cy + cz * cz) * weight, jnp.zeros_like(weight),
    )
    parts = [three_parts(line) for line in lines]
    return [part[k] for k in range(3) for part in parts]


def target_matrix(coef):
    one, two, three = coef[0:8], coef[8:16], coef[16:24]
    stacked = jnp.concatenate([one, one, two, two, one, three], axis=0)
    return stacked.T.astype(BF16)


def source_matrix(line, root, squares):
    value = jnp.where(squares, line * line, line) * (root * root)
    one, two, three = three_parts(value)
    first = jnp.concatenate([one, two], axis=0).astype(BF16)
    last = jnp.concatenate([three, one], axis=0).astype(BF16)
    return jnp.concatenate([first, first, last], axis=0)


def fifth_root(mass):
    root = jnp.exp(0.2 * jnp.log(mass))
    square = root * root
    return 0.8 * root + 0.2 * mass / (square * square)


def store_source(nat_ref, start, count, columns, mass):
    cx, cy, cz = [column - 0.5 for column in columns]
    one = jnp.ones_like(cx)
    for kind, line in enumerate((cx, cy, cz, cx, cy, cz, one, fifth_root(mass))):
        nat_ref[start + kind * 8 : start + kind * 8 + count, :] = line


def pair_sums(sides, pieces=()):
    rows = 32
    steps = []
    for target, sources, roots, total, base in sides:
        count = roots.shape[0]
        for first in range(0, count, 2):
            steps.append((target, sources, roots, total, base, first, min(2, count - first), count))

    def product(step):
        target, sources, _, _, _, first, width, _ = step
        right = sources[:, first * LANES : (first + width) * LANES]
        return jnp.dot(target[...], right, preferred_element_type=F32)

    ready = product(steps[0])
    chunks = None
    for number, (_, _, roots, total, base, first, width, count) in enumerate(steps):
        squared = ready
        if number + 1 < len(steps):
            ready = product(steps[number + 1])
        if first == 0:
            chunks = [None] * (LANES // rows)
            if base is not None:
                chunks = [base[r * rows : (r + 1) * rows, :] for r in range(len(chunks))]
        limits = []
        for k in range(width):
            root = roots[first + k : first + k + 1, :]
            reach = 4.0 * root
            limits.append(
                [jnp.broadcast_to(line, (rows, LANES)) for line in (root, reach, reach * reach)]
            )
        for r in range(len(chunks)):
            for k, (root, reach, most) in enumerate(limits):
                t = squared[r * rows : (r + 1) * rows, k * LANES : (k + 1) * LANES]
                t = jnp.maximum(jnp.minimum(t, most), 1e-12)
                u = t * lax.rsqrt(t)
                f = reach - u
                f = f * f
                f = f * f
                term = f * (root + u)
                chunks[r] = term if chunks[r] is None else chunks[r] + term
        if first + width == count:
            for r, chunk in enumerate(chunks):
                total[r * rows : (r + 1) * rows, :] = chunk
        if number < len(pieces) and pieces[number] is not None:
            pieces[number]()
    for piece in pieces[len(steps) :]:
        piece()


def column_sums(totals):
    lane = lax.broadcasted_iota(jnp.int32, (LANES, LANES), 1)
    columns = jnp.zeros((LANES, LANES), F32)
    for k, total in enumerate(totals):
        columns = jnp.where(lane == k, jnp.sum(total, axis=1, keepdims=True), columns)
    return columns.T[: len(totals), :]


def square_mask():
    kind = lax.broadcasted_iota(jnp.int32, (8, LANES), 0)
    return (kind >= 3) & (kind < 6)


def shift_rows(step_x, step_y):
    kind = lax.broadcasted_iota(jnp.int32, (8, LANES), 0)
    along_x = jnp.where((kind == 0) | (kind == 3), float(step_x), 0.0)
    return along_x + jnp.where((kind == 1) | (kind == 4), float(step_y), 0.0)


def put_shifts(shift_ref):
    for code in range(9):
        shift_ref[code] = shift_rows(code // 3 - 1, code % 3 - 1)


def put_source(near_ref, root_ref, number, k, line, shift, squares):
    root = jnp.broadcast_to(line[7:8], line.shape)
    near_ref[number, :, k * LANES : (k + 1) * LANES] = source_matrix(line + shift, root, squares)
    root_ref[number, k : k + 1, :] = root[0:1]


def sides_of(count, first, end, mat_ref, near_ref, root_ref, total_ref, base_ref=None):
    lanes, rows = pl.ds(first * LANES, (end - first) * LANES), pl.ds(first, end - first)
    return [
        (
            mat_ref.at[n], near_ref.at[n, :, lanes], root_ref.at[n, rows], total_ref.at[n],
            None if base_ref is None else base_ref.at[n],
        )
        for n in range(count)
    ]


def put_moments(lhs_ref, ys, sums, mass, radius, rows):
    owners = lhs_ref.shape[0] // 2
    owner_ids = lax.broadcasted_iota(jnp.int32, (owners, LANES), 0)
    moment = mass * (sums * DENSITY_FACTOR / (radius * radius * radius))
    high_part = rounded(moment)
    low_part = moment - high_part
    owner = rows >> 7
    for y in ys:
        mine = jnp.broadcast_to(owner[y : y + 1, :], owner_ids.shape) == owner_ids
        lhs_ref[:, y * LANES : (y + 1) * LANES] = jnp.concatenate(
            [
                jnp.where(mine, jnp.broadcast_to(part[y : y + 1, :], mine.shape), 0.0)
                for part in (high_part, low_part)
            ],
            axis=0,
        ).astype(BF16)


def inner_moments(total_ref, first, hot, lhs_ref, sums, mass, radius, rows):
    last = mass.shape[0] - 1
    put_moments(lhs_ref, range(1, last), sums, mass, radius, rows)
    lanes = slice(LANES, last * LANES)
    product = lax.dot_general(hot[:, lanes], lhs_ref[:, lanes], NT, preferred_element_type=F32)
    total_ref[...] = product if first else total_ref[...] + product


def start_rim(
    src_ref, pos_ref, mass_ref, smooth_ref, middle_ref, rows_ref, hot_ref,
    mat_ref, self_ref, moment_ref, tgt_ref, near_ref, root_ref, lhs_ref,
):
    blocks_x, blocks_y, _ = mass_ref.shape
    squares = square_mask()
    rim = [(x, side * (blocks_y - 1)) for x in range(blocks_x) for side in range(2)]
    for x in range(blocks_x):
        lines = target_rows([pos_ref[c, x] for c in range(3)], smooth_ref[x])
        for row, line in enumerate(lines):
            tgt_ref[x, row * blocks_y : (row + 1) * blocks_y, :] = line
    for n, (x, y) in enumerate(rim):
        mat_ref[n] = target_matrix(tgt_ref[x, pl.ds(y, 24, stride=blocks_y), :])
    for n, (x, y) in enumerate(rim):
        put_source(near_ref, root_ref, n, 0, src_ref[(x + 1) * blocks_y + y], 0.0, squares)

    def middle_moments(turn):
        x = turn + 1
        inner_moments(
            moment_ref, turn == 0, hot_ref[x], lhs_ref.at[turn], middle_ref[turn],
            mass_ref[x], smooth_ref[x], rows_ref[x],
        )

    pair_sums(
        sides_of(len(rim), 0, 1, mat_ref, near_ref, root_ref, self_ref),
        [functools.partial(middle_moments, turn) for turn in range(blocks_x - 2)],
    )


def load_codes(far_ref, code_ref, sem):
    copy = pltpu.make_async_copy(far_ref, code_ref, sem)
    copy.start()
    return copy


def block_pairs(
    listed, x_first, x_step, x_count, known_ref, far_code_ref, pos_ref, mass_ref, smooth_ref, prev_ref, next_ref,
    out_ref, src_ref, code_ref, sem, nat_ref, shift_ref, tgt_ref, mat_ref, near_ref, root_ref, total_ref,
    ahead=None,
):
    blocks_x, blocks_y, _ = mass_ref.shape
    codes = load_codes(far_code_ref, code_ref, sem)
    for xe in range(blocks_x + 2):
        if xe == 0 or xe == blocks_x + 1:
            ref = prev_ref if xe == 0 else next_ref
            if ref is None:
                continue
            store_source(nat_ref, xe * 64, blocks_y, [ref[c] for c in range(3)], ref[3])
        elif known_ref is None:
            columns = [pos_ref[c, xe - 1] for c in range(3)]
            store_source(nat_ref, xe * 64, blocks_y, columns, mass_ref[xe - 1])
        else:
            part = pl.ds(xe * blocks_y, blocks_y)
            src_ref[part] = known_ref[part]
            continue
        for y in range(blocks_y):
            src_ref[xe * blocks_y + y] = nat_ref[pl.ds(xe * 64 + y, 8, stride=8), :]
    put_shifts(shift_ref)
    squares = square_mask()
    blocks = [(turn, y) for turn in range(x_count) for y in range(1, blocks_y - 1)]
    for turn in range(x_count):
        x = x_first + turn * x_step
        lines = target_rows([pos_ref[c, x] for c in range(3)], smooth_ref[x])
        for row, line in enumerate(lines):
            tgt_ref[turn, row * blocks_y : (row + 1) * blocks_y, :] = line
    for number, (turn, y) in enumerate(blocks):
        mat_ref[number] = target_matrix(tgt_ref[turn, pl.ds(y, 24, stride=blocks_y), :])
    for number, (turn, y) in enumerate(blocks):
        line = src_ref[(x_first + turn * x_step + 1) * blocks_y + y]
        put_source(near_ref, root_ref, number, 0, line, 0.0, squares)
    pair_sums(sides_of(len(blocks), 0, 1, mat_ref, near_ref, root_ref, total_ref))
    if ahead is not None:
        ahead()
    codes.wait()
    for number, (turn, y) in enumerate(blocks):
        x = x_first + turn * x_step
        word = code_ref[x * blocks_y + y]
        for k in range(1, listed):
            code = (word >> (4 * k)) & 15
            step_x = (code * 11) >> 5
            line = src_ref[(x + step_x) * blocks_y + y + code - 3 * step_x - 1]
            put_source(near_ref, root_ref, number, k, line, shift_ref[code], squares)
    inner = blocks_y - 2
    per_row = inner * (listed // 2)

    def row_sums(turn):
        sums = column_sums([total_ref[turn * inner + k] for k in range(inner)])
        out_ref[turn, 1 : blocks_y - 1, :] = sums

    pieces = [None] * (x_count * per_row + 1)
    for turn in range(x_count):
        pieces[(turn + 1) * per_row] = functools.partial(row_sums, turn)
    sides = sides_of(len(blocks), 1, listed, mat_ref, near_ref, root_ref, total_ref, total_ref)
    pair_sums(sides, pieces)


def middle_kernel(
    listed, code_ref, pos_ref, mass_ref, smooth_ref, group_ref, row_ref, column_ref, out_ref, src_ref, *scratch
):
    blocks_x, blocks_y, _ = mass_ref.shape
    for side in range(2):
        y = side * (blocks_y - 1)
        for x in range(blocks_x):
            for c in range(3):
                column_ref[side, c, x : x + 1, :] = pos_ref[c, x, y : y + 1, :]
            column_ref[side, 3, x : x + 1, :] = mass_ref[x, y : y + 1, :]
    block_pairs(
        listed, 1, 1, blocks_x - 2, None, code_ref, pos_ref, mass_ref, smooth_ref, None, None,
        out_ref, src_ref, *scratch,
    )


def edge_kernel(
    listed, code_ref, pos_ref, mass_ref, smooth_ref, prev_ref, next_ref, known_ref,
    middle_ref, rows_ref, hot_ref,
    out_ref, src_ref, rim_mat_ref, self_ref, moment_ref,
    rim_tgt_ref, rim_near_ref, rim_root_ref, lhs_ref, *scratch
):
    blocks_x = mass_ref.shape[0]
    ahead = functools.partial(
        start_rim, src_ref, pos_ref, mass_ref, smooth_ref, middle_ref, rows_ref, hot_ref,
        rim_mat_ref, self_ref, moment_ref, rim_tgt_ref, rim_near_ref, rim_root_ref, lhs_ref,
    )
    block_pairs(
        listed, 0, blocks_x - 1, 2, known_ref, code_ref, pos_ref, mass_ref, smooth_ref, prev_ref, next_ref,
        out_ref, src_ref, *scratch, ahead=ahead,
    )


def pair_scratch(blocks_x, blocks_y, x_count, listed):
    return [
        pltpu.SMEM((blocks_x * blocks_y,), jnp.int32),
        pltpu.SemaphoreType.DMA(()),
        pltpu.VMEM(((blocks_x + 2) * 64, LANES), F32),
        pltpu.VMEM((9, 8, LANES), F32),
        pltpu.VMEM((x_count, 24 * blocks_y, LANES), F32),
    ] + product_scratch(x_count * (blocks_y - 2), listed)


def product_scratch(blocks, listed):
    return [
        pltpu.VMEM((blocks, LANES, 48), BF16),
        pltpu.VMEM((blocks, 48, listed * LANES), BF16),
        pltpu.VMEM((blocks, 8, LANES), F32),
        pltpu.VMEM((blocks, LANES, LANES), F32),
    ]


def rim_kernel(
    listed, far_code_ref, middle_ref, edge_ref, known_ref, mat_ref, self_ref, moment_ref,
    mass_ref, smooth_ref, low_ref, high_ref, rows_ref, hot_ref, early_ref,
    sum_ref, table_ref, code_ref, sem, nat_ref, src_ref, md_ref, lhs_ref, total_moment_ref,
    shift_ref, near_ref, root_ref, total_ref,
):
    blocks_x, blocks_y, _ = mass_ref.shape
    owners = early_ref.shape[0]
    wide = blocks_x + 2
    last = blocks_y - 1
    codes = load_codes(far_code_ref, code_ref, sem)
    for side, ref in enumerate((low_ref, high_ref)):
        store_source(nat_ref, side * 64, wide, [ref[c] for c in range(3)], ref[3])
        for xe in range(wide):
            ghost = 5 * side * wide + xe
            src_ref[ghost] = nat_ref[pl.ds(side * 64 + xe, 8, stride=8), :]
            for k in range(2):
                y = k + side * (blocks_y - 2)
                place = (1 + k + 2 * side) * wide + xe
                src_ref[place] = known_ref[xe * blocks_y + y]
    put_shifts(shift_ref)
    squares = square_mask()
    for x in range(blocks_x):
        edge = x == 0 or x == blocks_x - 1
        sum_ref[x] = (edge_ref if edge else middle_ref)[(1 if x else 0) if edge else x - 1]
    total_moment_ref[...] = moment_ref[...]
    for x in (0, blocks_x - 1):
        inner_moments(
            total_moment_ref, False, hot_ref[x], lhs_ref.at[x], sum_ref[x],
            mass_ref[x], smooth_ref[x], rows_ref[x],
        )
    codes.wait()
    for x in range(blocks_x):
        for side in range(2):
            word = code_ref[x * blocks_y + side * last]
            for k in range(1, listed):
                code = (word >> (4 * k)) & 15
                step_x = (code * 11) >> 5
                line = src_ref[(3 * side + code - 3 * step_x) * wide + x + step_x]
                put_source(near_ref, root_ref, 2 * x + side, k, line, shift_ref[code], squares)
    pair_sums(sides_of(2 * blocks_x, 1, listed, mat_ref, near_ref, root_ref, total_ref, self_ref))
    sums = column_sums([total_ref[number] for number in range(2 * blocks_x)])
    for x in range(blocks_x):
        for side in range(2):
            y = side * last
            sum_ref[x, y : y + 1, :] = sums[2 * x + side : 2 * x + side + 1, :]
        put_moments(lhs_ref.at[x], (0, last), sum_ref[x], mass_ref[x], smooth_ref[x], rows_ref[x])
    ends = [(x, slice(y * LANES, (y + 1) * LANES)) for x in range(blocks_x) for y in (0, last)]
    total = total_moment_ref[...] + lax.dot_general(
        jnp.concatenate([hot_ref[x, :, lanes] for x, lanes in ends], axis=1),
        jnp.concatenate([lhs_ref[x, :, lanes] for x, lanes in ends], axis=1),
        NT,
        preferred_element_type=F32,
    )
    total = total.T
    md_ref[...] = total[:owners] + total[owners:]
    core, my_chip = lax.axis_index("core"), lax.axis_index("chip")
    for other in range(2):
        for step in range(owners // 2):
            owner = 2 * (my_chip ^ step) + (core ^ other)
            table_ref[other, step, :EARLY, :] = early_ref[owner]
            table_ref[other, step, EARLY : EARLY + 1, :] = md_ref[pl.ds(owner, 1), :]


def swap(value, axis, step):
    count = lax.axis_size(axis)
    return lax.ppermute(value, axis, [(i, i ^ step) for i in range(count)])


def neighbours_of(low_edge, high_edge, axis, parity):
    count = lax.axis_size(axis)
    even = parity == 0
    inner = lax.ppermute(
        jnp.where(even, high_edge, low_edge), axis, [(i, i ^ 1) for i in range(count)]
    )
    outer = lax.ppermute(
        jnp.where(even, low_edge, high_edge),
        axis,
        [(i, (i + 1 if i & 1 else i - 1) % count) for i in range(count)],
    )
    return jnp.where(even, outer, inner), jnp.where(even, inner, outer)


def added(parts):
    while len(parts) > 1:
        parts = [sum(parts[k : k + 2][1:], parts[k]) for k in range(0, len(parts), 2)]
    return parts[0]


def to_owner(table):
    table = table[0] + swap(table[1], "core", 1)
    while table.shape[0] > 1:
        ways = min(4, table.shape[0])
        part = table.shape[0] // ways
        table = added(
            [table[:part]]
            + [swap(table[k * part : (k + 1) * part], "chip", k * part) for k in range(1, ways)]
        )
    return table[0]


def summed(value, axis):
    count = lax.axis_size(axis)
    if count & (count - 1):
        return lax.psum(value, axis)
    step = 1
    while step < count:
        ways = min(4, count // step)
        value = added([value] + [swap(value, axis, k * step) for k in range(1, ways)])
        step *= ways
    return value


def shards(positions, velocities, masses, smoothing, neighbours, particle_group, group_row):
    blocks_x, blocks_y, block_len = masses.shape
    dom_count, sub_count = lax.axis_size("dom"), lax.axis_size("chip") * lax.axis_size("core")
    owners = sub_count
    chunk = blocks_y * block_len
    shape = jax.ShapeDtypeStruct
    listed = neighbours.shape[2]
    codes = sum(neighbours[:, :, k] << (4 * k) for k in range(listed)).reshape(-1)
    table_rows = group_row.reshape(-1, LANES)
    packed = jnp.concatenate([positions, masses[None]], axis=0)
    prev, following = neighbours_of(
        packed[:, 0], packed[:, blocks_x - 1], "dom", lax.axis_index("dom") & 1
    )
    sources = ((blocks_x + 2) * blocks_y, 8, LANES)
    columns, middle, own = pl.pallas_call(
        functools.partial(middle_kernel, listed),
        out_shape=(
            shape((2, 4, blocks_x, LANES), F32),
            shape((blocks_x - 2, blocks_y, LANES), F32),
            shape(sources, F32),
        ),
        in_specs=[ANY] + [VMEM] * 5,
        out_specs=(VMEM,) * 3,
        scratch_shapes=pair_scratch(blocks_x, blocks_y, blocks_x - 2, listed),
        compiler_params=params(),
        cost_estimate=pl.CostEstimate(
            flops=4_000_000_000, bytes_accessed=400_000, transcendentals=1_300_000
        ),
        name="middle_pairs",
    )(codes, positions, masses, smoothing, particle_group, table_rows)
    early, rows, hot = pl.pallas_call(
        functools.partial(moments_kernel, blocks_x * dom_count, blocks_y * sub_count),
        out_shape=(
            shape((owners, EARLY, LANES), F32),
            shape(masses.shape, jnp.int32),
            shape((blocks_x, LANES, chunk), BF16),
        ),
        in_specs=[VMEM] * 6,
        out_specs=(VMEM,) * 3,
        scratch_shapes=[
            pltpu.VMEM((blocks_x * EARLY * blocks_y, LANES), F32),
            pltpu.VMEM((blocks_x, owners * 2 * EARLY, chunk), BF16),
            pltpu.VMEM((owners * 2 * EARLY, LANES), F32),
        ],
        compiler_params=params(),
        cost_estimate=pl.CostEstimate(
            flops=2_000_000_000, bytes_accessed=1_400_000, transcendentals=0
        ),
        name="moments_by_row",
    )(middle, positions, velocities, masses, particle_group, table_rows)
    edges = [
        jnp.concatenate([prev[:, y : y + 1], columns[side], following[:, y : y + 1]], axis=1)
        for side, y in ((0, 0), (1, blocks_y - 1))
    ]
    low, high = neighbours_of(*edges, ("chip", "core"), lax.axis_index("core"))
    rims = 2 * blocks_x
    edge, known, rim_match, rim_self, middle_moment = pl.pallas_call(
        functools.partial(edge_kernel, listed),
        out_shape=(
            shape((2, blocks_y, LANES), F32),
            shape(sources, F32),
            shape((rims, LANES, 48), BF16),
            shape((rims, LANES, LANES), F32),
            shape((LANES, 2 * owners), F32),
        ),
        in_specs=[ANY] + [VMEM] * 9,
        out_specs=(VMEM,) * 5,
        scratch_shapes=[
            pltpu.VMEM((blocks_x, 24 * blocks_y, LANES), F32),
            pltpu.VMEM((rims, 48, LANES), BF16),
            pltpu.VMEM((rims, 8, LANES), F32),
            pltpu.VMEM((blocks_x - 2, 2 * owners, chunk), BF16),
        ]
        + pair_scratch(blocks_x, blocks_y, 2, listed),
        compiler_params=params(),
        cost_estimate=pl.CostEstimate(
            flops=4_000_000_000, bytes_accessed=400_000, transcendentals=1_300_000
        ),
        name="edge_pairs",
    )(codes, positions, masses, smoothing, prev, following, own, middle, rows, hot)
    sums, table = pl.pallas_call(
        functools.partial(rim_kernel, listed),
        out_shape=(shape(masses.shape, F32), shape((2, owners // 2, EARLY + 1, LANES), F32)),
        in_specs=[ANY] + [VMEM] * 13,
        out_specs=(VMEM, VMEM),
        scratch_shapes=[
            pltpu.SMEM((blocks_x * blocks_y,), jnp.int32),
            pltpu.SemaphoreType.DMA(()),
            pltpu.VMEM((128, LANES), F32),
            pltpu.VMEM((6 * (blocks_x + 2), 8, LANES), F32),
            pltpu.VMEM((owners, LANES), F32),
            pltpu.VMEM((blocks_x, 2 * owners, chunk), BF16),
            pltpu.VMEM((LANES, 2 * owners), F32),
            pltpu.VMEM((9, 8, LANES), F32),
        ]
        + product_scratch(rims, listed)[1:],
        compiler_params=params(),
        cost_estimate=pl.CostEstimate(
            flops=200_000_000, bytes_accessed=400_000, transcendentals=400_000
        ),
        name="rim_pairs_and_table",
    )(
        codes, middle, edge, known, rim_match, rim_self, middle_moment,
        masses, smoothing, low, high, rows, hot, early,
    )
    density = sums * DENSITY_FACTOR / (smoothing * smoothing * smoothing)
    return (density, summed(to_owner(table), "dom"))


def solution(mesh):
    dom_count, sub_count = mesh.devices.shape
    mesh = jax.sharding.Mesh(
        mesh.devices.reshape(dom_count, sub_count // 2, 2), ("dom", "chip", "core")
    )
    sub = ("chip", "core")
    in_specs = (
        P(None, "dom", sub, None),
        P(None, "dom", sub, None),
        P("dom", sub, None),
        P("dom", sub, None),
        P("dom", sub, None),
        P("dom", sub, None),
        P(),
    )
    out_specs = (P("dom", sub, None), P(None, sub))
    return jax.shard_map(shards, mesh=mesh, in_specs=in_specs, out_specs=out_specs, check_vma=False)
```

```python
import functools
import math

import jax
import jax.numpy as jnp
from jax import lax
from jax.experimental import pallas as pl
from jax.experimental.pallas import tpu as pltpu
from jax.sharding import PartitionSpec as P

F32 = jnp.float32
BF16 = jnp.bfloat16
LANES = 128
EARLY = 16
DENSITY_FACTOR = 21.0 / (16.0 * math.pi) / 256.0
VMEM = pl.BlockSpec(memory_space=pltpu.VMEM)
NT = (((1,), (1,)), ((), ()))


def params():
    return pltpu.CompilerParams(vmem_limit_bytes=40 * 1024 * 1024)


def rounded(value):
    return value.astype(BF16).astype(F32)


def three_parts(value):
    first = rounded(value)
    rest = value - first
    second = rounded(rest)
    return first, second, rest - second


def spread(numbers, y, count):
    row = jnp.broadcast_to(numbers[y : y + 1, :].astype(F32), (16, LANES)).astype(BF16)
    return jnp.concatenate([row] * (count // 16), axis=0)


def row_numbers(count):
    return lax.broadcasted_iota(jnp.int32, (count, LANES), 0).astype(F32).astype(BF16)


def slot_one_hot(slots, y):
    return jnp.where(
        row_numbers(LANES) == spread(slots, y, LANES), jnp.ones((), BF16), jnp.zeros((), BF16)
    )


def moments_kernel(
    nx_total, ny_total, after_ref, pos_ref, vel_ref, mass_ref, group_ref, row_ref,
    table_ref, rows_ref, hot_ref, feat_ref, lhs_ref, total_ref,
):
    blocks_x, blocks_y, _ = mass_ref.shape
    owners = table_ref.shape[0]
    table_rows = row_ref.shape[0]
    base_x = (lax.axis_index("dom") * blocks_x).astype(F32)
    base_y = ((2 * lax.axis_index("chip") + lax.axis_index("core")) * blocks_y).astype(F32)
    y_iota = lax.broadcasted_iota(jnp.int32, (blocks_y, LANES), 0).astype(F32)

    def features_of(x):
        group = group_ref[x]
        low = group & (LANES - 1)
        high = group >> 7
        rows = jnp.zeros_like(group)
        for r in range(table_rows):
            line = jnp.broadcast_to(row_ref[r : r + 1, :], group.shape)
            picked = jnp.take_along_axis(line, low, axis=1)
            rows = jnp.where(high == r, picked, rows)
        rows_ref[x] = rows
        mass = mass_ref[x]
        gx = (base_x + float(x) + pos_ref[0, x]) / float(nx_total)
        gy = (base_y + y_iota + pos_ref[1, x]) / float(ny_total)
        gz = pos_ref[2, x]
        vx, vy, vz = vel_ref[0, x], vel_ref[1, x], vel_ref[2, x]
        mx, my, mz = mass * gx, mass * gy, mass * gz
        features = (
            mass, mx, my, mz, mass * vx, mass * vy, mass * vz,
            mass * (gy * vz - gz * vy), mass * (gz * vx - gx * vz), mass * (gx * vy - gy * vx),
            mx * gx, my * gy, mz * gz, mx * gy, mx * gz, my * gz,
        )
        for f, feature in enumerate(features):
            start = (x * EARLY + f) * blocks_y
            feat_ref[start : start + blocks_y, :] = feature

    def operands_of(x, y):
        lanes = slice(y * LANES, (y + 1) * LANES)
        feats = feat_ref[pl.ds(x * EARLY * blocks_y + y, EARLY, stride=blocks_y), :]
        high_part = rounded(feats)
        both = jnp.concatenate([high_part, feats - high_part], axis=0).astype(BF16)
        rows = rows_ref[x]
        owner_row = spread(rows >> 7, y, 2 * EARLY)
        for o in range(owners):
            lhs_ref[x, o * 2 * EARLY : (o + 1) * 2 * EARLY, lanes] = jnp.where(
                owner_row == jnp.asarray(o, BF16), both, jnp.zeros((), BF16)
            )
        hot_ref[x, :, lanes] = slot_one_hot(rows & (LANES - 1), y)

    def add_product(x):
        product = lax.dot_general(lhs_ref[x], hot_ref[x], NT, preferred_element_type=F32)
        total_ref[...] = product if x == 0 else total_ref[...] + product

    def finish():
        total = total_ref[...].reshape(owners, 2 * EARLY, LANES)
        table_ref[...] = total[:, :EARLY, :] + total[:, EARLY:, :]

    for x in range(blocks_x):
        features_of(x)
        for y in range(blocks_y):
            operands_of(x, y)
        add_product(x)
    finish()


def target_rows(pos, radius):
    weight = 4.0 / (radius * radius)
    cx, cy, cz = pos[0] - 0.5, pos[1] - 0.5, pos[2] - 0.5
    lines = (
        -2.0 * cx * weight, -2.0 * cy * weight, -2.0 * cz * weight,
        weight, weight, weight,
        (cx * cx + cy * cy + cz * cz) * weight, jnp.zeros_like(weight),
    )
    parts = [three_parts(line) for line in lines]
    return [part[k] for k in range(3) for part in parts]


def target_matrix(coef):
    one, two, three = coef[0:8], coef[8:16], coef[16:24]
    stacked = jnp.concatenate([one, one, two, two, one, three], axis=0)
    return stacked.T.astype(BF16)


def source_matrix(line, root, squares):
    value = jnp.where(squares, line * line, line) * (root * root)
    one, two, three = three_parts(value)
    first = jnp.concatenate([one, two], axis=0).astype(BF16)
    last = jnp.concatenate([three, one], axis=0).astype(BF16)
    return jnp.concatenate([first, first, last], axis=0)


def fifth_root(mass):
    root = jnp.exp(0.2 * jnp.log(mass))
    square = root * root
    return 0.8 * root + 0.2 * mass / (square * square)


def store_source(nat_ref, start, count, columns, mass):
    cx, cy, cz = [column - 0.5 for column in columns]
    one = jnp.ones_like(cx)
    for kind, line in enumerate((cx, cy, cz, cx, cy, cz, one, fifth_root(mass))):
        nat_ref[start + kind * 8 : start + kind * 8 + count, :] = line


def pair_sums(sides, pieces=(), add=False):
    rows = 32
    steps = []
    for target, sources, roots, total in sides:
        count = roots.shape[0]
        for first in range(0, count, 2):
            steps.append((target, sources, roots, total, first, min(2, count - first), count))

    def product(step):
        target, sources, _, _, first, width, _ = step
        right = sources[:, first * LANES : (first + width) * LANES]
        return jnp.dot(target[...], right, preferred_element_type=F32)

    ready = product(steps[0])
    chunks = None
    for number, (_, _, roots, total, first, width, count) in enumerate(steps):
        squared = ready
        if number + 1 < len(steps):
            ready = product(steps[number + 1])
        if first == 0:
            chunks = [None] * (LANES // rows)
            if add:
                chunks = [total[r * rows : (r + 1) * rows, :] for r in range(len(chunks))]
        limits = []
        for k in range(width):
            root = roots[first + k : first + k + 1, :]
            reach = 4.0 * root
            limits.append(
                [jnp.broadcast_to(line, (rows, LANES)) for line in (root, reach, reach * reach)]
            )
        for r in range(len(chunks)):
            for k, (root, reach, most) in enumerate(limits):
                t = squared[r * rows : (r + 1) * rows, k * LANES : (k + 1) * LANES]
                t = jnp.maximum(jnp.minimum(t, most), 1e-12)
                u = t * lax.rsqrt(t)
                f = reach - u
                f = f * f
                f = f * f
                term = f * (root + u)
                chunks[r] = term if chunks[r] is None else chunks[r] + term
        if first + width == count:
            for r, chunk in enumerate(chunks):
                total[r * rows : (r + 1) * rows, :] = chunk
        if number < len(pieces) and pieces[number] is not None:
            pieces[number]()
    for piece in pieces[len(steps) :]:
        piece()


def column_sums(totals):
    lane = lax.broadcasted_iota(jnp.int32, (LANES, LANES), 1)
    columns = jnp.zeros((LANES, LANES), F32)
    for k, total in enumerate(totals):
        columns = jnp.where(lane == k, jnp.sum(total, axis=1, keepdims=True), columns)
    return columns.T[: len(totals), :]


def square_mask():
    kind = lax.broadcasted_iota(jnp.int32, (8, LANES), 0)
    return (kind >= 3) & (kind < 6)


def shift_rows(step_x, step_y):
    kind = lax.broadcasted_iota(jnp.int32, (8, LANES), 0)
    along_x = jnp.where((kind == 0) | (kind == 3), float(step_x), 0.0)
    return along_x + jnp.where((kind == 1) | (kind == 4), float(step_y), 0.0)


def put_shifts(shift_ref):
    for code in range(9):
        shift_ref[code] = shift_rows(code // 3 - 1, code % 3 - 1)


def put_source(near_ref, root_ref, number, k, line, shift, squares):
    root = jnp.broadcast_to(line[7:8], line.shape)
    near_ref[number, :, k * LANES : (k + 1) * LANES] = source_matrix(line + shift, root, squares)
    root_ref[number, k : k + 1, :] = root[0:1]


def sides_of(count, first, end, mat_ref, near_ref, root_ref, total_ref):
    lanes, rows = pl.ds(first * LANES, (end - first) * LANES), pl.ds(first, end - first)
    return [
        (mat_ref.at[n], near_ref.at[n, :, lanes], root_ref.at[n, rows], total_ref.at[n])
        for n in range(count)
    ]


def block_pairs(
    listed, x_first, x_step, x_count, known_ref, code_ref, pos_ref, mass_ref, smooth_ref, prev_ref, next_ref,
    out_ref, src_ref, nat_ref, shift_ref, tgt_ref, mat_ref, near_ref, root_ref, total_ref,
):
    blocks_x, blocks_y, _ = mass_ref.shape
    for xe in range(blocks_x + 2):
        if xe == 0 or xe == blocks_x + 1:
            ref = prev_ref if xe == 0 else next_ref
            if ref is None:
                continue
            store_source(nat_ref, xe * 64, blocks_y, [ref[c] for c in range(3)], ref[3])
        elif known_ref is None:
            columns = [pos_ref[c, xe - 1] for c in range(3)]
            store_source(nat_ref, xe * 64, blocks_y, columns, mass_ref[xe - 1])
        else:
            part = pl.ds(xe * blocks_y, blocks_y)
            src_ref[part] = known_ref[part]
            continue
        for y in range(blocks_y):
            src_ref[xe * blocks_y + y] = nat_ref[pl.ds(xe * 64 + y, 8, stride=8), :]
    put_shifts(shift_ref)
    squares = square_mask()
    blocks = [(turn, y) for turn in range(x_count) for y in range(1, blocks_y - 1)]
    for turn in range(x_count):
        x = x_first + turn * x_step
        lines = target_rows([pos_ref[c, x] for c in range(3)], smooth_ref[x])
        for row, line in enumerate(lines):
            tgt_ref[turn, row * blocks_y : (row + 1) * blocks_y, :] = line
    for number, (turn, y) in enumerate(blocks):
        mat_ref[number] = target_matrix(tgt_ref[turn, pl.ds(y, 24, stride=blocks_y), :])
    for number, (turn, y) in enumerate(blocks):
        line = src_ref[(x_first + turn * x_step + 1) * blocks_y + y]
        put_source(near_ref, root_ref, number, 0, line, 0.0, squares)
    pair_sums(sides_of(len(blocks), 0, 1, mat_ref, near_ref, root_ref, total_ref))
    words = code_ref[...]
    for number, (turn, y) in enumerate(blocks):
        x = x_first + turn * x_step
        word = words[x, y]
        for k in range(1, listed):
            code = (word >> (4 * k)) & 15
            step_x = (code * 11) >> 5
            line = src_ref[(x + step_x) * blocks_y + y + code - 3 * step_x - 1]
            put_source(near_ref, root_ref, number, k, line, shift_ref[code], squares)
    inner = blocks_y - 2
    per_row = inner * (listed // 2)

    def row_sums(turn):
        sums = column_sums([total_ref[turn * inner + k] for k in range(inner)])
        out_ref[turn, 1 : blocks_y - 1, :] = sums

    pieces = [None] * (x_count * per_row + 1)
    for turn in range(x_count):
        pieces[(turn + 1) * per_row] = functools.partial(row_sums, turn)
    sides = sides_of(len(blocks), 1, listed, mat_ref, near_ref, root_ref, total_ref)
    pair_sums(sides, pieces, add=True)


def middle_kernel(
    listed, code_ref, pos_ref, mass_ref, smooth_ref, group_ref, row_ref, column_ref, out_ref, src_ref, *scratch
):
    blocks_x, blocks_y, _ = mass_ref.shape
    for side in range(2):
        y = side * (blocks_y - 1)
        for x in range(blocks_x):
            for c in range(3):
                column_ref[side, c, x : x + 1, :] = pos_ref[c, x, y : y + 1, :]
            column_ref[side, 3, x : x + 1, :] = mass_ref[x, y : y + 1, :]
    block_pairs(
        listed, 1, 1, blocks_x - 2, None, code_ref, pos_ref, mass_ref, smooth_ref, None, None,
        out_ref, src_ref, *scratch,
    )


def edge_kernel(
    listed, code_ref, pos_ref, mass_ref, smooth_ref, prev_ref, next_ref, known_ref, out_ref, src_ref, *scratch
):
    blocks_x = mass_ref.shape[0]
    block_pairs(
        listed, 0, blocks_x - 1, 2, known_ref, code_ref, pos_ref, mass_ref, smooth_ref, prev_ref, next_ref,
        out_ref, src_ref, *scratch,
    )


def pair_scratch(blocks_x, blocks_y, x_count, listed):
    return [
        pltpu.VMEM(((blocks_x + 2) * 64, LANES), F32),
        pltpu.VMEM((9, 8, LANES), F32),
        pltpu.VMEM((x_count, 24 * blocks_y, LANES), F32),
    ] + product_scratch(x_count * (blocks_y - 2), listed)


def product_scratch(blocks, listed):
    return [
        pltpu.VMEM((blocks, LANES, 48), BF16),
        pltpu.VMEM((blocks, 48, listed * LANES), BF16),
        pltpu.VMEM((blocks, 8, LANES), F32),
        pltpu.VMEM((blocks, LANES, LANES), F32),
    ]


def rim_kernel(
    listed, code_ref, middle_ref, edge_ref, known_ref, pos_ref, mass_ref, smooth_ref,
    low_ref, high_ref, rows_ref, hot_ref, early_ref,
    sum_ref, table_ref, nat_ref, src_ref, md_ref, lhs_ref, row_sum_ref,
    shift_ref, tgt_ref, mat_ref, near_ref, root_ref, total_ref,
):
    blocks_x, blocks_y, _ = mass_ref.shape
    owners = early_ref.shape[0]
    wide = blocks_x + 2
    for side, ref in enumerate((low_ref, high_ref)):
        store_source(nat_ref, side * 64, wide, [ref[c] for c in range(3)], ref[3])
        for xe in range(wide):
            ghost = 5 * side * wide + xe
            src_ref[ghost] = nat_ref[pl.ds(side * 64 + xe, 8, stride=8), :]
            for k in range(2):
                y = k + side * (blocks_y - 2)
                place = (1 + k + 2 * side) * wide + xe
                src_ref[place] = known_ref[xe * blocks_y + y]
    put_shifts(shift_ref)
    squares = square_mask()
    for x in range(blocks_x):
        edge = x == 0 or x == blocks_x - 1
        turn = (1 if x else 0) if edge else x - 1
        sum_ref[x] = (edge_ref if edge else middle_ref)[turn]
        lines = target_rows([pos_ref[c, x] for c in range(3)], smooth_ref[x])
        for row, line in enumerate(lines):
            tgt_ref[x, row * blocks_y : (row + 1) * blocks_y, :] = line
    for x in range(blocks_x):
        for side in range(2):
            y = side * (blocks_y - 1)
            mat_ref[2 * x + side] = target_matrix(tgt_ref[x, pl.ds(y, 24, stride=blocks_y), :])
    for x in range(blocks_x):
        for side in range(2):
            line = src_ref[(3 * side + 1) * wide + x + 1]
            put_source(near_ref, root_ref, 2 * x + side, 0, line, 0.0, squares)

    owner_ids = lax.broadcasted_iota(jnp.int32, (owners, LANES), 0)
    last = blocks_y - 1

    def put_moments(x, ys):
        radius = smooth_ref[x]
        moment = mass_ref[x] * (sum_ref[x] * DENSITY_FACTOR / (radius * radius * radius))
        high_part = rounded(moment)
        low_part = moment - high_part
        owner = rows_ref[x] >> 7
        for y in ys:
            mine = jnp.broadcast_to(owner[y : y + 1, :], owner_ids.shape) == owner_ids
            lhs_ref[x, :, y * LANES : (y + 1) * LANES] = jnp.concatenate(
                [
                    jnp.where(mine, jnp.broadcast_to(part[y : y + 1, :], mine.shape), 0.0)
                    for part in (high_part, low_part)
                ],
                axis=0,
            ).astype(BF16)

    def inner_moments(x):
        put_moments(x, range(1, last))
        lanes = slice(LANES, last * LANES)
        product = lax.dot_general(
            hot_ref[x, :, lanes], lhs_ref[x, :, lanes], NT, preferred_element_type=F32
        )
        row_sum_ref[...] = product if x == 0 else row_sum_ref[...] + product

    products = (mat_ref, near_ref, root_ref, total_ref)
    pair_sums(
        sides_of(2 * blocks_x, 0, 1, *products),
        [functools.partial(inner_moments, x) for x in range(blocks_x)],
    )
    words = code_ref[...]
    for x in range(blocks_x):
        for side in range(2):
            word = words[x, side * last]
            for k in range(1, listed):
                code = (word >> (4 * k)) & 15
                step_x = (code * 11) >> 5
                line = src_ref[(3 * side + code - 3 * step_x) * wide + x + step_x]
                put_source(near_ref, root_ref, 2 * x + side, k, line, shift_ref[code], squares)
    pair_sums(sides_of(2 * blocks_x, 1, listed, *products), add=True)
    sums = column_sums([total_ref[number] for number in range(2 * blocks_x)])
    for x in range(blocks_x):
        for side in range(2):
            y = side * last
            sum_ref[x, y : y + 1, :] = sums[2 * x + side : 2 * x + side + 1, :]
        put_moments(x, (0, last))
    ends = [(x, slice(y * LANES, (y + 1) * LANES)) for x in range(blocks_x) for y in (0, last)]
    total = row_sum_ref[...] + lax.dot_general(
        jnp.concatenate([hot_ref[x, :, lanes] for x, lanes in ends], axis=1),
        jnp.concatenate([lhs_ref[x, :, lanes] for x, lanes in ends], axis=1),
        NT,
        preferred_element_type=F32,
    )
    total = total.T
    md_ref[...] = total[:owners] + total[owners:]
    core, my_chip = lax.axis_index("core"), lax.axis_index("chip")
    for other in range(2):
        for step in range(owners // 2):
            owner = 2 * (my_chip ^ step) + (core ^ other)
            table_ref[other, step, :EARLY, :] = early_ref[owner]
            table_ref[other, step, EARLY : EARLY + 1, :] = md_ref[pl.ds(owner, 1), :]


def swap(value, axis, step):
    count = lax.axis_size(axis)
    return lax.ppermute(value, axis, [(i, i ^ step) for i in range(count)])


def neighbours_of(low_edge, high_edge, axis, parity):
    count = lax.axis_size(axis)
    even = parity == 0
    inner = lax.ppermute(
        jnp.where(even, high_edge, low_edge), axis, [(i, i ^ 1) for i in range(count)]
    )
    outer = lax.ppermute(
        jnp.where(even, low_edge, high_edge),
        axis,
        [(i, (i + 1 if i & 1 else i - 1) % count) for i in range(count)],
    )
    return jnp.where(even, outer, inner), jnp.where(even, inner, outer)


def added(parts):
    while len(parts) > 1:
        parts = [sum(parts[k : k + 2][1:], parts[k]) for k in range(0, len(parts), 2)]
    return parts[0]


def to_owner(table):
    table = table[0] + swap(table[1], "core", 1)
    while table.shape[0] > 1:
        ways = min(4, table.shape[0])
        part = table.shape[0] // ways
        table = added(
            [table[:part]]
            + [swap(table[k * part : (k + 1) * part], "chip", k * part) for k in range(1, ways)]
        )
    return table[0]


def summed(value, axis):
    count = lax.axis_size(axis)
    if count & (count - 1):
        return lax.psum(value, axis)
    step = 1
    while step < count:
        ways = min(4, count // step)
        value = added([value] + [swap(value, axis, k * step) for k in range(1, ways)])
        step *= ways
    return value


def shards(positions, velocities, masses, smoothing, neighbours, particle_group, group_row):
    blocks_x, blocks_y, block_len = masses.shape
    dom_count, sub_count = lax.axis_size("dom"), lax.axis_size("chip") * lax.axis_size("core")
    owners = sub_count
    chunk = blocks_y * block_len
    shape = jax.ShapeDtypeStruct
    listed = neighbours.shape[2]
    codes = sum(neighbours[:, :, k] << (4 * k) for k in range(listed))
    table_rows = group_row.reshape(-1, LANES)
    packed = jnp.concatenate([positions, masses[None]], axis=0)
    prev, following = neighbours_of(
        packed[:, 0], packed[:, blocks_x - 1], "dom", lax.axis_index("dom") & 1
    )
    sources = ((blocks_x + 2) * blocks_y, 8, LANES)
    columns, middle, own = pl.pallas_call(
        functools.partial(middle_kernel, listed),
        out_shape=(
            shape((2, 4, blocks_x, LANES), F32),
            shape((blocks_x - 2, blocks_y, LANES), F32),
            shape(sources, F32),
        ),
        in_specs=[VMEM] * 6,
        out_specs=(VMEM,) * 3,
        scratch_shapes=pair_scratch(blocks_x, blocks_y, blocks_x - 2, listed),
        compiler_params=params(),
        cost_estimate=pl.CostEstimate(
            flops=4_000_000_000, bytes_accessed=400_000, transcendentals=1_300_000
        ),
        name="middle_pairs",
    )(codes, positions, masses, smoothing, particle_group, table_rows)
    early, rows, hot = pl.pallas_call(
        functools.partial(moments_kernel, blocks_x * dom_count, blocks_y * sub_count),
        out_shape=(
            shape((owners, EARLY, LANES), F32),
            shape(masses.shape, jnp.int32),
            shape((blocks_x, LANES, chunk), BF16),
        ),
        in_specs=[VMEM] * 6,
        out_specs=(VMEM,) * 3,
        scratch_shapes=[
            pltpu.VMEM((blocks_x * EARLY * blocks_y, LANES), F32),
            pltpu.VMEM((blocks_x, owners * 2 * EARLY, chunk), BF16),
            pltpu.VMEM((owners * 2 * EARLY, LANES), F32),
        ],
        compiler_params=params(),
        cost_estimate=pl.CostEstimate(
            flops=2_000_000_000, bytes_accessed=1_400_000, transcendentals=0
        ),
        name="moments_by_row",
    )(middle, positions, velocities, masses, particle_group, table_rows)
    edges = [
        jnp.concatenate([prev[:, y : y + 1], columns[side], following[:, y : y + 1]], axis=1)
        for side, y in ((0, 0), (1, blocks_y - 1))
    ]
    low, high = neighbours_of(*edges, ("chip", "core"), lax.axis_index("core"))
    edge, known = pl.pallas_call(
        functools.partial(edge_kernel, listed),
        out_shape=(shape((2, blocks_y, LANES), F32), shape(sources, F32)),
        in_specs=[VMEM] * 7,
        out_specs=(VMEM,) * 2,
        scratch_shapes=pair_scratch(blocks_x, blocks_y, 2, listed),
        compiler_params=params(),
        cost_estimate=pl.CostEstimate(
            flops=4_000_000_000, bytes_accessed=400_000, transcendentals=1_300_000
        ),
        name="edge_pairs",
    )(codes, positions, masses, smoothing, prev, following, own)
    sums, table = pl.pallas_call(
        functools.partial(rim_kernel, listed),
        out_shape=(shape(masses.shape, F32), shape((2, owners // 2, EARLY + 1, LANES), F32)),
        in_specs=[VMEM] * 12,
        out_specs=(VMEM, VMEM),
        scratch_shapes=[
            pltpu.VMEM((128, LANES), F32),
            pltpu.VMEM((6 * (blocks_x + 2), 8, LANES), F32),
            pltpu.VMEM((owners, LANES), F32),
            pltpu.VMEM((blocks_x, 2 * owners, chunk), BF16),
            pltpu.VMEM((LANES, 2 * owners), F32),
            pltpu.VMEM((9, 8, LANES), F32),
            pltpu.VMEM((blocks_x, 24 * blocks_y, LANES), F32),
        ]
        + product_scratch(2 * blocks_x, listed),
        compiler_params=params(),
        cost_estimate=pl.CostEstimate(
            flops=200_000_000, bytes_accessed=400_000, transcendentals=400_000
        ),
        name="rim_pairs_and_table",
    )(
        codes, middle, edge, known, positions, masses, smoothing, low, high, rows, hot, early
    )
    density = sums * DENSITY_FACTOR / (smoothing * smoothing * smoothing)
    return (density, summed(to_owner(table), "dom"))


def solution(mesh):
    dom_count, sub_count = mesh.devices.shape
    mesh = jax.sharding.Mesh(
        mesh.devices.reshape(dom_count, sub_count // 2, 2), ("dom", "chip", "core")
    )
    sub = ("chip", "core")
    in_specs = (
        P(None, "dom", sub, None),
        P(None, "dom", sub, None),
        P("dom", sub, None),
        P("dom", sub, None),
        P("dom", sub, None),
        P("dom", sub, None),
        P(),
    )
    out_specs = (P("dom", sub, None), P(None, sub))
    return jax.shard_map(shards, mesh=mesh, in_specs=in_specs, out_specs=out_specs, check_vma=False)
```

```python
import functools
import math

import jax
import jax.numpy as jnp
from jax import lax
from jax.experimental import pallas as pl
from jax.experimental.pallas import tpu as pltpu
from jax.sharding import PartitionSpec as P

F32 = jnp.float32
BF16 = jnp.bfloat16
LANES = 128
EARLY = 16
DENSITY_FACTOR = 21.0 / (16.0 * math.pi) / 256.0
VMEM = pl.BlockSpec(memory_space=pltpu.VMEM)
NT = (((1,), (1,)), ((), ()))


def params():
    return pltpu.CompilerParams(vmem_limit_bytes=40 * 1024 * 1024)


def rounded(value):
    return value.astype(BF16).astype(F32)


def three_parts(value):
    first = rounded(value)
    rest = value - first
    second = rounded(rest)
    return first, second, rest - second


def spread(numbers, y, count):
    row = jnp.broadcast_to(numbers[y : y + 1, :].astype(F32), (16, LANES)).astype(BF16)
    return jnp.concatenate([row] * (count // 16), axis=0)


def row_numbers(count):
    return lax.broadcasted_iota(jnp.int32, (count, LANES), 0).astype(F32).astype(BF16)


def slot_one_hot(slots, y):
    return jnp.where(
        row_numbers(LANES) == spread(slots, y, LANES), jnp.ones((), BF16), jnp.zeros((), BF16)
    )


def moments_kernel(
    nx_total, ny_total, after_ref, pos_ref, vel_ref, mass_ref, group_ref, row_ref,
    table_ref, rows_ref, hot_ref, feat_ref, lhs_ref, total_ref,
):
    blocks_x, blocks_y, _ = mass_ref.shape
    owners = table_ref.shape[0]
    table_rows = row_ref.shape[0]
    base_x = (lax.axis_index("dom") * blocks_x).astype(F32)
    base_y = ((2 * lax.axis_index("chip") + lax.axis_index("core")) * blocks_y).astype(F32)
    y_iota = lax.broadcasted_iota(jnp.int32, (blocks_y, LANES), 0).astype(F32)

    def features_of(x):
        group = group_ref[x]
        low = group & (LANES - 1)
        high = group >> 7
        rows = jnp.zeros_like(group)
        for r in range(table_rows):
            line = jnp.broadcast_to(row_ref[r : r + 1, :], group.shape)
            picked = jnp.take_along_axis(line, low, axis=1)
            rows = jnp.where(high == r, picked, rows)
        rows_ref[x] = rows
        mass = mass_ref[x]
        gx = (base_x + float(x) + pos_ref[0, x]) / float(nx_total)
        gy = (base_y + y_iota + pos_ref[1, x]) / float(ny_total)
        gz = pos_ref[2, x]
        vx, vy, vz = vel_ref[0, x], vel_ref[1, x], vel_ref[2, x]
        mx, my, mz = mass * gx, mass * gy, mass * gz
        features = (
            mass, mx, my, mz, mass * vx, mass * vy, mass * vz,
            mass * (gy * vz - gz * vy), mass * (gz * vx - gx * vz), mass * (gx * vy - gy * vx),
            mx * gx, my * gy, mz * gz, mx * gy, mx * gz, my * gz,
        )
        for f, feature in enumerate(features):
            start = (x * EARLY + f) * blocks_y
            feat_ref[start : start + blocks_y, :] = feature

    def operands_of(x, y):
        lanes = slice(y * LANES, (y + 1) * LANES)
        feats = feat_ref[pl.ds(x * EARLY * blocks_y + y, EARLY, stride=blocks_y), :]
        high_part = rounded(feats)
        both = jnp.concatenate([high_part, feats - high_part], axis=0).astype(BF16)
        rows = rows_ref[x]
        owner_row = spread(rows >> 7, y, 2 * EARLY)
        for o in range(owners):
            lhs_ref[x, o * 2 * EARLY : (o + 1) * 2 * EARLY, lanes] = jnp.where(
                owner_row == jnp.asarray(o, BF16), both, jnp.zeros((), BF16)
            )
        hot_ref[x, :, lanes] = slot_one_hot(rows & (LANES - 1), y)

    def add_product(x):
        product = lax.dot_general(lhs_ref[x], hot_ref[x], NT, preferred_element_type=F32)
        total_ref[...] = product if x == 0 else total_ref[...] + product

    def finish():
        total = total_ref[...].reshape(owners, 2 * EARLY, LANES)
        table_ref[...] = total[:, :EARLY, :] + total[:, EARLY:, :]

    for x in range(blocks_x):
        features_of(x)
        for y in range(blocks_y):
            operands_of(x, y)
        add_product(x)
    finish()


def target_rows(pos, radius):
    weight = 4.0 / (radius * radius)
    cx, cy, cz = pos[0] - 0.5, pos[1] - 0.5, pos[2] - 0.5
    lines = (
        -2.0 * cx * weight, -2.0 * cy * weight, -2.0 * cz * weight,
        weight, weight, weight,
        (cx * cx + cy * cy + cz * cz) * weight, jnp.zeros_like(weight),
    )
    parts = [three_parts(line) for line in lines]
    return [part[k] for k in range(3) for part in parts]


def target_matrix(coef):
    one, two, three = coef[0:8], coef[8:16], coef[16:24]
    stacked = jnp.concatenate([one, one, two, two, one, three], axis=0)
    return stacked.T.astype(BF16)


def source_matrix(line, root, squares):
    value = jnp.where(squares, line * line, line) * (root * root)
    one, two, three = three_parts(value)
    first = jnp.concatenate([one, two], axis=0).astype(BF16)
    last = jnp.concatenate([three, one], axis=0).astype(BF16)
    return jnp.concatenate([first, first, last], axis=0)


def fifth_root(mass):
    root = jnp.exp(0.2 * jnp.log(mass))
    square = root * root
    return 0.8 * root + 0.2 * mass / (square * square)


def store_source(nat_ref, start, count, columns, mass):
    cx, cy, cz = [column - 0.5 for column in columns]
    one = jnp.ones_like(cx)
    for kind, line in enumerate((cx, cy, cz, cx, cy, cz, one, fifth_root(mass))):
        nat_ref[start + kind * 8 : start + kind * 8 + count, :] = line


def pair_sums(sides, pieces=()):
    rows = 32
    steps = []
    for target, sources, roots, total, base in sides:
        count = roots.shape[0]
        for first in range(0, count, 2):
            steps.append((target, sources, roots, total, base, first, min(2, count - first), count))

    def product(step):
        target, sources, _, _, _, first, width, _ = step
        right = sources[:, first * LANES : (first + width) * LANES]
        return jnp.dot(target[...], right, preferred_element_type=F32)

    ready = product(steps[0])
    chunks = None
    for number, (_, _, roots, total, base, first, width, count) in enumerate(steps):
        squared = ready
        if number + 1 < len(steps):
            ready = product(steps[number + 1])
        if first == 0:
            chunks = [None] * (LANES // rows)
            if base is not None:
                chunks = [base[r * rows : (r + 1) * rows, :] for r in range(len(chunks))]
        limits = []
        for k in range(width):
            root = roots[first + k : first + k + 1, :]
            reach = 4.0 * root
            limits.append(
                [jnp.broadcast_to(line, (rows, LANES)) for line in (root, reach, reach * reach)]
            )
        for r in range(len(chunks)):
            for k, (root, reach, most) in enumerate(limits):
                t = squared[r * rows : (r + 1) * rows, k * LANES : (k + 1) * LANES]
                t = jnp.maximum(jnp.minimum(t, most), 1e-12)
                u = t * lax.rsqrt(t)
                f = reach - u
                f = f * f
                f = f * f
                term = f * (root + u)
                chunks[r] = term if chunks[r] is None else chunks[r] + term
        if first + width == count:
            for r, chunk in enumerate(chunks):
                total[r * rows : (r + 1) * rows, :] = chunk
        if number < len(pieces) and pieces[number] is not None:
            pieces[number]()
    for piece in pieces[len(steps) :]:
        piece()


def column_sums(totals):
    lane = lax.broadcasted_iota(jnp.int32, (LANES, LANES), 1)
    columns = jnp.zeros((LANES, LANES), F32)
    for k, total in enumerate(totals):
        columns = jnp.where(lane == k, jnp.sum(total, axis=1, keepdims=True), columns)
    return columns.T[: len(totals), :]


def square_mask():
    kind = lax.broadcasted_iota(jnp.int32, (8, LANES), 0)
    return (kind >= 3) & (kind < 6)


def shift_rows(step_x, step_y):
    kind = lax.broadcasted_iota(jnp.int32, (8, LANES), 0)
    along_x = jnp.where((kind == 0) | (kind == 3), float(step_x), 0.0)
    return along_x + jnp.where((kind == 1) | (kind == 4), float(step_y), 0.0)


def put_shifts(shift_ref):
    for code in range(9):
        shift_ref[code] = shift_rows(code // 3 - 1, code % 3 - 1)


def put_source(near_ref, root_ref, number, k, line, shift, squares):
    root = jnp.broadcast_to(line[7:8], line.shape)
    near_ref[number, :, k * LANES : (k + 1) * LANES] = source_matrix(line + shift, root, squares)
    root_ref[number, k : k + 1, :] = root[0:1]


def sides_of(count, first, end, mat_ref, near_ref, root_ref, total_ref, base_ref=None):
    lanes, rows = pl.ds(first * LANES, (end - first) * LANES), pl.ds(first, end - first)
    return [
        (
            mat_ref.at[n], near_ref.at[n, :, lanes], root_ref.at[n, rows], total_ref.at[n],
            None if base_ref is None else base_ref.at[n],
        )
        for n in range(count)
    ]


def put_moments(lhs_ref, ys, sums, mass, radius, rows):
    owners = lhs_ref.shape[0] // 2
    owner_ids = lax.broadcasted_iota(jnp.int32, (owners, LANES), 0)
    moment = mass * (sums * DENSITY_FACTOR / (radius * radius * radius))
    high_part = rounded(moment)
    low_part = moment - high_part
    owner = rows >> 7
    for y in ys:
        mine = jnp.broadcast_to(owner[y : y + 1, :], owner_ids.shape) == owner_ids
        lhs_ref[:, y * LANES : (y + 1) * LANES] = jnp.concatenate(
            [
                jnp.where(mine, jnp.broadcast_to(part[y : y + 1, :], mine.shape), 0.0)
                for part in (high_part, low_part)
            ],
            axis=0,
        ).astype(BF16)


def inner_moments(total_ref, first, hot, lhs_ref, sums, mass, radius, rows):
    last = mass.shape[0] - 1
    put_moments(lhs_ref, range(1, last), sums, mass, radius, rows)
    lanes = slice(LANES, last * LANES)
    product = lax.dot_general(hot[:, lanes], lhs_ref[:, lanes], NT, preferred_element_type=F32)
    total_ref[...] = product if first else total_ref[...] + product


def start_rim(
    src_ref, pos_ref, mass_ref, smooth_ref, middle_ref, rows_ref, hot_ref,
    mat_ref, self_ref, moment_ref, tgt_ref, near_ref, root_ref, lhs_ref,
):
    blocks_x, blocks_y, _ = mass_ref.shape
    squares = square_mask()
    rim = [(x, side * (blocks_y - 1)) for x in range(blocks_x) for side in range(2)]
    for x in range(blocks_x):
        lines = target_rows([pos_ref[c, x] for c in range(3)], smooth_ref[x])
        for row, line in enumerate(lines):
            tgt_ref[x, row * blocks_y : (row + 1) * blocks_y, :] = line
    for n, (x, y) in enumerate(rim):
        mat_ref[n] = target_matrix(tgt_ref[x, pl.ds(y, 24, stride=blocks_y), :])
    for n, (x, y) in enumerate(rim):
        put_source(near_ref, root_ref, n, 0, src_ref[(x + 1) * blocks_y + y], 0.0, squares)

    def middle_moments(turn):
        x = turn + 1
        inner_moments(
            moment_ref, turn == 0, hot_ref[x], lhs_ref.at[turn], middle_ref[turn],
            mass_ref[x], smooth_ref[x], rows_ref[x],
        )

    pair_sums(
        sides_of(len(rim), 0, 1, mat_ref, near_ref, root_ref, self_ref),
        [functools.partial(middle_moments, turn) for turn in range(blocks_x - 2)],
    )


def block_pairs(
    listed, x_first, x_step, x_count, known_ref, code_ref, pos_ref, mass_ref, smooth_ref, prev_ref, next_ref,
    out_ref, src_ref, nat_ref, shift_ref, tgt_ref, mat_ref, near_ref, root_ref, total_ref,
    ahead=None,
):
    blocks_x, blocks_y, _ = mass_ref.shape
    for xe in range(blocks_x + 2):
        if xe == 0 or xe == blocks_x + 1:
            ref = prev_ref if xe == 0 else next_ref
            if ref is None:
                continue
            store_source(nat_ref, xe * 64, blocks_y, [ref[c] for c in range(3)], ref[3])
        elif known_ref is None:
            columns = [pos_ref[c, xe - 1] for c in range(3)]
            store_source(nat_ref, xe * 64, blocks_y, columns, mass_ref[xe - 1])
        else:
            part = pl.ds(xe * blocks_y, blocks_y)
            src_ref[part] = known_ref[part]
            continue
        for y in range(blocks_y):
            src_ref[xe * blocks_y + y] = nat_ref[pl.ds(xe * 64 + y, 8, stride=8), :]
    put_shifts(shift_ref)
    squares = square_mask()
    blocks = [(turn, y) for turn in range(x_count) for y in range(1, blocks_y - 1)]
    for turn in range(x_count):
        x = x_first + turn * x_step
        lines = target_rows([pos_ref[c, x] for c in range(3)], smooth_ref[x])
        for row, line in enumerate(lines):
            tgt_ref[turn, row * blocks_y : (row + 1) * blocks_y, :] = line
    for number, (turn, y) in enumerate(blocks):
        mat_ref[number] = target_matrix(tgt_ref[turn, pl.ds(y, 24, stride=blocks_y), :])
    for number, (turn, y) in enumerate(blocks):
        line = src_ref[(x_first + turn * x_step + 1) * blocks_y + y]
        put_source(near_ref, root_ref, number, 0, line, 0.0, squares)
    pair_sums(sides_of(len(blocks), 0, 1, mat_ref, near_ref, root_ref, total_ref))
    if ahead is not None:
        ahead()
    words = code_ref[...]
    for number, (turn, y) in enumerate(blocks):
        x = x_first + turn * x_step
        word = words[x, y]
        for k in range(1, listed):
            code = (word >> (4 * k)) & 15
            step_x = (code * 11) >> 5
            line = src_ref[(x + step_x) * blocks_y + y + code - 3 * step_x - 1]
            put_source(near_ref, root_ref, number, k, line, shift_ref[code], squares)
    inner = blocks_y - 2
    per_row = inner * (listed // 2)

    def row_sums(turn):
        sums = column_sums([total_ref[turn * inner + k] for k in range(inner)])
        out_ref[turn, 1 : blocks_y - 1, :] = sums

    pieces = [None] * (x_count * per_row + 1)
    for turn in range(x_count):
        pieces[(turn + 1) * per_row] = functools.partial(row_sums, turn)
    sides = sides_of(len(blocks), 1, listed, mat_ref, near_ref, root_ref, total_ref, total_ref)
    pair_sums(sides, pieces)


def middle_kernel(
    listed, code_ref, pos_ref, mass_ref, smooth_ref, group_ref, row_ref, column_ref, out_ref, src_ref, *scratch
):
    blocks_x, blocks_y, _ = mass_ref.shape
    for side in range(2):
        y = side * (blocks_y - 1)
        for x in range(blocks_x):
            for c in range(3):
                column_ref[side, c, x : x + 1, :] = pos_ref[c, x, y : y + 1, :]
            column_ref[side, 3, x : x + 1, :] = mass_ref[x, y : y + 1, :]
    block_pairs(
        listed, 1, 1, blocks_x - 2, None, code_ref, pos_ref, mass_ref, smooth_ref, None, None,
        out_ref, src_ref, *scratch,
    )


def edge_kernel(
    listed, code_ref, pos_ref, mass_ref, smooth_ref, prev_ref, next_ref, known_ref,
    middle_ref, rows_ref, hot_ref,
    out_ref, src_ref, rim_mat_ref, self_ref, moment_ref,
    rim_tgt_ref, rim_near_ref, rim_root_ref, lhs_ref, *scratch
):
    blocks_x = mass_ref.shape[0]
    ahead = functools.partial(
        start_rim, src_ref, pos_ref, mass_ref, smooth_ref, middle_ref, rows_ref, hot_ref,
        rim_mat_ref, self_ref, moment_ref, rim_tgt_ref, rim_near_ref, rim_root_ref, lhs_ref,
    )
    block_pairs(
        listed, 0, blocks_x - 1, 2, known_ref, code_ref, pos_ref, mass_ref, smooth_ref, prev_ref, next_ref,
        out_ref, src_ref, *scratch, ahead=ahead,
    )


def pair_scratch(blocks_x, blocks_y, x_count, listed):
    return [
        pltpu.VMEM(((blocks_x + 2) * 64, LANES), F32),
        pltpu.VMEM((9, 8, LANES), F32),
        pltpu.VMEM((x_count, 24 * blocks_y, LANES), F32),
    ] + product_scratch(x_count * (blocks_y - 2), listed)


def product_scratch(blocks, listed):
    return [
        pltpu.VMEM((blocks, LANES, 48), BF16),
        pltpu.VMEM((blocks, 48, listed * LANES), BF16),
        pltpu.VMEM((blocks, 8, LANES), F32),
        pltpu.VMEM((blocks, LANES, LANES), F32),
    ]


def rim_kernel(
    listed, code_ref, middle_ref, edge_ref, known_ref, mat_ref, self_ref, moment_ref,
    mass_ref, smooth_ref, low_ref, high_ref, rows_ref, hot_ref, early_ref,
    sum_ref, table_ref, nat_ref, src_ref, md_ref, lhs_ref, total_moment_ref,
    shift_ref, near_ref, root_ref, total_ref,
):
    blocks_x, blocks_y, _ = mass_ref.shape
    owners = early_ref.shape[0]
    wide = blocks_x + 2
    last = blocks_y - 1
    for side, ref in enumerate((low_ref, high_ref)):
        store_source(nat_ref, side * 64, wide, [ref[c] for c in range(3)], ref[3])
        for xe in range(wide):
            ghost = 5 * side * wide + xe
            src_ref[ghost] = nat_ref[pl.ds(side * 64 + xe, 8, stride=8), :]
            for k in range(2):
                y = k + side * (blocks_y - 2)
                place = (1 + k + 2 * side) * wide + xe
                src_ref[place] = known_ref[xe * blocks_y + y]
    put_shifts(shift_ref)
    squares = square_mask()
    for x in range(blocks_x):
        edge = x == 0 or x == blocks_x - 1
        sum_ref[x] = (edge_ref if edge else middle_ref)[(1 if x else 0) if edge else x - 1]
    total_moment_ref[...] = moment_ref[...]
    for x in (0, blocks_x - 1):
        inner_moments(
            total_moment_ref, False, hot_ref[x], lhs_ref.at[x], sum_ref[x],
            mass_ref[x], smooth_ref[x], rows_ref[x],
        )
    words = code_ref[...]
    for x in range(blocks_x):
        for side in range(2):
            word = words[x, side * last]
            for k in range(1, listed):
                code = (word >> (4 * k)) & 15
                step_x = (code * 11) >> 5
                line = src_ref[(3 * side + code - 3 * step_x) * wide + x + step_x]
                put_source(near_ref, root_ref, 2 * x + side, k, line, shift_ref[code], squares)
    pair_sums(sides_of(2 * blocks_x, 1, listed, mat_ref, near_ref, root_ref, total_ref, self_ref))
    sums = column_sums([total_ref[number] for number in range(2 * blocks_x)])
    for x in range(blocks_x):
        for side in range(2):
            y = side * last
            sum_ref[x, y : y + 1, :] = sums[2 * x + side : 2 * x + side + 1, :]
        put_moments(lhs_ref.at[x], (0, last), sum_ref[x], mass_ref[x], smooth_ref[x], rows_ref[x])
    ends = [(x, slice(y * LANES, (y + 1) * LANES)) for x in range(blocks_x) for y in (0, last)]
    total = total_moment_ref[...] + lax.dot_general(
        jnp.concatenate([hot_ref[x, :, lanes] for x, lanes in ends], axis=1),
        jnp.concatenate([lhs_ref[x, :, lanes] for x, lanes in ends], axis=1),
        NT,
        preferred_element_type=F32,
    )
    total = total.T
    md_ref[...] = total[:owners] + total[owners:]
    core, my_chip = lax.axis_index("core"), lax.axis_index("chip")
    for other in range(2):
        for step in range(owners // 2):
            owner = 2 * (my_chip ^ step) + (core ^ other)
            table_ref[other, step, :EARLY, :] = early_ref[owner]
            table_ref[other, step, EARLY : EARLY + 1, :] = md_ref[pl.ds(owner, 1), :]


def swap(value, axis, step):
    count = lax.axis_size(axis)
    return lax.ppermute(value, axis, [(i, i ^ step) for i in range(count)])


def neighbours_of(low_edge, high_edge, axis, parity):
    count = lax.axis_size(axis)
    even = parity == 0
    inner = lax.ppermute(
        jnp.where(even, high_edge, low_edge), axis, [(i, i ^ 1) for i in range(count)]
    )
    outer = lax.ppermute(
        jnp.where(even, low_edge, high_edge),
        axis,
        [(i, (i + 1 if i & 1 else i - 1) % count) for i in range(count)],
    )
    return jnp.where(even, outer, inner), jnp.where(even, inner, outer)


def added(parts):
    while len(parts) > 1:
        parts = [sum(parts[k : k + 2][1:], parts[k]) for k in range(0, len(parts), 2)]
    return parts[0]


def to_owner(table):
    table = table[0] + swap(table[1], "core", 1)
    while table.shape[0] > 1:
        ways = min(4, table.shape[0])
        part = table.shape[0] // ways
        got = [
            swap(table[k * part : (k + 1) * part], "chip", k * part)
            for k in reversed(range(1, ways))
        ]
        table = added([table[:part]] + got)
    return table[0]


def summed(value, axis):
    count = lax.axis_size(axis)
    if count & (count - 1):
        return lax.psum(value, axis)
    step = 1
    while step < count:
        ways = min(4, count // step)
        value = added([value] + [swap(value, axis, k * step) for k in range(1, ways)])
        step *= ways
    return value


def shards(positions, velocities, masses, smoothing, neighbours, particle_group, group_row):
    blocks_x, blocks_y, block_len = masses.shape
    dom_count, sub_count = lax.axis_size("dom"), lax.axis_size("chip") * lax.axis_size("core")
    owners = sub_count
    chunk = blocks_y * block_len
    shape = jax.ShapeDtypeStruct
    listed = neighbours.shape[2]
    codes = sum(neighbours[:, :, k] << (4 * k) for k in range(listed))
    table_rows = group_row.reshape(-1, LANES)
    packed = jnp.concatenate([positions, masses[None]], axis=0)
    prev, following = neighbours_of(
        packed[:, 0], packed[:, blocks_x - 1], "dom", lax.axis_index("dom") & 1
    )
    sources = ((blocks_x + 2) * blocks_y, 8, LANES)
    columns, middle, own = pl.pallas_call(
        functools.partial(middle_kernel, listed),
        out_shape=(
            shape((2, 4, blocks_x, LANES), F32),
            shape((blocks_x - 2, blocks_y, LANES), F32),
            shape(sources, F32),
        ),
        in_specs=[VMEM] * 6,
        out_specs=(VMEM,) * 3,
        scratch_shapes=pair_scratch(blocks_x, blocks_y, blocks_x - 2, listed),
        compiler_params=params(),
        cost_estimate=pl.CostEstimate(
            flops=4_000_000_000, bytes_accessed=400_000, transcendentals=1_300_000
        ),
        name="middle_pairs",
    )(codes, positions, masses, smoothing, particle_group, table_rows)
    early, rows, hot = pl.pallas_call(
        functools.partial(moments_kernel, blocks_x * dom_count, blocks_y * sub_count),
        out_shape=(
            shape((owners, EARLY, LANES), F32),
            shape(masses.shape, jnp.int32),
            shape((blocks_x, LANES, chunk), BF16),
        ),
        in_specs=[VMEM] * 6,
        out_specs=(VMEM,) * 3,
        scratch_shapes=[
            pltpu.VMEM((blocks_x * EARLY * blocks_y, LANES), F32),
            pltpu.VMEM((blocks_x, owners * 2 * EARLY, chunk), BF16),
            pltpu.VMEM((owners * 2 * EARLY, LANES), F32),
        ],
        compiler_params=params(),
        cost_estimate=pl.CostEstimate(
            flops=2_000_000_000, bytes_accessed=1_400_000, transcendentals=0
        ),
        name="moments_by_row",
    )(middle, positions, velocities, masses, particle_group, table_rows)
    edges = [
        jnp.concatenate([prev[:, y : y + 1], columns[side], following[:, y : y + 1]], axis=1)
        for side, y in ((0, 0), (1, blocks_y - 1))
    ]
    low, high = neighbours_of(*edges, ("chip", "core"), lax.axis_index("core"))
    rims = 2 * blocks_x
    edge, known, rim_match, rim_self, middle_moment = pl.pallas_call(
        functools.partial(edge_kernel, listed),
        out_shape=(
            shape((2, blocks_y, LANES), F32),
            shape(sources, F32),
            shape((rims, LANES, 48), BF16),
            shape((rims, LANES, LANES), F32),
            shape((LANES, 2 * owners), F32),
        ),
        in_specs=[VMEM] * 10,
        out_specs=(VMEM,) * 5,
        scratch_shapes=[
            pltpu.VMEM((blocks_x, 24 * blocks_y, LANES), F32),
            pltpu.VMEM((rims, 48, LANES), BF16),
            pltpu.VMEM((rims, 8, LANES), F32),
            pltpu.VMEM((blocks_x - 2, 2 * owners, chunk), BF16),
        ]
        + pair_scratch(blocks_x, blocks_y, 2, listed),
        compiler_params=params(),
        cost_estimate=pl.CostEstimate(
            flops=4_000_000_000, bytes_accessed=400_000, transcendentals=1_300_000
        ),
        name="edge_pairs",
    )(codes, positions, masses, smoothing, prev, following, own, middle, rows, hot)
    sums, table = pl.pallas_call(
        functools.partial(rim_kernel, listed),
        out_shape=(shape(masses.shape, F32), shape((2, owners // 2, EARLY + 1, LANES), F32)),
        in_specs=[VMEM] * 14,
        out_specs=(VMEM, VMEM),
        scratch_shapes=[
            pltpu.VMEM((128, LANES), F32),
            pltpu.VMEM((6 * (blocks_x + 2), 8, LANES), F32),
            pltpu.VMEM((owners, LANES), F32),
            pltpu.VMEM((blocks_x, 2 * owners, chunk), BF16),
            pltpu.VMEM((LANES, 2 * owners), F32),
            pltpu.VMEM((9, 8, LANES), F32),
        ]
        + product_scratch(rims, listed)[1:],
        compiler_params=params(),
        cost_estimate=pl.CostEstimate(
            flops=200_000_000, bytes_accessed=400_000, transcendentals=400_000
        ),
        name="rim_pairs_and_table",
    )(
        codes, middle, edge, known, rim_match, rim_self, middle_moment,
        masses, smoothing, low, high, rows, hot, early,
    )
    density = sums * DENSITY_FACTOR / (smoothing * smoothing * smoothing)
    return (density, summed(to_owner(table), "dom"))


def solution(mesh):
    dom_count, sub_count = mesh.devices.shape
    mesh = jax.sharding.Mesh(
        mesh.devices.reshape(dom_count, sub_count // 2, 2), ("dom", "chip", "core")
    )
    sub = ("chip", "core")
    in_specs = (
        P(None, "dom", sub, None),
        P(None, "dom", sub, None),
        P("dom", sub, None),
        P("dom", sub, None),
        P("dom", sub, None),
        P("dom", sub, None),
        P(),
    )
    out_specs = (P("dom", sub, None), P(None, sub))
    return jax.shard_map(shards, mesh=mesh, in_specs=in_specs, out_specs=out_specs, check_vma=False)
```

```python
import functools
import math

import jax
import jax.numpy as jnp
from jax import lax
from jax.experimental import pallas as pl
from jax.experimental.pallas import tpu as pltpu
from jax.sharding import PartitionSpec as P

F32 = jnp.float32
BF16 = jnp.bfloat16
LANES = 128
EARLY = 16
DENSITY_FACTOR = 21.0 / (16.0 * math.pi) / 256.0
VMEM = pl.BlockSpec(memory_space=pltpu.VMEM)
NT = (((1,), (1,)), ((), ()))


def params():
    return pltpu.CompilerParams(vmem_limit_bytes=40 * 1024 * 1024)


def rounded(value):
    return value.astype(BF16).astype(F32)


def three_parts(value):
    first = rounded(value)
    rest = value - first
    second = rounded(rest)
    return first, second, rest - second


def spread(numbers, y, count):
    row = jnp.broadcast_to(numbers[y : y + 1, :].astype(F32), (16, LANES)).astype(BF16)
    return jnp.concatenate([row] * (count // 16), axis=0)


def row_numbers(count):
    return lax.broadcasted_iota(jnp.int32, (count, LANES), 0).astype(F32).astype(BF16)


def slot_one_hot(slots, y):
    return jnp.where(
        row_numbers(LANES) == spread(slots, y, LANES), jnp.ones((), BF16), jnp.zeros((), BF16)
    )


def moments_kernel(
    nx_total, ny_total, after_ref, pos_ref, vel_ref, mass_ref, group_ref, row_ref,
    table_ref, rows_ref, hot_ref, feat_ref, lhs_ref, total_ref,
):
    blocks_x, blocks_y, _ = mass_ref.shape
    owners = table_ref.shape[0]
    table_rows = row_ref.shape[0]
    base_x = (lax.axis_index("dom") * blocks_x).astype(F32)
    base_y = ((2 * lax.axis_index("chip") + lax.axis_index("core")) * blocks_y).astype(F32)
    y_iota = lax.broadcasted_iota(jnp.int32, (blocks_y, LANES), 0).astype(F32)

    def features_of(x):
        group = group_ref[x]
        low = group & (LANES - 1)
        high = group >> 7
        rows = jnp.zeros_like(group)
        for r in range(table_rows):
            line = jnp.broadcast_to(row_ref[r : r + 1, :], group.shape)
            picked = jnp.take_along_axis(line, low, axis=1)
            rows = jnp.where(high == r, picked, rows)
        rows_ref[x] = rows
        mass = mass_ref[x]
        gx = (base_x + float(x) + pos_ref[0, x]) / float(nx_total)
        gy = (base_y + y_iota + pos_ref[1, x]) / float(ny_total)
        gz = pos_ref[2, x]
        vx, vy, vz = vel_ref[0, x], vel_ref[1, x], vel_ref[2, x]
        mx, my, mz = mass * gx, mass * gy, mass * gz
        features = (
            mass, mx, my, mz, mass * vx, mass * vy, mass * vz,
            mass * (gy * vz - gz * vy), mass * (gz * vx - gx * vz), mass * (gx * vy - gy * vx),
            mx * gx, my * gy, mz * gz, mx * gy, mx * gz, my * gz,
        )
        for f, feature in enumerate(features):
            start = (x * EARLY + f) * blocks_y
            feat_ref[start : start + blocks_y, :] = feature

    def operands_of(x, y):
        lanes = slice(y * LANES, (y + 1) * LANES)
        feats = feat_ref[pl.ds(x * EARLY * blocks_y + y, EARLY, stride=blocks_y), :]
        high_part = rounded(feats)
        both = jnp.concatenate([high_part, feats - high_part], axis=0).astype(BF16)
        rows = rows_ref[x]
        owner_row = spread(rows >> 7, y, 2 * EARLY)
        for o in range(owners):
            lhs_ref[x, o * 2 * EARLY : (o + 1) * 2 * EARLY, lanes] = jnp.where(
                owner_row == jnp.asarray(o, BF16), both, jnp.zeros((), BF16)
            )
        hot_ref[x, :, lanes] = slot_one_hot(rows & (LANES - 1), y)

    def add_product(x):
        product = lax.dot_general(lhs_ref[x], hot_ref[x], NT, preferred_element_type=F32)
        total_ref[...] = product if x == 0 else total_ref[...] + product

    def finish():
        total = total_ref[...].reshape(owners, 2 * EARLY, LANES)
        table_ref[...] = total[:, :EARLY, :] + total[:, EARLY:, :]

    for x in range(blocks_x):
        features_of(x)
        for y in range(blocks_y):
            operands_of(x, y)
        add_product(x)
    finish()


def target_rows(pos, radius):
    weight = 4.0 / (radius * radius)
    cx, cy, cz = pos[0] - 0.5, pos[1] - 0.5, pos[2] - 0.5
    lines = (
        -2.0 * cx * weight, -2.0 * cy * weight, -2.0 * cz * weight,
        weight, weight, weight,
        (cx * cx + cy * cy + cz * cz) * weight, jnp.zeros_like(weight),
    )
    parts = [three_parts(line) for line in lines]
    return [part[k] for k in range(3) for part in parts]


def target_matrix(coef):
    one, two, three = coef[0:8], coef[8:16], coef[16:24]
    stacked = jnp.concatenate([one, one, two, two, one, three], axis=0)
    return stacked.T.astype(BF16)


def source_matrix(line, root, squares):
    value = jnp.where(squares, line * line, line) * (root * root)
    one, two, three = three_parts(value)
    first = jnp.concatenate([one, two], axis=0).astype(BF16)
    last = jnp.concatenate([three, one], axis=0).astype(BF16)
    return jnp.concatenate([first, first, last], axis=0)


def fifth_root(mass):
    root = jnp.exp(0.2 * jnp.log(mass))
    square = root * root
    return 0.8 * root + 0.2 * mass / (square * square)


def store_source(nat_ref, start, count, columns, mass):
    cx, cy, cz = [column - 0.5 for column in columns]
    one = jnp.ones_like(cx)
    for kind, line in enumerate((cx, cy, cz, cx, cy, cz, one, fifth_root(mass))):
        nat_ref[start + kind * 8 : start + kind * 8 + count, :] = line


def pair_sums(sides, pieces=()):
    rows = 32
    steps = []
    for target, sources, roots, total, base in sides:
        count = roots.shape[0]
        for first in range(0, count, 2):
            steps.append((target, sources, roots, total, base, first, min(2, count - first), count))

    def product(step):
        target, sources, _, _, _, first, width, _ = step
        right = sources[:, first * LANES : (first + width) * LANES]
        return jnp.dot(target[...], right, preferred_element_type=F32)

    ready = product(steps[0])
    chunks = None
    for number, (_, _, roots, total, base, first, width, count) in enumerate(steps):
        squared = ready
        if number + 1 < len(steps):
            ready = product(steps[number + 1])
        if first == 0:
            chunks = [None] * (LANES // rows)
            if base is not None:
                chunks = [base[r * rows : (r + 1) * rows, :] for r in range(len(chunks))]
        limits = []
        for k in range(width):
            root = roots[first + k : first + k + 1, :]
            reach = 4.0 * root
            limits.append(
                [jnp.broadcast_to(line, (rows, LANES)) for line in (root, reach, reach * reach)]
            )
        for r in range(len(chunks)):
            for k, (root, reach, most) in enumerate(limits):
                t = squared[r * rows : (r + 1) * rows, k * LANES : (k + 1) * LANES]
                t = jnp.maximum(jnp.minimum(t, most), 1e-12)
                u = t * lax.rsqrt(t)
                f = reach - u
                f = f * f
                f = f * f
                term = f * (root + u)
                chunks[r] = term if chunks[r] is None else chunks[r] + term
        if first + width == count:
            for r, chunk in enumerate(chunks):
                total[r * rows : (r + 1) * rows, :] = chunk
        if number < len(pieces) and pieces[number] is not None:
            pieces[number]()
    for piece in pieces[len(steps) :]:
        piece()


def column_sums(totals):
    lane = lax.broadcasted_iota(jnp.int32, (LANES, LANES), 1)
    columns = jnp.zeros((LANES, LANES), F32)
    for k, total in enumerate(totals):
        columns = jnp.where(lane == k, jnp.sum(total, axis=1, keepdims=True), columns)
    return columns.T[: len(totals), :]


def square_mask():
    kind = lax.broadcasted_iota(jnp.int32, (8, LANES), 0)
    return (kind >= 3) & (kind < 6)


def shift_rows(step_x, step_y):
    kind = lax.broadcasted_iota(jnp.int32, (8, LANES), 0)
    along_x = jnp.where((kind == 0) | (kind == 3), float(step_x), 0.0)
    return along_x + jnp.where((kind == 1) | (kind == 4), float(step_y), 0.0)


def put_shifts(shift_ref):
    for code in range(9):
        shift_ref[code] = shift_rows(code // 3 - 1, code % 3 - 1)


def put_source(near_ref, root_ref, number, k, line, shift, squares):
    root = jnp.broadcast_to(line[7:8], line.shape)
    near_ref[number, :, k * LANES : (k + 1) * LANES] = source_matrix(line + shift, root, squares)
    root_ref[number, k : k + 1, :] = root[0:1]


def sides_of(count, first, end, mat_ref, near_ref, root_ref, total_ref, base_ref=None):
    lanes, rows = pl.ds(first * LANES, (end - first) * LANES), pl.ds(first, end - first)
    return [
        (
            mat_ref.at[n], near_ref.at[n, :, lanes], root_ref.at[n, rows], total_ref.at[n],
            None if base_ref is None else base_ref.at[n],
        )
        for n in range(count)
    ]


def put_moments(lhs_ref, ys, sums, mass, radius, rows):
    owners = lhs_ref.shape[0] // 2
    owner_ids = lax.broadcasted_iota(jnp.int32, (owners, LANES), 0)
    moment = mass * (sums * DENSITY_FACTOR / (radius * radius * radius))
    high_part = rounded(moment)
    low_part = moment - high_part
    owner = rows >> 7
    for y in ys:
        mine = jnp.broadcast_to(owner[y : y + 1, :], owner_ids.shape) == owner_ids
        lhs_ref[:, y * LANES : (y + 1) * LANES] = jnp.concatenate(
            [
                jnp.where(mine, jnp.broadcast_to(part[y : y + 1, :], mine.shape), 0.0)
                for part in (high_part, low_part)
            ],
            axis=0,
        ).astype(BF16)


def inner_moments(total_ref, first, hot, lhs_ref, sums, mass, radius, rows):
    last = mass.shape[0] - 1
    put_moments(lhs_ref, range(1, last), sums, mass, radius, rows)
    lanes = slice(LANES, last * LANES)
    product = lax.dot_general(hot[:, lanes], lhs_ref[:, lanes], NT, preferred_element_type=F32)
    total_ref[...] = product if first else total_ref[...] + product


def start_rim(
    src_ref, pos_ref, mass_ref, smooth_ref, middle_ref, rows_ref, hot_ref,
    mat_ref, self_ref, moment_ref, tgt_ref, near_ref, root_ref, lhs_ref,
):
    blocks_x, blocks_y, _ = mass_ref.shape
    squares = square_mask()
    rim = [(x, side * (blocks_y - 1)) for x in range(blocks_x) for side in range(2)]
    for x in range(blocks_x):
        lines = target_rows([pos_ref[c, x] for c in range(3)], smooth_ref[x])
        for row, line in enumerate(lines):
            tgt_ref[x, row * blocks_y : (row + 1) * blocks_y, :] = line
    for n, (x, y) in enumerate(rim):
        mat_ref[n] = target_matrix(tgt_ref[x, pl.ds(y, 24, stride=blocks_y), :])
    for n, (x, y) in enumerate(rim):
        put_source(near_ref, root_ref, n, 0, src_ref[(x + 1) * blocks_y + y], 0.0, squares)

    def middle_moments(turn):
        x = turn + 1
        inner_moments(
            moment_ref, turn == 0, hot_ref[x], lhs_ref.at[turn], middle_ref[turn],
            mass_ref[x], smooth_ref[x], rows_ref[x],
        )

    pair_sums(
        sides_of(len(rim), 0, 1, mat_ref, near_ref, root_ref, self_ref),
        [functools.partial(middle_moments, turn) for turn in range(blocks_x - 2)],
    )


def block_pairs(
    listed, x_first, x_step, x_count, known_ref, code_ref, pos_ref, mass_ref, smooth_ref, prev_ref, next_ref,
    out_ref, src_ref, nat_ref, shift_ref, tgt_ref, mat_ref, near_ref, root_ref, total_ref,
    ahead=None,
):
    blocks_x, blocks_y, _ = mass_ref.shape
    for xe in range(blocks_x + 2):
        if xe == 0 or xe == blocks_x + 1:
            ref = prev_ref if xe == 0 else next_ref
            if ref is None:
                continue
            store_source(nat_ref, xe * 64, blocks_y, [ref[c] for c in range(3)], ref[3])
        elif known_ref is None:
            columns = [pos_ref[c, xe - 1] for c in range(3)]
            store_source(nat_ref, xe * 64, blocks_y, columns, mass_ref[xe - 1])
        else:
            part = pl.ds(xe * blocks_y, blocks_y)
            src_ref[part] = known_ref[part]
            continue
        for y in range(blocks_y):
            src_ref[xe * blocks_y + y] = nat_ref[pl.ds(xe * 64 + y, 8, stride=8), :]
    put_shifts(shift_ref)
    squares = square_mask()
    blocks = [(turn, y) for turn in range(x_count) for y in range(1, blocks_y - 1)]
    for turn in range(x_count):
        x = x_first + turn * x_step
        lines = target_rows([pos_ref[c, x] for c in range(3)], smooth_ref[x])
        for row, line in enumerate(lines):
            tgt_ref[turn, row * blocks_y : (row + 1) * blocks_y, :] = line
    for number, (turn, y) in enumerate(blocks):
        mat_ref[number] = target_matrix(tgt_ref[turn, pl.ds(y, 24, stride=blocks_y), :])
    for number, (turn, y) in enumerate(blocks):
        line = src_ref[(x_first + turn * x_step + 1) * blocks_y + y]
        put_source(near_ref, root_ref, number, 0, line, 0.0, squares)
    pair_sums(sides_of(len(blocks), 0, 1, mat_ref, near_ref, root_ref, total_ref))
    if ahead is not None:
        ahead()
    words = code_ref[...]
    for number, (turn, y) in enumerate(blocks):
        x = x_first + turn * x_step
        word = words[x, y]
        for k in range(1, listed):
            code = (word >> (4 * k)) & 15
            step_x = (code * 11) >> 5
            line = src_ref[(x + step_x) * blocks_y + y + code - 3 * step_x - 1]
            put_source(near_ref, root_ref, number, k, line, shift_ref[code], squares)
    inner = blocks_y - 2
    per_row = inner * (listed // 2)

    def row_sums(turn):
        sums = column_sums([total_ref[turn * inner + k] for k in range(inner)])
        out_ref[turn, 1 : blocks_y - 1, :] = sums

    pieces = [None] * (x_count * per_row + 1)
    for turn in range(x_count):
        pieces[(turn + 1) * per_row] = functools.partial(row_sums, turn)
    sides = sides_of(len(blocks), 1, listed, mat_ref, near_ref, root_ref, total_ref, total_ref)
    pair_sums(sides, pieces)


def middle_kernel(
    listed, code_ref, pos_ref, mass_ref, smooth_ref, group_ref, row_ref, column_ref, out_ref, src_ref, *scratch
):
    blocks_x, blocks_y, _ = mass_ref.shape
    for side in range(2):
        y = side * (blocks_y - 1)
        for x in range(blocks_x):
            for c in range(3):
                column_ref[side, c, x : x + 1, :] = pos_ref[c, x, y : y + 1, :]
            column_ref[side, 3, x : x + 1, :] = mass_ref[x, y : y + 1, :]
    block_pairs(
        listed, 1, 1, blocks_x - 2, None, code_ref, pos_ref, mass_ref, smooth_ref, None, None,
        out_ref, src_ref, *scratch,
    )


def edge_kernel(
    listed, code_ref, pos_ref, mass_ref, smooth_ref, prev_ref, next_ref, known_ref,
    middle_ref, rows_ref, hot_ref,
    out_ref, src_ref, rim_mat_ref, self_ref, moment_ref,
    rim_tgt_ref, rim_near_ref, rim_root_ref, lhs_ref, *scratch
):
    blocks_x = mass_ref.shape[0]
    ahead = functools.partial(
        start_rim, src_ref, pos_ref, mass_ref, smooth_ref, middle_ref, rows_ref, hot_ref,
        rim_mat_ref, self_ref, moment_ref, rim_tgt_ref, rim_near_ref, rim_root_ref, lhs_ref,
    )
    block_pairs(
        listed, 0, blocks_x - 1, 2, known_ref, code_ref, pos_ref, mass_ref, smooth_ref, prev_ref, next_ref,
        out_ref, src_ref, *scratch, ahead=ahead,
    )


def pair_scratch(blocks_x, blocks_y, x_count, listed):
    return [
        pltpu.VMEM(((blocks_x + 2) * 64, LANES), F32),
        pltpu.VMEM((9, 8, LANES), F32),
        pltpu.VMEM((x_count, 24 * blocks_y, LANES), F32),
    ] + product_scratch(x_count * (blocks_y - 2), listed)


def product_scratch(blocks, listed):
    return [
        pltpu.VMEM((blocks, LANES, 48), BF16),
        pltpu.VMEM((blocks, 48, listed * LANES), BF16),
        pltpu.VMEM((blocks, 8, LANES), F32),
        pltpu.VMEM((blocks, LANES, LANES), F32),
    ]


def rim_kernel(
    listed, code_ref, middle_ref, edge_ref, known_ref, mat_ref, self_ref, moment_ref,
    mass_ref, smooth_ref, low_ref, high_ref, rows_ref, hot_ref, early_ref,
    sum_ref, table_ref, nat_ref, src_ref, md_ref, lhs_ref, total_moment_ref,
    shift_ref, near_ref, root_ref, total_ref,
):
    blocks_x, blocks_y, _ = mass_ref.shape
    owners = early_ref.shape[0]
    wide = blocks_x + 2
    last = blocks_y - 1
    for side, ref in enumerate((low_ref, high_ref)):
        store_source(nat_ref, side * 64, wide, [ref[c] for c in range(3)], ref[3])
        for xe in range(wide):
            ghost = 5 * side * wide + xe
            src_ref[ghost] = nat_ref[pl.ds(side * 64 + xe, 8, stride=8), :]
            for k in range(2):
                y = k + side * (blocks_y - 2)
                place = (1 + k + 2 * side) * wide + xe
                src_ref[place] = known_ref[xe * blocks_y + y]
    put_shifts(shift_ref)
    squares = square_mask()
    for x in range(blocks_x):
        edge = x == 0 or x == blocks_x - 1
        sum_ref[x] = (edge_ref if edge else middle_ref)[(1 if x else 0) if edge else x - 1]
    total_moment_ref[...] = moment_ref[...]
    for x in (0, blocks_x - 1):
        inner_moments(
            total_moment_ref, False, hot_ref[x], lhs_ref.at[x], sum_ref[x],
            mass_ref[x], smooth_ref[x], rows_ref[x],
        )
    words = code_ref[...]
    for x in range(blocks_x):
        for side in range(2):
            word = words[x, side * last]
            for k in range(1, listed):
                code = (word >> (4 * k)) & 15
                step_x = (code * 11) >> 5
                line = src_ref[(3 * side + code - 3 * step_x) * wide + x + step_x]
                put_source(near_ref, root_ref, 2 * x + side, k, line, shift_ref[code], squares)
    pair_sums(sides_of(2 * blocks_x, 1, listed, mat_ref, near_ref, root_ref, total_ref, self_ref))
    sums = column_sums([total_ref[number] for number in range(2 * blocks_x)])
    for x in range(blocks_x):
        for side in range(2):
            y = side * last
            sum_ref[x, y : y + 1, :] = sums[2 * x + side : 2 * x + side + 1, :]
        put_moments(lhs_ref.at[x], (0, last), sum_ref[x], mass_ref[x], smooth_ref[x], rows_ref[x])
    ends = [(x, slice(y * LANES, (y + 1) * LANES)) for x in range(blocks_x) for y in (0, last)]
    total = total_moment_ref[...] + lax.dot_general(
        jnp.concatenate([hot_ref[x, :, lanes] for x, lanes in ends], axis=1),
        jnp.concatenate([lhs_ref[x, :, lanes] for x, lanes in ends], axis=1),
        NT,
        preferred_element_type=F32,
    )
    total = total.T
    md_ref[...] = total[:owners] + total[owners:]
    core, my_chip = lax.axis_index("core"), lax.axis_index("chip")
    for other in range(2):
        for step in range(owners // 2):
            owner = 2 * (my_chip ^ step) + (core ^ other)
            table_ref[other, step, :EARLY, :] = early_ref[owner]
            table_ref[other, step, EARLY : EARLY + 1, :] = md_ref[pl.ds(owner, 1), :]


def swap(value, axis, step):
    count = lax.axis_size(axis)
    return lax.ppermute(value, axis, [(i, i ^ step) for i in range(count)])


def neighbours_of(low_edge, high_edge, axis, parity):
    count = lax.axis_size(axis)
    odd = parity == 1
    outer = lax.ppermute(
        jnp.where(odd, high_edge, low_edge),
        axis,
        [(i, (i + 1 if i & 1 else i - 1) % count) for i in range(count)],
    )
    inner = lax.ppermute(
        jnp.where(odd, low_edge, high_edge), axis, [(i, i ^ 1) for i in range(count)]
    )
    return jnp.where(odd, inner, outer), jnp.where(odd, outer, inner)


def added(parts):
    while len(parts) > 1:
        parts = [sum(parts[k : k + 2][1:], parts[k]) for k in range(0, len(parts), 2)]
    return parts[0]


def to_owner(table):
    table = table[0] + swap(table[1], "core", 1)
    while table.shape[0] > 1:
        ways = min(4, table.shape[0])
        part = table.shape[0] // ways
        got = [
            swap(table[k * part : (k + 1) * part], "chip", k * part)
            for k in reversed(range(1, ways))
        ]
        table = added([table[:part]] + got)
    return table[0]


def summed(value, axis):
    count = lax.axis_size(axis)
    if count & (count - 1):
        return lax.psum(value, axis)
    step = 1
    while step < count:
        ways = min(4, count // step)
        value = added([value] + [swap(value, axis, k * step) for k in range(1, ways)])
        step *= ways
    return value


def shards(positions, velocities, masses, smoothing, neighbours, particle_group, group_row):
    blocks_x, blocks_y, block_len = masses.shape
    dom_count, sub_count = lax.axis_size("dom"), lax.axis_size("chip") * lax.axis_size("core")
    owners = sub_count
    chunk = blocks_y * block_len
    shape = jax.ShapeDtypeStruct
    listed = neighbours.shape[2]
    codes = sum(neighbours[:, :, k] << (4 * k) for k in range(listed))
    table_rows = group_row.reshape(-1, LANES)
    packed = jnp.concatenate([positions, masses[None]], axis=0)
    prev, following = neighbours_of(
        packed[:, 0], packed[:, blocks_x - 1], "dom", lax.axis_index("dom") & 1
    )
    sources = ((blocks_x + 2) * blocks_y, 8, LANES)
    columns, middle, own = pl.pallas_call(
        functools.partial(middle_kernel, listed),
        out_shape=(
            shape((2, 4, blocks_x, LANES), F32),
            shape((blocks_x - 2, blocks_y, LANES), F32),
            shape(sources, F32),
        ),
        in_specs=[VMEM] * 6,
        out_specs=(VMEM,) * 3,
        scratch_shapes=pair_scratch(blocks_x, blocks_y, blocks_x - 2, listed),
        compiler_params=params(),
        cost_estimate=pl.CostEstimate(
            flops=4_000_000_000, bytes_accessed=400_000, transcendentals=1_300_000
        ),
        name="middle_pairs",
    )(codes, positions, masses, smoothing, particle_group, table_rows)
    early, rows, hot = pl.pallas_call(
        functools.partial(moments_kernel, blocks_x * dom_count, blocks_y * sub_count),
        out_shape=(
            shape((owners, EARLY, LANES), F32),
            shape(masses.shape, jnp.int32),
            shape((blocks_x, LANES, chunk), BF16),
        ),
        in_specs=[VMEM] * 6,
        out_specs=(VMEM,) * 3,
        scratch_shapes=[
            pltpu.VMEM((blocks_x * EARLY * blocks_y, LANES), F32),
            pltpu.VMEM((blocks_x, owners * 2 * EARLY, chunk), BF16),
            pltpu.VMEM((owners * 2 * EARLY, LANES), F32),
        ],
        compiler_params=params(),
        cost_estimate=pl.CostEstimate(
            flops=2_000_000_000, bytes_accessed=1_400_000, transcendentals=0
        ),
        name="moments_by_row",
    )(middle, positions, velocities, masses, particle_group, table_rows)
    edges = [
        jnp.concatenate([prev[:, y : y + 1], columns[side], following[:, y : y + 1]], axis=1)
        for side, y in ((0, 0), (1, blocks_y - 1))
    ]
    low, high = neighbours_of(*edges, ("chip", "core"), lax.axis_index("core"))
    rims = 2 * blocks_x
    edge, known, rim_match, rim_self, middle_moment = pl.pallas_call(
        functools.partial(edge_kernel, listed),
        out_shape=(
            shape((2, blocks_y, LANES), F32),
            shape(sources, F32),
            shape((rims, LANES, 48), BF16),
            shape((rims, LANES, LANES), F32),
            shape((LANES, 2 * owners), F32),
        ),
        in_specs=[VMEM] * 10,
        out_specs=(VMEM,) * 5,
        scratch_shapes=[
            pltpu.VMEM((blocks_x, 24 * blocks_y, LANES), F32),
            pltpu.VMEM((rims, 48, LANES), BF16),
            pltpu.VMEM((rims, 8, LANES), F32),
            pltpu.VMEM((blocks_x - 2, 2 * owners, chunk), BF16),
        ]
        + pair_scratch(blocks_x, blocks_y, 2, listed),
        compiler_params=params(),
        cost_estimate=pl.CostEstimate(
            flops=4_000_000_000, bytes_accessed=400_000, transcendentals=1_300_000
        ),
        name="edge_pairs",
    )(codes, positions, masses, smoothing, prev, following, own, middle, rows, hot)
    sums, table = pl.pallas_call(
        functools.partial(rim_kernel, listed),
        out_shape=(shape(masses.shape, F32), shape((2, owners // 2, EARLY + 1, LANES), F32)),
        in_specs=[VMEM] * 14,
        out_specs=(VMEM, VMEM),
        scratch_shapes=[
            pltpu.VMEM((128, LANES), F32),
            pltpu.VMEM((6 * (blocks_x + 2), 8, LANES), F32),
            pltpu.VMEM((owners, LANES), F32),
            pltpu.VMEM((blocks_x, 2 * owners, chunk), BF16),
            pltpu.VMEM((LANES, 2 * owners), F32),
            pltpu.VMEM((9, 8, LANES), F32),
        ]
        + product_scratch(rims, listed)[1:],
        compiler_params=params(),
        cost_estimate=pl.CostEstimate(
            flops=200_000_000, bytes_accessed=400_000, transcendentals=400_000
        ),
        name="rim_pairs_and_table",
    )(
        codes, middle, edge, known, rim_match, rim_self, middle_moment,
        masses, smoothing, low, high, rows, hot, early,
    )
    density = sums * DENSITY_FACTOR / (smoothing * smoothing * smoothing)
    return (density, summed(to_owner(table), "dom"))


def solution(mesh):
    dom_count, sub_count = mesh.devices.shape
    mesh = jax.sharding.Mesh(
        mesh.devices.reshape(dom_count, sub_count // 2, 2), ("dom", "chip", "core")
    )
    sub = ("chip", "core")
    in_specs = (
        P(None, "dom", sub, None),
        P(None, "dom", sub, None),
        P("dom", sub, None),
        P("dom", sub, None),
        P("dom", sub, None),
        P("dom", sub, None),
        P(),
    )
    out_specs = (P("dom", sub, None), P(None, sub))
    return jax.shard_map(shards, mesh=mesh, in_specs=in_specs, out_specs=out_specs, check_vma=False)
```

```python
import functools
import math

import jax
import jax.numpy as jnp
from jax import lax
from jax.experimental import pallas as pl
from jax.experimental.pallas import tpu as pltpu
from jax.sharding import PartitionSpec as P

F32 = jnp.float32
BF16 = jnp.bfloat16
LANES = 128
EARLY = 16
DENSITY_FACTOR = 21.0 / (16.0 * math.pi) / 256.0
VMEM = pl.BlockSpec(memory_space=pltpu.VMEM)
NT = (((1,), (1,)), ((), ()))


def params():
    return pltpu.CompilerParams(vmem_limit_bytes=40 * 1024 * 1024)


def rounded(value):
    return value.astype(BF16).astype(F32)


def three_parts(value):
    first = rounded(value)
    rest = value - first
    second = rounded(rest)
    return first, second, rest - second


def spread(numbers, y, count):
    row = jnp.broadcast_to(numbers[y : y + 1, :].astype(F32), (16, LANES)).astype(BF16)
    return jnp.concatenate([row] * (count // 16), axis=0)


def row_numbers(count):
    return lax.broadcasted_iota(jnp.int32, (count, LANES), 0).astype(F32).astype(BF16)


def slot_one_hot(slots, y):
    return jnp.where(
        row_numbers(LANES) == spread(slots, y, LANES), jnp.ones((), BF16), jnp.zeros((), BF16)
    )


def moments_kernel(
    nx_total, ny_total, after_ref, pos_ref, vel_ref, mass_ref, group_ref, row_ref,
    table_ref, rows_ref, hot_ref, feat_ref, lhs_ref, total_ref,
):
    blocks_x, blocks_y, _ = mass_ref.shape
    owners = table_ref.shape[0]
    table_rows = row_ref.shape[0]
    base_x = (lax.axis_index("dom") * blocks_x).astype(F32)
    base_y = ((2 * lax.axis_index("chip") + lax.axis_index("core")) * blocks_y).astype(F32)
    y_iota = lax.broadcasted_iota(jnp.int32, (blocks_y, LANES), 0).astype(F32)

    def features_of(x):
        group = group_ref[x]
        low = group & (LANES - 1)
        high = group >> 7
        rows = jnp.zeros_like(group)
        for r in range(table_rows):
            line = jnp.broadcast_to(row_ref[r : r + 1, :], group.shape)
            picked = jnp.take_along_axis(line, low, axis=1)
            rows = jnp.where(high == r, picked, rows)
        rows_ref[x] = rows
        mass = mass_ref[x]
        gx = (base_x + float(x) + pos_ref[0, x]) / float(nx_total)
        gy = (base_y + y_iota + pos_ref[1, x]) / float(ny_total)
        gz = pos_ref[2, x]
        vx, vy, vz = vel_ref[0, x], vel_ref[1, x], vel_ref[2, x]
        mx, my, mz = mass * gx, mass * gy, mass * gz
        features = (
            mass, mx, my, mz, mass * vx, mass * vy, mass * vz,
            mass * (gy * vz - gz * vy), mass * (gz * vx - gx * vz), mass * (gx * vy - gy * vx),
            mx * gx, my * gy, mz * gz, mx * gy, mx * gz, my * gz,
        )
        for f, feature in enumerate(features):
            start = (x * EARLY + f) * blocks_y
            feat_ref[start : start + blocks_y, :] = feature

    def operands_of(x, y):
        lanes = slice(y * LANES, (y + 1) * LANES)
        feats = feat_ref[pl.ds(x * EARLY * blocks_y + y, EARLY, stride=blocks_y), :]
        high_part = rounded(feats)
        both = jnp.concatenate([high_part, feats - high_part], axis=0).astype(BF16)
        rows = rows_ref[x]
        owner_row = spread(rows >> 7, y, 2 * EARLY)
        for o in range(owners):
            lhs_ref[x, o * 2 * EARLY : (o + 1) * 2 * EARLY, lanes] = jnp.where(
                owner_row == jnp.asarray(o, BF16), both, jnp.zeros((), BF16)
            )
        hot_ref[x, :, lanes] = slot_one_hot(rows & (LANES - 1), y)

    def add_product(x):
        product = lax.dot_general(lhs_ref[x], hot_ref[x], NT, preferred_element_type=F32)
        total_ref[...] = product if x == 0 else total_ref[...] + product

    def finish():
        total = total_ref[...].reshape(owners, 2 * EARLY, LANES)
        table_ref[...] = total[:, :EARLY, :] + total[:, EARLY:, :]

    for x in range(blocks_x):
        features_of(x)
        for y in range(blocks_y):
            operands_of(x, y)
        add_product(x)
    finish()


def target_rows(pos, radius):
    weight = 4.0 / (radius * radius)
    cx, cy, cz = pos[0] - 0.5, pos[1] - 0.5, pos[2] - 0.5
    lines = (
        -2.0 * cx * weight, -2.0 * cy * weight, -2.0 * cz * weight,
        weight, weight, weight,
        (cx * cx + cy * cy + cz * cz) * weight, jnp.zeros_like(weight),
    )
    parts = [three_parts(line) for line in lines]
    return [part[k] for k in range(3) for part in parts]


def target_matrix(coef):
    one, two, three = coef[0:8], coef[8:16], coef[16:24]
    stacked = jnp.concatenate([one, one, two, two, one, three], axis=0)
    return stacked.T.astype(BF16)


def source_matrix(line, root, squares):
    value = jnp.where(squares, line * line, line) * (root * root)
    one, two, three = three_parts(value)
    first = jnp.concatenate([one, two], axis=0).astype(BF16)
    last = jnp.concatenate([three, one], axis=0).astype(BF16)
    return jnp.concatenate([first, first, last], axis=0)


def fifth_root(mass):
    root = jnp.exp(0.2 * jnp.log(mass))
    square = root * root
    return 0.8 * root + 0.2 * mass / (square * square)


def store_source(nat_ref, start, count, columns, mass):
    cx, cy, cz = [column - 0.5 for column in columns]
    one = jnp.ones_like(cx)
    for kind, line in enumerate((cx, cy, cz, cx, cy, cz, one, fifth_root(mass))):
        nat_ref[start + kind * 8 : start + kind * 8 + count, :] = line


def pair_sums(sides, pieces=()):
    rows = 32
    steps = []
    for target, sources, roots, total, base in sides:
        count = roots.shape[0]
        for first in range(0, count, 2):
            steps.append((target, sources, roots, total, base, first, min(2, count - first), count))

    def product(step):
        target, sources, _, _, _, first, width, _ = step
        right = sources[:, first * LANES : (first + width) * LANES]
        return jnp.dot(target[...], right, preferred_element_type=F32)

    ready = product(steps[0])
    chunks = None
    for number, (_, _, roots, total, base, first, width, count) in enumerate(steps):
        squared = ready
        if number + 1 < len(steps):
            ready = product(steps[number + 1])
        if first == 0:
            chunks = [None] * (LANES // rows)
            if base is not None:
                chunks = [base[r * rows : (r + 1) * rows, :] for r in range(len(chunks))]
        limits = []
        for k in range(width):
            root = roots[first + k : first + k + 1, :]
            reach = 4.0 * root
            limits.append(
                [jnp.broadcast_to(line, (rows, LANES)) for line in (root, reach, reach * reach)]
            )
        for r in range(len(chunks)):
            for k, (root, reach, most) in enumerate(limits):
                t = squared[r * rows : (r + 1) * rows, k * LANES : (k + 1) * LANES]
                t = jnp.maximum(jnp.minimum(t, most), 1e-12)
                u = t * lax.rsqrt(t)
                f = reach - u
                f = f * f
                f = f * f
                term = f * (root + u)
                chunks[r] = term if chunks[r] is None else chunks[r] + term
        if first + width == count:
            for r, chunk in enumerate(chunks):
                total[r * rows : (r + 1) * rows, :] = chunk
        if number < len(pieces) and pieces[number] is not None:
            pieces[number]()
    for piece in pieces[len(steps) :]:
        piece()


def column_sums(totals):
    lane = lax.broadcasted_iota(jnp.int32, (LANES, LANES), 1)
    columns = jnp.zeros((LANES, LANES), F32)
    for k, total in enumerate(totals):
        columns = jnp.where(lane == k, jnp.sum(total, axis=1, keepdims=True), columns)
    return columns.T[: len(totals), :]


def square_mask():
    kind = lax.broadcasted_iota(jnp.int32, (8, LANES), 0)
    return (kind >= 3) & (kind < 6)


def shift_rows(step_x, step_y):
    kind = lax.broadcasted_iota(jnp.int32, (8, LANES), 0)
    along_x = jnp.where((kind == 0) | (kind == 3), float(step_x), 0.0)
    return along_x + jnp.where((kind == 1) | (kind == 4), float(step_y), 0.0)


def put_shifts(shift_ref):
    for code in range(9):
        shift_ref[code] = shift_rows(code // 3 - 1, code % 3 - 1)


def put_source(near_ref, root_ref, number, k, line, shift, squares):
    root = jnp.broadcast_to(line[7:8], line.shape)
    near_ref[number, :, k * LANES : (k + 1) * LANES] = source_matrix(line + shift, root, squares)
    root_ref[number, k : k + 1, :] = root[0:1]


def sides_of(count, first, end, mat_ref, near_ref, root_ref, total_ref, base_ref=None):
    lanes, rows = pl.ds(first * LANES, (end - first) * LANES), pl.ds(first, end - first)
    return [
        (
            mat_ref.at[n], near_ref.at[n, :, lanes], root_ref.at[n, rows], total_ref.at[n],
            None if base_ref is None else base_ref.at[n],
        )
        for n in range(count)
    ]


def put_moments(lhs_ref, ys, sums, mass, radius, rows):
    owners = lhs_ref.shape[0] // 2
    owner_ids = lax.broadcasted_iota(jnp.int32, (owners, LANES), 0)
    moment = mass * (sums * DENSITY_FACTOR / (radius * radius * radius))
    high_part = rounded(moment)
    low_part = moment - high_part
    owner = rows >> 7
    for y in ys:
        mine = jnp.broadcast_to(owner[y : y + 1, :], owner_ids.shape) == owner_ids
        lhs_ref[:, y * LANES : (y + 1) * LANES] = jnp.concatenate(
            [
                jnp.where(mine, jnp.broadcast_to(part[y : y + 1, :], mine.shape), 0.0)
                for part in (high_part, low_part)
            ],
            axis=0,
        ).astype(BF16)


def inner_moments(total_ref, first, hot, lhs_ref, sums, mass, radius, rows):
    last = mass.shape[0] - 1
    put_moments(lhs_ref, range(1, last), sums, mass, radius, rows)
    lanes = slice(LANES, last * LANES)
    product = lax.dot_general(hot[:, lanes], lhs_ref[:, lanes], NT, preferred_element_type=F32)
    total_ref[...] = product if first else total_ref[...] + product


def start_rim(
    src_ref, pos_ref, mass_ref, smooth_ref, middle_ref, rows_ref, hot_ref,
    mat_ref, self_ref, moment_ref, tgt_ref, near_ref, root_ref, lhs_ref,
):
    blocks_x, blocks_y, _ = mass_ref.shape
    squares = square_mask()
    rim = [(x, side * (blocks_y - 1)) for x in range(blocks_x) for side in range(2)]
    for x in range(blocks_x):
        lines = target_rows([pos_ref[c, x] for c in range(3)], smooth_ref[x])
        for row, line in enumerate(lines):
            tgt_ref[x, row * blocks_y : (row + 1) * blocks_y, :] = line
    for n, (x, y) in enumerate(rim):
        mat_ref[n] = target_matrix(tgt_ref[x, pl.ds(y, 24, stride=blocks_y), :])
    for n, (x, y) in enumerate(rim):
        put_source(near_ref, root_ref, n, 0, src_ref[(x + 1) * blocks_y + y], 0.0, squares)

    def middle_moments(turn):
        x = turn + 1
        inner_moments(
            moment_ref, turn == 0, hot_ref[x], lhs_ref.at[turn], middle_ref[turn],
            mass_ref[x], smooth_ref[x], rows_ref[x],
        )

    pair_sums(
        sides_of(len(rim), 0, 1, mat_ref, near_ref, root_ref, self_ref),
        [functools.partial(middle_moments, turn) for turn in range(blocks_x - 2)],
    )


def block_pairs(
    listed, x_first, x_step, x_count, known_ref, code_ref, pos_ref, mass_ref, smooth_ref, prev_ref, next_ref,
    out_ref, src_ref, nat_ref, shift_ref, tgt_ref, mat_ref, near_ref, root_ref, total_ref,
    ahead=None,
):
    blocks_x, blocks_y, _ = mass_ref.shape
    for xe in range(blocks_x + 2):
        if xe == 0 or xe == blocks_x + 1:
            ref = prev_ref if xe == 0 else next_ref
            if ref is None:
                continue
            store_source(nat_ref, xe * 64, blocks_y, [ref[c] for c in range(3)], ref[3])
        elif known_ref is None:
            columns = [pos_ref[c, xe - 1] for c in range(3)]
            store_source(nat_ref, xe * 64, blocks_y, columns, mass_ref[xe - 1])
        else:
            part = pl.ds(xe * blocks_y, blocks_y)
            src_ref[part] = known_ref[part]
            continue
        for y in range(blocks_y):
            src_ref[xe * blocks_y + y] = nat_ref[pl.ds(xe * 64 + y, 8, stride=8), :]
    put_shifts(shift_ref)
    squares = square_mask()
    blocks = [(turn, y) for turn in range(x_count) for y in range(1, blocks_y - 1)]
    for turn in range(x_count):
        x = x_first + turn * x_step
        lines = target_rows([pos_ref[c, x] for c in range(3)], smooth_ref[x])
        for row, line in enumerate(lines):
            tgt_ref[turn, row * blocks_y : (row + 1) * blocks_y, :] = line
    for number, (turn, y) in enumerate(blocks):
        mat_ref[number] = target_matrix(tgt_ref[turn, pl.ds(y, 24, stride=blocks_y), :])
    for number, (turn, y) in enumerate(blocks):
        line = src_ref[(x_first + turn * x_step + 1) * blocks_y + y]
        put_source(near_ref, root_ref, number, 0, line, 0.0, squares)
    pair_sums(sides_of(len(blocks), 0, 1, mat_ref, near_ref, root_ref, total_ref))
    if ahead is not None:
        ahead()
    words = code_ref[...]
    for number, (turn, y) in enumerate(blocks):
        x = x_first + turn * x_step
        word = words[x, y]
        for k in range(1, listed):
            code = (word >> (4 * k)) & 15
            step_x = (code * 11) >> 5
            line = src_ref[(x + step_x) * blocks_y + y + code - 3 * step_x - 1]
            put_source(near_ref, root_ref, number, k, line, shift_ref[code], squares)
    inner = blocks_y - 2
    per_row = inner * (listed // 2)

    def row_sums(turn):
        sums = column_sums([total_ref[turn * inner + k] for k in range(inner)])
        out_ref[turn, 1 : blocks_y - 1, :] = sums

    pieces = [None] * (x_count * per_row + 1)
    for turn in range(x_count):
        pieces[(turn + 1) * per_row] = functools.partial(row_sums, turn)
    sides = sides_of(len(blocks), 1, listed, mat_ref, near_ref, root_ref, total_ref, total_ref)
    pair_sums(sides, pieces)


def middle_kernel(
    listed, code_ref, pos_ref, mass_ref, smooth_ref, group_ref, row_ref, column_ref, out_ref, src_ref, *scratch
):
    blocks_x, blocks_y, _ = mass_ref.shape
    for side in range(2):
        y = side * (blocks_y - 1)
        for x in range(blocks_x):
            for c in range(3):
                column_ref[side, c, x : x + 1, :] = pos_ref[c, x, y : y + 1, :]
            column_ref[side, 3, x : x + 1, :] = mass_ref[x, y : y + 1, :]
    block_pairs(
        listed, 1, 1, blocks_x - 2, None, code_ref, pos_ref, mass_ref, smooth_ref, None, None,
        out_ref, src_ref, *scratch,
    )


def edge_kernel(
    listed, code_ref, pos_ref, mass_ref, smooth_ref, prev_ref, next_ref, known_ref,
    middle_ref, rows_ref, hot_ref,
    out_ref, src_ref, rim_mat_ref, self_ref, moment_ref,
    rim_tgt_ref, rim_near_ref, rim_root_ref, lhs_ref, *scratch
):
    blocks_x = mass_ref.shape[0]
    ahead = functools.partial(
        start_rim, src_ref, pos_ref, mass_ref, smooth_ref, middle_ref, rows_ref, hot_ref,
        rim_mat_ref, self_ref, moment_ref, rim_tgt_ref, rim_near_ref, rim_root_ref, lhs_ref,
    )
    block_pairs(
        listed, 0, blocks_x - 1, 2, known_ref, code_ref, pos_ref, mass_ref, smooth_ref, prev_ref, next_ref,
        out_ref, src_ref, *scratch, ahead=ahead,
    )


def pair_scratch(blocks_x, blocks_y, x_count, listed):
    return [
        pltpu.VMEM(((blocks_x + 2) * 64, LANES), F32),
        pltpu.VMEM((9, 8, LANES), F32),
        pltpu.VMEM((x_count, 24 * blocks_y, LANES), F32),
    ] + product_scratch(x_count * (blocks_y - 2), listed)


def product_scratch(blocks, listed):
    return [
        pltpu.VMEM((blocks, LANES, 48), BF16),
        pltpu.VMEM((blocks, 48, listed * LANES), BF16),
        pltpu.VMEM((blocks, 8, LANES), F32),
        pltpu.VMEM((blocks, LANES, LANES), F32),
    ]


def rim_kernel(
    listed, code_ref, middle_ref, edge_ref, known_ref, mat_ref, self_ref, moment_ref,
    mass_ref, smooth_ref, low_ref, high_ref, rows_ref, hot_ref, early_ref,
    sum_ref, table_ref, nat_ref, src_ref, md_ref, lhs_ref, total_moment_ref,
    shift_ref, near_ref, root_ref, total_ref,
):
    blocks_x, blocks_y, _ = mass_ref.shape
    owners = early_ref.shape[0]
    wide = blocks_x + 2
    last = blocks_y - 1
    for side, ref in enumerate((low_ref, high_ref)):
        store_source(nat_ref, side * 64, wide, [ref[c] for c in range(3)], ref[3])
        for xe in range(wide):
            ghost = 5 * side * wide + xe
            src_ref[ghost] = nat_ref[pl.ds(side * 64 + xe, 8, stride=8), :]
            for k in range(2):
                y = k + side * (blocks_y - 2)
                place = (1 + k + 2 * side) * wide + xe
                src_ref[place] = known_ref[xe * blocks_y + y]
    put_shifts(shift_ref)
    squares = square_mask()
    for x in range(blocks_x):
        edge = x == 0 or x == blocks_x - 1
        sum_ref[x] = (edge_ref if edge else middle_ref)[(1 if x else 0) if edge else x - 1]
    total_moment_ref[...] = moment_ref[...]
    for x in (0, blocks_x - 1):
        inner_moments(
            total_moment_ref, False, hot_ref[x], lhs_ref.at[x], sum_ref[x],
            mass_ref[x], smooth_ref[x], rows_ref[x],
        )
    words = code_ref[...]
    for x in range(blocks_x):
        for side in range(2):
            word = words[x, side * last]
            for k in range(1, listed):
                code = (word >> (4 * k)) & 15
                step_x = (code * 11) >> 5
                line = src_ref[(3 * side + code - 3 * step_x) * wide + x + step_x]
                put_source(near_ref, root_ref, 2 * x + side, k, line, shift_ref[code], squares)
    pair_sums(sides_of(2 * blocks_x, 1, listed, mat_ref, near_ref, root_ref, total_ref, self_ref))
    sums = column_sums([total_ref[number] for number in range(2 * blocks_x)])
    for x in range(blocks_x):
        for side in range(2):
            y = side * last
            sum_ref[x, y : y + 1, :] = sums[2 * x + side : 2 * x + side + 1, :]
        put_moments(lhs_ref.at[x], (0, last), sum_ref[x], mass_ref[x], smooth_ref[x], rows_ref[x])
    ends = [(x, slice(y * LANES, (y + 1) * LANES)) for x in range(blocks_x) for y in (0, last)]
    total = total_moment_ref[...] + lax.dot_general(
        jnp.concatenate([hot_ref[x, :, lanes] for x, lanes in ends], axis=1),
        jnp.concatenate([lhs_ref[x, :, lanes] for x, lanes in ends], axis=1),
        NT,
        preferred_element_type=F32,
    )
    total = total.T
    md_ref[...] = total[:owners] + total[owners:]
    core, my_chip = lax.axis_index("core"), lax.axis_index("chip")
    for other in range(2):
        for step in range(owners // 2):
            owner = 2 * (my_chip ^ step) + (core ^ other)
            table_ref[other, step, :EARLY, :] = early_ref[owner]
            table_ref[other, step, EARLY : EARLY + 1, :] = md_ref[pl.ds(owner, 1), :]


def swap(value, axis, step):
    count = lax.axis_size(axis)
    return lax.ppermute(value, axis, [(i, i ^ step) for i in range(count)])


def neighbours_of(low_edge, high_edge, axis, odd):
    count = lax.axis_size(axis)
    inner = lax.ppermute(
        jnp.where(odd, low_edge, high_edge), axis, [(i, i ^ 1) for i in range(count)]
    )
    outer = lax.ppermute(
        jnp.where(odd, high_edge, low_edge),
        axis,
        [(i, (i + 1 if i & 1 else i - 1) % count) for i in range(count)],
    )
    return inner, outer


def added(parts):
    while len(parts) > 1:
        parts = [sum(parts[k : k + 2][1:], parts[k]) for k in range(0, len(parts), 2)]
    return parts[0]


def to_owner(table):
    table = table[0] + swap(table[1], "core", 1)
    while table.shape[0] > 1:
        ways = min(4, table.shape[0])
        part = table.shape[0] // ways
        got = [
            swap(table[k * part : (k + 1) * part], "chip", k * part)
            for k in reversed(range(1, ways))
        ]
        table = added([table[:part]] + got)
    return table[0]


def summed(value, axis):
    count = lax.axis_size(axis)
    if count & (count - 1):
        return lax.psum(value, axis)
    step = 1
    while step < count:
        ways = min(4, count // step)
        value = added([value] + [swap(value, axis, k * step) for k in range(1, ways)])
        step *= ways
    return value


def shards(positions, velocities, masses, smoothing, neighbours, particle_group, group_row):
    blocks_x, blocks_y, block_len = masses.shape
    dom_count, sub_count = lax.axis_size("dom"), lax.axis_size("chip") * lax.axis_size("core")
    owners = sub_count
    chunk = blocks_y * block_len
    shape = jax.ShapeDtypeStruct
    listed = neighbours.shape[2]
    codes = sum(neighbours[:, :, k] << (4 * k) for k in range(listed))
    table_rows = group_row.reshape(-1, LANES)
    packed = jnp.concatenate([positions, masses[None]], axis=0)
    odd_dom, odd_sub = (lax.axis_index("dom") & 1) == 1, lax.axis_index("core") == 1
    inner, outer = neighbours_of(packed[:, 0], packed[:, blocks_x - 1], "dom", odd_dom)
    even_dom = jnp.logical_not(odd_dom)
    prev, following = jnp.where(even_dom, outer, inner), jnp.where(even_dom, inner, outer)
    sources = ((blocks_x + 2) * blocks_y, 8, LANES)
    columns, middle, own = pl.pallas_call(
        functools.partial(middle_kernel, listed),
        out_shape=(
            shape((2, 4, blocks_x, LANES), F32),
            shape((blocks_x - 2, blocks_y, LANES), F32),
            shape(sources, F32),
        ),
        in_specs=[VMEM] * 6,
        out_specs=(VMEM,) * 3,
        scratch_shapes=pair_scratch(blocks_x, blocks_y, blocks_x - 2, listed),
        compiler_params=params(),
        cost_estimate=pl.CostEstimate(
            flops=4_000_000_000, bytes_accessed=400_000, transcendentals=1_300_000
        ),
        name="middle_pairs",
    )(codes, positions, masses, smoothing, particle_group, table_rows)
    early, rows, hot = pl.pallas_call(
        functools.partial(moments_kernel, blocks_x * dom_count, blocks_y * sub_count),
        out_shape=(
            shape((owners, EARLY, LANES), F32),
            shape(masses.shape, jnp.int32),
            shape((blocks_x, LANES, chunk), BF16),
        ),
        in_specs=[VMEM] * 6,
        out_specs=(VMEM,) * 3,
        scratch_shapes=[
            pltpu.VMEM((blocks_x * EARLY * blocks_y, LANES), F32),
            pltpu.VMEM((blocks_x, owners * 2 * EARLY, chunk), BF16),
            pltpu.VMEM((owners * 2 * EARLY, LANES), F32),
        ],
        compiler_params=params(),
        cost_estimate=pl.CostEstimate(
            flops=2_000_000_000, bytes_accessed=1_400_000, transcendentals=0
        ),
        name="moments_by_row",
    )(middle, positions, velocities, masses, particle_group, table_rows)
    edges = [
        jnp.concatenate([prev[:, y : y + 1], columns[side], following[:, y : y + 1]], axis=1)
        for side, y in ((0, 0), (1, blocks_y - 1))
    ]
    inner, outer = neighbours_of(*edges, ("chip", "core"), odd_sub)
    low, high = jnp.where(odd_sub, inner, outer), jnp.where(odd_sub, outer, inner)
    rims = 2 * blocks_x
    edge, known, rim_match, rim_self, middle_moment = pl.pallas_call(
        functools.partial(edge_kernel, listed),
        out_shape=(
            shape((2, blocks_y, LANES), F32),
            shape(sources, F32),
            shape((rims, LANES, 48), BF16),
            shape((rims, LANES, LANES), F32),
            shape((LANES, 2 * owners), F32),
        ),
        in_specs=[VMEM] * 10,
        out_specs=(VMEM,) * 5,
        scratch_shapes=[
            pltpu.VMEM((blocks_x, 24 * blocks_y, LANES), F32),
            pltpu.VMEM((rims, 48, LANES), BF16),
            pltpu.VMEM((rims, 8, LANES), F32),
            pltpu.VMEM((blocks_x - 2, 2 * owners, chunk), BF16),
        ]
        + pair_scratch(blocks_x, blocks_y, 2, listed),
        compiler_params=params(),
        cost_estimate=pl.CostEstimate(
            flops=4_000_000_000, bytes_accessed=400_000, transcendentals=1_300_000
        ),
        name="edge_pairs",
    )(codes, positions, masses, smoothing, prev, following, own, middle, rows, hot)
    sums, table = pl.pallas_call(
        functools.partial(rim_kernel, listed),
        out_shape=(shape(masses.shape, F32), shape((2, owners // 2, EARLY + 1, LANES), F32)),
        in_specs=[VMEM] * 14,
        out_specs=(VMEM, VMEM),
        scratch_shapes=[
            pltpu.VMEM((128, LANES), F32),
            pltpu.VMEM((6 * (blocks_x + 2), 8, LANES), F32),
            pltpu.VMEM((owners, LANES), F32),
            pltpu.VMEM((blocks_x, 2 * owners, chunk), BF16),
            pltpu.VMEM((LANES, 2 * owners), F32),
            pltpu.VMEM((9, 8, LANES), F32),
        ]
        + product_scratch(rims, listed)[1:],
        compiler_params=params(),
        cost_estimate=pl.CostEstimate(
            flops=200_000_000, bytes_accessed=400_000, transcendentals=400_000
        ),
        name="rim_pairs_and_table",
    )(
        codes, middle, edge, known, rim_match, rim_self, middle_moment,
        masses, smoothing, low, high, rows, hot, early,
    )
    density = sums * DENSITY_FACTOR / (smoothing * smoothing * smoothing)
    return (density, summed(to_owner(table), "dom"))


def solution(mesh):
    dom_count, sub_count = mesh.devices.shape
    mesh = jax.sharding.Mesh(
        mesh.devices.reshape(dom_count, sub_count // 2, 2), ("dom", "chip", "core")
    )
    sub = ("chip", "core")
    in_specs = (
        P(None, "dom", sub, None),
        P(None, "dom", sub, None),
        P("dom", sub, None),
        P("dom", sub, None),
        P("dom", sub, None),
        P("dom", sub, None),
        P(),
    )
    out_specs = (P("dom", sub, None), P(None, sub))
    return jax.shard_map(shards, mesh=mesh, in_specs=in_specs, out_specs=out_specs, check_vma=False)
```

```python
import functools
import math

import jax
import jax.numpy as jnp
from jax import lax
from jax.experimental import pallas as pl
from jax.experimental.pallas import tpu as pltpu
from jax.sharding import PartitionSpec as P

F32 = jnp.float32
BF16 = jnp.bfloat16
LANES = 128
EARLY = 16
DENSITY_FACTOR = 21.0 / (16.0 * math.pi) / 256.0
VMEM = pl.BlockSpec(memory_space=pltpu.VMEM)
NT = (((1,), (1,)), ((), ()))


def params():
    return pltpu.CompilerParams(vmem_limit_bytes=40 * 1024 * 1024)


def rounded(value):
    return value.astype(BF16).astype(F32)


def three_parts(value):
    first = rounded(value)
    rest = value - first
    second = rounded(rest)
    return first, second, rest - second


def spread(numbers, y, count):
    row = jnp.broadcast_to(numbers[y : y + 1, :].astype(F32), (16, LANES)).astype(BF16)
    return jnp.concatenate([row] * (count // 16), axis=0)


def row_numbers(count):
    return lax.broadcasted_iota(jnp.int32, (count, LANES), 0).astype(F32).astype(BF16)


def slot_one_hot(slots, y):
    return jnp.where(
        row_numbers(LANES) == spread(slots, y, LANES), jnp.ones((), BF16), jnp.zeros((), BF16)
    )


def moments_kernel(
    nx_total, ny_total, after_ref, pos_ref, vel_ref, mass_ref, group_ref, row_ref,
    table_ref, rows_ref, hot_ref, feat_ref, lhs_ref, total_ref,
):
    blocks_x, blocks_y, _ = mass_ref.shape
    owners = table_ref.shape[0]
    table_rows = row_ref.shape[0]
    base_x = (lax.axis_index("dom") * blocks_x).astype(F32)
    base_y = ((2 * lax.axis_index("chip") + lax.axis_index("core")) * blocks_y).astype(F32)
    y_iota = lax.broadcasted_iota(jnp.int32, (blocks_y, LANES), 0).astype(F32)

    def features_of(x):
        group = group_ref[x]
        low = group & (LANES - 1)
        high = group >> 7
        rows = jnp.zeros_like(group)
        for r in range(table_rows):
            line = jnp.broadcast_to(row_ref[r : r + 1, :], group.shape)
            picked = jnp.take_along_axis(line, low, axis=1)
            rows = jnp.where(high == r, picked, rows)
        rows_ref[x] = rows
        mass = mass_ref[x]
        gx = (base_x + float(x) + pos_ref[0, x]) / float(nx_total)
        gy = (base_y + y_iota + pos_ref[1, x]) / float(ny_total)
        gz = pos_ref[2, x]
        vx, vy, vz = vel_ref[0, x], vel_ref[1, x], vel_ref[2, x]
        mx, my, mz = mass * gx, mass * gy, mass * gz
        features = (
            mass, mx, my, mz, mass * vx, mass * vy, mass * vz,
            mass * (gy * vz - gz * vy), mass * (gz * vx - gx * vz), mass * (gx * vy - gy * vx),
            mx * gx, my * gy, mz * gz, mx * gy, mx * gz, my * gz,
        )
        for f, feature in enumerate(features):
            start = (x * EARLY + f) * blocks_y
            feat_ref[start : start + blocks_y, :] = feature

    def operands_of(x, y):
        lanes = slice(y * LANES, (y + 1) * LANES)
        feats = feat_ref[pl.ds(x * EARLY * blocks_y + y, EARLY, stride=blocks_y), :]
        high_part = rounded(feats)
        both = jnp.concatenate([high_part, feats - high_part], axis=0).astype(BF16)
        rows = rows_ref[x]
        owner_row = spread(rows >> 7, y, 2 * EARLY)
        for o in range(owners):
            lhs_ref[x, o * 2 * EARLY : (o + 1) * 2 * EARLY, lanes] = jnp.where(
                owner_row == jnp.asarray(o, BF16), both, jnp.zeros((), BF16)
            )
        hot_ref[x, :, lanes] = slot_one_hot(rows & (LANES - 1), y)

    def add_product(x):
        product = lax.dot_general(hot_ref[x], lhs_ref[x], NT, preferred_element_type=F32)
        total_ref[...] = product if x == 0 else total_ref[...] + product

    def finish():
        total = total_ref[...].T.reshape(owners, 2 * EARLY, LANES)
        table_ref[...] = total[:, :EARLY, :] + total[:, EARLY:, :]

    for x in range(blocks_x):
        features_of(x)
        for y in range(blocks_y):
            operands_of(x, y)
        add_product(x)
    finish()


def target_rows(pos, radius):
    weight = 4.0 / (radius * radius)
    cx, cy, cz = pos[0] - 0.5, pos[1] - 0.5, pos[2] - 0.5
    lines = (
        -2.0 * cx * weight, -2.0 * cy * weight, -2.0 * cz * weight,
        weight, weight, weight,
        (cx * cx + cy * cy + cz * cz) * weight, jnp.zeros_like(weight),
    )
    parts = [three_parts(line) for line in lines]
    return [part[k] for k in range(3) for part in parts]


def target_matrix(coef):
    one, two, three = coef[0:8], coef[8:16], coef[16:24]
    stacked = jnp.concatenate([one, one, two, two, one, three], axis=0)
    return stacked.T.astype(BF16)


def source_matrix(line, root, squares):
    value = jnp.where(squares, line * line, line) * (root * root)
    one, two, three = three_parts(value)
    first = jnp.concatenate([one, two], axis=0).astype(BF16)
    last = jnp.concatenate([three, one], axis=0).astype(BF16)
    return jnp.concatenate([first, first, last], axis=0)


def fifth_root(mass):
    root = jnp.exp(0.2 * jnp.log(mass))
    square = root * root
    return 0.8 * root + 0.2 * mass / (square * square)


def store_source(nat_ref, start, count, columns, mass):
    cx, cy, cz = [column - 0.5 for column in columns]
    one = jnp.ones_like(cx)
    for kind, line in enumerate((cx, cy, cz, cx, cy, cz, one, fifth_root(mass))):
        nat_ref[start + kind * 8 : start + kind * 8 + count, :] = line


def pair_sums(sides, pieces=()):
    rows = 32
    steps = []
    for target, sources, roots, total, base in sides:
        count = roots.shape[0]
        for first in range(0, count, 2):
            steps.append((target, sources, roots, total, base, first, min(2, count - first), count))

    def product(step):
        target, sources, _, _, _, first, width, _ = step
        right = sources[:, first * LANES : (first + width) * LANES]
        return jnp.dot(target[...], right, preferred_element_type=F32)

    ready = product(steps[0])
    chunks = None
    for number, (_, _, roots, total, base, first, width, count) in enumerate(steps):
        squared = ready
        if number + 1 < len(steps):
            ready = product(steps[number + 1])
        if first == 0:
            chunks = [None] * (LANES // rows)
            if base is not None:
                chunks = [base[r * rows : (r + 1) * rows, :] for r in range(len(chunks))]
        limits = []
        for k in range(width):
            root = roots[first + k : first + k + 1, :]
            reach = 4.0 * root
            limits.append(
                [jnp.broadcast_to(line, (rows, LANES)) for line in (root, reach, reach * reach)]
            )
        for r in range(len(chunks)):
            for k, (root, reach, most) in enumerate(limits):
                t = squared[r * rows : (r + 1) * rows, k * LANES : (k + 1) * LANES]
                t = jnp.maximum(jnp.minimum(t, most), 1e-12)
                u = t * lax.rsqrt(t)
                f = reach - u
                f = f * f
                f = f * f
                term = f * (root + u)
                chunks[r] = term if chunks[r] is None else chunks[r] + term
        if first + width == count:
            for r, chunk in enumerate(chunks):
                total[r * rows : (r + 1) * rows, :] = chunk
        if number < len(pieces) and pieces[number] is not None:
            pieces[number]()
    for piece in pieces[len(steps) :]:
        piece()


def column_sums(totals):
    lane = lax.broadcasted_iota(jnp.int32, (LANES, LANES), 1)
    columns = jnp.zeros((LANES, LANES), F32)
    for k, total in enumerate(totals):
        columns = jnp.where(lane == k, jnp.sum(total, axis=1, keepdims=True), columns)
    return columns.T[: len(totals), :]


def square_mask():
    kind = lax.broadcasted_iota(jnp.int32, (8, LANES), 0)
    return (kind >= 3) & (kind < 6)


def shift_rows(step_x, step_y):
    kind = lax.broadcasted_iota(jnp.int32, (8, LANES), 0)
    along_x = jnp.where((kind == 0) | (kind == 3), float(step_x), 0.0)
    return along_x + jnp.where((kind == 1) | (kind == 4), float(step_y), 0.0)


def put_shifts(shift_ref):
    for code in range(9):
        shift_ref[code] = shift_rows(code // 3 - 1, code % 3 - 1)


def put_source(near_ref, root_ref, number, k, line, shift, squares):
    root = jnp.broadcast_to(line[7:8], line.shape)
    near_ref[number, :, k * LANES : (k + 1) * LANES] = source_matrix(line + shift, root, squares)
    root_ref[number, k : k + 1, :] = root[0:1]


def sides_of(count, first, end, mat_ref, near_ref, root_ref, total_ref, base_ref=None):
    lanes, rows = pl.ds(first * LANES, (end - first) * LANES), pl.ds(first, end - first)
    return [
        (
            mat_ref.at[n], near_ref.at[n, :, lanes], root_ref.at[n, rows], total_ref.at[n],
            None if base_ref is None else base_ref.at[n],
        )
        for n in range(count)
    ]


def put_moments(lhs_ref, ys, sums, mass, radius, rows):
    owners = lhs_ref.shape[0] // 2
    owner_ids = lax.broadcasted_iota(jnp.int32, (owners, LANES), 0)
    moment = mass * (sums * DENSITY_FACTOR / (radius * radius * radius))
    high_part = rounded(moment)
    low_part = moment - high_part
    owner = rows >> 7
    for y in ys:
        mine = jnp.broadcast_to(owner[y : y + 1, :], owner_ids.shape) == owner_ids
        lhs_ref[:, y * LANES : (y + 1) * LANES] = jnp.concatenate(
            [
                jnp.where(mine, jnp.broadcast_to(part[y : y + 1, :], mine.shape), 0.0)
                for part in (high_part, low_part)
            ],
            axis=0,
        ).astype(BF16)


def inner_moments(total_ref, first, hot, lhs_ref, sums, mass, radius, rows):
    last = mass.shape[0] - 1
    put_moments(lhs_ref, range(1, last), sums, mass, radius, rows)
    lanes = slice(LANES, last * LANES)
    product = lax.dot_general(hot[:, lanes], lhs_ref[:, lanes], NT, preferred_element_type=F32)
    total_ref[...] = product if first else total_ref[...] + product


def start_rim(
    src_ref, pos_ref, mass_ref, smooth_ref, middle_ref, rows_ref, hot_ref,
    mat_ref, self_ref, moment_ref, tgt_ref, near_ref, root_ref, lhs_ref,
):
    blocks_x, blocks_y, _ = mass_ref.shape
    squares = square_mask()
    rim = [(x, side * (blocks_y - 1)) for x in range(blocks_x) for side in range(2)]
    for x in range(blocks_x):
        lines = target_rows([pos_ref[c, x] for c in range(3)], smooth_ref[x])
        for row, line in enumerate(lines):
            tgt_ref[x, row * blocks_y : (row + 1) * blocks_y, :] = line
    for n, (x, y) in enumerate(rim):
        mat_ref[n] = target_matrix(tgt_ref[x, pl.ds(y, 24, stride=blocks_y), :])
    for n, (x, y) in enumerate(rim):
        put_source(near_ref, root_ref, n, 0, src_ref[(x + 1) * blocks_y + y], 0.0, squares)

    def middle_moments(turn):
        x = turn + 1
        inner_moments(
            moment_ref, turn == 0, hot_ref[x], lhs_ref.at[turn], middle_ref[turn],
            mass_ref[x], smooth_ref[x], rows_ref[x],
        )

    pair_sums(
        sides_of(len(rim), 0, 1, mat_ref, near_ref, root_ref, self_ref),
        [functools.partial(middle_moments, turn) for turn in range(blocks_x - 2)],
    )


def block_pairs(
    listed, x_first, x_step, x_count, known_ref, code_ref, pos_ref, mass_ref, smooth_ref, prev_ref, next_ref,
    out_ref, src_ref, nat_ref, shift_ref, tgt_ref, mat_ref, near_ref, root_ref, total_ref,
    ahead=None,
):
    blocks_x, blocks_y, _ = mass_ref.shape
    for xe in range(blocks_x + 2):
        if xe == 0 or xe == blocks_x + 1:
            ref = prev_ref if xe == 0 else next_ref
            if ref is None:
                continue
            store_source(nat_ref, xe * 64, blocks_y, [ref[c] for c in range(3)], ref[3])
        elif known_ref is None:
            columns = [pos_ref[c, xe - 1] for c in range(3)]
            store_source(nat_ref, xe * 64, blocks_y, columns, mass_ref[xe - 1])
        else:
            part = pl.ds(xe * blocks_y, blocks_y)
            src_ref[part] = known_ref[part]
            continue
        for y in range(blocks_y):
            src_ref[xe * blocks_y + y] = nat_ref[pl.ds(xe * 64 + y, 8, stride=8), :]
    put_shifts(shift_ref)
    squares = square_mask()
    blocks = [(turn, y) for turn in range(x_count) for y in range(1, blocks_y - 1)]
    for turn in range(x_count):
        x = x_first + turn * x_step
        lines = target_rows([pos_ref[c, x] for c in range(3)], smooth_ref[x])
        for row, line in enumerate(lines):
            tgt_ref[turn, row * blocks_y : (row + 1) * blocks_y, :] = line
    for number, (turn, y) in enumerate(blocks):
        mat_ref[number] = target_matrix(tgt_ref[turn, pl.ds(y, 24, stride=blocks_y), :])
    for number, (turn, y) in enumerate(blocks):
        line = src_ref[(x_first + turn * x_step + 1) * blocks_y + y]
        put_source(near_ref, root_ref, number, 0, line, 0.0, squares)
    pair_sums(sides_of(len(blocks), 0, 1, mat_ref, near_ref, root_ref, total_ref))
    if ahead is not None:
        ahead()
    words = code_ref[...]
    for number, (turn, y) in enumerate(blocks):
        x = x_first + turn * x_step
        word = words[x, y]
        for k in range(1, listed):
            code = (word >> (4 * k)) & 15
            step_x = (code * 11) >> 5
            line = src_ref[(x + step_x) * blocks_y + y + code - 3 * step_x - 1]
            put_source(near_ref, root_ref, number, k, line, shift_ref[code], squares)
    inner = blocks_y - 2
    per_row = inner * (listed // 2)

    def row_sums(turn):
        sums = column_sums([total_ref[turn * inner + k] for k in range(inner)])
        out_ref[turn, 1 : blocks_y - 1, :] = sums

    pieces = [None] * (x_count * per_row + 1)
    for turn in range(x_count):
        pieces[(turn + 1) * per_row] = functools.partial(row_sums, turn)
    sides = sides_of(len(blocks), 1, listed, mat_ref, near_ref, root_ref, total_ref, total_ref)
    pair_sums(sides, pieces)


def middle_kernel(
    listed, code_ref, pos_ref, mass_ref, smooth_ref, group_ref, row_ref, column_ref, out_ref, src_ref, *scratch
):
    blocks_x, blocks_y, _ = mass_ref.shape
    for side in range(2):
        y = side * (blocks_y - 1)
        for x in range(blocks_x):
            for c in range(3):
                column_ref[side, c, x : x + 1, :] = pos_ref[c, x, y : y + 1, :]
            column_ref[side, 3, x : x + 1, :] = mass_ref[x, y : y + 1, :]
    block_pairs(
        listed, 1, 1, blocks_x - 2, None, code_ref, pos_ref, mass_ref, smooth_ref, None, None,
        out_ref, src_ref, *scratch,
    )


def edge_kernel(
    listed, code_ref, pos_ref, mass_ref, smooth_ref, prev_ref, next_ref, known_ref,
    middle_ref, rows_ref, hot_ref,
    out_ref, src_ref, rim_mat_ref, self_ref, moment_ref,
    rim_tgt_ref, rim_near_ref, rim_root_ref, lhs_ref, *scratch
):
    blocks_x = mass_ref.shape[0]
    ahead = functools.partial(
        start_rim, src_ref, pos_ref, mass_ref, smooth_ref, middle_ref, rows_ref, hot_ref,
        rim_mat_ref, self_ref, moment_ref, rim_tgt_ref, rim_near_ref, rim_root_ref, lhs_ref,
    )
    block_pairs(
        listed, 0, blocks_x - 1, 2, known_ref, code_ref, pos_ref, mass_ref, smooth_ref, prev_ref, next_ref,
        out_ref, src_ref, *scratch, ahead=ahead,
    )


def pair_scratch(blocks_x, blocks_y, x_count, listed):
    return [
        pltpu.VMEM(((blocks_x + 2) * 64, LANES), F32),
        pltpu.VMEM((9, 8, LANES), F32),
        pltpu.VMEM((x_count, 24 * blocks_y, LANES), F32),
    ] + product_scratch(x_count * (blocks_y - 2), listed)


def product_scratch(blocks, listed):
    return [
        pltpu.VMEM((blocks, LANES, 48), BF16),
        pltpu.VMEM((blocks, 48, listed * LANES), BF16),
        pltpu.VMEM((blocks, 8, LANES), F32),
        pltpu.VMEM((blocks, LANES, LANES), F32),
    ]


def rim_kernel(
    listed, code_ref, middle_ref, edge_ref, known_ref, mat_ref, self_ref, moment_ref,
    mass_ref, smooth_ref, low_ref, high_ref, rows_ref, hot_ref, early_ref,
    sum_ref, table_ref, nat_ref, src_ref, md_ref, lhs_ref, total_moment_ref,
    shift_ref, near_ref, root_ref, total_ref,
):
    blocks_x, blocks_y, _ = mass_ref.shape
    owners = early_ref.shape[0]
    wide = blocks_x + 2
    last = blocks_y - 1
    for side, ref in enumerate((low_ref, high_ref)):
        store_source(nat_ref, side * 64, wide, [ref[c] for c in range(3)], ref[3])
        for xe in range(wide):
            ghost = 5 * side * wide + xe
            src_ref[ghost] = nat_ref[pl.ds(side * 64 + xe, 8, stride=8), :]
            for k in range(2):
                y = k + side * (blocks_y - 2)
                place = (1 + k + 2 * side) * wide + xe
                src_ref[place] = known_ref[xe * blocks_y + y]
    put_shifts(shift_ref)
    squares = square_mask()
    for x in range(blocks_x):
        edge = x == 0 or x == blocks_x - 1
        sum_ref[x] = (edge_ref if edge else middle_ref)[(1 if x else 0) if edge else x - 1]
    total_moment_ref[...] = moment_ref[...]
    for x in (0, blocks_x - 1):
        inner_moments(
            total_moment_ref, False, hot_ref[x], lhs_ref.at[x], sum_ref[x],
            mass_ref[x], smooth_ref[x], rows_ref[x],
        )
    words = code_ref[...]
    for x in range(blocks_x):
        for side in range(2):
            word = words[x, side * last]
            for k in range(1, listed):
                code = (word >> (4 * k)) & 15
                step_x = (code * 11) >> 5
                line = src_ref[(3 * side + code - 3 * step_x) * wide + x + step_x]
                put_source(near_ref, root_ref, 2 * x + side, k, line, shift_ref[code], squares)
    pair_sums(sides_of(2 * blocks_x, 1, listed, mat_ref, near_ref, root_ref, total_ref, self_ref))
    sums = column_sums([total_ref[number] for number in range(2 * blocks_x)])
    for x in range(blocks_x):
        for side in range(2):
            y = side * last
            sum_ref[x, y : y + 1, :] = sums[2 * x + side : 2 * x + side + 1, :]
        put_moments(lhs_ref.at[x], (0, last), sum_ref[x], mass_ref[x], smooth_ref[x], rows_ref[x])
    ends = [(x, slice(y * LANES, (y + 1) * LANES)) for x in range(blocks_x) for y in (0, last)]
    total = total_moment_ref[...] + lax.dot_general(
        jnp.concatenate([hot_ref[x, :, lanes] for x, lanes in ends], axis=1),
        jnp.concatenate([lhs_ref[x, :, lanes] for x, lanes in ends], axis=1),
        NT,
        preferred_element_type=F32,
    )
    total = total.T
    md_ref[...] = total[:owners] + total[owners:]
    core, my_chip = lax.axis_index("core"), lax.axis_index("chip")
    for other in range(2):
        for step in range(owners // 2):
            owner = 2 * (my_chip ^ step) + (core ^ other)
            table_ref[other, step, :EARLY, :] = early_ref[owner]
            table_ref[other, step, EARLY : EARLY + 1, :] = md_ref[pl.ds(owner, 1), :]


def swap(value, axis, step):
    count = lax.axis_size(axis)
    return lax.ppermute(value, axis, [(i, i ^ step) for i in range(count)])


def neighbours_of(low_edge, high_edge, axis, odd):
    count = lax.axis_size(axis)
    inner = lax.ppermute(
        jnp.where(odd, low_edge, high_edge), axis, [(i, i ^ 1) for i in range(count)]
    )
    outer = lax.ppermute(
        jnp.where(odd, high_edge, low_edge),
        axis,
        [(i, (i + 1 if i & 1 else i - 1) % count) for i in range(count)],
    )
    return inner, outer


def added(parts):
    while len(parts) > 1:
        parts = [sum(parts[k : k + 2][1:], parts[k]) for k in range(0, len(parts), 2)]
    return parts[0]


def to_owner(table):
    table = table[0] + swap(table[1], "core", 1)
    while table.shape[0] > 1:
        ways = min(4, table.shape[0])
        part = table.shape[0] // ways
        got = [
            swap(table[k * part : (k + 1) * part], "chip", k * part)
            for k in reversed(range(1, ways))
        ]
        table = added([table[:part]] + got)
    return table[0]


def summed(value, axis):
    count = lax.axis_size(axis)
    if count & (count - 1):
        return lax.psum(value, axis)
    step = 1
    while step < count:
        ways = min(4, count // step)
        value = added([value] + [swap(value, axis, k * step) for k in range(1, ways)])
        step *= ways
    return value


def shards(positions, velocities, masses, smoothing, neighbours, particle_group, group_row):
    blocks_x, blocks_y, block_len = masses.shape
    dom_count, sub_count = lax.axis_size("dom"), lax.axis_size("chip") * lax.axis_size("core")
    owners = sub_count
    chunk = blocks_y * block_len
    shape = jax.ShapeDtypeStruct
    listed = neighbours.shape[2]
    codes = sum(neighbours[:, :, k] << (4 * k) for k in range(listed))
    table_rows = group_row.reshape(-1, LANES)
    packed = jnp.concatenate([positions, masses[None]], axis=0)
    odd_dom, odd_sub = (lax.axis_index("dom") & 1) == 1, lax.axis_index("core") == 1
    inner, outer = neighbours_of(packed[:, 0], packed[:, blocks_x - 1], "dom", odd_dom)
    even_dom = jnp.logical_not(odd_dom)
    prev, following = jnp.where(even_dom, outer, inner), jnp.where(even_dom, inner, outer)
    sources = ((blocks_x + 2) * blocks_y, 8, LANES)
    columns, middle, own = pl.pallas_call(
        functools.partial(middle_kernel, listed),
        out_shape=(
            shape((2, 4, blocks_x, LANES), F32),
            shape((blocks_x - 2, blocks_y, LANES), F32),
            shape(sources, F32),
        ),
        in_specs=[VMEM] * 6,
        out_specs=(VMEM,) * 3,
        scratch_shapes=pair_scratch(blocks_x, blocks_y, blocks_x - 2, listed),
        compiler_params=params(),
        cost_estimate=pl.CostEstimate(
            flops=4_000_000_000, bytes_accessed=400_000, transcendentals=1_300_000
        ),
        name="middle_pairs",
    )(codes, positions, masses, smoothing, particle_group, table_rows)
    early, rows, hot = pl.pallas_call(
        functools.partial(moments_kernel, blocks_x * dom_count, blocks_y * sub_count),
        out_shape=(
            shape((owners, EARLY, LANES), F32),
            shape(masses.shape, jnp.int32),
            shape((blocks_x, LANES, chunk), BF16),
        ),
        in_specs=[VMEM] * 6,
        out_specs=(VMEM,) * 3,
        scratch_shapes=[
            pltpu.VMEM((blocks_x * EARLY * blocks_y, LANES), F32),
            pltpu.VMEM((blocks_x, owners * 2 * EARLY, chunk), BF16),
            pltpu.VMEM((LANES, owners * 2 * EARLY), F32),
        ],
        compiler_params=params(),
        cost_estimate=pl.CostEstimate(
            flops=2_000_000_000, bytes_accessed=1_400_000, transcendentals=0
        ),
        name="moments_by_row",
    )(middle, positions, velocities, masses, particle_group, table_rows)
    edges = [
        jnp.concatenate([prev[:, y : y + 1], columns[side], following[:, y : y + 1]], axis=1)
        for side, y in ((0, 0), (1, blocks_y - 1))
    ]
    inner, outer = neighbours_of(*edges, ("chip", "core"), odd_sub)
    low, high = jnp.where(odd_sub, inner, outer), jnp.where(odd_sub, outer, inner)
    rims = 2 * blocks_x
    edge, known, rim_match, rim_self, middle_moment = pl.pallas_call(
        functools.partial(edge_kernel, listed),
        out_shape=(
            shape((2, blocks_y, LANES), F32),
            shape(sources, F32),
            shape((rims, LANES, 48), BF16),
            shape((rims, LANES, LANES), F32),
            shape((LANES, 2 * owners), F32),
        ),
        in_specs=[VMEM] * 10,
        out_specs=(VMEM,) * 5,
        scratch_shapes=[
            pltpu.VMEM((blocks_x, 24 * blocks_y, LANES), F32),
            pltpu.VMEM((rims, 48, LANES), BF16),
            pltpu.VMEM((rims, 8, LANES), F32),
            pltpu.VMEM((blocks_x - 2, 2 * owners, chunk), BF16),
        ]
        + pair_scratch(blocks_x, blocks_y, 2, listed),
        compiler_params=params(),
        cost_estimate=pl.CostEstimate(
            flops=4_000_000_000, bytes_accessed=400_000, transcendentals=1_300_000
        ),
        name="edge_pairs",
    )(codes, positions, masses, smoothing, prev, following, own, middle, rows, hot)
    sums, table = pl.pallas_call(
        functools.partial(rim_kernel, listed),
        out_shape=(shape(masses.shape, F32), shape((2, owners // 2, EARLY + 1, LANES), F32)),
        in_specs=[VMEM] * 14,
        out_specs=(VMEM, VMEM),
        scratch_shapes=[
            pltpu.VMEM((128, LANES), F32),
            pltpu.VMEM((6 * (blocks_x + 2), 8, LANES), F32),
            pltpu.VMEM((owners, LANES), F32),
            pltpu.VMEM((blocks_x, 2 * owners, chunk), BF16),
            pltpu.VMEM((LANES, 2 * owners), F32),
            pltpu.VMEM((9, 8, LANES), F32),
        ]
        + product_scratch(rims, listed)[1:],
        compiler_params=params(),
        cost_estimate=pl.CostEstimate(
            flops=200_000_000, bytes_accessed=400_000, transcendentals=400_000
        ),
        name="rim_pairs_and_table",
    )(
        codes, middle, edge, known, rim_match, rim_self, middle_moment,
        masses, smoothing, low, high, rows, hot, early,
    )
    density = sums * DENSITY_FACTOR / (smoothing * smoothing * smoothing)
    return (density, summed(to_owner(table), "dom"))


def solution(mesh):
    dom_count, sub_count = mesh.devices.shape
    mesh = jax.sharding.Mesh(
        mesh.devices.reshape(dom_count, sub_count // 2, 2), ("dom", "chip", "core")
    )
    sub = ("chip", "core")
    in_specs = (
        P(None, "dom", sub, None),
        P(None, "dom", sub, None),
        P("dom", sub, None),
        P("dom", sub, None),
        P("dom", sub, None),
        P("dom", sub, None),
        P(),
    )
    out_specs = (P("dom", sub, None), P(None, sub))
    return jax.shard_map(shards, mesh=mesh, in_specs=in_specs, out_specs=out_specs, check_vma=False)
```

```python
import functools
import math

import jax
import jax.numpy as jnp
from jax import lax
from jax.experimental import pallas as pl
from jax.experimental.pallas import tpu as pltpu
from jax.sharding import PartitionSpec as P

F32 = jnp.float32
BF16 = jnp.bfloat16
LANES = 128
EARLY = 16
DENSITY_FACTOR = 21.0 / (16.0 * math.pi) / 256.0
VMEM = pl.BlockSpec(memory_space=pltpu.VMEM)
NT = (((1,), (1,)), ((), ()))


def params():
    return pltpu.CompilerParams(vmem_limit_bytes=40 * 1024 * 1024)


def rounded(value):
    return value.astype(BF16).astype(F32)


def three_parts(value):
    first = rounded(value)
    rest = value - first
    second = rounded(rest)
    return first, second, rest - second


def spread(numbers, y, count):
    row = jnp.broadcast_to(numbers[y : y + 1, :].astype(F32), (16, LANES)).astype(BF16)
    return jnp.concatenate([row] * (count // 16), axis=0)


def row_numbers(count):
    return lax.broadcasted_iota(jnp.int32, (count, LANES), 0).astype(F32).astype(BF16)


def slot_one_hot(slots, y):
    return jnp.where(
        row_numbers(LANES) == spread(slots, y, LANES), jnp.ones((), BF16), jnp.zeros((), BF16)
    )


def moments_kernel(
    nx_total, ny_total, after_ref, pos_ref, vel_ref, mass_ref, group_ref, row_ref,
    table_ref, rows_ref, hot_ref, feat_ref, lhs_ref, total_ref,
):
    blocks_x, blocks_y, _ = mass_ref.shape
    owners = table_ref.shape[0]
    table_rows = row_ref.shape[0]
    base_x = (lax.axis_index("dom") * blocks_x).astype(F32)
    base_y = ((2 * lax.axis_index("chip") + lax.axis_index("core")) * blocks_y).astype(F32)
    y_iota = lax.broadcasted_iota(jnp.int32, (blocks_y, LANES), 0).astype(F32)

    def features_of(x):
        group = group_ref[x]
        low = group & (LANES - 1)
        high = group >> 7
        rows = jnp.zeros_like(group)
        for r in range(table_rows):
            line = jnp.broadcast_to(row_ref[r : r + 1, :], group.shape)
            picked = jnp.take_along_axis(line, low, axis=1)
            rows = jnp.where(high == r, picked, rows)
        rows_ref[x] = rows
        mass = mass_ref[x]
        gx = (base_x + float(x) + pos_ref[0, x]) / float(nx_total)
        gy = (base_y + y_iota + pos_ref[1, x]) / float(ny_total)
        gz = pos_ref[2, x]
        vx, vy, vz = vel_ref[0, x], vel_ref[1, x], vel_ref[2, x]
        mx, my, mz = mass * gx, mass * gy, mass * gz
        features = (
            mass, mx, my, mz, mass * vx, mass * vy, mass * vz,
            mass * (gy * vz - gz * vy), mass * (gz * vx - gx * vz), mass * (gx * vy - gy * vx),
            mx * gx, my * gy, mz * gz, mx * gy, mx * gz, my * gz,
        )
        for f, feature in enumerate(features):
            start = (x * EARLY + f) * blocks_y
            feat_ref[start : start + blocks_y, :] = feature

    def operands_of(x, y):
        lanes = slice(y * LANES, (y + 1) * LANES)
        feats = feat_ref[pl.ds(x * EARLY * blocks_y + y, EARLY, stride=blocks_y), :]
        high_part = rounded(feats)
        both = jnp.concatenate([high_part, feats - high_part], axis=0).astype(BF16)
        rows = rows_ref[x]
        owner_row = spread(rows >> 7, y, 2 * EARLY)
        for o in range(owners):
            lhs_ref[x, o * 2 * EARLY : (o + 1) * 2 * EARLY, lanes] = jnp.where(
                owner_row == jnp.asarray(o, BF16), both, jnp.zeros((), BF16)
            )
        hot_ref[x, :, lanes] = slot_one_hot(rows & (LANES - 1), y)

    def add_product(x):
        product = lax.dot_general(lhs_ref[x], hot_ref[x], NT, preferred_element_type=F32)
        total_ref[...] = product if x == 0 else total_ref[...] + product

    def finish():
        total = total_ref[...].reshape(owners, 2 * EARLY, LANES)
        table_ref[...] = total[:, :EARLY, :] + total[:, EARLY:, :]

    for x in range(blocks_x):
        features_of(x)
        for y in range(blocks_y):
            operands_of(x, y)
        add_product(x)
    finish()


def target_rows(pos, radius):
    weight = 4.0 / (radius * radius)
    cx, cy, cz = pos[0] - 0.5, pos[1] - 0.5, pos[2] - 0.5
    lines = (
        -2.0 * cx * weight, -2.0 * cy * weight, -2.0 * cz * weight,
        weight, weight, weight,
        (cx * cx + cy * cy + cz * cz) * weight, jnp.zeros_like(weight),
    )
    parts = [three_parts(line) for line in lines]
    return [part[k] for k in range(3) for part in parts]


def target_matrix(coef):
    one, two, three = coef[0:8], coef[8:16], coef[16:24]
    stacked = jnp.concatenate([one, one, two, two, one, three], axis=0)
    return stacked.T.astype(BF16)


def source_matrix(line, root, squares):
    value = jnp.where(squares, line * line, line) * (root * root)
    one, two, three = three_parts(value)
    first = jnp.concatenate([one, two], axis=0).astype(BF16)
    last = jnp.concatenate([three, one], axis=0).astype(BF16)
    return jnp.concatenate([first, first, last], axis=0)


def fifth_root(mass):
    root = jnp.exp(0.2 * jnp.log(mass))
    square = root * root
    return 0.8 * root + 0.2 * mass / (square * square)


def store_source(nat_ref, start, count, columns, mass):
    cx, cy, cz = [column - 0.5 for column in columns]
    one = jnp.ones_like(cx)
    for kind, line in enumerate((cx, cy, cz, cx, cy, cz, one, fifth_root(mass))):
        nat_ref[start + kind * 8 : start + kind * 8 + count, :] = line


def pair_sums(sides, pieces=()):
    rows = 32
    steps = []
    for target, sources, roots, total, base in sides:
        count = roots.shape[0]
        for first in range(0, count, 2):
            steps.append((target, sources, roots, total, base, first, min(2, count - first), count))

    def product(step):
        target, sources, _, _, _, first, width, _ = step
        right = sources[:, first * LANES : (first + width) * LANES]
        return jnp.dot(target[...], right, preferred_element_type=F32)

    ready = product(steps[0])
    chunks = None
    for number, (_, _, roots, total, base, first, width, count) in enumerate(steps):
        squared = ready
        if number + 1 < len(steps):
            ready = product(steps[number + 1])
        if first == 0:
            chunks = [None] * (LANES // rows)
            if base is not None:
                chunks = [base[r * rows : (r + 1) * rows, :] for r in range(len(chunks))]
        limits = []
        for k in range(width):
            root = roots[first + k : first + k + 1, :]
            reach = 4.0 * root
            limits.append(
                [jnp.broadcast_to(line, (rows, LANES)) for line in (root, reach, reach * reach)]
            )
        for r in range(len(chunks)):
            for k, (root, reach, most) in enumerate(limits):
                t = squared[r * rows : (r + 1) * rows, k * LANES : (k + 1) * LANES]
                t = jnp.maximum(jnp.minimum(t, most), 1e-12)
                u = t * lax.rsqrt(t)
                f = reach - u
                f = f * f
                f = f * f
                term = f * (root + u)
                chunks[r] = term if chunks[r] is None else chunks[r] + term
        if first + width == count:
            for r, chunk in enumerate(chunks):
                total[r * rows : (r + 1) * rows, :] = chunk
        if number < len(pieces) and pieces[number] is not None:
            pieces[number]()
    for piece in pieces[len(steps) :]:
        piece()


def column_sums(totals):
    lane = lax.broadcasted_iota(jnp.int32, (LANES, LANES), 1)
    columns = jnp.zeros((LANES, LANES), F32)
    for k, total in enumerate(totals):
        columns = jnp.where(lane == k, jnp.sum(total, axis=1, keepdims=True), columns)
    return columns.T[: len(totals), :]


def square_mask():
    kind = lax.broadcasted_iota(jnp.int32, (8, LANES), 0)
    return (kind >= 3) & (kind < 6)


def shift_rows(step_x, step_y):
    kind = lax.broadcasted_iota(jnp.int32, (8, LANES), 0)
    along_x = jnp.where((kind == 0) | (kind == 3), float(step_x), 0.0)
    return along_x + jnp.where((kind == 1) | (kind == 4), float(step_y), 0.0)


def put_shifts(shift_ref):
    for code in range(9):
        shift_ref[code] = shift_rows(code // 3 - 1, code % 3 - 1)


def put_source(near_ref, root_ref, number, k, line, shift, squares):
    root = jnp.broadcast_to(line[7:8], line.shape)
    near_ref[number, :, k * LANES : (k + 1) * LANES] = source_matrix(line + shift, root, squares)
    root_ref[number, k : k + 1, :] = root[0:1]


def sides_of(count, first, end, mat_ref, near_ref, root_ref, total_ref, base_ref=None):
    lanes, rows = pl.ds(first * LANES, (end - first) * LANES), pl.ds(first, end - first)
    return [
        (
            mat_ref.at[n], near_ref.at[n, :, lanes], root_ref.at[n, rows], total_ref.at[n],
            None if base_ref is None else base_ref.at[n],
        )
        for n in range(count)
    ]


def put_moments(lhs_ref, ys, sums, mass, radius, rows):
    owners = lhs_ref.shape[0] // 2
    owner_ids = lax.broadcasted_iota(jnp.int32, (owners, LANES), 0)
    moment = mass * (sums * DENSITY_FACTOR / (radius * radius * radius))
    high_part = rounded(moment)
    low_part = moment - high_part
    owner = rows >> 7
    for y in ys:
        mine = jnp.broadcast_to(owner[y : y + 1, :], owner_ids.shape) == owner_ids
        lhs_ref[:, y * LANES : (y + 1) * LANES] = jnp.concatenate(
            [
                jnp.where(mine, jnp.broadcast_to(part[y : y + 1, :], mine.shape), 0.0)
                for part in (high_part, low_part)
            ],
            axis=0,
        ).astype(BF16)


def inner_moments(total_ref, first, hot, lhs_ref, sums, mass, radius, rows):
    last = mass.shape[0] - 1
    put_moments(lhs_ref, range(1, last), sums, mass, radius, rows)
    lanes = slice(LANES, last * LANES)
    product = lax.dot_general(hot[:, lanes], lhs_ref[:, lanes], NT, preferred_element_type=F32)
    total_ref[...] = product if first else total_ref[...] + product


def start_rim(
    src_ref, pos_ref, mass_ref, smooth_ref, middle_ref, rows_ref, hot_ref,
    mat_ref, self_ref, moment_ref, tgt_ref, near_ref, root_ref, lhs_ref,
):
    blocks_x, blocks_y, _ = mass_ref.shape
    squares = square_mask()
    rim = [(x, side * (blocks_y - 1)) for x in range(blocks_x) for side in range(2)]
    for x in range(blocks_x):
        lines = target_rows([pos_ref[c, x] for c in range(3)], smooth_ref[x])
        for row, line in enumerate(lines):
            tgt_ref[x, row * blocks_y : (row + 1) * blocks_y, :] = line
    for n, (x, y) in enumerate(rim):
        mat_ref[n] = target_matrix(tgt_ref[x, pl.ds(y, 24, stride=blocks_y), :])
    for n, (x, y) in enumerate(rim):
        put_source(near_ref, root_ref, n, 0, src_ref[(x + 1) * blocks_y + y], 0.0, squares)

    def middle_moments(turn):
        x = turn + 1
        inner_moments(
            moment_ref, turn == 0, hot_ref[x], lhs_ref.at[turn], middle_ref[turn],
            mass_ref[x], smooth_ref[x], rows_ref[x],
        )

    pair_sums(
        sides_of(len(rim), 0, 1, mat_ref, near_ref, root_ref, self_ref),
        [functools.partial(middle_moments, turn) for turn in range(blocks_x - 2)],
    )


def block_pairs(
    listed, x_first, x_step, x_count, known_ref, code_ref, pos_ref, mass_ref, smooth_ref, prev_ref, next_ref,
    out_ref, src_ref, nat_ref, shift_ref, tgt_ref, mat_ref, near_ref, root_ref, total_ref,
    ahead=None,
):
    blocks_x, blocks_y, _ = mass_ref.shape
    def table_row(xe, columns, mass):
        store_source(nat_ref, xe * 64, blocks_y, columns, mass)
        for y in range(blocks_y):
            src_ref[xe * blocks_y + y] = nat_ref[pl.ds(xe * 64 + y, 8, stride=8), :]

    for x in range(blocks_x):
        if known_ref is None:
            table_row(x + 1, [pos_ref[c, x] for c in range(3)], mass_ref[x])
        else:
            part = pl.ds((x + 1) * blocks_y, blocks_y)
            src_ref[part] = known_ref[part]
    put_shifts(shift_ref)
    squares = square_mask()
    blocks = [(turn, y) for turn in range(x_count) for y in range(1, blocks_y - 1)]
    for turn in range(x_count):
        x = x_first + turn * x_step
        lines = target_rows([pos_ref[c, x] for c in range(3)], smooth_ref[x])
        for row, line in enumerate(lines):
            tgt_ref[turn, row * blocks_y : (row + 1) * blocks_y, :] = line
    for number, (turn, y) in enumerate(blocks):
        mat_ref[number] = target_matrix(tgt_ref[turn, pl.ds(y, 24, stride=blocks_y), :])
    for number, (turn, y) in enumerate(blocks):
        line = src_ref[(x_first + turn * x_step + 1) * blocks_y + y]
        put_source(near_ref, root_ref, number, 0, line, 0.0, squares)
    pair_sums(sides_of(len(blocks), 0, 1, mat_ref, near_ref, root_ref, total_ref))
    if ahead is not None:
        ahead()
    for xe, ref in ((0, prev_ref), (blocks_x + 1, next_ref)):
        if ref is not None:
            table_row(xe, [ref[c] for c in range(3)], ref[3])
    words = code_ref[...]
    for number, (turn, y) in enumerate(blocks):
        x = x_first + turn * x_step
        word = words[x, y]
        for k in range(1, listed):
            code = (word >> (4 * k)) & 15
            step_x = (code * 11) >> 5
            line = src_ref[(x + step_x) * blocks_y + y + code - 3 * step_x - 1]
            put_source(near_ref, root_ref, number, k, line, shift_ref[code], squares)
    inner = blocks_y - 2
    per_row = inner * (listed // 2)

    def row_sums(turn):
        sums = column_sums([total_ref[turn * inner + k] for k in range(inner)])
        out_ref[turn, 1 : blocks_y - 1, :] = sums

    pieces = [None] * (x_count * per_row + 1)
    for turn in range(x_count):
        pieces[(turn + 1) * per_row] = functools.partial(row_sums, turn)
    sides = sides_of(len(blocks), 1, listed, mat_ref, near_ref, root_ref, total_ref, total_ref)
    pair_sums(sides, pieces)


def middle_kernel(
    listed, code_ref, pos_ref, mass_ref, smooth_ref, group_ref, row_ref, column_ref, out_ref, src_ref, *scratch
):
    blocks_x, blocks_y, _ = mass_ref.shape
    for side in range(2):
        y = side * (blocks_y - 1)
        for x in range(blocks_x):
            for c in range(3):
                column_ref[side, c, x : x + 1, :] = pos_ref[c, x, y : y + 1, :]
            column_ref[side, 3, x : x + 1, :] = mass_ref[x, y : y + 1, :]
    block_pairs(
        listed, 1, 1, blocks_x - 2, None, code_ref, pos_ref, mass_ref, smooth_ref, None, None,
        out_ref, src_ref, *scratch,
    )


def edge_kernel(
    listed, code_ref, pos_ref, mass_ref, smooth_ref, prev_ref, next_ref, known_ref,
    middle_ref, rows_ref, hot_ref,
    out_ref, src_ref, rim_mat_ref, self_ref, moment_ref,
    rim_tgt_ref, rim_near_ref, rim_root_ref, lhs_ref, *scratch
):
    blocks_x = mass_ref.shape[0]
    ahead = functools.partial(
        start_rim, src_ref, pos_ref, mass_ref, smooth_ref, middle_ref, rows_ref, hot_ref,
        rim_mat_ref, self_ref, moment_ref, rim_tgt_ref, rim_near_ref, rim_root_ref, lhs_ref,
    )
    block_pairs(
        listed, 0, blocks_x - 1, 2, known_ref, code_ref, pos_ref, mass_ref, smooth_ref, prev_ref, next_ref,
        out_ref, src_ref, *scratch, ahead=ahead,
    )


def pair_scratch(blocks_x, blocks_y, x_count, listed):
    return [
        pltpu.VMEM(((blocks_x + 2) * 64, LANES), F32),
        pltpu.VMEM((9, 8, LANES), F32),
        pltpu.VMEM((x_count, 24 * blocks_y, LANES), F32),
    ] + product_scratch(x_count * (blocks_y - 2), listed)


def product_scratch(blocks, listed):
    return [
        pltpu.VMEM((blocks, LANES, 48), BF16),
        pltpu.VMEM((blocks, 48, listed * LANES), BF16),
        pltpu.VMEM((blocks, 8, LANES), F32),
        pltpu.VMEM((blocks, LANES, LANES), F32),
    ]


def rim_kernel(
    listed, code_ref, middle_ref, edge_ref, known_ref, mat_ref, self_ref, moment_ref,
    mass_ref, smooth_ref, low_ref, high_ref, rows_ref, hot_ref, early_ref,
    sum_ref, table_ref, nat_ref, src_ref, md_ref, lhs_ref, total_moment_ref,
    shift_ref, near_ref, root_ref, total_ref,
):
    blocks_x, blocks_y, _ = mass_ref.shape
    owners = early_ref.shape[0]
    wide = blocks_x + 2
    last = blocks_y - 1
    for side, ref in enumerate((low_ref, high_ref)):
        store_source(nat_ref, side * 64, wide, [ref[c] for c in range(3)], ref[3])
        for xe in range(wide):
            ghost = 5 * side * wide + xe
            src_ref[ghost] = nat_ref[pl.ds(side * 64 + xe, 8, stride=8), :]
            for k in range(2):
                y = k + side * (blocks_y - 2)
                place = (1 + k + 2 * side) * wide + xe
                src_ref[place] = known_ref[xe * blocks_y + y]
    put_shifts(shift_ref)
    squares = square_mask()
    for x in range(blocks_x):
        edge = x == 0 or x == blocks_x - 1
        sum_ref[x] = (edge_ref if edge else middle_ref)[(1 if x else 0) if edge else x - 1]
    total_moment_ref[...] = moment_ref[...]
    for x in (0, blocks_x - 1):
        inner_moments(
            total_moment_ref, False, hot_ref[x], lhs_ref.at[x], sum_ref[x],
            mass_ref[x], smooth_ref[x], rows_ref[x],
        )
    words = code_ref[...]
    for x in range(blocks_x):
        for side in range(2):
            word = words[x, side * last]
            for k in range(1, listed):
                code = (word >> (4 * k)) & 15
                step_x = (code * 11) >> 5
                line = src_ref[(3 * side + code - 3 * step_x) * wide + x + step_x]
                put_source(near_ref, root_ref, 2 * x + side, k, line, shift_ref[code], squares)
    pair_sums(sides_of(2 * blocks_x, 1, listed, mat_ref, near_ref, root_ref, total_ref, self_ref))
    sums = column_sums([total_ref[number] for number in range(2 * blocks_x)])
    for x in range(blocks_x):
        for side in range(2):
            y = side * last
            sum_ref[x, y : y + 1, :] = sums[2 * x + side : 2 * x + side + 1, :]
        put_moments(lhs_ref.at[x], (0, last), sum_ref[x], mass_ref[x], smooth_ref[x], rows_ref[x])
    ends = [(x, slice(y * LANES, (y + 1) * LANES)) for x in range(blocks_x) for y in (0, last)]
    total = total_moment_ref[...] + lax.dot_general(
        jnp.concatenate([hot_ref[x, :, lanes] for x, lanes in ends], axis=1),
        jnp.concatenate([lhs_ref[x, :, lanes] for x, lanes in ends], axis=1),
        NT,
        preferred_element_type=F32,
    )
    total = total.T
    md_ref[...] = total[:owners] + total[owners:]
    core, my_chip = lax.axis_index("core"), lax.axis_index("chip")
    for other in range(2):
        for step in range(owners // 2):
            owner = 2 * (my_chip ^ step) + (core ^ other)
            table_ref[other, step, :EARLY, :] = early_ref[owner]
            table_ref[other, step, EARLY : EARLY + 1, :] = md_ref[pl.ds(owner, 1), :]


def swap(value, axis, step):
    count = lax.axis_size(axis)
    return lax.ppermute(value, axis, [(i, i ^ step) for i in range(count)])


def neighbours_of(low_edge, high_edge, axis, odd):
    count = lax.axis_size(axis)
    inner = lax.ppermute(
        jnp.where(odd, low_edge, high_edge), axis, [(i, i ^ 1) for i in range(count)]
    )
    outer = lax.ppermute(
        jnp.where(odd, high_edge, low_edge),
        axis,
        [(i, (i + 1 if i & 1 else i - 1) % count) for i in range(count)],
    )
    return inner, outer


def added(parts):
    while len(parts) > 1:
        parts = [sum(parts[k : k + 2][1:], parts[k]) for k in range(0, len(parts), 2)]
    return parts[0]


def to_owner(table):
    table = table[0] + swap(table[1], "core", 1)
    while table.shape[0] > 1:
        ways = min(4, table.shape[0])
        part = table.shape[0] // ways
        got = [
            swap(table[k * part : (k + 1) * part], "chip", k * part)
            for k in reversed(range(1, ways))
        ]
        table = added([table[:part]] + got)
    return table[0]


def summed(value, axis):
    count = lax.axis_size(axis)
    if count & (count - 1):
        return lax.psum(value, axis)
    step = 1
    while step < count:
        ways = min(4, count // step)
        value = added([value] + [swap(value, axis, k * step) for k in range(1, ways)])
        step *= ways
    return value


def shards(positions, velocities, masses, smoothing, neighbours, particle_group, group_row):
    blocks_x, blocks_y, block_len = masses.shape
    dom_count, sub_count = lax.axis_size("dom"), lax.axis_size("chip") * lax.axis_size("core")
    owners = sub_count
    chunk = blocks_y * block_len
    shape = jax.ShapeDtypeStruct
    listed = neighbours.shape[2]
    codes = sum(neighbours[:, :, k] << (4 * k) for k in range(listed))
    table_rows = group_row.reshape(-1, LANES)
    packed = jnp.concatenate([positions, masses[None]], axis=0)
    odd_dom, odd_sub = (lax.axis_index("dom") & 1) == 1, lax.axis_index("core") == 1
    inner, outer = neighbours_of(packed[:, 0], packed[:, blocks_x - 1], "dom", odd_dom)
    even_dom = jnp.logical_not(odd_dom)
    prev, following = jnp.where(even_dom, outer, inner), jnp.where(even_dom, inner, outer)
    sources = ((blocks_x + 2) * blocks_y, 8, LANES)
    columns, middle, own = pl.pallas_call(
        functools.partial(middle_kernel, listed),
        out_shape=(
            shape((2, 4, blocks_x, LANES), F32),
            shape((blocks_x - 2, blocks_y, LANES), F32),
            shape(sources, F32),
        ),
        in_specs=[VMEM] * 6,
        out_specs=(VMEM,) * 3,
        scratch_shapes=pair_scratch(blocks_x, blocks_y, blocks_x - 2, listed),
        compiler_params=params(),
        cost_estimate=pl.CostEstimate(
            flops=4_000_000_000, bytes_accessed=400_000, transcendentals=1_300_000
        ),
        name="middle_pairs",
    )(codes, positions, masses, smoothing, particle_group, table_rows)
    early, rows, hot = pl.pallas_call(
        functools.partial(moments_kernel, blocks_x * dom_count, blocks_y * sub_count),
        out_shape=(
            shape((owners, EARLY, LANES), F32),
            shape(masses.shape, jnp.int32),
            shape((blocks_x, LANES, chunk), BF16),
        ),
        in_specs=[VMEM] * 6,
        out_specs=(VMEM,) * 3,
        scratch_shapes=[
            pltpu.VMEM((blocks_x * EARLY * blocks_y, LANES), F32),
            pltpu.VMEM((blocks_x, owners * 2 * EARLY, chunk), BF16),
            pltpu.VMEM((owners * 2 * EARLY, LANES), F32),
        ],
        compiler_params=params(),
        cost_estimate=pl.CostEstimate(
            flops=2_000_000_000, bytes_accessed=1_400_000, transcendentals=0
        ),
        name="moments_by_row",
    )(middle, positions, velocities, masses, particle_group, table_rows)
    edges = [
        jnp.concatenate([prev[:, y : y + 1], columns[side], following[:, y : y + 1]], axis=1)
        for side, y in ((0, 0), (1, blocks_y - 1))
    ]
    inner, outer = neighbours_of(*edges, ("chip", "core"), odd_sub)
    low, high = jnp.where(odd_sub, inner, outer), jnp.where(odd_sub, outer, inner)
    rims = 2 * blocks_x
    edge, known, rim_match, rim_self, middle_moment = pl.pallas_call(
        functools.partial(edge_kernel, listed),
        out_shape=(
            shape((2, blocks_y, LANES), F32),
            shape(sources, F32),
            shape((rims, LANES, 48), BF16),
            shape((rims, LANES, LANES), F32),
            shape((LANES, 2 * owners), F32),
        ),
        in_specs=[VMEM] * 10,
        out_specs=(VMEM,) * 5,
        scratch_shapes=[
            pltpu.VMEM((blocks_x, 24 * blocks_y, LANES), F32),
            pltpu.VMEM((rims, 48, LANES), BF16),
            pltpu.VMEM((rims, 8, LANES), F32),
            pltpu.VMEM((blocks_x - 2, 2 * owners, chunk), BF16),
        ]
        + pair_scratch(blocks_x, blocks_y, 2, listed),
        compiler_params=params(),
        cost_estimate=pl.CostEstimate(
            flops=4_000_000_000, bytes_accessed=400_000, transcendentals=1_300_000
        ),
        name="edge_pairs",
    )(codes, positions, masses, smoothing, prev, following, own, middle, rows, hot)
    sums, table = pl.pallas_call(
        functools.partial(rim_kernel, listed),
        out_shape=(shape(masses.shape, F32), shape((2, owners // 2, EARLY + 1, LANES), F32)),
        in_specs=[VMEM] * 14,
        out_specs=(VMEM, VMEM),
        scratch_shapes=[
            pltpu.VMEM((128, LANES), F32),
            pltpu.VMEM((6 * (blocks_x + 2), 8, LANES), F32),
            pltpu.VMEM((owners, LANES), F32),
            pltpu.VMEM((blocks_x, 2 * owners, chunk), BF16),
            pltpu.VMEM((LANES, 2 * owners), F32),
            pltpu.VMEM((9, 8, LANES), F32),
        ]
        + product_scratch(rims, listed)[1:],
        compiler_params=params(),
        cost_estimate=pl.CostEstimate(
            flops=200_000_000, bytes_accessed=400_000, transcendentals=400_000
        ),
        name="rim_pairs_and_table",
    )(
        codes, middle, edge, known, rim_match, rim_self, middle_moment,
        masses, smoothing, low, high, rows, hot, early,
    )
    density = sums * DENSITY_FACTOR / (smoothing * smoothing * smoothing)
    return (density, summed(to_owner(table), "dom"))


def solution(mesh):
    dom_count, sub_count = mesh.devices.shape
    mesh = jax.sharding.Mesh(
        mesh.devices.reshape(dom_count, sub_count // 2, 2), ("dom", "chip", "core")
    )
    sub = ("chip", "core")
    in_specs = (
        P(None, "dom", sub, None),
        P(None, "dom", sub, None),
        P("dom", sub, None),
        P("dom", sub, None),
        P("dom", sub, None),
        P("dom", sub, None),
        P(),
    )
    out_specs = (P("dom", sub, None), P(None, sub))
    return jax.shard_map(shards, mesh=mesh, in_specs=in_specs, out_specs=out_specs, check_vma=False)
```

```python
import functools
import math

import jax
import jax.numpy as jnp
from jax import lax
from jax.experimental import pallas as pl
from jax.experimental.pallas import tpu as pltpu
from jax.sharding import PartitionSpec as P

F32 = jnp.float32
BF16 = jnp.bfloat16
LANES = 128
EARLY = 16
DENSITY_FACTOR = 21.0 / (16.0 * math.pi) / 256.0
VMEM = pl.BlockSpec(memory_space=pltpu.VMEM)
NT = (((1,), (1,)), ((), ()))


def params():
    return pltpu.CompilerParams(vmem_limit_bytes=40 * 1024 * 1024)


def rounded(value):
    return value.astype(BF16).astype(F32)


def three_parts(value):
    first = rounded(value)
    rest = value - first
    second = rounded(rest)
    return first, second, rest - second


def spread(numbers, y, count):
    row = jnp.broadcast_to(numbers[y : y + 1, :].astype(F32), (16, LANES)).astype(BF16)
    return jnp.concatenate([row] * (count // 16), axis=0)


def row_numbers(count):
    return lax.broadcasted_iota(jnp.int32, (count, LANES), 0).astype(F32).astype(BF16)


def slot_one_hot(slots, y):
    return jnp.where(
        row_numbers(LANES) == spread(slots, y, LANES), jnp.ones((), BF16), jnp.zeros((), BF16)
    )


def moments_kernel(
    nx_total, ny_total, after_ref, pos_ref, vel_ref, mass_ref, group_ref, row_ref,
    table_ref, rows_ref, hot_ref, feat_ref, lhs_ref, total_ref,
):
    blocks_x, blocks_y, _ = mass_ref.shape
    owners = table_ref.shape[0]
    table_rows = row_ref.shape[0]
    base_x = (lax.axis_index("dom") * blocks_x).astype(F32)
    base_y = ((2 * lax.axis_index("chip") + lax.axis_index("core")) * blocks_y).astype(F32)
    y_iota = lax.broadcasted_iota(jnp.int32, (blocks_y, LANES), 0).astype(F32)

    def features_of(x):
        group = group_ref[x]
        low = group & (LANES - 1)
        high = group >> 7
        rows = jnp.zeros_like(group)
        for r in range(table_rows):
            line = jnp.broadcast_to(row_ref[r : r + 1, :], group.shape)
            picked = jnp.take_along_axis(line, low, axis=1)
            rows = jnp.where(high == r, picked, rows)
        rows_ref[x] = rows
        mass = mass_ref[x]
        gx = (base_x + float(x) + pos_ref[0, x]) / float(nx_total)
        gy = (base_y + y_iota + pos_ref[1, x]) / float(ny_total)
        gz = pos_ref[2, x]
        vx, vy, vz = vel_ref[0, x], vel_ref[1, x], vel_ref[2, x]
        mx, my, mz = mass * gx, mass * gy, mass * gz
        features = (
            mass, mx, my, mz, mass * vx, mass * vy, mass * vz,
            mass * (gy * vz - gz * vy), mass * (gz * vx - gx * vz), mass * (gx * vy - gy * vx),
            mx * gx, my * gy, mz * gz, mx * gy, mx * gz, my * gz,
        )
        for f, feature in enumerate(features):
            start = (x * EARLY + f) * blocks_y
            feat_ref[start : start + blocks_y, :] = feature

    def operands_of(x, y):
        lanes = slice(y * LANES, (y + 1) * LANES)
        feats = feat_ref[pl.ds(x * EARLY * blocks_y + y, EARLY, stride=blocks_y), :]
        high_part = rounded(feats)
        both = jnp.concatenate([high_part, feats - high_part], axis=0).astype(BF16)
        rows = rows_ref[x]
        owner_row = spread(rows >> 7, y, 2 * EARLY)
        for o in range(owners):
            lhs_ref[x, o * 2 * EARLY : (o + 1) * 2 * EARLY, lanes] = jnp.where(
                owner_row == jnp.asarray(o, BF16), both, jnp.zeros((), BF16)
            )
        hot_ref[x, :, lanes] = slot_one_hot(rows & (LANES - 1), y)

    def add_product(x):
        product = lax.dot_general(lhs_ref[x], hot_ref[x], NT, preferred_element_type=F32)
        total_ref[...] = product if x == 0 else total_ref[...] + product

    def finish():
        total = total_ref[...].reshape(owners, 2 * EARLY, LANES)
        table_ref[...] = total[:, :EARLY, :] + total[:, EARLY:, :]

    for x in range(blocks_x):
        features_of(x)
        for y in range(blocks_y):
            operands_of(x, y)
        add_product(x)
    finish()


def target_rows(pos, radius):
    weight = 4.0 / (radius * radius)
    cx, cy, cz = pos[0] - 0.5, pos[1] - 0.5, pos[2] - 0.5
    lines = (
        -2.0 * cx * weight, -2.0 * cy * weight, -2.0 * cz * weight,
        weight, weight, weight,
        (cx * cx + cy * cy + cz * cz) * weight, jnp.zeros_like(weight),
    )
    parts = [three_parts(line) for line in lines]
    return [part[k] for k in range(3) for part in parts]


def target_matrix(coef):
    one, two, three = coef[0:8], coef[8:16], coef[16:24]
    stacked = jnp.concatenate([one, one, two, two, one, three], axis=0)
    return stacked.T.astype(BF16)


def source_matrix(line, root, squares):
    value = jnp.where(squares, line * line, line) * (root * root)
    one, two, three = three_parts(value)
    first = jnp.concatenate([one, two], axis=0).astype(BF16)
    last = jnp.concatenate([three, one], axis=0).astype(BF16)
    return jnp.concatenate([first, first, last], axis=0)


def fifth_root(mass):
    root = jnp.exp(0.2 * jnp.log(mass))
    square = root * root
    return 0.8 * root + 0.2 * mass / (square * square)


def store_source(nat_ref, start, count, columns, mass):
    cx, cy, cz = [column - 0.5 for column in columns]
    one = jnp.ones_like(cx)
    for kind, line in enumerate((cx, cy, cz, cx, cy, cz, one, fifth_root(mass))):
        nat_ref[start + kind * 8 : start + kind * 8 + count, :] = line


def pair_sums(sides, pieces=()):
    rows = 32
    steps = []
    for target, sources, roots, total, base in sides:
        count = roots.shape[0]
        for first in range(0, count, 2):
            steps.append((target, sources, roots, total, base, first, min(2, count - first), count))

    def product(step):
        target, sources, _, _, _, first, width, _ = step
        right = sources[:, first * LANES : (first + width) * LANES]
        return jnp.dot(target[...], right, preferred_element_type=F32)

    ready = product(steps[0])
    chunks = None
    for number, (_, _, roots, total, base, first, width, count) in enumerate(steps):
        squared = ready
        if number + 1 < len(steps):
            ready = product(steps[number + 1])
        if first == 0:
            chunks = [None] * (LANES // rows)
            if base is not None:
                chunks = [base[r * rows : (r + 1) * rows, :] for r in range(len(chunks))]
        limits = []
        for k in range(width):
            root = roots[first + k : first + k + 1, :]
            reach = 4.0 * root
            limits.append(
                [jnp.broadcast_to(line, (rows, LANES)) for line in (root, reach, reach * reach)]
            )
        for r in range(len(chunks)):
            for k, (root, reach, most) in enumerate(limits):
                t = squared[r * rows : (r + 1) * rows, k * LANES : (k + 1) * LANES]
                t = jnp.maximum(jnp.minimum(t, most), 1e-12)
                u = t * lax.rsqrt(t)
                f = reach - u
                f = f * f
                f = f * f
                term = f * (root + u)
                chunks[r] = term if chunks[r] is None else chunks[r] + term
        if first + width == count:
            for r, chunk in enumerate(chunks):
                total[r * rows : (r + 1) * rows, :] = chunk
        if number < len(pieces) and pieces[number] is not None:
            pieces[number]()
    for piece in pieces[len(steps) :]:
        piece()


def column_sums(totals):
    lane = lax.broadcasted_iota(jnp.int32, (LANES, LANES), 1)
    columns = jnp.zeros((LANES, LANES), F32)
    for k, total in enumerate(totals):
        columns = jnp.where(lane == k, jnp.sum(total, axis=1, keepdims=True), columns)
    return columns.T[: len(totals), :]


def square_mask():
    kind = lax.broadcasted_iota(jnp.int32, (8, LANES), 0)
    return (kind >= 3) & (kind < 6)


def shift_rows(step_x, step_y):
    kind = lax.broadcasted_iota(jnp.int32, (8, LANES), 0)
    along_x = jnp.where((kind == 0) | (kind == 3), float(step_x), 0.0)
    return along_x + jnp.where((kind == 1) | (kind == 4), float(step_y), 0.0)


def put_shifts(shift_ref):
    for code in range(9):
        shift_ref[code] = shift_rows(code // 3 - 1, code % 3 - 1)


def put_source(near_ref, root_ref, number, k, line, shift, squares):
    root = jnp.broadcast_to(line[7:8], line.shape)
    near_ref[number, :, k * LANES : (k + 1) * LANES] = source_matrix(line + shift, root, squares)
    root_ref[number, k : k + 1, :] = root[0:1]


def sides_of(count, first, end, mat_ref, near_ref, root_ref, total_ref, base_ref=None):
    lanes, rows = pl.ds(first * LANES, (end - first) * LANES), pl.ds(first, end - first)
    return [
        (
            mat_ref.at[n], near_ref.at[n, :, lanes], root_ref.at[n, rows], total_ref.at[n],
            None if base_ref is None else base_ref.at[n],
        )
        for n in range(count)
    ]


def put_moments(lhs_ref, ys, sums, mass, radius, rows):
    owners = lhs_ref.shape[0] // 2
    owner_ids = lax.broadcasted_iota(jnp.int32, (owners, LANES), 0)
    moment = mass * (sums * DENSITY_FACTOR / (radius * radius * radius))
    high_part = rounded(moment)
    low_part = moment - high_part
    owner = rows >> 7
    for y in ys:
        mine = jnp.broadcast_to(owner[y : y + 1, :], owner_ids.shape) == owner_ids
        lhs_ref[:, y * LANES : (y + 1) * LANES] = jnp.concatenate(
            [
                jnp.where(mine, jnp.broadcast_to(part[y : y + 1, :], mine.shape), 0.0)
                for part in (high_part, low_part)
            ],
            axis=0,
        ).astype(BF16)


def inner_moments(total_ref, first, hot, lhs_ref, sums, mass, radius, rows):
    last = mass.shape[0] - 1
    put_moments(lhs_ref, range(1, last), sums, mass, radius, rows)
    lanes = slice(LANES, last * LANES)
    product = lax.dot_general(hot[:, lanes], lhs_ref[:, lanes], NT, preferred_element_type=F32)
    total_ref[...] = product if first else total_ref[...] + product


def start_rim(
    src_ref, pos_ref, mass_ref, smooth_ref, middle_ref, rows_ref, hot_ref,
    mat_ref, self_ref, moment_ref, tgt_ref, near_ref, root_ref, lhs_ref,
):
    blocks_x, blocks_y, _ = mass_ref.shape
    squares = square_mask()
    rim = [(x, side * (blocks_y - 1)) for x in range(blocks_x) for side in range(2)]
    for x in range(blocks_x):
        lines = target_rows([pos_ref[c, x] for c in range(3)], smooth_ref[x])
        for row, line in enumerate(lines):
            tgt_ref[x, row * blocks_y : (row + 1) * blocks_y, :] = line
    for n, (x, y) in enumerate(rim):
        mat_ref[n] = target_matrix(tgt_ref[x, pl.ds(y, 24, stride=blocks_y), :])
    for n, (x, y) in enumerate(rim):
        put_source(near_ref, root_ref, n, 0, src_ref[(x + 1) * blocks_y + y], 0.0, squares)

    def middle_moments(turn):
        x = turn + 1
        inner_moments(
            moment_ref, turn == 0, hot_ref[x], lhs_ref.at[turn], middle_ref[turn],
            mass_ref[x], smooth_ref[x], rows_ref[x],
        )

    pair_sums(
        sides_of(len(rim), 0, 1, mat_ref, near_ref, root_ref, self_ref),
        [functools.partial(middle_moments, turn) for turn in range(blocks_x - 2)],
    )


def block_pairs(
    listed, x_first, x_step, x_count, known_ref, code_ref, pos_ref, mass_ref, smooth_ref, prev_ref, next_ref,
    out_ref, src_ref, nat_ref, shift_ref, tgt_ref, mat_ref, near_ref, root_ref, total_ref,
    ahead=None,
):
    blocks_x, blocks_y, _ = mass_ref.shape
    for xe in range(blocks_x + 2):
        if xe == 0 or xe == blocks_x + 1:
            ref = prev_ref if xe == 0 else next_ref
            if ref is None:
                continue
            store_source(nat_ref, xe * 64, blocks_y, [ref[c] for c in range(3)], ref[3])
        elif known_ref is None:
            columns = [pos_ref[c, xe - 1] for c in range(3)]
            store_source(nat_ref, xe * 64, blocks_y, columns, mass_ref[xe - 1])
        else:
            part = pl.ds(xe * blocks_y, blocks_y)
            src_ref[part] = known_ref[part]
            continue
        for y in range(blocks_y):
            src_ref[xe * blocks_y + y] = nat_ref[pl.ds(xe * 64 + y, 8, stride=8), :]
    put_shifts(shift_ref)
    squares = square_mask()
    blocks = [(turn, y) for turn in range(x_count) for y in range(1, blocks_y - 1)]
    for turn in range(x_count):
        x = x_first + turn * x_step
        lines = target_rows([pos_ref[c, x] for c in range(3)], smooth_ref[x])
        for row, line in enumerate(lines):
            tgt_ref[turn, row * blocks_y : (row + 1) * blocks_y, :] = line
    for number, (turn, y) in enumerate(blocks):
        mat_ref[number] = target_matrix(tgt_ref[turn, pl.ds(y, 24, stride=blocks_y), :])
    for number, (turn, y) in enumerate(blocks):
        line = src_ref[(x_first + turn * x_step + 1) * blocks_y + y]
        put_source(near_ref, root_ref, number, 0, line, 0.0, squares)
    pair_sums(sides_of(len(blocks), 0, 1, mat_ref, near_ref, root_ref, total_ref))
    if ahead is not None:
        ahead()
    words = code_ref[...]
    for number, (turn, y) in enumerate(blocks):
        x = x_first + turn * x_step
        word = words[x, y]
        for k in range(1, listed):
            code = (word >> (4 * k)) & 15
            step_x = (code * 11) >> 5
            line = src_ref[(x + step_x) * blocks_y + y + code - 3 * step_x - 1]
            put_source(near_ref, root_ref, number, k, line, shift_ref[code], squares)
    inner = blocks_y - 2
    per_row = inner * (listed // 2)

    def row_sums(turn):
        sums = column_sums([total_ref[turn * inner + k] for k in range(inner)])
        out_ref[turn, 1 : blocks_y - 1, :] = sums

    pieces = [None] * (x_count * per_row + 1)
    for turn in range(x_count):
        pieces[(turn + 1) * per_row] = functools.partial(row_sums, turn)
    sides = sides_of(len(blocks), 1, listed, mat_ref, near_ref, root_ref, total_ref, total_ref)
    pair_sums(sides, pieces)


def middle_kernel(
    listed, code_ref, pos_ref, mass_ref, smooth_ref, group_ref, row_ref, column_ref, out_ref, src_ref, *scratch
):
    blocks_x, blocks_y, _ = mass_ref.shape
    for side in range(2):
        y = side * (blocks_y - 1)
        for x in range(blocks_x):
            for c in range(3):
                column_ref[side, c, x : x + 1, :] = pos_ref[c, x, y : y + 1, :]
            column_ref[side, 3, x : x + 1, :] = mass_ref[x, y : y + 1, :]
    block_pairs(
        listed, 1, 1, blocks_x - 2, None, code_ref, pos_ref, mass_ref, smooth_ref, None, None,
        out_ref, src_ref, *scratch,
    )


def edge_kernel(
    listed, code_ref, pos_ref, mass_ref, smooth_ref, prev_ref, next_ref, known_ref,
    middle_ref, rows_ref, hot_ref,
    out_ref, src_ref, rim_mat_ref, self_ref, moment_ref,
    rim_tgt_ref, rim_near_ref, rim_root_ref, lhs_ref, *scratch
):
    blocks_x = mass_ref.shape[0]
    ahead = functools.partial(
        start_rim, src_ref, pos_ref, mass_ref, smooth_ref, middle_ref, rows_ref, hot_ref,
        rim_mat_ref, self_ref, moment_ref, rim_tgt_ref, rim_near_ref, rim_root_ref, lhs_ref,
    )
    block_pairs(
        listed, 0, blocks_x - 1, 2, known_ref, code_ref, pos_ref, mass_ref, smooth_ref, prev_ref, next_ref,
        out_ref, src_ref, *scratch, ahead=ahead,
    )


def pair_scratch(blocks_x, blocks_y, x_count, listed):
    return [
        pltpu.VMEM(((blocks_x + 2) * 64, LANES), F32),
        pltpu.VMEM((9, 8, LANES), F32),
        pltpu.VMEM((x_count, 24 * blocks_y, LANES), F32),
    ] + product_scratch(x_count * (blocks_y - 2), listed)


def product_scratch(blocks, listed):
    return [
        pltpu.VMEM((blocks, LANES, 48), BF16),
        pltpu.VMEM((blocks, 48, listed * LANES), BF16),
        pltpu.VMEM((blocks, 8, LANES), F32),
        pltpu.VMEM((blocks, LANES, LANES), F32),
    ]


def rim_kernel(
    listed, code_ref, middle_ref, edge_ref, known_ref, mat_ref, self_ref, moment_ref,
    mass_ref, smooth_ref, low_ref, high_ref, rows_ref, hot_ref, early_ref,
    sum_ref, table_ref, nat_ref, src_ref, md_ref, lhs_ref, total_moment_ref,
    shift_ref, near_ref, root_ref, total_ref,
):
    blocks_x, blocks_y, _ = mass_ref.shape
    owners = early_ref.shape[0]
    wide = blocks_x + 2
    last = blocks_y - 1
    for side, ref in enumerate((low_ref, high_ref)):
        store_source(nat_ref, side * 64, wide, [ref[c] for c in range(3)], ref[3])
        for xe in range(wide):
            ghost = 5 * side * wide + xe
            src_ref[ghost] = nat_ref[pl.ds(side * 64 + xe, 8, stride=8), :]
            for k in range(2):
                y = k + side * (blocks_y - 2)
                place = (1 + k + 2 * side) * wide + xe
                src_ref[place] = known_ref[xe * blocks_y + y]
    put_shifts(shift_ref)
    squares = square_mask()
    for x in range(blocks_x):
        edge = x == 0 or x == blocks_x - 1
        sum_ref[x] = (edge_ref if edge else middle_ref)[(1 if x else 0) if edge else x - 1]
    total_moment_ref[...] = moment_ref[...]
    for x in (0, blocks_x - 1):
        inner_moments(
            total_moment_ref, False, hot_ref[x], lhs_ref.at[x], sum_ref[x],
            mass_ref[x], smooth_ref[x], rows_ref[x],
        )
    words = code_ref[...]
    for x in range(blocks_x):
        for side in range(2):
            word = words[x, side * last]
            for k in range(1, listed):
                code = (word >> (4 * k)) & 15
                step_x = (code * 11) >> 5
                line = src_ref[(3 * side + code - 3 * step_x) * wide + x + step_x]
                put_source(near_ref, root_ref, 2 * x + side, k, line, shift_ref[code], squares)
    pair_sums(sides_of(2 * blocks_x, 1, listed, mat_ref, near_ref, root_ref, total_ref, self_ref))
    sums = column_sums([total_ref[number] for number in range(2 * blocks_x)])
    for x in range(blocks_x):
        for side in range(2):
            y = side * last
            sum_ref[x, y : y + 1, :] = sums[2 * x + side : 2 * x + side + 1, :]
        put_moments(lhs_ref.at[x], (0, last), sum_ref[x], mass_ref[x], smooth_ref[x], rows_ref[x])
    ends = [(x, slice(y * LANES, (y + 1) * LANES)) for x in range(blocks_x) for y in (0, last)]
    total = total_moment_ref[...] + lax.dot_general(
        jnp.concatenate([hot_ref[x, :, lanes] for x, lanes in ends], axis=1),
        jnp.concatenate([lhs_ref[x, :, lanes] for x, lanes in ends], axis=1),
        NT,
        preferred_element_type=F32,
    )
    total = total.T
    md_ref[...] = total[:owners] + total[owners:]
    core, my_chip = lax.axis_index("core"), lax.axis_index("chip")
    for other in range(2):
        for step in range(owners // 2):
            owner = 2 * (my_chip ^ step) + (core ^ other)
            table_ref[other, step, :EARLY, :] = early_ref[owner]
            table_ref[other, step, EARLY : EARLY + 1, :] = md_ref[pl.ds(owner, 1), :]


def swap(value, axis, step):
    count = lax.axis_size(axis)
    return lax.ppermute(value, axis, [(i, i ^ step) for i in range(count)])


def neighbours_of(low_edge, high_edge, axis, odd):
    count = lax.axis_size(axis)
    inner = lax.ppermute(
        jnp.where(odd, low_edge, high_edge), axis, [(i, i ^ 1) for i in range(count)]
    )
    outer = lax.ppermute(
        jnp.where(odd, high_edge, low_edge),
        axis,
        [(i, (i + 1 if i & 1 else i - 1) % count) for i in range(count)],
    )
    return inner, outer


def added(parts):
    while len(parts) > 1:
        parts = [sum(parts[k : k + 2][1:], parts[k]) for k in range(0, len(parts), 2)]
    return parts[0]


def to_owner(table):
    table = table[0] + swap(table[1], "core", 1)
    while table.shape[0] > 1:
        ways = min(4, table.shape[0])
        part = table.shape[0] // ways
        got = [
            swap(table[k * part : (k + 1) * part], "chip", k * part)
            for k in sorted(range(1, ways), key=lambda step: (step == 1, step))
        ]
        table = added([table[:part]] + got)
    return table[0]


def summed(value, axis):
    count = lax.axis_size(axis)
    if count & (count - 1):
        return lax.psum(value, axis)
    step = 1
    while step < count:
        ways = min(4, count // step)
        value = added([value] + [swap(value, axis, k * step) for k in range(1, ways)])
        step *= ways
    return value


def shards(positions, velocities, masses, smoothing, neighbours, particle_group, group_row):
    blocks_x, blocks_y, block_len = masses.shape
    dom_count, sub_count = lax.axis_size("dom"), lax.axis_size("chip") * lax.axis_size("core")
    owners = sub_count
    chunk = blocks_y * block_len
    shape = jax.ShapeDtypeStruct
    listed = neighbours.shape[2]
    codes = sum(neighbours[:, :, k] << (4 * k) for k in range(listed))
    table_rows = group_row.reshape(-1, LANES)
    packed = jnp.concatenate([positions, masses[None]], axis=0)
    odd_dom, odd_sub = (lax.axis_index("dom") & 1) == 1, lax.axis_index("core") == 1
    inner, outer = neighbours_of(packed[:, 0], packed[:, blocks_x - 1], "dom", odd_dom)
    even_dom = jnp.logical_not(odd_dom)
    prev, following = jnp.where(even_dom, outer, inner), jnp.where(even_dom, inner, outer)
    sources = ((blocks_x + 2) * blocks_y, 8, LANES)
    columns, middle, own = pl.pallas_call(
        functools.partial(middle_kernel, listed),
        out_shape=(
            shape((2, 4, blocks_x, LANES), F32),
            shape((blocks_x - 2, blocks_y, LANES), F32),
            shape(sources, F32),
        ),
        in_specs=[VMEM] * 6,
        out_specs=(VMEM,) * 3,
        scratch_shapes=pair_scratch(blocks_x, blocks_y, blocks_x - 2, listed),
        compiler_params=params(),
        cost_estimate=pl.CostEstimate(
            flops=4_000_000_000, bytes_accessed=400_000, transcendentals=1_300_000
        ),
        name="middle_pairs",
    )(codes, positions, masses, smoothing, particle_group, table_rows)
    early, rows, hot = pl.pallas_call(
        functools.partial(moments_kernel, blocks_x * dom_count, blocks_y * sub_count),
        out_shape=(
            shape((owners, EARLY, LANES), F32),
            shape(masses.shape, jnp.int32),
            shape((blocks_x, LANES, chunk), BF16),
        ),
        in_specs=[VMEM] * 6,
        out_specs=(VMEM,) * 3,
        scratch_shapes=[
            pltpu.VMEM((blocks_x * EARLY * blocks_y, LANES), F32),
            pltpu.VMEM((blocks_x, owners * 2 * EARLY, chunk), BF16),
            pltpu.VMEM((owners * 2 * EARLY, LANES), F32),
        ],
        compiler_params=params(),
        cost_estimate=pl.CostEstimate(
            flops=2_000_000_000, bytes_accessed=1_400_000, transcendentals=0
        ),
        name="moments_by_row",
    )(middle, positions, velocities, masses, particle_group, table_rows)
    edges = [
        jnp.concatenate([prev[:, y : y + 1], columns[side], following[:, y : y + 1]], axis=1)
        for side, y in ((0, 0), (1, blocks_y - 1))
    ]
    inner, outer = neighbours_of(*edges, ("chip", "core"), odd_sub)
    low, high = jnp.where(odd_sub, inner, outer), jnp.where(odd_sub, outer, inner)
    rims = 2 * blocks_x
    edge, known, rim_match, rim_self, middle_moment = pl.pallas_call(
        functools.partial(edge_kernel, listed),
        out_shape=(
            shape((2, blocks_y, LANES), F32),
            shape(sources, F32),
            shape((rims, LANES, 48), BF16),
            shape((rims, LANES, LANES), F32),
            shape((LANES, 2 * owners), F32),
        ),
        in_specs=[VMEM] * 10,
        out_specs=(VMEM,) * 5,
        scratch_shapes=[
            pltpu.VMEM((blocks_x, 24 * blocks_y, LANES), F32),
            pltpu.VMEM((rims, 48, LANES), BF16),
            pltpu.VMEM((rims, 8, LANES), F32),
            pltpu.VMEM((blocks_x - 2, 2 * owners, chunk), BF16),
        ]
        + pair_scratch(blocks_x, blocks_y, 2, listed),
        compiler_params=params(),
        cost_estimate=pl.CostEstimate(
            flops=4_000_000_000, bytes_accessed=400_000, transcendentals=1_300_000
        ),
        name="edge_pairs",
    )(codes, positions, masses, smoothing, prev, following, own, middle, rows, hot)
    sums, table = pl.pallas_call(
        functools.partial(rim_kernel, listed),
        out_shape=(shape(masses.shape, F32), shape((2, owners // 2, EARLY + 1, LANES), F32)),
        in_specs=[VMEM] * 14,
        out_specs=(VMEM, VMEM),
        scratch_shapes=[
            pltpu.VMEM((128, LANES), F32),
            pltpu.VMEM((6 * (blocks_x + 2), 8, LANES), F32),
            pltpu.VMEM((owners, LANES), F32),
            pltpu.VMEM((blocks_x, 2 * owners, chunk), BF16),
            pltpu.VMEM((LANES, 2 * owners), F32),
            pltpu.VMEM((9, 8, LANES), F32),
        ]
        + product_scratch(rims, listed)[1:],
        compiler_params=params(),
        cost_estimate=pl.CostEstimate(
            flops=200_000_000, bytes_accessed=400_000, transcendentals=400_000
        ),
        name="rim_pairs_and_table",
    )(
        codes, middle, edge, known, rim_match, rim_self, middle_moment,
        masses, smoothing, low, high, rows, hot, early,
    )
    density = sums * DENSITY_FACTOR / (smoothing * smoothing * smoothing)
    return (density, summed(to_owner(table), "dom"))


def solution(mesh):
    dom_count, sub_count = mesh.devices.shape
    mesh = jax.sharding.Mesh(
        mesh.devices.reshape(dom_count, sub_count // 2, 2), ("dom", "chip", "core")
    )
    sub = ("chip", "core")
    in_specs = (
        P(None, "dom", sub, None),
        P(None, "dom", sub, None),
        P("dom", sub, None),
        P("dom", sub, None),
        P("dom", sub, None),
        P("dom", sub, None),
        P(),
    )
    out_specs = (P("dom", sub, None), P(None, sub))
    return jax.shard_map(shards, mesh=mesh, in_specs=in_specs, out_specs=out_specs, check_vma=False)
```
